32 devices in a mesh: fsdp: 32 (over z, y, x, core).
Axes of the slice: x: 2, y: 2, z: 4, core: 2. Of those that a mesh axis runs over, the one named last changes fastest.
Arguments:
- tokens: bfloat16 [8192, 2048], P('fsdp'), may hold values from -6 to 6
- block_of: int32 [8192], P('fsdp'), may hold values from 0 to 7, as said below
- clip_limit: int32 [], replicated, may hold values from 4 to 9
- norm_attn: bfloat16 [2048], P('fsdp'), may hold values from 0.5 to 1.5
- w_query: bfloat16 [2048, 2048], P('fsdp'), may hold values from -0.3314563 to 0.3314563
- w_key: bfloat16 [2048, 2048], P('fsdp'), may hold values from -0.125 to 0.125
- w_value: bfloat16 [2048, 2048], P('fsdp'), may hold values from -0.125 to 0.125
- w_out: bfloat16 [2048, 2048], P('fsdp'), may hold values from -0.5 to 0.5
- norm_ffn: bfloat16 [2048], P('fsdp'), may hold values from 0.5 to 1.5
- w_gate: bfloat16 [2048, 8192], P('fsdp'), may hold values from -0.125 to 0.125
- w_up: bfloat16 [2048, 8192], P('fsdp'), may hold values from -0.125 to 0.125
- w_down: bfloat16 [8192, 2048], P('fsdp'), may hold values from -0.0625 to 0.0625
- cotangent: bfloat16 [8192, 2048], P('fsdp'), may hold values from -6 to 6
Outputs:
- mixed: bfloat16 [8192, 2048], P('fsdp')
- d_tokens: float32 [8192, 2048], P('fsdp')
- d_norm_attn: float32 [2048], P('fsdp')
- d_query: float32 [2048, 2048], P('fsdp')
- d_key: float32 [2048, 2048], P('fsdp')
- d_value: float32 [2048, 2048], P('fsdp')
- d_out: float32 [2048, 2048], P('fsdp')
- d_norm_ffn: float32 [2048], P('fsdp')
- d_gate: float32 [2048, 8192], P('fsdp')
- d_up: float32 [2048, 8192], P('fsdp')
- d_down: float32 [8192, 2048], P('fsdp')
- head_peak: float32 [32], replicated
- clipped_query: bfloat16 [2048, 2048], P('fsdp')
- clipped_key: bfloat16 [2048, 2048], P('fsdp')
The draws below stay inside these ranges and needn't reach their ends.
Inputs may be any that keep to these rules, and one draw needn't show every extreme that they name: `block_of`: within each sequence of 2048 tokens the block number starts at 0 and never falls; block j begins at a position between j * 256 - 256 // 2 + 1 and j * 256.
All inputs are finite; a program needn't handle non-finite values.
Results may differ from the reference program's by a relative error of at most 0.015.
Values may be sent and summed in bfloat16 or wider, within the bound.
A program may use at most 832 MiB of HBM per device.

```python
import math
import jax
import jax.numpy as jnp
from jax import lax

D = 2048
HEADS = 32
HEAD_DIM = 64
FF = 8192
SEQ = 2048
BLOCK = 256
TOKENS = 8192


def draw_block_of(key, part):
    key = jax.random.fold_in(key, 11)
    seq_total = TOKENS // SEQ
    block_count = SEQ // BLOCK
    pulled = jax.random.randint(key, (seq_total, block_count), 0, BLOCK // 2)
    starts = jnp.arange(block_count, dtype=jnp.int32)[None, :] * BLOCK - pulled
    positions = jnp.arange(SEQ, dtype=jnp.int32)
    passed = (positions[None, :, None] >= starts[:, None, 1:]).astype(jnp.int32)
    return jnp.sum(passed, -1).reshape(TOKENS).astype(jnp.int32)


def draw_w_query(key, part):
    key = jax.random.fold_in(key, 5)
    standard = jnp.clip(jax.random.normal(jax.random.fold_in(key, 1), (D, D), jnp.float32), -6.0, 6.0) / math.sqrt(D)
    spread = jnp.exp(jax.random.uniform(jax.random.fold_in(key, 2), (HEADS,), jnp.float32, math.log(0.8), math.log(2.5)))
    return (standard * jnp.repeat(spread, HEAD_DIM)[None, :]).astype(jnp.bfloat16)


def steps_of(key, shape, cuts, low, top_value):
    factor_of, own = 1.0, jax.random.fold_in(key, 6)
    for position, parts in cuts:
        draws = jnp.exp(jax.random.uniform(jax.random.fold_in(own, position), (parts,), jnp.float32, low / len(cuts), top_value / len(cuts)))
        factor_of = factor_of * jnp.repeat(draws, shape[position] // parts).reshape([-1 if axis == position else 1 for axis in range(len(shape))])
    return factor_of


def centred(stream_key, dims, scale, limit, split=(), held_as=jnp.bfloat16):
    values = scale * jax.random.normal(stream_key, dims, jnp.float32)
    if split:
        values = values * steps_of(stream_key, dims, split, -0.22, 0.18)
    return jnp.clip(values, -limit, limit).astype(held_as)


def setup_inputs(seed: int = 0) -> dict:
    streams_of = jax.random.split(jax.random.key(seed), 14)
    tokens = centred(streams_of[0], (TOKENS, D), 1.0, 6.0, ((0, 32),))
    block_of = draw_block_of(jax.random.fold_in(streams_of[13], 71), 0)
    clip_limit = jax.random.randint(streams_of[2], (), 4, 10).astype(jnp.int32)
    norm_attn = jnp.clip(1.0 + 0.1 * jax.random.normal(streams_of[3], (D,), jnp.float32), 0.5, 1.5).astype(jnp.bfloat16)
    w_query = draw_w_query(jax.random.fold_in(streams_of[13], 71), 0)
    w_key = centred(streams_of[5], (D, D), D ** -0.5, 0.125, ((0, 32),))
    w_value = centred(streams_of[6], (D, D), D ** -0.5, 0.125, ((0, 32),))
    w_out = centred(streams_of[7], (D, D), (D // 16) ** -0.5, 0.5, ((0, 32),))
    norm_ffn = jnp.clip(1.0 + 0.1 * jax.random.normal(streams_of[8], (D,), jnp.float32), 0.5, 1.5).astype(jnp.bfloat16)
    w_gate = centred(streams_of[9], (D, FF), D ** -0.5, 0.125, ((0, 32),))
    w_up = centred(streams_of[10], (D, FF), D ** -0.5, 0.125, ((0, 32),))
    w_down = centred(streams_of[11], (FF, D), FF ** -0.5, 0.0625, ((0, 32),))
    cotangent = centred(streams_of[12], (TOKENS, D), 1.0, 6.0, ((0, 32),))
    return {"tokens": tokens, "block_of": block_of, "clip_limit": clip_limit, "norm_attn": norm_attn, "w_query": w_query, "w_key": w_key, "w_value": w_value, "w_out": w_out, "norm_ffn": norm_ffn, "w_gate": w_gate, "w_up": w_up, "w_down": w_down, "cotangent": cotangent}


epsilon = 1e-05
rope_base = 130000.0

@jax.custom_vjp
def low(v):
    return lax.optimization_barrier(v.astype(jnp.bfloat16)).astype(jnp.float32)

@jax.custom_vjp
def low_back(v):
    return v

def low_keep(v):
    return (low(v), None)

def low_pass(kept, grad):
    return (grad,)

def back_keep(v):
    return (v, None)

def back_low(kept, grad):
    return (low(grad),)
low.defvjp(low_keep, low_pass)
low_back.defvjp(back_keep, back_low)

def matmul(left, right):
    return jnp.dot(left, right, precision=lax.Precision.HIGHEST)

def rope_tables(length):
    half_dim = HEAD_DIM // 2
    inverse = rope_base ** (-jnp.arange(half_dim, dtype=jnp.float32) * 2.0 / HEAD_DIM)
    angles = jnp.arange(length, dtype=jnp.float32)[:, None] * inverse[None, :]
    return (jnp.cos(angles), jnp.sin(angles))

def rotate(stacked, cosine_table, sine_table):
    half_dim = stacked.shape[-1] // 2
    first_half = stacked[..., :half_dim]
    second_half = stacked[..., half_dim:]
    cos_rows = cosine_table[:, None, :]
    sin_rows = sine_table[:, None, :]
    return jnp.concatenate([first_half * cos_rows - second_half * sin_rows, second_half * cos_rows + first_half * sin_rows], -1)

def rms_norm(hidden_in, gain_in):
    return hidden_in * lax.rsqrt(lax.optimization_barrier(jnp.mean(hidden_in * hidden_in, -1, keepdims=True)) + epsilon) * gain_in

def layer_seq(inputs, blocks, gain_attn, query_weight, key_weight, value_weight, out_weight, gain_ffn, gate_weight, up_weight, down_weight):
    cosine_table, sine_table = rope_tables(SEQ)
    normed_attn = low(rms_norm(inputs, gain_attn))

    def as_heads(matrix):
        return matrix.reshape(SEQ, HEADS, HEAD_DIM)
    query_heads = low(rotate(as_heads(low_back(matmul(normed_attn, query_weight))), cosine_table, sine_table))
    key_heads = low(rotate(as_heads(low_back(matmul(normed_attn, key_weight))), cosine_table, sine_table))
    value_heads = low(as_heads(low_back(matmul(normed_attn, value_weight))))
    visible = blocks[None, :] <= blocks[:, None]

    def one_head(operands):
        query_head, key_head, value_head = operands
        scores = low_back(matmul(query_head, key_head.T) * HEAD_DIM ** (-0.5))
        masked = jnp.where(visible, scores, -jnp.inf)
        row_max = lax.optimization_barrier(jnp.max(masked, -1, keepdims=True))
        numerators = jnp.exp(masked - row_max)
        attention = numerators / lax.optimization_barrier(jnp.sum(numerators, -1, keepdims=True))
        return (matmul(low(attention), value_head), jnp.max(row_max))
    head_out, head_peaks = lax.map(jax.checkpoint(one_head), (query_heads.transpose(1, 0, 2), key_heads.transpose(1, 0, 2), value_heads.transpose(1, 0, 2)))
    attended = low(low_back(head_out.transpose(1, 0, 2).reshape(SEQ, D)))
    after_attn = inputs + low_back(matmul(attended, out_weight))
    normed_ffn = low(rms_norm(after_attn, gain_ffn))
    gate_pre = low_back(matmul(normed_ffn, gate_weight))
    up_pre = low_back(matmul(normed_ffn, up_weight))
    hidden = low(jax.nn.silu(gate_pre) * up_pre)
    return (after_attn + low_back(matmul(hidden, down_weight)), head_peaks)

def reference(tokens, block_of, clip_limit, norm_attn, w_query, w_key, w_value, w_out, norm_ffn, w_gate, w_up, w_down, cotangent):
    weights = tuple((weight_arg.astype(jnp.float32) for weight_arg in (norm_attn, w_query, w_key, w_value, w_out, norm_ffn, w_gate, w_up, w_down)))
    seq_count = tokens.shape[0] // SEQ
    inputs = tokens.astype(jnp.float32).reshape(seq_count, SEQ, D)
    blocks = block_of.reshape(seq_count, SEQ)

    def forward(inputs_in, weights_in):

        def one_sequence(operands):
            return layer_seq(operands[0], operands[1], *weights_in)
        return lax.map(one_sequence, (inputs_in, blocks))
    outputs, pullback, head_peaks = jax.vjp(forward, inputs, weights, has_aux=True)
    d_inputs, d_weights = pullback(cotangent.astype(jnp.float32).reshape(seq_count, SEQ, D))
    head_peak = lax.optimization_barrier(jnp.max(head_peaks, 0))
    clip_value = clip_limit.astype(jnp.float32)
    factor = jnp.sqrt(clip_value / jnp.maximum(head_peak, clip_value))
    columns = jnp.repeat(factor, HEAD_DIM)
    clipped_query = (w_query.astype(jnp.float32) * columns[None, :]).astype(jnp.bfloat16)
    clipped_key = (w_key.astype(jnp.float32) * columns[None, :]).astype(jnp.bfloat16)
    return (outputs.reshape(TOKENS, D).astype(jnp.bfloat16), d_inputs.reshape(TOKENS, D), d_weights[0], d_weights[1], d_weights[2], d_weights[3], d_weights[4], d_weights[5], d_weights[6], d_weights[7], d_weights[8], head_peak, clipped_query, clipped_key)
```

```python
import functools

import jax
import jax.numpy as jnp
from jax import lax
from jax.experimental import pallas as pl
from jax.experimental.pallas import tpu as pltpu
from jax.sharding import PartitionSpec as P

HEAD_DIM = 64
SEQ = 2048
BLOCK = 256
AXIS = "fsdp"
MESH = pl.DeviceIdType.MESH

epsilon = 1e-05
rope_base = 130000.0
bf16 = jnp.bfloat16
f32 = jnp.float32


def contract(left, right, left_dim, right_dim):
    return lax.dot_general(
        left, right, (((left_dim,), (right_dim,)), ((), ())), preferred_element_type=f32
    )


def rope_tables(length, width):
    half_dim = HEAD_DIM // 2
    inverse = rope_base ** (-jnp.arange(half_dim, dtype=f32) * 2.0 / HEAD_DIM)
    angles = jnp.arange(length, dtype=f32)[:, None] * inverse[None, :]
    cosine, sine = jnp.cos(angles), jnp.sin(angles)
    repeats = width // HEAD_DIM
    return (
        jnp.tile(jnp.concatenate([cosine, cosine], 1), (1, repeats)),
        jnp.tile(jnp.concatenate([-sine, sine], 1), (1, repeats)),
    )


def swap_halves(rows):
    width = rows.shape[1]
    half = HEAD_DIM // 2
    lane = lax.broadcasted_iota(jnp.int32, rows.shape, 1)
    return jnp.where(
        lane % HEAD_DIM < half, pltpu.roll(rows, width - half, 1), pltpu.roll(rows, half, 1)
    )


def head_mask(shape, head):
    lane = lax.broadcasted_iota(jnp.int32, shape, 1)
    return (lane >= head * HEAD_DIM) & (lane < (head + 1) * HEAD_DIM)


def visible_tail(row_ref, col_ref, q0, cols):
    tail = min(2 * BLOCK, cols)
    q_blocks = col_ref[pl.ds(q0, BLOCK), :]
    k_blocks = row_ref[:, pl.ds(cols - tail, tail)]
    return k_blocks <= q_blocks


def attend_forward_kernel(
    heads, qkv_ref, cos_ref, sin_ref, row_ref, col_ref, q_ref, k_ref, v_ref, out_ref, lse_ref, peak_ref
):
    length = qkv_ref.shape[0]
    width = heads * HEAD_DIM
    for t in range(length // BLOCK):
        rows = pl.ds(t * BLOCK, BLOCK)
        cosine, sine = cos_ref[rows, :], sin_ref[rows, :]
        query = qkv_ref[rows, 0:width]
        q_ref[rows, :] = ((query * cosine + swap_halves(query) * sine).astype(bf16).astype(f32)
                          * HEAD_DIM ** (-0.5)).astype(bf16)
        key = qkv_ref[rows, width : 2 * width]
        k_ref[rows, :] = (key * cosine + swap_halves(key) * sine).astype(bf16)
        v_ref[rows, :] = qkv_ref[rows, 2 * width : 3 * width].astype(bf16)
    peak_ref[...] = jnp.full(peak_ref.shape, -jnp.inf, f32)
    for t in range(length // BLOCK):
        q0 = t * BLOCK
        rows = pl.ds(q0, BLOCK)
        cols = min(q0 + 2 * BLOCK, length)
        tail = min(2 * BLOCK, cols)

        def one_head(head, total):
            query = jnp.where(head_mask((BLOCK, width), head), q_ref[rows, :], 0).astype(bf16)
            scores = contract(query, k_ref[0:cols, :], 1, 1)
            hidden = jnp.where(visible_tail(row_ref, col_ref, q0, cols), scores[:, cols - tail :], -jnp.inf)
            if tail < cols:
                scores = jnp.concatenate([scores[:, : cols - tail], hidden], 1)
            else:
                scores = hidden
            row_max = jnp.max(scores, 1, keepdims=True)
            numerators = jnp.exp(scores - row_max)
            totals = jnp.sum(numerators, 1, keepdims=True)
            mixed = contract(numerators.astype(bf16), v_ref[0:cols, :], 1, 0) / totals
            lse_ref[rows, pl.ds(0, 128)] = jnp.where(
                lax.broadcasted_iota(jnp.int32, (BLOCK, 128), 1) == head,
                row_max + jnp.log(totals),
                lse_ref[rows, pl.ds(0, 128)],
            )
            peak_ref[...] = jnp.where(
                lax.broadcasted_iota(jnp.int32, peak_ref.shape, 1) == head,
                jnp.maximum(peak_ref[...], jnp.max(row_max)),
                peak_ref[...],
            )
            return jnp.where(head_mask((BLOCK, width), head), mixed, total)

        total = lax.fori_loop(0, heads, one_head, jnp.zeros((BLOCK, width), f32))
        out_ref[rows, :] = total.astype(bf16)


def attend_forward(qkv, cosine, sine, blocks, heads):
    length = qkv.shape[0]
    width = heads * HEAD_DIM
    shape = jax.ShapeDtypeStruct
    return pl.pallas_call(
        functools.partial(attend_forward_kernel, heads),
        out_shape=(
            shape((length, width), bf16),
            shape((length, width), bf16),
            shape((length, width), bf16),
            shape((length, width), bf16),
            shape((length, 128), f32),
            shape((8, 128), f32),
        ),
        in_specs=[pl.BlockSpec(memory_space=pltpu.VMEM)] * 5,
        out_specs=tuple([pl.BlockSpec(memory_space=pltpu.VMEM)] * 6),
        compiler_params=pltpu.CompilerParams(vmem_limit_bytes=56 * 1024 * 1024),
        cost_estimate=pl.CostEstimate(
            flops=8 * heads * length * length * HEAD_DIM, bytes_accessed=length * width * 24,
            transcendentals=heads * length * length,
        ),
        name="attend_forward",
    )(qkv, cosine, sine, blocks.reshape(1, length), blocks.reshape(length, 1))


def attend_backward_kernel(
    heads, q_ref, k_ref, v_ref, grad_ref, lse_ref, cos_ref, sin_ref, row_ref, col_ref, out_ref, dk_ref, dv_ref
):
    length = q_ref.shape[0]
    width = heads * HEAD_DIM
    dk_ref[...] = jnp.zeros_like(dk_ref)
    dv_ref[...] = jnp.zeros_like(dv_ref)
    for t in range(length // BLOCK):
        q0 = t * BLOCK
        rows = pl.ds(q0, BLOCK)
        cols = min(q0 + 2 * BLOCK, length)
        tail = min(2 * BLOCK, cols)

        def one_head(head, dq):
            mask = head_mask((BLOCK, width), head)
            query = jnp.where(mask, q_ref[rows, :], 0).astype(bf16)
            grad = jnp.where(mask, grad_ref[rows, :], 0).astype(bf16)
            lse = jnp.sum(
                jnp.where(
                    lax.broadcasted_iota(jnp.int32, (BLOCK, 128), 1) == head, lse_ref[rows, :], 0.0
                ),
                1,
                keepdims=True,
            )
            scores = contract(query, k_ref[0:cols, :], 1, 1)
            hidden = jnp.where(visible_tail(row_ref, col_ref, q0, cols), scores[:, cols - tail :], -jnp.inf)
            if tail < cols:
                scores = jnp.concatenate([scores[:, : cols - tail], hidden], 1)
            else:
                scores = hidden
            attention = jnp.exp(scores - lse)
            grad_attention = contract(grad, v_ref[0:cols, :], 1, 1)
            weighted = attention * grad_attention
            centre = jnp.sum(weighted, 1, keepdims=True)
            grad_scores = (weighted - attention * centre).astype(bf16)
            dv_ref[0:cols, :] += contract(attention.astype(bf16), grad, 0, 0)
            dk_ref[0:cols, :] += contract(grad_scores, query, 0, 0)
            return jnp.where(mask, contract(grad_scores, k_ref[0:cols, :], 1, 0), dq)

        dq = lax.fori_loop(0, heads, one_head, jnp.zeros((BLOCK, width), f32)) * HEAD_DIM ** (-0.5)
        out_ref[rows, 0:width] = (
            dq * cos_ref[rows, :] - swap_halves(dq) * sin_ref[rows, :]
        ).astype(bf16)
    for t in range(length // BLOCK):
        rows = pl.ds(t * BLOCK, BLOCK)
        dk = dk_ref[rows, :]
        out_ref[rows, width : 2 * width] = (
            dk * cos_ref[rows, :] - swap_halves(dk) * sin_ref[rows, :]
        ).astype(bf16)
        out_ref[rows, 2 * width : 3 * width] = dv_ref[rows, :].astype(bf16)


def attend_backward(query, key, value, grad, lse, cosine, sine, blocks, heads):
    length = query.shape[0]
    width = heads * HEAD_DIM
    return pl.pallas_call(
        functools.partial(attend_backward_kernel, heads),
        out_shape=jax.ShapeDtypeStruct((length, 3 * width), bf16),
        in_specs=[pl.BlockSpec(memory_space=pltpu.VMEM)] * 9,
        out_specs=pl.BlockSpec(memory_space=pltpu.VMEM),
        scratch_shapes=[pltpu.VMEM((length, width), f32), pltpu.VMEM((length, width), f32)],
        compiler_params=pltpu.CompilerParams(vmem_limit_bytes=56 * 1024 * 1024),
        cost_estimate=pl.CostEstimate(
            flops=20 * heads * length * length * HEAD_DIM, bytes_accessed=length * width * 24,
            transcendentals=heads * length * length,
        ),
        name="attend_backward",
    )(query, key, value, grad, lse, cosine, sine, blocks.reshape(1, length), blocks.reshape(length, 1))


def bit_of(index, bit):
    return lax.rem(lax.div(index, bit), 2)


def flip_bit(index, bit):
    return index + bit - 2 * bit * bit_of(index, bit)


class Links:

    def __init__(self, send_sems, recv_sems):
        self.send_sems, self.recv_sems = send_sems, recv_sems

    def copy(self, slot, src, dst, device):
        return pltpu.make_async_remote_copy(
            src_ref=src, dst_ref=dst, send_sem=self.send_sems.at[slot],
            recv_sem=self.recv_sems.at[slot], device_id=(device,), device_id_type=MESH,
        )


def greet(partners):
    barrier = pltpu.get_barrier_semaphore()
    for partner in partners:
        pl.semaphore_signal(barrier, inc=1, device_id=(partner,), device_id_type=MESH)
    pl.semaphore_wait(barrier, len(partners))


def spread_block(bits, own_ref, out_ref, links, local_sem):
    core, first, second = bits
    me = lax.axis_index(AXIS)
    sibling, next_a, next_b = (flip_bit(me, bit) for bit in bits)
    block = own_ref.shape[0]
    half = block // 2
    in_a, in_b = bit_of(me, first), bit_of(me, second)

    def rows(flip_a, flip_b, part):
        place = bit_of(me, core)
        place = place + 2 * lax.rem(in_a + flip_a, 2) + 4 * lax.rem(in_b + flip_b, 2)
        start, size = (0, block) if part is None else (part * half, half)
        return pl.ds(pl.multiple_of(place * block + start, half), size)

    def passed(slot, where, device):
        return links.copy(slot, out_ref.at[where], out_ref.at[where], device)

    def first_hand(slot, part, device):
        return links.copy(
            slot, own_ref.at[pl.ds(part * half, half)], out_ref.at[rows(0, 0, part)], device
        )

    copies = {
        0: first_hand(0, 0, next_a),
        1: first_hand(1, 1, next_b),
        2: first_hand(2, 1, next_a),
        3: first_hand(3, 0, next_b),
        4: links.copy(4, own_ref, out_ref.at[rows(0, 0, None)], sibling),
        5: passed(5, rows(1, 0, 0), next_b),
        6: passed(6, rows(1, 0, 0), sibling),
        7: passed(7, rows(0, 1, 1), next_a),
        8: passed(8, rows(0, 1, 1), sibling),
        9: passed(9, rows(1, 0, 1), sibling),
        10: passed(10, rows(0, 1, 0), sibling),
        11: passed(11, rows(1, 1, 0), sibling),
        12: passed(12, rows(1, 1, 1), sibling),
    }
    for slot in range(5):
        copies[slot].start()
    keep = pltpu.make_async_copy(own_ref, out_ref.at[rows(0, 0, None)], local_sem)
    keep.start()
    copies[0].wait_recv()
    copies[5].start()
    copies[6].start()
    copies[1].wait_recv()
    copies[7].start()
    copies[8].start()
    copies[2].wait_recv()
    copies[9].start()
    copies[3].wait_recv()
    copies[10].start()
    copies[5].wait_recv()
    copies[11].start()
    copies[7].wait_recv()
    copies[12].start()
    for slot in (4, 6, 8, 9, 10, 11, 12):
        copies[slot].wait_recv()
    keep.wait()
    for slot in copies:
        copies[slot].wait_send()


SPREAD_COPIES = 13
SUM_COPIES = 10


def sum_block(bits, product, total, to_core, from_core, chip_sum, arrived, links):
    core, first, second = bits
    me = lax.axis_index(AXIS)
    sibling, next_a, next_b = (flip_bit(me, bit) for bit in bits)
    block, width = total.shape
    half = block // 2
    tile = 512

    def place(step, other_core):
        flip_a, flip_b = 1 - step // 2, 1 - step % 2
        return (
            lax.rem(bit_of(me, core) + other_core, 2)
            + 2 * lax.rem(bit_of(me, first) + flip_a, 2)
            + 4 * lax.rem(bit_of(me, second) + flip_b, 2)
        )

    def part(index):
        return pl.ds(index * half, half)

    diag_a = links.copy(4, chip_sum.at[0, part(0)], arrived.at[0], next_a)
    diag_b = links.copy(5, chip_sum.at[0, part(1)], arrived.at[1], next_b)
    plain_a = links.copy(6, chip_sum.at[1, part(0)], arrived.at[2], next_a)
    plain_b = links.copy(7, chip_sum.at[2, part(1)], arrived.at[3], next_b)
    last_a = links.copy(8, chip_sum.at[1, part(1)], arrived.at[4], next_a)
    last_b = links.copy(9, chip_sum.at[2, part(0)], arrived.at[5], next_b)

    def core_copy(step):
        return links.copy(step, to_core.at[step], from_core.at[step], sibling)

    @pl.loop(0, 4)
    def _(step):
        @pl.loop(0, width // tile)
        def _(column):
            columns = pl.ds(pl.multiple_of(column * tile, tile), tile)
            to_core[step, :, columns] = product(place(step, 1), columns).astype(bf16)

        core_copy(step).start()

    @pl.loop(0, 4)
    def _(step):
        core_copy(step).wait_recv()

        @pl.loop(0, width // tile)
        def _(column):
            columns = pl.ds(pl.multiple_of(column * tile, tile), tile)
            summed = product(place(step, 0), columns) + from_core[step, :, columns].astype(f32)
            total[:, columns] = summed
            chip_sum[step, :, columns] = summed.astype(bf16)

        @pl.when(step == 0)
        def _():
            diag_a.start()
            diag_b.start()

        @pl.when(step == 1)
        def _():
            plain_a.start()

        @pl.when(step == 2)
        def _():
            plain_b.start()

    diag_a.wait_recv()
    chip_sum[2, 0:half, :] = (chip_sum[2, 0:half, :].astype(f32) + arrived[0].astype(f32)).astype(bf16)
    last_b.start()
    diag_b.wait_recv()
    chip_sum[1, half:block, :] = (
        chip_sum[1, half:block, :].astype(f32) + arrived[1].astype(f32)
    ).astype(bf16)
    last_a.start()
    plain_a.wait_recv()
    total[0:half, :] += arrived[2].astype(f32)
    plain_b.wait_recv()
    total[half:block, :] += arrived[3].astype(f32)
    last_b.wait_recv()
    total[0:half, :] += arrived[5].astype(f32)
    last_a.wait_recv()
    total[half:block, :] += arrived[4].astype(f32)

    @pl.loop(0, 4)
    def _(step):
        core_copy(step).wait_send()

    for copy in (diag_a, diag_b, plain_a, plain_b, last_a, last_b):
        copy.wait_send()


def sum_scratch(block, width):
    return [
        pltpu.VMEM((block, width), f32),
        pltpu.VMEM((4, block, width), bf16),
        pltpu.VMEM((4, block, width), bf16),
        pltpu.VMEM((4, block, width), bf16),
        pltpu.VMEM((6, block // 2, width), bf16),
        pltpu.SemaphoreType.DMA((SUM_COPIES,)),
        pltpu.SemaphoreType.DMA((SUM_COPIES,)),
    ]


def spread_scratch(block, width):
    return [
        pltpu.VMEM((block, width), bf16),
        pltpu.SemaphoreType.DMA((SPREAD_COPIES,)),
        pltpu.SemaphoreType.DMA((SPREAD_COPIES,)),
        pltpu.SemaphoreType.DMA,
    ]


vmem = pl.BlockSpec(memory_space=pltpu.VMEM)
anywhere = pl.BlockSpec(memory_space=pl.ANY)


def link_params(collective_id):
    return pltpu.CompilerParams(
        collective_id=collective_id, has_side_effects=True, vmem_limit_bytes=60 * 1024 * 1024
    )


def cost(flops, size):
    return pl.CostEstimate(flops=int(flops), bytes_accessed=int(size), transcendentals=0)


def tokens_kernel(bits, own_ref, out_ref, send_sems, recv_sems, local_sem):
    me = lax.axis_index(AXIS)
    greet([flip_bit(me, bit) for bit in bits])
    spread_block(bits, own_ref, out_ref, Links(send_sems, recv_sems), local_sem)


def gather_tokens(tokens, bits):
    block, width = tokens.shape
    return pl.pallas_call(
        functools.partial(tokens_kernel, bits),
        out_shape=jax.ShapeDtypeStruct((8 * block, width), bf16),
        in_specs=[vmem],
        out_specs=anywhere,
        scratch_shapes=spread_scratch(block, width)[1:],
        compiler_params=link_params(1),
        cost_estimate=cost(0, 100e6),
        name="gather_tokens",
    )(tokens)


def row_scale(values):
    return lax.rsqrt(jnp.mean(values * values, -1, keepdims=True) + epsilon)


def branch_kernel(
    sum_bits, spread_bits, left_ref, right_ref, residual_ref, gain_ref, h2_ref, out_ref,
    total, to_core, from_core, chip_sum, arrived, sum_send, sum_recv, own, send_sems, recv_sems, local_sem,
):
    me = lax.axis_index(AXIS)
    block = total.shape[0]
    greet([flip_bit(me, bit) for bit in sorted(set(sum_bits) | set(spread_bits))])

    def product(place, columns):
        rows = pl.ds(pl.multiple_of(place * block, block), block)
        return contract(left_ref[rows, :], right_ref[:, columns], 1, 0)

    sum_block(
        sum_bits, product, total, to_core, from_core, chip_sum, arrived, Links(sum_send, sum_recv)
    )
    h2 = residual_ref[...].astype(f32) + total[...]
    h2_ref[...] = h2
    own[...] = (h2 * row_scale(h2) * gain_ref[...]).astype(bf16)
    spread_block(spread_bits, own, out_ref, Links(send_sems, recv_sems), local_sem)


def branch(left, right, residual, gain, sum_bits, spread_bits):
    block, width = residual.shape
    return pl.pallas_call(
        functools.partial(branch_kernel, sum_bits, spread_bits),
        out_shape=(
            jax.ShapeDtypeStruct((block, width), f32),
            jax.ShapeDtypeStruct((8 * block, width), bf16),
        ),
        in_specs=[vmem] * 4,
        out_specs=(vmem, anywhere),
        scratch_shapes=sum_scratch(block, width) + spread_scratch(block, width),
        compiler_params=link_params(2),
        cost_estimate=cost(16 * block * left.shape[1] * width, 250e6),
        name="attention_branch",
    )(left, right, residual, gain)


def norm_back(values, gain, upstream):
    scaled = upstream * gain
    scale = row_scale(values)
    inner = jnp.mean(scaled * values, -1, keepdims=True)
    return scale * scaled - scale * scale * scale * values * inner


def ffn_back_kernel(
    sum_bits, spread_bits, gate_ref, up_ref, gate_w_ref, up_w_ref, h2_ref, cot_ref, gain_ref, residual_ref, out_ref,
    total, to_core, from_core, chip_sum, arrived, sum_send, sum_recv, own, send_sems, recv_sems, local_sem,
):
    me = lax.axis_index(AXIS)
    block = total.shape[0]
    greet([flip_bit(me, bit) for bit in sorted(set(sum_bits) | set(spread_bits))])

    def product(place, columns):
        rows = pl.ds(pl.multiple_of(place * block, block), block)
        return contract(gate_ref[rows, :], gate_w_ref[columns, :], 1, 1) + contract(
            up_ref[rows, :], up_w_ref[columns, :], 1, 1
        )

    sum_block(
        sum_bits, product, total, to_core, from_core, chip_sum, arrived, Links(sum_send, sum_recv)
    )
    residual = cot_ref[...].astype(f32) + norm_back(h2_ref[...], gain_ref[...], total[...])
    residual_ref[...] = residual
    own[...] = residual.astype(bf16)
    spread_block(spread_bits, own, out_ref, Links(send_sems, recv_sems), local_sem)


def ffn_back(gate, up, gate_w, up_w, h2, cot, gain, sum_bits, spread_bits):
    block, width = h2.shape
    return pl.pallas_call(
        functools.partial(ffn_back_kernel, sum_bits, spread_bits),
        out_shape=(
            jax.ShapeDtypeStruct((block, width), f32),
            jax.ShapeDtypeStruct((8 * block, width), bf16),
        ),
        in_specs=[vmem] * 7,
        out_specs=(vmem, anywhere),
        scratch_shapes=sum_scratch(block, width) + spread_scratch(block, width),
        compiler_params=link_params(3),
        cost_estimate=cost(32 * block * gate.shape[1] * width, 250e6),
        name="ffn_back",
    )(gate, up, gate_w, up_w, h2, cot, gain)


def first_back_kernel(
    sum_bits, left_ref, right_ref, tokens_ref, gain_ref, residual_ref, out_ref,
    total, to_core, from_core, chip_sum, arrived, sum_send, sum_recv,
):
    me = lax.axis_index(AXIS)
    block = total.shape[0]
    greet([flip_bit(me, bit) for bit in sum_bits])

    def product(place, columns):
        rows = pl.ds(pl.multiple_of(place * block, block), block)
        return contract(left_ref[rows, :], right_ref[columns, :], 1, 1)

    sum_block(
        sum_bits, product, total, to_core, from_core, chip_sum, arrived, Links(sum_send, sum_recv)
    )
    out_ref[...] = residual_ref[...] + norm_back(
        tokens_ref[...].astype(f32), gain_ref[...], total[...]
    )


def first_back(left, right, tokens, gain, residual, sum_bits):
    block, width = tokens.shape
    return pl.pallas_call(
        functools.partial(first_back_kernel, sum_bits),
        out_shape=jax.ShapeDtypeStruct((block, width), f32),
        in_specs=[vmem] * 5,
        out_specs=vmem,
        scratch_shapes=sum_scratch(block, width),
        compiler_params=link_params(4),
        cost_estimate=cost(16 * block * left.shape[1] * width, 150e6),
        name="first_back",
    )(left, right, tokens, gain, residual)


def body(
    tokens, block_of, clip_limit, norm_attn, w_query, w_key, w_value, w_out,
    norm_ffn, w_gate, w_up, w_down, cotangent,
):
    tok_rows, width = tokens.shape
    devices = lax.axis_size(AXIS)
    team = SEQ // tok_rows
    teams = devices // team
    head_total = width // HEAD_DIM
    heads = head_total // team
    head_cols = heads * HEAD_DIM
    ff_rows = w_down.shape[0]
    weight_rows = w_gate.shape[0]
    ff_cols = w_gate.shape[1] // team
    device = lax.axis_index(AXIS)
    mate = device % team
    bit_count = devices.bit_length() - 1
    attn_bits, ffn_bits = (1, 2, 4), (1, 2, 8)
    data_bits = [4] + [1 << k for k in range(4, bit_count)]
    in_team = [[g * team + b for b in range(team)] for g in range(teams)]
    across = [[g * team + b for g in range(teams)] for b in range(team)]
    ffn_team = [
        [g * 16 + z * 8 + y * 4 + c for z in range(2) for c in range(4)]
        for g in range(devices // 16)
        for y in range(2)
    ]

    def flip(x, bit):
        return lax.ppermute(x, AXIS, [(i, i ^ bit) for i in range(devices)])

    def gather_across(x):
        return lax.all_gather(x, AXIS, axis=0, tiled=True, axis_index_groups=across)

    def scatter_across(x):
        return lax.psum_scatter(
            x.astype(bf16), AXIS, scatter_dimension=0, tiled=True, axis_index_groups=across
        )

    def swap(x, groups):
        return lax.all_to_all(x, AXIS, 0, 0, tiled=True, axis_index_groups=groups)

    def dim_of(bit):
        return bit_count - bit.bit_length()

    def data_pieces(x):
        pieces = {0: x}
        for bit in reversed(data_bits):
            for key in list(pieces):
                pieces[key | bit] = flip(pieces[key], bit)
        return pieces

    def place_pieces(pieces, dims, shape):
        total = jnp.zeros(shape, bf16)
        for key, piece in pieces.items():
            start = [0] * len(shape)
            size = list(shape)
            for bit in data_bits:
                start[dims[bit]] = ((device // bit) + (1 if key & bit else 0)) % 2
                size[dims[bit]] = 1
            total = lax.dynamic_update_slice(total, piece.reshape(size), start)
        return total

    def data_sum(x, dims):
        alive = dict(dims)
        for bit in data_bits:
            dim = alive.pop(bit)
            alive = {b: d - (d > dim) for b, d in alive.items()}
            mine = (device // bit) % 2
            keep = lax.dynamic_index_in_dim(x, mine, dim, False)
            sent = flip(lax.dynamic_index_in_dim(x, 1 - mine, dim, False), bit)
            x = (keep.astype(f32) + sent.astype(f32)).astype(bf16)
        return x

    def columns_out(weight, piece):
        rows, cols = weight.shape
        split = weight.reshape(rows, cols // (team * piece), team, piece)
        return split.transpose(2, 0, 1, 3).reshape(team, rows, cols // team)

    def columns_back(weight, piece):
        rows, cols = weight.shape[1:]
        split = weight.reshape(team, rows, cols // piece, piece)
        return split.transpose(1, 2, 0, 3).reshape(rows, team * cols)

    def ffn_out(weight):
        split = weight.reshape(weight_rows, devices // 16, 2, 2, 4, ff_rows)
        return split.transpose(2, 4, 0, 1, 3, 5).reshape(team, weight_rows, ff_cols)

    def ffn_home(grad):
        split = grad.reshape(2, 4, weight_rows, devices // 16, 2, ff_rows)
        return split.transpose(2, 3, 0, 4, 1, 5).reshape(weight_rows, team * ff_cols)

    row_dims = {bit: dim_of(bit) for bit in data_bits}
    row_shape = (2,) * bit_count
    unit_dims = {bit: i for i, bit in enumerate(reversed(data_bits))}
    unit_shape = (2,) * len(data_bits)

    def gather_small(x):
        for k in range(bit_count):
            other = flip(x, 1 << k)
            high = (device // (1 << k)) % 2 == 1
            x = jnp.concatenate([jnp.where(high, other, x), jnp.where(high, x, other)], 1)
        return x

    gains = gather_small(jnp.stack([norm_attn, norm_ffn])).astype(f32)
    gain_attn, gain_ffn = gains[0:1], gains[1:2]
    blocks = block_of.reshape(1, tok_rows)
    for k in range(3):
        other = flip(blocks, 1 << k)
        high = (device // (1 << k)) % 2 == 1
        blocks = jnp.concatenate([jnp.where(high, other, blocks), jnp.where(high, blocks, other)], 1)

    qkv_mine = jnp.concatenate([columns_out(w, HEAD_DIM) for w in (w_query, w_key, w_value)], 2)
    qkv_w = gather_across(swap(qkv_mine, in_team).reshape(team * weight_rows, 3 * head_cols))
    if weight_rows == HEAD_DIM:
        out_w = gather_across(w_out)
    else:
        out_all = lax.all_gather(w_out, AXIS, axis=0, tiled=True)
        out_w = lax.dynamic_index_in_dim(
            out_all.reshape(heads, team, HEAD_DIM, width), mate, 1, False
        ).reshape(head_cols, width)
    gate_up = swap(jnp.concatenate([ffn_out(w_gate), ffn_out(w_up)], 2), ffn_team)
    gate_up, down_mine, qkv_w = lax.optimization_barrier((gate_up, w_down, qkv_w))

    def whole_rows(mine):
        shape = row_shape + (weight_rows, ff_cols)
        return place_pieces(data_pieces(mine), row_dims, shape).reshape(width, ff_cols)

    gate_w = whole_rows(gate_up[:, :, :ff_cols])
    up_w = whole_rows(gate_up[:, :, ff_cols:])
    down_w = place_pieces(
        data_pieces(down_mine), unit_dims, unit_shape + (ff_rows, width)
    ).reshape(ff_cols, width)

    team_tokens = gather_tokens(tokens, attn_bits).astype(f32)
    normed_attn = (team_tokens * row_scale(team_tokens) * gain_attn).astype(bf16)
    qkv = contract(normed_attn, qkv_w, 1, 0)
    cosine, sine = rope_tables(SEQ, head_cols)
    query, key, value, attended, lse, peak = attend_forward(qkv, cosine, sine, blocks, heads)
    head_peak = jnp.where(
        (jnp.arange(head_total) % team) == mate, jnp.repeat(peak[0, :heads], team), -jnp.inf
    )
    for k in range(bit_count):
        head_peak = jnp.maximum(head_peak, flip(head_peak, 1 << k))
    after_attn, normed_ffn = branch(attended, out_w, tokens, gain_ffn, attn_bits, ffn_bits)
    gate_pre = contract(normed_ffn, gate_w, 1, 0)
    up_pre = contract(normed_ffn, up_w, 1, 0)
    sigmoid_gate = jax.nn.sigmoid(gate_pre)
    silu_gate = gate_pre * sigmoid_gate
    hidden = (silu_gate * up_pre).astype(bf16)
    down_part = contract(hidden, down_w, 1, 0).astype(bf16)
    mixed = (
        after_attn
        + lax.psum_scatter(
            down_part, AXIS, scatter_dimension=0, tiled=True, axis_index_groups=ffn_team
        ).astype(f32)
    ).astype(bf16)

    team_cot = lax.all_gather(cotangent, AXIS, axis=0, tiled=True, axis_index_groups=ffn_team)
    d_down = data_sum(
        contract(hidden, team_cot, 0, 0).astype(bf16).reshape(unit_shape + (ff_rows, width)), unit_dims
    ).astype(f32)
    d_hidden = contract(team_cot, down_w, 1, 1)
    grad_gate = (d_hidden * up_pre * sigmoid_gate * (1.0 + gate_pre * (1.0 - sigmoid_gate))).astype(bf16)
    grad_up = (d_hidden * silu_gate).astype(bf16)
    d_residual, branch_grad = ffn_back(
        grad_gate, grad_up, gate_w, up_w, after_attn, cotangent, gain_ffn, ffn_bits, attn_bits
    )

    def row_sums(part):
        part = data_sum(part.astype(bf16).reshape(row_shape + (weight_rows, ff_cols)), row_dims)
        return part.reshape(team, weight_rows, ff_cols)

    d_gate_up = swap(
        jnp.concatenate(
            [row_sums(contract(normed_ffn, g, 0, 0)) for g in (grad_gate, grad_up)], 2
        ),
        ffn_team,
    )
    d_gate = ffn_home(d_gate_up[:, :, :ff_cols]).astype(f32)
    d_up = ffn_home(d_gate_up[:, :, ff_cols:]).astype(f32)
    grad_attended = contract(branch_grad, out_w, 1, 1).astype(bf16)
    grad_qkv = attend_backward(
        query, key, value, grad_attended, lse, cosine, sine, blocks, heads
    )
    out_part = contract(attended, branch_grad, 0, 0)
    if weight_rows == HEAD_DIM:
        d_out = scatter_across(out_part).astype(f32)
    else:
        spread = jnp.where(
            (jnp.arange(team) == mate)[None, :, None, None],
            out_part.reshape(heads, 1, HEAD_DIM, width), 0.0,
        ).reshape(width, width)
        d_out = lax.psum_scatter(spread, AXIS, scatter_dimension=0, tiled=True)
    d_qkv = scatter_across(contract(normed_attn, grad_qkv, 0, 0))
    d_qkv = swap(d_qkv.reshape(team, weight_rows, 3 * head_cols), in_team)
    d_query, d_key, d_value = (
        columns_back(d_qkv[:, :, i * head_cols : (i + 1) * head_cols], HEAD_DIM).astype(f32)
        for i in range(3)
    )
    d_tokens = first_back(grad_qkv, qkv_w, tokens, gain_attn, d_residual, attn_bits)

    def gain_grad(pairs, gain):
        return sum(jnp.sum(w.astype(f32) * g, 1) for w, g in pairs) / gain.astype(f32)

    d_norm_attn = gain_grad(((w_query, d_query), (w_key, d_key), (w_value, d_value)), norm_attn)
    d_norm_ffn = gain_grad(((w_gate, d_gate), (w_up, d_up)), norm_ffn)
    clip_value = clip_limit.astype(f32)
    factor = jnp.sqrt(clip_value / jnp.maximum(head_peak, clip_value))
    factors = jnp.repeat(factor, HEAD_DIM)[None, :]
    clipped_query = (w_query.astype(f32) * factors).astype(bf16)
    clipped_key = (w_key.astype(f32) * factors).astype(bf16)
    return (
        mixed, d_tokens, d_norm_attn, d_query, d_key, d_value, d_out, d_norm_ffn,
        d_gate, d_up, d_down, head_peak, clipped_query, clipped_key,
    )


def solution(mesh):
    rows, whole = P(AXIS, None), P(AXIS)
    return jax.shard_map(
        body,
        mesh=mesh,
        in_specs=(rows, whole, P(), whole, rows, rows, rows, rows, whole, rows, rows, rows, rows),
        out_specs=(
            rows, rows, whole, rows, rows, rows, rows, whole, rows, rows, rows, P(), rows, rows,
        ),
        check_vma=False,
    )
```

```python
import functools

import jax
import jax.numpy as jnp
from jax import lax
from jax.experimental import pallas as pl
from jax.experimental.pallas import tpu as pltpu
from jax.sharding import PartitionSpec as P

HEAD_DIM = 64
SEQ = 2048
BLOCK = 256
AXIS = "fsdp"
MESH = pl.DeviceIdType.MESH

epsilon = 1e-05
rope_base = 130000.0
bf16 = jnp.bfloat16
f32 = jnp.float32
vmem = pl.BlockSpec(memory_space=pltpu.VMEM)
anywhere = pl.BlockSpec(memory_space=pl.ANY)


def contract(left, right, left_dim, right_dim):
    return lax.dot_general(
        left, right, (((left_dim,), (right_dim,)), ((), ())), preferred_element_type=f32
    )


def rope_tables(length, width):
    half_dim = HEAD_DIM // 2
    inverse = rope_base ** (-jnp.arange(half_dim, dtype=f32) * 2.0 / HEAD_DIM)
    angles = jnp.arange(length, dtype=f32)[:, None] * inverse[None, :]
    cosine, sine = jnp.cos(angles), jnp.sin(angles)
    repeats = width // HEAD_DIM
    return (
        jnp.tile(jnp.concatenate([cosine, cosine], 1), (1, repeats)),
        jnp.tile(jnp.concatenate([-sine, sine], 1), (1, repeats)),
    )


def swap_halves(rows):
    width = rows.shape[1]
    half = HEAD_DIM // 2
    lane = lax.broadcasted_iota(jnp.int32, rows.shape, 1)
    return jnp.where(
        lane % HEAD_DIM < half, pltpu.roll(rows, width - half, 1), pltpu.roll(rows, half, 1)
    )


PAIR = 2 * HEAD_DIM


def head_mask(shape, head):
    lane = lax.broadcasted_iota(jnp.int32, shape, 1)
    return (lane >= head * HEAD_DIM) & (lane < (head + 1) * HEAD_DIM)


def masked_scores(query, key_ref, row_ref, col_ref, q0, cols):
    tail = min(2 * BLOCK, cols)
    scores = contract(query, key_ref[0:cols, :], 1, 1)
    shown = row_ref[:, pl.ds(cols - tail, tail)] <= col_ref[pl.ds(q0, BLOCK), :]
    hidden = jnp.where(shown, scores[:, cols - tail :], -jnp.inf)
    return jnp.concatenate([scores[:, : cols - tail], hidden], 1) if tail < cols else hidden


def attend_forward_kernel(
    qkv_ref, cos_ref, sin_ref, row_ref, col_ref, q_ref, k_ref, v_ref, out_ref, lse_ref, peak_ref
):
    pairs, length, _ = q_ref.shape
    for t in range(length // BLOCK):
        rows = pl.ds(t * BLOCK, BLOCK)
        cosine, sine = cos_ref[rows, :], sin_ref[rows, :]
        for pair in range(pairs):
            first = 3 * pair * PAIR
            query = qkv_ref[rows, first : first + PAIR]
            query = (query * cosine + swap_halves(query) * sine).astype(bf16)
            q_ref[pair, rows, :] = (query.astype(f32) * HEAD_DIM ** (-0.5)).astype(bf16)
            key = qkv_ref[rows, first + PAIR : first + 2 * PAIR]
            k_ref[pair, rows, :] = (key * cosine + swap_halves(key) * sine).astype(bf16)
            v_ref[pair, rows, :] = qkv_ref[rows, first + 2 * PAIR : first + 3 * PAIR].astype(bf16)
    peak_ref[...] = jnp.full(peak_ref.shape, -jnp.inf, f32)
    lane = lax.broadcasted_iota(jnp.int32, (BLOCK, 128), 1)
    for t in range(length // BLOCK):
        q0 = t * BLOCK
        rows = pl.ds(q0, BLOCK)
        cols = min(q0 + 2 * BLOCK, length)

        @pl.loop(0, pairs)
        def _(pair):
            total = jnp.zeros((BLOCK, PAIR), f32)
            for sub in range(2):
                head = 2 * pair + sub
                mask = head_mask((BLOCK, PAIR), sub)
                query = jnp.where(mask, q_ref[pair, rows, :], 0).astype(bf16)
                scores = masked_scores(query, k_ref.at[pair], row_ref, col_ref, q0, cols)
                row_max = jnp.max(scores, 1, keepdims=True)
                numerators = jnp.exp(scores - row_max)
                totals = jnp.sum(numerators, 1, keepdims=True)
                mixed = contract(numerators.astype(bf16), v_ref[pair, 0:cols, :], 1, 0) / totals
                total = jnp.where(mask, mixed, total)
                lse_ref[rows, :] = jnp.where(lane == head, row_max + jnp.log(totals), lse_ref[rows, :])
                peak_ref[...] = jnp.where(
                    lax.broadcasted_iota(jnp.int32, peak_ref.shape, 1) == head,
                    jnp.maximum(peak_ref[...], jnp.max(row_max)),
                    peak_ref[...],
                )
            out_ref[rows, pl.ds(pl.multiple_of(pair * PAIR, PAIR), PAIR)] = total.astype(bf16)


def attend_forward(qkv, cosine, sine, row_blocks, col_blocks):
    length = qkv.shape[0]
    pairs = qkv.shape[1] // (3 * PAIR)
    shape = jax.ShapeDtypeStruct
    return pl.pallas_call(
        attend_forward_kernel,
        out_shape=(
            shape((pairs, length, PAIR), bf16),
            shape((pairs, length, PAIR), bf16),
            shape((pairs, length, PAIR), bf16),
            shape((length, pairs * PAIR), bf16),
            shape((length, 128), f32),
            shape((8, 128), f32),
        ),
        in_specs=[vmem] * 5,
        out_specs=tuple([vmem] * 6),
        compiler_params=pltpu.CompilerParams(vmem_limit_bytes=56 * 1024 * 1024),
        cost_estimate=pl.CostEstimate(
            flops=16 * pairs * length * length * PAIR, bytes_accessed=length * PAIR * pairs * 24,
            transcendentals=2 * pairs * length * length,
        ),
        name="attend_forward",
    )(qkv, cosine, sine, row_blocks, col_blocks)


def attend_backward_kernel(
    first_head, q_ref, k_ref, v_ref, grad_ref, lse_ref, cos_ref, sin_ref, row_ref, col_ref, out_ref, dk_ref, dv_ref
):
    length = q_ref.shape[0]
    dk_ref[...] = jnp.zeros_like(dk_ref)
    dv_ref[...] = jnp.zeros_like(dv_ref)
    lane = lax.broadcasted_iota(jnp.int32, (BLOCK, 128), 1)
    for t in range(length // BLOCK):
        q0 = t * BLOCK
        rows = pl.ds(q0, BLOCK)
        cols = min(q0 + 2 * BLOCK, length)

        def one_head(sub, dq):
            mask = head_mask((BLOCK, PAIR), sub)
            query = jnp.where(mask, q_ref[rows, :], 0).astype(bf16)
            grad = jnp.where(mask, grad_ref[rows, :], 0).astype(bf16)
            lse = jnp.sum(
                jnp.where(lane == first_head + sub, lse_ref[rows, :], 0.0), 1, keepdims=True
            )
            scores = masked_scores(query, k_ref, row_ref, col_ref, q0, cols)
            attention = jnp.exp(scores - lse)
            grad_attention = contract(grad, v_ref[0:cols, :], 1, 1)
            weighted = attention * grad_attention
            centre = jnp.sum(weighted, 1, keepdims=True)
            grad_scores = (weighted - attention * centre).astype(bf16)
            dv_ref[0:cols, :] += contract(attention.astype(bf16), grad, 0, 0)
            dk_ref[0:cols, :] += contract(grad_scores, query, 0, 0)
            return jnp.where(mask, contract(grad_scores, k_ref[0:cols, :], 1, 0), dq)

        dq = lax.fori_loop(0, 2, one_head, jnp.zeros((BLOCK, PAIR), f32)) * HEAD_DIM ** (-0.5)
        out_ref[rows, 0:PAIR] = (dq * cos_ref[rows, :] - swap_halves(dq) * sin_ref[rows, :]).astype(bf16)
    for t in range(length // BLOCK):
        rows = pl.ds(t * BLOCK, BLOCK)
        dk = dk_ref[rows, :]
        out_ref[rows, PAIR : 2 * PAIR] = (
            dk * cos_ref[rows, :] - swap_halves(dk) * sin_ref[rows, :]
        ).astype(bf16)
        out_ref[rows, 2 * PAIR : 3 * PAIR] = dv_ref[rows, :].astype(bf16)


def attend_backward(pair, query, key, value, grad, lse, cosine, sine, row_blocks, col_blocks):
    length = query.shape[1]
    heads = pl.BlockSpec((None, length, PAIR), lambda _: (pair, 0, 0))
    return pl.pallas_call(
        functools.partial(attend_backward_kernel, 2 * pair),
        grid=(1,),
        out_shape=jax.ShapeDtypeStruct((length, 3 * PAIR), bf16),
        in_specs=[heads] * 3 + [pl.BlockSpec((length, PAIR), lambda _: (0, pair))] + [vmem] * 5,
        out_specs=vmem,
        scratch_shapes=[pltpu.VMEM((length, PAIR), f32), pltpu.VMEM((length, PAIR), f32)],
        compiler_params=pltpu.CompilerParams(vmem_limit_bytes=56 * 1024 * 1024),
        cost_estimate=pl.CostEstimate(
            flops=40 * length * length * PAIR, bytes_accessed=length * PAIR * 24,
            transcendentals=2 * length * length,
        ),
        name="attend_backward",
    )(query, key, value, grad, lse, cosine, sine, row_blocks, col_blocks)


def bit_of(index, bit):
    return lax.rem(lax.div(index, bit), 2)


def flip_bit(index, bit):
    return index + bit - 2 * bit * bit_of(index, bit)


class Links:

    def __init__(self, send_sems, recv_sems):
        self.send_sems, self.recv_sems = send_sems, recv_sems

    def copy(self, slot, src, dst, device):
        return pltpu.make_async_remote_copy(
            src_ref=src, dst_ref=dst, send_sem=self.send_sems.at[slot],
            recv_sem=self.recv_sems.at[slot], device_id=(device,), device_id_type=MESH,
        )


def greet(partners):
    barrier = pltpu.get_barrier_semaphore()
    for partner in partners:
        pl.semaphore_signal(barrier, inc=1, device_id=(partner,), device_id_type=MESH)
    pl.semaphore_wait(barrier, len(partners))


def spread_block(bits, own_ref, out_ref, links, local_sem):
    core, first, second = bits
    me = lax.axis_index(AXIS)
    sibling, next_a, next_b = (flip_bit(me, bit) for bit in bits)
    block = own_ref.shape[0]
    half = block // 2
    in_a, in_b = bit_of(me, first), bit_of(me, second)

    def rows(flip_a, flip_b, part):
        place = bit_of(me, core)
        place = place + 2 * lax.rem(in_a + flip_a, 2) + 4 * lax.rem(in_b + flip_b, 2)
        start, size = (0, block) if part is None else (part * half, half)
        return pl.ds(pl.multiple_of(place * block + start, half), size)

    def passed(slot, where, device):
        return links.copy(slot, out_ref.at[where], out_ref.at[where], device)

    def first_hand(slot, part, device):
        return links.copy(
            slot, own_ref.at[pl.ds(part * half, half)], out_ref.at[rows(0, 0, part)], device
        )

    copies = {
        0: first_hand(0, 0, next_a),
        1: first_hand(1, 1, next_b),
        2: first_hand(2, 1, next_a),
        3: first_hand(3, 0, next_b),
        4: links.copy(4, own_ref, out_ref.at[rows(0, 0, None)], sibling),
        5: passed(5, rows(1, 0, 0), next_b),
        6: passed(6, rows(1, 0, 0), sibling),
        7: passed(7, rows(0, 1, 1), next_a),
        8: passed(8, rows(0, 1, 1), sibling),
        9: passed(9, rows(1, 0, 1), sibling),
        10: passed(10, rows(0, 1, 0), sibling),
        11: passed(11, rows(1, 1, 0), sibling),
        12: passed(12, rows(1, 1, 1), sibling),
    }
    keep = pltpu.make_async_copy(own_ref, out_ref.at[rows(0, 0, None)], local_sem)

    def begin():
        for slot in range(5):
            copies[slot].start()
        keep.start()

    def hand_on(arrived, *sent):
        def phase():
            copies[arrived].wait_recv()
            for slot in sent:
                copies[slot].start()

        return phase

    def finish():
        for slot in (4, 6, 8, 9, 10, 11, 12):
            copies[slot].wait_recv()
        keep.wait()
        for slot in copies:
            copies[slot].wait_send()

    return [
        begin, hand_on(0, 5, 6), hand_on(1, 7, 8), hand_on(2, 9), hand_on(3, 10),
        hand_on(5, 11), hand_on(7, 12), finish,
    ]


def run(phases):
    for phase in phases:
        phase()


SPREAD_COPIES = 13
SUM_COPIES = 10


def sum_block(bits, product, total, to_core, from_core, chip_sum, arrived, links):
    core, first, second = bits
    me = lax.axis_index(AXIS)
    sibling, next_a, next_b = (flip_bit(me, bit) for bit in bits)
    block, width = total.shape
    half = block // 2
    tile = 512

    def place(step, other_core):
        flip_a, flip_b = 1 - step // 2, 1 - step % 2
        return (
            lax.rem(bit_of(me, core) + other_core, 2)
            + 2 * lax.rem(bit_of(me, first) + flip_a, 2)
            + 4 * lax.rem(bit_of(me, second) + flip_b, 2)
        )

    def part(index):
        return pl.ds(index * half, half)

    diag_a = links.copy(4, chip_sum.at[0, part(0)], arrived.at[0], next_a)
    diag_b = links.copy(5, chip_sum.at[0, part(1)], arrived.at[1], next_b)
    plain_a = links.copy(6, chip_sum.at[1, part(0)], arrived.at[2], next_a)
    plain_b = links.copy(7, chip_sum.at[2, part(1)], arrived.at[3], next_b)
    last_a = links.copy(8, chip_sum.at[1, part(1)], arrived.at[4], next_a)
    last_b = links.copy(9, chip_sum.at[2, part(0)], arrived.at[5], next_b)

    def core_copy(step):
        return links.copy(step, to_core.at[step], from_core.at[step], sibling)

    def for_sibling():
        @pl.loop(0, 4)
        def _(step):
            @pl.loop(0, width // tile)
            def _(column):
                columns = pl.ds(pl.multiple_of(column * tile, tile), tile)
                to_core[step, :, columns] = product(place(step, 1), columns).astype(bf16)

            core_copy(step).start()

    def for_chip():
        @pl.loop(0, 4)
        def _(step):
            core_copy(step).wait_recv()

            @pl.loop(0, width // tile)
            def _(column):
                columns = pl.ds(pl.multiple_of(column * tile, tile), tile)
                summed = product(place(step, 0), columns) + from_core[step, :, columns].astype(f32)
                total[:, columns] = summed

                @pl.when(step < 3)
                def _():
                    chip_sum[step, :, columns] = summed.astype(bf16)

            @pl.when(step == 0)
            def _():
                diag_a.start()
                diag_b.start()

            @pl.when(step == 1)
            def _():
                plain_a.start()

            @pl.when(step == 2)
            def _():
                plain_b.start()

    def hand_on():
        diag_a.wait_recv()
        chip_sum[2, 0:half, :] = (
            chip_sum[2, 0:half, :].astype(f32) + arrived[0].astype(f32)
        ).astype(bf16)
        last_b.start()
        diag_b.wait_recv()
        chip_sum[1, half:block, :] = (
            chip_sum[1, half:block, :].astype(f32) + arrived[1].astype(f32)
        ).astype(bf16)
        last_a.start()

    def finish():
        plain_a.wait_recv()
        total[0:half, :] += arrived[2].astype(f32)
        plain_b.wait_recv()
        total[half:block, :] += arrived[3].astype(f32)
        last_b.wait_recv()
        total[0:half, :] += arrived[5].astype(f32)
        last_a.wait_recv()
        total[half:block, :] += arrived[4].astype(f32)

        @pl.loop(0, 4)
        def _(step):
            core_copy(step).wait_send()

        for copy in (diag_a, diag_b, plain_a, plain_b, last_a, last_b):
            copy.wait_send()

    return for_sibling, for_chip, hand_on, finish


def sum_scratch(block, width):
    return [
        pltpu.VMEM((block, width), f32),
        pltpu.VMEM((4, block, width), bf16),
        pltpu.VMEM((4, block, width), bf16),
        pltpu.VMEM((3, block, width), bf16),
        pltpu.VMEM((6, block // 2, width), bf16),
        pltpu.SemaphoreType.DMA((SUM_COPIES,)),
        pltpu.SemaphoreType.DMA((SUM_COPIES,)),
    ]


def spread_scratch(block, width):
    return [
        pltpu.VMEM((block, width), bf16),
        pltpu.SemaphoreType.DMA((SPREAD_COPIES,)),
        pltpu.SemaphoreType.DMA((SPREAD_COPIES,)),
        pltpu.SemaphoreType.DMA,
    ]


def link_params(collective_id):
    return pltpu.CompilerParams(
        collective_id=collective_id, has_side_effects=True, vmem_limit_bytes=60 * 1024 * 1024
    )


def cost(flops, size):
    return pl.CostEstimate(flops=int(flops), bytes_accessed=int(size), transcendentals=0)


def front_kernel(
    team, teams, tokens_ref, mine_ref, small_ref, tokens_out, weights_out, small_out,
    send_sems, recv_sems, local_sem, swap_send, swap_recv, swap_local, line_send, line_recv, small_send, small_recv, small_local,
):
    me = lax.axis_index(AXIS)
    mate, group = lax.rem(me, team), lax.div(me, team)
    devices = team * teams
    bits = [1 << k for k in range(devices.bit_length() - 1)]
    mates = [group * team + lax.rem(mate + k, team) for k in range(1, team)]
    above, below = lax.rem(me + team, devices), lax.rem(me + devices - team, devices)
    greet(mates + [above, below] + [flip_bit(me, bit) for bit in bits if bit >= team])
    rows = mine_ref.shape[1]
    swaps, line, small = Links(swap_send, swap_recv), Links(line_send, line_recv), Links(small_send, small_recv)

    def share(place):
        return pl.ds(pl.multiple_of(place * rows, rows), rows)

    swap_copies = [
        swaps.copy(k, mine_ref.at[lax.rem(mate + k + 1, team)], weights_out.at[group, share(mate)], mates[k])
        for k in range(team - 1)
    ]
    for copy in swap_copies:
        copy.start()
    keep = pltpu.make_async_copy(mine_ref.at[mate], weights_out.at[group, share(mate)], swap_local)
    keep.start()
    spread = spread_block(
        (1, 2, 4), tokens_ref, tokens_out, Links(send_sems, recv_sems), local_sem
    )
    spread[0]()
    small_keep = pltpu.make_async_copy(small_ref, small_out.at[me], small_local)
    small_keep.start()
    small_keep.wait()

    def small_copy(k):
        block = pl.ds(pl.multiple_of(me - lax.rem(me, bits[k]), bits[k]), bits[k])
        return small.copy(k, small_out.at[block], small_out.at[block], flip_bit(me, bits[k]))

    def small_step(k):
        if k:
            small_copy(k - 1).wait_recv()
        if k < len(bits):
            small_copy(k).start()

    small_step(0)

    def passed(slot, shard, device):
        return line.copy(slot, weights_out.at[shard], weights_out.at[shard], device)

    steps = teams - 1

    def up(step):
        return passed(step - 1, group - (step - 1), above)

    def down(step):
        return passed(steps + step - 1, group + (step - 1), below)

    def line_start(step):
        pl.when((group < teams - 1) & (group >= step - 1))(lambda: up(step).start())
        pl.when((group > 0) & (group + step - 1 < teams))(lambda: down(step).start())

    def line_wait(step):
        pl.when(group >= step)(lambda: up(step).wait_recv())
        pl.when(group + step < teams)(lambda: down(step).wait_recv())

    def line_sent(step):
        pl.when((group < teams - 1) & (group >= step - 1))(lambda: up(step).wait_send())
        pl.when((group > 0) & (group + step - 1 < teams))(lambda: down(step).wait_send())

    for copy in swap_copies:
        copy.wait_recv()
    keep.wait()
    line_start(1)
    small_step(1)
    spread[1]()
    spread[2]()
    small_step(2)
    spread[3]()
    spread[4]()
    line_wait(1)
    line_start(2)
    for k in range(3, len(bits) + 1):
        small_step(k)
    for phase in spread[5:]:
        phase()
    for step in range(2, teams):
        line_wait(step)
        if step < steps:
            line_start(step + 1)
    for copy in swap_copies:
        copy.wait_send()
    for step in range(1, teams):
        line_sent(step)
    for k in range(len(bits)):
        small_copy(k).wait_send()


def front(tokens, mine, small, teams):
    block, width = tokens.shape
    team, rows, cols = mine.shape
    devices = team * teams
    bits = devices.bit_length() - 1
    dma = pltpu.SemaphoreType.DMA
    shape = jax.ShapeDtypeStruct
    return pl.pallas_call(
        functools.partial(front_kernel, team, teams),
        out_shape=(
            shape((team * block, width), bf16),
            shape((teams, team * rows, cols), bf16),
            shape((devices,) + small.shape, f32),
        ),
        in_specs=[vmem] * 3,
        out_specs=(anywhere,) * 3,
        scratch_shapes=spread_scratch(block, width)[1:]
        + [dma((team - 1,)), dma((team - 1,)), dma, dma((2 * teams,)), dma((2 * teams,)), dma((bits,)), dma((bits,)), dma],
        compiler_params=link_params(1),
        cost_estimate=cost(0, 200e6),
        name="front",
    )(tokens, mine, small)


def row_scale(values):
    return lax.rsqrt(jnp.mean(values * values, -1, keepdims=True) + epsilon)


def branch_kernel(
    carry, sum_bits, spread_bits, left_ref, right_ref, residual_ref, gain_ref, peak_ref, *refs,
):
    if carry:
        (both_own, both_y, gate_z, down_own, down_y), refs = refs[:5], refs[5:]
        (h2_ref, out_ref, peak_out, gate_full, up_full, down_full), refs = refs[:6], refs[6:]
        (total, to_core, from_core, chip_sum, arrived, sum_send, sum_recv, own, send_sems, recv_sems, local_sem,
         peak_in, peak_send, peak_recv, carry_send, carry_recv, carry_local) = refs
    else:
        (h2_ref, out_ref, peak_out), refs = refs[:3], refs[3:]
        (total, to_core, from_core, chip_sum, arrived, sum_send, sum_recv, own, send_sems, recv_sems, local_sem,
         peak_in, peak_send, peak_recv) = refs
    me = lax.axis_index(AXIS)
    block = total.shape[0]
    bits = [1 << k for k in range(peak_in.shape[0])]
    greet([flip_bit(me, bit) for bit in bits])
    peaks = Links(peak_send, peak_recv)

    def peak_copy(k):
        return peaks.copy(k, peak_out, peak_in.at[k], flip_bit(me, bits[k]))

    def peak_step(k):
        if k:
            peak_copy(k - 1).wait()
            peak_out[...] = jnp.maximum(peak_out[...], peak_in[k - 1])
        if k < len(bits):
            peak_copy(k).start()

    if carry:
        carried = Links(carry_send, carry_recv)
        high, middle = bit_of(me, 16), bit_of(me, 4)
        by_y, by_z = flip_bit(me, 4), flip_bit(me, 16)

        def rows_of(part, flip_z, flip_y):
            z, y = lax.rem(high + flip_z, 2), lax.rem(middle + flip_y, 2)
            return pl.ds(pl.multiple_of(z * 16 + part * 8 + y * 4, 4), 4)

        cols = gate_z.shape[2]

        def half(source, part, up=0):
            return source.at[pl.ds(part * 4, 4), :, pl.ds(up * cols, cols)]

        def unit(flip_z, flip_y):
            return lax.rem(high + flip_z, 2) * 2 + lax.rem(middle + flip_y, 2)

        kept = []
        for source, up, full, flips in (
            (both_own, 0, gate_full, (0, 0)), (both_y, 0, gate_full, (0, 1)), (gate_z, 0, gate_full, (1, 0)),
            (both_own, 1, up_full, (0, 0)), (both_y, 1, up_full, (0, 1)),
        ):
            for part in range(2):
                kept.append((half(source, part, up), full.at[rows_of(part, *flips)]))
        kept.append((down_own, down_full.at[unit(0, 0)]))
        kept.append((down_y, down_full.at[unit(0, 1)]))
        kept = [pltpu.make_async_copy(a, b, carry_local.at[i]) for i, (a, b) in enumerate(kept)]
        up_z = [
            carried.copy(part, half(both_own, part, 1), up_full.at[rows_of(part, 0, 0)], by_z)
            for part in range(2)
        ]
        gate_yz = [
            carried.copy(2 + part, half(gate_z, part), gate_full.at[rows_of(part, 1, 0)], by_y)
            for part in range(2)
        ]
        up_yz = [
            carried.copy(4 + part, up_full.at[rows_of(part, 1, 0)], up_full.at[rows_of(part, 1, 0)], by_y)
            for part in range(2)
        ]
        down_z = carried.copy(6, down_own, down_full.at[unit(0, 0)], by_z)
        for copy in up_z + gate_yz + kept:
            copy.start()

    def product(place, columns):
        rows = pl.ds(pl.multiple_of(place * block, block), block)
        return contract(left_ref[rows, :], right_ref[:, columns], 1, 0)

    peak_out[...] = peak_ref[...]
    peak_step(0)
    run(
        sum_block(
            sum_bits, product, total, to_core, from_core, chip_sum, arrived, Links(sum_send, sum_recv)
        )
    )
    h2 = residual_ref[...].astype(f32) + total[...]
    h2_ref[...] = h2
    own[...] = (h2 * row_scale(h2) * gain_ref[...]).astype(bf16)
    spread = spread_block(spread_bits, own, out_ref, Links(send_sems, recv_sems), local_sem)
    spread[0]()
    if carry:
        for part in range(2):
            up_z[part].wait_recv()
            up_yz[part].start()
        down_z.start()
    for k, phase in enumerate(spread[1:-1]):
        phase()
        if k < len(bits):
            peak_step(k + 1)
    for k in range(len(spread) - 2, len(bits)):
        peak_step(k + 1)
    spread[-1]()
    if carry:
        for copy in kept:
            copy.wait()
        for copy in gate_yz + up_yz + [down_z]:
            copy.wait_recv()
        for copy in up_z + gate_yz + up_yz + [down_z]:
            copy.wait_send()


def branch(left, right, residual, gain, peak, carry, sum_bits, spread_bits, bit_count):
    block, width = residual.shape
    dma = pltpu.SemaphoreType.DMA
    shape = jax.ShapeDtypeStruct
    out_shape = [shape((block, width), f32), shape((8 * block, width), bf16), shape((8, 128), f32)]
    scratch = sum_scratch(block, width) + spread_scratch(block, width)
    scratch += [pltpu.VMEM((bit_count, 8, 128), f32), dma((bit_count,)), dma((bit_count,))]
    if carry:
        out_shape += [
            shape((32,) + carry[2].shape[1:], bf16), shape((32,) + carry[2].shape[1:], bf16),
            shape((4,) + carry[3].shape, bf16),
        ]
        scratch += [dma((7,)), dma((7,)), dma((12,))]
    return pl.pallas_call(
        functools.partial(branch_kernel, bool(carry), sum_bits, spread_bits),
        out_shape=tuple(out_shape),
        in_specs=[vmem] * 5 + [anywhere] * len(carry),
        out_specs=tuple([vmem, anywhere, vmem] + [anywhere] * (len(out_shape) - 3)),
        scratch_shapes=scratch,
        compiler_params=link_params(2),
        cost_estimate=cost(16 * block * left.shape[1] * width, 300e6),
        name="attention_branch",
    )(left, right, residual, gain, peak, *carry)


def norm_back(values, gain, upstream):
    scaled = upstream * gain
    scale = row_scale(values)
    inner = jnp.mean(scaled * values, -1, keepdims=True)
    return scale * scaled - scale * scale * scale * values * inner


def ffn_back_kernel(
    sum_bits, spread_bits, gate_ref, up_ref, gate_w_ref, up_w_ref, h2_ref, cot_ref, gain_ref, residual_ref, out_ref,
    total, to_core, from_core, chip_sum, arrived, sum_send, sum_recv, own, send_sems, recv_sems, local_sem,
):
    me = lax.axis_index(AXIS)
    block = total.shape[0]
    greet([flip_bit(me, bit) for bit in sorted(set(sum_bits) | set(spread_bits))])

    def product(place, columns):
        rows = pl.ds(pl.multiple_of(place * block, block), block)
        return contract(gate_ref[rows, :], gate_w_ref[columns, :], 1, 1) + contract(
            up_ref[rows, :], up_w_ref[columns, :], 1, 1
        )

    run(
        sum_block(
            sum_bits, product, total, to_core, from_core, chip_sum, arrived, Links(sum_send, sum_recv)
        )
    )
    residual = cot_ref[...].astype(f32) + norm_back(h2_ref[...], gain_ref[...], total[...])
    residual_ref[...] = residual
    own[...] = residual.astype(bf16)
    run(spread_block(spread_bits, own, out_ref, Links(send_sems, recv_sems), local_sem))


def ffn_back(gate, up, gate_w, up_w, h2, cot, gain, sum_bits, spread_bits):
    block, width = h2.shape
    return pl.pallas_call(
        functools.partial(ffn_back_kernel, sum_bits, spread_bits),
        out_shape=(
            jax.ShapeDtypeStruct((block, width), f32),
            jax.ShapeDtypeStruct((8 * block, width), bf16),
        ),
        in_specs=[vmem] * 7,
        out_specs=(vmem, anywhere),
        scratch_shapes=sum_scratch(block, width) + spread_scratch(block, width),
        compiler_params=link_params(3),
        cost_estimate=cost(32 * block * gate.shape[1] * width, 250e6),
        name="ffn_back",
    )(gate, up, gate_w, up_w, h2, cot, gain)


def last_sums_kernel(
    sum_bits, ffn_bits, left_ref, other_ref, right_ref, tokens_ref, gain_ref, residual_ref, hidden_ref, down_ref, h2_ref,
    out_ref, mixed_ref, *scratch,
):
    count = len(scratch) // 2
    me = lax.axis_index(AXIS)
    total, ffn_total = scratch[0], scratch[count]
    block = total.shape[0]
    greet([flip_bit(me, bit) for bit in sorted(set(sum_bits) | set(ffn_bits))])

    def rows_of(place):
        return pl.ds(pl.multiple_of(place * block, block), block)

    def product(place, columns):
        rows = rows_of(place)
        middle = left_ref.shape[1]
        return contract(left_ref[rows, :], right_ref[columns, 0:middle], 1, 1) + contract(
            other_ref[rows, :], right_ref[columns, middle : 2 * middle], 1, 1
        )

    def ffn_product(place, columns):
        return contract(hidden_ref[rows_of(place), :], down_ref[:, columns], 1, 0)

    first = sum_block(sum_bits, product, *scratch[: count - 2], Links(*scratch[count - 2 : count]))
    second = sum_block(ffn_bits, ffn_product, *scratch[count:-2], Links(*scratch[-2:]))
    for one, other in zip(first, second):
        one()
        other()
    out_ref[...] = residual_ref[...] + norm_back(
        tokens_ref[...].astype(f32), gain_ref[...], total[...]
    )
    mixed_ref[...] = (h2_ref[...] + ffn_total[...]).astype(bf16)


def last_sums(left, other, right, tokens, gain, residual, hidden, down, h2, sum_bits, ffn_bits):
    block, width = tokens.shape
    return pl.pallas_call(
        functools.partial(last_sums_kernel, sum_bits, ffn_bits),
        out_shape=(
            jax.ShapeDtypeStruct((block, width), f32), jax.ShapeDtypeStruct((block, width), bf16),
        ),
        in_specs=[vmem] * 9,
        out_specs=(vmem, vmem),
        scratch_shapes=sum_scratch(block, width) * 2,
        compiler_params=link_params(4),
        cost_estimate=cost(16 * block * right.size // 8, 300e6),
        name="last_sums",
    )(left, other, right, tokens, gain, residual, hidden, down, h2)


def home_kernel(bits, places, sources, *refs):
    count = len(places)
    mine, refs = refs[:sources], refs[sources:]
    weights, gain_ref, outs, gain_out = refs[:count], refs[count], refs[count + 1 : 2 * count + 1], refs[2 * count + 1]
    arrived, (send_sems, recv_sems, local_sems) = refs[2 * count + 2 : -3], refs[-3:]
    me = lax.axis_index(AXIS)
    team = mine[0].shape[0]

    def mate(offset):
        device, place = me, 0
        for k, bit in enumerate(bits):
            moved = (offset >> k) % 2
            place = place + lax.rem(bit_of(me, bit) + moved, 2) * (1 << k)
            device = flip_bit(device, bit) if moved else device
        return device, place

    greet([mate(k)[0] for k in range(1, team)])
    links = Links(send_sems, recv_sems)
    own = mate(0)[1]
    copies, kept = [], []
    for i, (source, landed) in enumerate(zip(mine, arrived)):
        kept.append(pltpu.make_async_copy(source.at[own], landed.at[own], local_sems.at[i]))
        for k in range(1, team):
            device, place = mate(k)
            copies.append(links.copy(i * team + k, source.at[place], landed.at[own], device))
    for copy in copies + kept:
        copy.start()
    for copy in copies:
        copy.wait_recv()
    for copy in kept:
        copy.wait()
    for out, moves in zip(outs, places):
        for source, member, first, target, columns in moves:
            out[:, target : target + columns] = arrived[source][member, :, first : first + columns].astype(f32)
    total = jnp.zeros(gain_ref.shape, f32)
    for out, weight in zip(outs, weights):
        for first in range(0, out.shape[1], 1024):
            product = out[:, first : first + 1024] * weight[:, first : first + 1024].astype(f32)
            total += jnp.sum(product, 1, keepdims=True)
    gain_out[...] = total / gain_ref[...]
    for copy in copies:
        copy.wait_send()


def home(parts, weights, gain, bits, places, collective_id, name):
    shape = jax.ShapeDtypeStruct
    dma = pltpu.SemaphoreType.DMA
    count, slots = len(weights), len(parts) * parts[0].shape[0]
    return pl.pallas_call(
        functools.partial(home_kernel, bits, places, len(parts)),
        out_shape=tuple(shape(w.shape, f32) for w in weights) + (shape((gain.shape[0], 1), f32),),
        in_specs=[vmem] * (len(parts) + count + 1),
        out_specs=tuple([vmem] * (count + 1)),
        scratch_shapes=[pltpu.VMEM(part.shape, bf16) for part in parts]
        + [dma((slots,)), dma((slots,)), dma((len(parts),))],
        compiler_params=link_params(collective_id),
        cost_estimate=cost(1e6, 30e6),
        name=name,
    )(*parts, *weights, gain.astype(f32).reshape(-1, 1))


def body(
    tokens, block_of, clip_limit, norm_attn, w_query, w_key, w_value, w_out,
    norm_ffn, w_gate, w_up, w_down, cotangent,
):
    tok_rows, width = tokens.shape
    devices = lax.axis_size(AXIS)
    team = SEQ // tok_rows
    teams = devices // team
    head_total = width // HEAD_DIM
    heads = head_total // team
    head_cols = heads * HEAD_DIM
    ff_rows = w_down.shape[0]
    weight_rows = w_gate.shape[0]
    ff_cols = w_gate.shape[1] // team
    device = lax.axis_index(AXIS)
    mate = device % team
    bit_count = devices.bit_length() - 1
    attn_bits, ffn_bits = (1, 2, 4), (1, 2, 8)
    data_bits = [4] + [1 << k for k in range(4, bit_count)]
    in_team = [[g * team + b for b in range(team)] for g in range(teams)]
    across = [[g * team + b for g in range(teams)] for b in range(team)]
    ffn_team = [
        [g * 16 + z * 8 + y * 4 + c for z in range(2) for c in range(4)]
        for g in range(devices // 16)
        for y in range(2)
    ]

    def flip(x, bit):
        return lax.ppermute(x, AXIS, [(i, i ^ bit) for i in range(devices)])

    def gather_across(x):
        return lax.all_gather(x, AXIS, axis=0, tiled=True, axis_index_groups=across)

    def scatter_across(x):
        return lax.psum_scatter(
            x.astype(bf16), AXIS, scatter_dimension=0, tiled=True, axis_index_groups=across
        )

    def swap(x, groups):
        return lax.all_to_all(x, AXIS, 0, 0, tiled=True, axis_index_groups=groups)

    def dim_of(bit):
        return bit_count - bit.bit_length()

    def data_pieces(x):
        pieces = {0: x}
        for bit in reversed(data_bits):
            for key in list(pieces):
                pieces[key | bit] = flip(pieces[key], bit)
        return pieces

    def place_pieces(pieces, dims, shape):
        total = jnp.zeros(shape, bf16)
        for key, piece in pieces.items():
            start = [0] * len(shape)
            size = list(shape)
            for bit in data_bits:
                start[dims[bit]] = ((device // bit) + (1 if key & bit else 0)) % 2
                size[dims[bit]] = 1
            total = lax.dynamic_update_slice(total, piece.reshape(size), start)
        return total

    def after_bit(dims, bit):
        return {b: d - (d > dims[bit]) for b, d in dims.items() if b != bit}

    def data_sum(x, dims, bits):
        for bit in bits:
            mine = (device // bit) % 2
            keep = lax.dynamic_index_in_dim(x, mine, dims[bit], False)
            sent = flip(lax.dynamic_index_in_dim(x, 1 - mine, dims[bit], False), bit)
            x = (keep.astype(f32) + sent.astype(f32)).astype(bf16)
            dims = after_bit(dims, bit)
        return x

    def head_columns(weight):
        split = weight.reshape(weight_rows, heads, team, HEAD_DIM)
        return split.transpose(2, 0, 1, 3).reshape(team, weight_rows, head_cols)

    def ffn_out(weight):
        split = weight.reshape(weight_rows, devices // 16, 2, 2, 4, ff_rows)
        return split.transpose(2, 4, 0, 1, 3, 5).reshape(team, weight_rows, ff_cols)

    row_dims = {bit: dim_of(bit) for bit in data_bits}
    row_shape = (2,) * bit_count
    unit_dims = {bit: i for i, bit in enumerate(reversed(data_bits))}
    unit_shape = (2,) * len(data_bits)

    def tie(*values):
        return lax.optimization_barrier(values)

    by_head = [head_columns(w) for w in (w_query, w_key, w_value)]
    qkv_mine = jnp.concatenate(
        [w[:, :, p * PAIR : (p + 1) * PAIR] for p in range(heads // 2) for w in by_head], 2
    )
    gain_row = jnp.concatenate([norm_attn, norm_ffn]).astype(f32)
    gain_row = jnp.pad(gain_row, (0, 128 - 2 * weight_rows)).reshape(1, 128)
    block_rows = block_of.astype(f32).reshape(tok_rows // 128, 128)
    small = jnp.concatenate([gain_row, block_rows, jnp.zeros((7 - tok_rows // 128, 128), f32)])
    qkv_mine, gate_rows, up_rows = tie(qkv_mine, w_gate, w_up)
    both_mine = swap(jnp.concatenate([ffn_out(gate_rows), ffn_out(up_rows)], 2), ffn_team)
    team_tokens, qkv_w, gathered = front(tokens, qkv_mine, small, teams)
    qkv_w = qkv_w.reshape(width, 3 * head_cols)
    gain_attn = gathered[:, 0, :weight_rows].reshape(1, width)
    gain_ffn = gathered[:, 0, weight_rows : 2 * weight_rows].reshape(1, width)
    blocks = lax.dynamic_slice_in_dim(gathered, device - mate, team, 0)
    blocks = blocks[:, 1 : 1 + tok_rows // 128].astype(jnp.int32).reshape(SEQ)
    row_blocks, col_blocks = blocks.reshape(1, SEQ), blocks.reshape(SEQ, 1)
    both_mine, down_mine, qkv_w, out_mine = tie(both_mine, w_down, qkv_w, w_out)
    if weight_rows == HEAD_DIM:
        out_w = gather_across(out_mine)
    else:
        out_all = lax.all_gather(out_mine, AXIS, axis=0, tiled=True)
        out_w = lax.dynamic_index_in_dim(
            out_all.reshape(heads, team, HEAD_DIM, width), mate, 1, False
        ).reshape(head_cols, width)

    def whole_rows(mine):
        shape = row_shape + (weight_rows, ff_cols)
        return place_pieces(data_pieces(mine), row_dims, shape).reshape(width, ff_cols)

    team_tokens = team_tokens.astype(f32)
    normed_attn = (team_tokens * row_scale(team_tokens) * gain_attn).astype(bf16)
    qkv = contract(normed_attn, qkv_w, 1, 0)
    cosine, sine = rope_tables(SEQ, PAIR)
    qkv, cot_mine = tie(qkv, cotangent)
    if data_bits == [4, 16]:
        gate_z = flip(both_mine[:, :, :ff_cols], 16)
        carry = [both_mine, flip(both_mine, 4), gate_z, down_mine, flip(down_mine, 4)]
    else:
        carry = []
    query, key, value, attended, lse, peak = attend_forward(qkv, cosine, sine, row_blocks, col_blocks)
    peaks = jnp.where(
        (jnp.arange(head_total) % team) == mate, jnp.repeat(peak[0, :heads], team), -jnp.inf
    )
    peaks = jnp.broadcast_to(jnp.pad(peaks, (0, 128 - head_total))[None], (8, 128))
    after_attn, normed_ffn, peaks, *full = branch(
        attended, out_w, tokens, gain_ffn, peaks, carry, attn_bits, ffn_bits, bit_count
    )
    head_peak = peaks[0, :head_total]
    if carry:
        gate_w, up_w = (w.reshape(width, ff_cols) for w in full[:2])
        z_side, y_side = (device // 16) % 2, (device // 4) % 2
        passed = lax.dynamic_index_in_dim(full[2], (1 - z_side) * 2 + y_side, 0, True)
        down_w = lax.dynamic_update_slice(
            full[2], flip(passed, 4), ((1 - z_side) * 2 + 1 - y_side, 0, 0)
        ).reshape(ff_cols, width)
    else:
        gate_w, up_w = whole_rows(both_mine[:, :, :ff_cols]), whole_rows(both_mine[:, :, ff_cols:])
        down_w = place_pieces(
            data_pieces(down_mine), unit_dims, unit_shape + (ff_rows, width)
        ).reshape(ff_cols, width)
    gate_pre = contract(normed_ffn, gate_w, 1, 0)
    up_pre = contract(normed_ffn, up_w, 1, 0)
    sigmoid_gate = jax.nn.sigmoid(gate_pre)
    silu_gate = gate_pre * sigmoid_gate
    hidden = (silu_gate * up_pre).astype(bf16)

    team_cot = lax.all_gather(cot_mine, AXIS, axis=0, tiled=True, axis_index_groups=ffn_team)
    d_down = contract(hidden, team_cot, 0, 0).astype(bf16).reshape(unit_shape + (ff_rows, width))
    team_cot, d_down = tie(team_cot, d_down)
    d_hidden = contract(team_cot, down_w, 1, 1)
    grad_gate = (d_hidden * up_pre * sigmoid_gate * (1.0 + gate_pre * (1.0 - sigmoid_gate))).astype(bf16)
    grad_up = (d_hidden * silu_gate).astype(bf16)

    def row_part(grad):
        part = contract(normed_ffn, grad, 0, 0).astype(bf16)
        return part.reshape(row_shape + (weight_rows, ff_cols))

    d_gate = row_part(grad_gate)
    d_down = data_sum(d_down, unit_dims, data_bits[:1])
    grad_gate, d_down, d_gate = tie(grad_gate, d_down, d_gate)
    d_residual, branch_grad = ffn_back(
        grad_gate, grad_up, gate_w, up_w, after_attn, cotangent, gain_ffn, ffn_bits, attn_bits
    )
    unit_rest, row_rest = after_bit(unit_dims, data_bits[0]), after_bit(row_dims, data_bits[0])
    d_down = data_sum(d_down, unit_rest, data_bits[1:])
    d_gate = data_sum(d_gate, row_dims, data_bits[:1])
    branch_grad, grad_up = tie(branch_grad, grad_up)
    d_up = row_part(grad_up)
    grad_attended = contract(branch_grad, out_w, 1, 1).astype(bf16)
    grad_attended, d_up, d_down, d_gate = tie(grad_attended, d_up, d_down, d_gate)

    def heads_back(pair):
        grads = attend_backward(
            pair, query, key, value, grad_attended, lse, cosine, sine, row_blocks, col_blocks
        )
        return grads, scatter_across(contract(normed_attn, grads, 0, 0))

    grad_pairs, shares = [None] * (heads // 2), [None] * (heads // 2)
    grad_pairs[0], shares[0] = heads_back(0)
    d_gate = data_sum(d_gate, row_rest, data_bits[1:])
    d_up = data_sum(d_up, row_dims, data_bits[:1])
    grad_attended, _, d_gate, d_up = tie(grad_attended, grad_pairs[0], d_gate, d_up)
    for p in range(1, heads // 2):
        grad_pairs[p], shares[p] = heads_back(p)
    d_up = data_sum(d_up, row_rest, data_bits[1:])
    out_part = contract(attended, branch_grad, 0, 0)
    if weight_rows == HEAD_DIM:
        d_out = scatter_across(out_part).astype(f32)
    else:
        spread = jnp.where(
            (jnp.arange(team) == mate)[None, :, None, None],
            out_part.reshape(heads, 1, HEAD_DIM, width), 0.0,
        ).reshape(width, width)
        d_out = lax.psum_scatter(spread, AXIS, scatter_dimension=0, tiled=True)
    d_tokens, mixed = last_sums(
        *grad_pairs, qkv_w, tokens, gain_attn, d_residual, hidden, down_w, after_attn, attn_bits, ffn_bits
    )
    d_down = d_down.astype(f32)
    attn_places = tuple(
        tuple(
            (g // 2, b, i * PAIR + (g % 2) * HEAD_DIM, (g * team + b) * HEAD_DIM, HEAD_DIM)
            for g in range(heads) for b in range(team)
        )
        for i in range(3)
    )
    ffn_places = tuple(
        tuple(
            (i, z * 4 + c, (2 * h + y) * ff_rows, (h * 16 + z * 8 + y * 4 + c) * ff_rows, ff_rows)
            for h in range(devices // 16) for z in range(2) for y in range(2) for c in range(4)
        )
        for i in range(2)
    )
    shares = [share.reshape(team, weight_rows, 3 * PAIR) for share in shares]
    d_query, d_key, d_value, d_norm_attn = home(
        shares, (w_query, w_key, w_value), norm_attn, attn_bits, attn_places, 5, "home_attn"
    )
    d_gate, d_up = (d.reshape(team, weight_rows, ff_cols) for d in (d_gate, d_up))
    d_gate, d_up, d_norm_ffn = home(
        (d_gate, d_up), (w_gate, w_up), norm_ffn, ffn_bits, ffn_places, 6, "home_ffn"
    )
    d_norm_attn, d_norm_ffn = d_norm_attn[:, 0], d_norm_ffn[:, 0]
    clip_value = clip_limit.astype(f32)
    factor = jnp.sqrt(clip_value / jnp.maximum(head_peak, clip_value))
    factors = jnp.repeat(factor, HEAD_DIM)[None, :]
    clipped_query = (w_query.astype(f32) * factors).astype(bf16)
    clipped_key = (w_key.astype(f32) * factors).astype(bf16)
    return (
        mixed, d_tokens, d_norm_attn, d_query, d_key, d_value, d_out, d_norm_ffn,
        d_gate, d_up, d_down, head_peak, clipped_query, clipped_key,
    )


def solution(mesh):
    rows, whole = P(AXIS, None), P(AXIS)
    return jax.shard_map(
        body,
        mesh=mesh,
        in_specs=(rows, whole, P(), whole, rows, rows, rows, rows, whole, rows, rows, rows, rows),
        out_specs=(
            rows, rows, whole, rows, rows, rows, rows, whole, rows, rows, rows, P(), rows, rows,
        ),
        check_vma=False,
    )
```

```python
import functools

import jax
import jax.numpy as jnp
import numpy as np
from jax import lax
from jax.experimental import pallas as pl
from jax.experimental.pallas import tpu as pltpu
from jax.sharding import PartitionSpec as P

HEAD_DIM = 64
SEQ = 2048
BLOCK = 256
HALF = 128
LAST_CUT = 0
EARLY_UP = 512
BRANCH_CUT = 128
AXIS = "fsdp"
MESH = pl.DeviceIdType.MESH

epsilon = 1e-05
rope_base = 130000.0
bf16 = jnp.bfloat16
f32 = jnp.float32
vmem = pl.BlockSpec(memory_space=pltpu.VMEM)
anywhere = pl.BlockSpec(memory_space=pl.ANY)


def contract(left, right, left_dim, right_dim):
    return lax.dot_general(
        left, right, (((left_dim,), (right_dim,)), ((), ())), preferred_element_type=f32
    )


def rope_tables(length, width):
    half_dim = HEAD_DIM // 2
    inverse = rope_base ** (-np.arange(half_dim) * 2.0 / HEAD_DIM)
    angles = (np.arange(length, dtype=np.float32)[:, None] * inverse.astype(np.float32)).astype(np.float64)
    cosine, sine = np.cos(angles).astype(np.float32), np.sin(angles).astype(np.float32)
    repeats = width // HEAD_DIM
    return (
        jnp.asarray(np.tile(np.concatenate([cosine, cosine], 1), (1, repeats))),
        jnp.asarray(np.tile(np.concatenate([-sine, sine], 1), (1, repeats))),
    )


def swap_halves(rows):
    width = rows.shape[1]
    half = HEAD_DIM // 2
    lane = lax.broadcasted_iota(jnp.int32, rows.shape, 1)
    return jnp.where(
        lane % HEAD_DIM < half, pltpu.roll(rows, width - half, 1), pltpu.roll(rows, half, 1)
    )


PAIR = 2 * HEAD_DIM


def head_mask(shape, head):
    lane = lax.broadcasted_iota(jnp.int32, shape, 1)
    return (lane >= head * HEAD_DIM) & (lane < (head + 1) * HEAD_DIM)


def masked_scores(query, key_ref, row_ref, col_ref, q0, cols):
    tail = min(2 * BLOCK, cols)
    scores = contract(query, key_ref[0:cols, :], 1, 1)
    shown = row_ref[:, pl.ds(cols - tail, tail)] <= col_ref[pl.ds(q0, BLOCK), :]
    hidden = jnp.where(shown, scores[:, cols - tail :], -jnp.inf)
    return jnp.concatenate([scores[:, : cols - tail], hidden], 1) if tail < cols else hidden


def attend_forward_kernel(
    qkv_ref, cos_ref, sin_ref, row_ref, col_ref, q_ref, k_ref, v_ref, out_ref, lse_ref, peak_ref
):
    pairs, length, _ = q_ref.shape
    for t in range(length // BLOCK):
        rows = pl.ds(t * BLOCK, BLOCK)
        cosine, sine = cos_ref[rows, :], sin_ref[rows, :]
        for pair in range(pairs):
            first = 3 * pair * PAIR
            query = qkv_ref[rows, first : first + PAIR]
            query = (query * cosine + swap_halves(query) * sine).astype(bf16)
            q_ref[pair, rows, :] = (query.astype(f32) * HEAD_DIM ** (-0.5)).astype(bf16)
            key = qkv_ref[rows, first + PAIR : first + 2 * PAIR]
            k_ref[pair, rows, :] = (key * cosine + swap_halves(key) * sine).astype(bf16)
            v_ref[pair, rows, :] = qkv_ref[rows, first + 2 * PAIR : first + 3 * PAIR].astype(bf16)
    peak_ref[...] = jnp.full(peak_ref.shape, -jnp.inf, f32)
    lane = lax.broadcasted_iota(jnp.int32, (BLOCK, 128), 1)
    for t in range(length // BLOCK):
        q0 = t * BLOCK
        rows = pl.ds(q0, BLOCK)
        cols = min(q0 + 2 * BLOCK, length)

        @pl.loop(0, pairs)
        def _(pair):
            total = jnp.zeros((BLOCK, PAIR), f32)
            for sub in range(2):
                head = 2 * pair + sub
                mask = head_mask((BLOCK, PAIR), sub)
                query = jnp.where(mask, q_ref[pair, rows, :], 0).astype(bf16)
                scores = masked_scores(query, k_ref.at[pair], row_ref, col_ref, q0, cols)
                row_max = jnp.max(scores, 1, keepdims=True)
                numerators = jnp.exp(scores - row_max)
                totals = jnp.sum(numerators, 1, keepdims=True)
                mixed = contract(numerators.astype(bf16), v_ref[pair, 0:cols, :], 1, 0) / totals
                total = jnp.where(mask, mixed, total)
                lse_ref[rows, :] = jnp.where(lane == head, row_max + jnp.log(totals), lse_ref[rows, :])
                peak_ref[...] = jnp.where(
                    lax.broadcasted_iota(jnp.int32, peak_ref.shape, 1) == head,
                    jnp.maximum(peak_ref[...], jnp.max(row_max)),
                    peak_ref[...],
                )
            out_ref[rows, pl.ds(pl.multiple_of(pair * PAIR, PAIR), PAIR)] = total.astype(bf16)


def attend_forward(qkv, cosine, sine, row_blocks, col_blocks):
    length = qkv.shape[0]
    pairs = qkv.shape[1] // (3 * PAIR)
    shape = jax.ShapeDtypeStruct
    return pl.pallas_call(
        attend_forward_kernel,
        out_shape=(
            shape((pairs, length, PAIR), bf16),
            shape((pairs, length, PAIR), bf16),
            shape((pairs, length, PAIR), bf16),
            shape((length, pairs * PAIR), bf16),
            shape((length, 128), f32),
            shape((8, 128), f32),
        ),
        in_specs=[vmem] * 5,
        out_specs=tuple([vmem] * 6),
        compiler_params=pltpu.CompilerParams(vmem_limit_bytes=56 * 1024 * 1024),
        cost_estimate=pl.CostEstimate(
            flops=16 * pairs * length * length * PAIR, bytes_accessed=length * PAIR * pairs * 24,
            transcendentals=2 * pairs * length * length,
        ),
        name="attend_forward",
    )(qkv, cosine, sine, row_blocks, col_blocks)


def attend_backward_kernel(
    first_head, q_ref, k_ref, v_ref, grad_ref, lse_ref, cos_ref, sin_ref, row_ref, col_ref, out_ref, dk_ref, dv_ref
):
    length = q_ref.shape[0]
    dk_ref[...] = jnp.zeros_like(dk_ref)
    dv_ref[...] = jnp.zeros_like(dv_ref)
    lane = lax.broadcasted_iota(jnp.int32, (BLOCK, 128), 1)
    for t in range(length // BLOCK):
        q0 = t * BLOCK
        rows = pl.ds(q0, BLOCK)
        cols = min(q0 + 2 * BLOCK, length)

        def one_head(sub, dq):
            mask = head_mask((BLOCK, PAIR), sub)
            query = jnp.where(mask, q_ref[rows, :], 0).astype(bf16)
            grad = jnp.where(mask, grad_ref[rows, :], 0).astype(bf16)
            lse = jnp.sum(
                jnp.where(lane == first_head + sub, lse_ref[rows, :], 0.0), 1, keepdims=True
            )
            scores = masked_scores(query, k_ref, row_ref, col_ref, q0, cols)
            attention = jnp.exp(scores - lse)
            grad_attention = contract(grad, v_ref[0:cols, :], 1, 1)
            weighted = attention * grad_attention
            centre = jnp.sum(weighted, 1, keepdims=True)
            grad_scores = (weighted - attention * centre).astype(bf16)
            dv_ref[0:cols, :] += contract(attention.astype(bf16), grad, 0, 0)
            dk_ref[0:cols, :] += contract(grad_scores, query, 0, 0)
            return jnp.where(mask, contract(grad_scores, k_ref[0:cols, :], 1, 0), dq)

        dq = lax.fori_loop(0, 2, one_head, jnp.zeros((BLOCK, PAIR), f32)) * HEAD_DIM ** (-0.5)
        out_ref[rows, 0:PAIR] = (dq * cos_ref[rows, :] - swap_halves(dq) * sin_ref[rows, :]).astype(bf16)
    for t in range(length // BLOCK):
        rows = pl.ds(t * BLOCK, BLOCK)
        dk = dk_ref[rows, :]
        out_ref[rows, PAIR : 2 * PAIR] = (
            dk * cos_ref[rows, :] - swap_halves(dk) * sin_ref[rows, :]
        ).astype(bf16)
        out_ref[rows, 2 * PAIR : 3 * PAIR] = dv_ref[rows, :].astype(bf16)


def attend_backward(pair, query, key, value, grad, lse, cosine, sine, row_blocks, col_blocks):
    length = query.shape[1]
    heads = pl.BlockSpec((None, length, PAIR), lambda _: (pair, 0, 0))
    return pl.pallas_call(
        functools.partial(attend_backward_kernel, 2 * pair),
        grid=(1,),
        out_shape=jax.ShapeDtypeStruct((length, 3 * PAIR), bf16),
        in_specs=[heads] * 3 + [pl.BlockSpec((length, PAIR), lambda _: (0, pair))] + [vmem] * 5,
        out_specs=vmem,
        scratch_shapes=[pltpu.VMEM((length, PAIR), f32), pltpu.VMEM((length, PAIR), f32)],
        compiler_params=pltpu.CompilerParams(vmem_limit_bytes=56 * 1024 * 1024),
        cost_estimate=pl.CostEstimate(
            flops=40 * length * length * PAIR, bytes_accessed=length * PAIR * 24,
            transcendentals=2 * length * length,
        ),
        name="attend_backward",
    )(query, key, value, grad, lse, cosine, sine, row_blocks, col_blocks)


def bit_of(index, bit):
    return lax.rem(lax.div(index, bit), 2)


def flip_bit(index, bit):
    return index + bit - 2 * bit * bit_of(index, bit)


def team_mate(me, bits, offset):
    device, place = me, 0
    for k, bit in enumerate(bits):
        moved = (offset >> k) % 2
        place = place + lax.rem(bit_of(me, bit) + moved, 2) * (1 << k)
        device = flip_bit(device, bit) if moved else device
    return device, place


class Links:

    def __init__(self, send_sems, recv_sems):
        self.send_sems, self.recv_sems = send_sems, recv_sems

    def copy(self, slot, src, dst, device):
        return pltpu.make_async_remote_copy(
            src_ref=src, dst_ref=dst, send_sem=self.send_sems.at[slot],
            recv_sem=self.recv_sems.at[slot], device_id=(device,), device_id_type=MESH,
        )


def greet(partners):
    barrier = pltpu.get_barrier_semaphore()
    for partner in partners:
        pl.semaphore_signal(barrier, inc=1, device_id=(partner,), device_id_type=MESH)
    pl.semaphore_wait(barrier, len(partners))


def spread_block(bits, cut, own_ref, out_ref, links, local_sem):
    core, first, second = bits
    me = lax.axis_index(AXIS)
    sibling, next_a, next_b = (flip_bit(me, bit) for bit in bits)
    block = own_ref.shape[0]
    in_a, in_b = bit_of(me, first), bit_of(me, second)
    spans = {None: (0, block), 0: (0, cut), 1: (cut, block - cut)}

    def rows(flip_a, flip_b, part):
        place = bit_of(me, core)
        place = place + 2 * lax.rem(in_a + flip_a, 2) + 4 * lax.rem(in_b + flip_b, 2)
        start, size = spans[part]
        return pl.ds(pl.multiple_of(place * block + start, 16), size)

    def passed(slot, where, device):
        return links.copy(slot, out_ref.at[where], out_ref.at[where], device)

    def first_hand(slot, part, device):
        start, size = spans[part]
        return links.copy(slot, own_ref.at[pl.ds(start, size)], out_ref.at[rows(0, 0, part)], device)

    makers = {
        0: lambda: first_hand(0, 0, next_a),
        1: lambda: first_hand(1, 1, next_b),
        2: lambda: first_hand(2, 1, next_a),
        3: lambda: first_hand(3, 0, next_b),
        4: lambda: links.copy(4, own_ref, out_ref.at[rows(0, 0, None)], sibling),
        5: lambda: passed(5, rows(1, 0, 0), next_b),
        6: lambda: passed(6, rows(1, 0, 0), sibling),
        7: lambda: passed(7, rows(0, 1, 1), next_a),
        8: lambda: passed(8, rows(0, 1, 1), sibling),
        9: lambda: passed(9, rows(1, 0, 1), sibling),
        10: lambda: passed(10, rows(0, 1, 0), sibling),
        11: lambda: passed(11, rows(1, 1, 0), sibling),
        12: lambda: passed(12, rows(1, 1, 1), sibling),
    }
    needs = {0: 0, 1: 1, 2: 1, 3: 0, 4: None, 5: 0, 6: 0, 7: 1, 8: 1, 9: 1, 10: 0, 11: 0, 12: 1}
    copies = {slot: make() for slot, make in makers.items() if spans[needs[slot]][1]}
    keep = pltpu.make_async_copy(own_ref, out_ref.at[rows(0, 0, None)], local_sem)

    def begin():
        for slot in range(5):
            if slot in copies:
                copies[slot].start()
        keep.start()

    def hand_on(arrived, *sent):
        def phase():
            if arrived in copies:
                copies[arrived].wait_recv()
                for slot in sent:
                    copies[slot].start()

        return phase

    def finish():
        for slot in (4, 6, 8, 9, 10, 11, 12):
            if slot in copies:
                copies[slot].wait_recv()
        keep.wait()
        for slot in copies:
            copies[slot].wait_send()

    return [
        begin, hand_on(0, 5, 6), hand_on(1, 7, 8), hand_on(2, 9), hand_on(3, 10),
        hand_on(5, 11), hand_on(7, 12), finish,
    ]


def run(phases):
    for phase in phases:
        phase()


SPREAD_COPIES = 13
SUM_COPIES = 10


def sum_block(bits, cut, product, total, to_core, from_core, chip_sum, arrived, links):
    core, first, second = bits
    me = lax.axis_index(AXIS)
    sibling, next_a, next_b = (flip_bit(me, bit) for bit in bits)
    block, width = total.shape
    tile = 512

    def place(step, other_core):
        flip_a, flip_b = 1 - step // 2, 1 - step % 2
        return (
            lax.rem(bit_of(me, core) + other_core, 2)
            + 2 * lax.rem(bit_of(me, first) + flip_a, 2)
            + 4 * lax.rem(bit_of(me, second) + flip_b, 2)
        )

    low, high = (0, cut), (cut, block - cut)
    landing = range(6) if cut else {1: 0, 3: 1, 4: 2}

    def link(slot, step, span, device):
        return links.copy(slot, chip_sum.at[step, pl.ds(*span)], arrived.at[landing[slot - 4], pl.ds(0, span[1])], device)

    diag_a, diag_b = (link(4, 0, low, next_a) if cut else None), link(5, 0, high, next_b)
    plain_a, plain_b = (link(6, 1, low, next_a) if cut else None), link(7, 2, high, next_b)
    last_a, last_b = link(8, 1, high, next_a), (link(9, 2, low, next_b) if cut else None)

    def core_copy(step):
        return links.copy(step, to_core.at[step], from_core.at[step], sibling)

    def for_sibling():
        @pl.loop(0, 4)
        def _(step):
            @pl.loop(0, width // tile)
            def _(column):
                columns = pl.ds(pl.multiple_of(column * tile, tile), tile)
                to_core[step, :, columns] = product(place(step, 1), columns).astype(bf16)

            core_copy(step).start()

    def for_chip():
        @pl.loop(0, 4)
        def _(step):
            core_copy(step).wait_recv()

            @pl.loop(0, width // tile)
            def _(column):
                columns = pl.ds(pl.multiple_of(column * tile, tile), tile)
                summed = product(place(step, 0), columns) + from_core[step, :, columns].astype(f32)
                total[:, columns] = summed

                @pl.when(step < 3)
                def _():
                    chip_sum[step, :, columns] = summed.astype(bf16)

            @pl.when(step == 0)
            def _():
                if cut:
                    diag_a.start()
                diag_b.start()

            @pl.when(step == 1)
            def _():
                if cut:
                    plain_a.start()

            @pl.when(step == 2)
            def _():
                plain_b.start()

    def add(step, span, slot):
        rows = pl.ds(*span)
        chip_sum[step, rows, :] = (
            chip_sum[step, rows, :].astype(f32) + arrived[landing[slot], 0 : span[1], :].astype(f32)
        ).astype(bf16)

    def take(span, slot):
        total[pl.ds(*span), :] += arrived[landing[slot], 0 : span[1], :].astype(f32)

    def hand_on():
        if cut:
            diag_a.wait_recv()
            add(2, low, 0)
            last_b.start()
        diag_b.wait_recv()
        add(1, high, 1)
        last_a.start()

    def finish():
        if cut:
            plain_a.wait_recv()
            take(low, 2)
        plain_b.wait_recv()
        take(high, 3)
        if cut:
            last_b.wait_recv()
            take(low, 5)
        last_a.wait_recv()
        take(high, 4)

        @pl.loop(0, 4)
        def _(step):
            core_copy(step).wait_send()

        for copy in (diag_a, diag_b, plain_a, plain_b, last_a, last_b):
            if copy is not None:
                copy.wait_send()

    return for_sibling, for_chip, hand_on, finish


def sum_scratch(block, width, cut):
    return [
        pltpu.VMEM((block, width), f32),
        pltpu.VMEM((4, block, width), bf16),
        pltpu.VMEM((4, block, width), bf16),
        pltpu.VMEM((3, block, width), bf16),
        pltpu.VMEM((6 if cut else 3, block - cut, width), bf16),
        pltpu.SemaphoreType.DMA((SUM_COPIES,)),
        pltpu.SemaphoreType.DMA((SUM_COPIES,)),
    ]


def spread_scratch(block, width):
    return [
        pltpu.VMEM((block, width), bf16),
        pltpu.SemaphoreType.DMA((SPREAD_COPIES,)),
        pltpu.SemaphoreType.DMA((SPREAD_COPIES,)),
        pltpu.SemaphoreType.DMA,
    ]


def link_params(collective_id):
    return pltpu.CompilerParams(
        collective_id=collective_id, has_side_effects=True, vmem_limit_bytes=60 * 1024 * 1024
    )


def cost(flops, size):
    return pl.CostEstimate(flops=int(flops), bytes_accessed=int(size), transcendentals=0)


def row_scale(values):
    return lax.rsqrt(jnp.mean(values * values, -1, keepdims=True) + epsilon)


def front_kernel(
    team, teams, qkv_moves, ffn_moves, tokens_ref, query_ref, key_ref, value_ref, gate_ref, up_ref, small_ref,
    normed_out, weights_out, both_out, small_out,
    tokens_all, mine, both_mine, gain,
    send_sems, recv_sems, local_sem, swap_send, swap_recv, swap_local, line_send, line_recv, small_send, small_recv,
    both_send, both_recv, both_local, out_sems,
):
    me = lax.axis_index(AXIS)
    mate, group = lax.rem(me, team), lax.div(me, team)
    devices = team * teams
    mates = [group * team + lax.rem(mate + k, team) for k in range(1, team)]
    above, below = lax.rem(me + team, devices), lax.rem(me + devices - team, devices)
    ffn_mates = [team_mate(me, (1, 2, 8), k) for k in range(team)]
    rows = mine.shape[1]
    swaps, line, small = Links(swap_send, swap_recv), Links(line_send, line_recv), Links(small_send, small_recv)
    both = Links(both_send, both_recv)
    for i, member, source, target, columns in qkv_moves:
        weight = (query_ref, key_ref, value_ref)[i]
        mine[member, :, target : target + columns] = weight[:, source : source + columns]
    greet(
        mates + [lax.rem(me + k * team, devices) for k in range(1, teams)]
        + [device for device, _ in ffn_mates[4:]]
    )

    def share(place):
        return pl.ds(pl.multiple_of(place * rows, rows), rows)

    swap_copies = [
        swaps.copy(k, mine.at[lax.rem(mate + k + 1, team)], weights_out.at[group, share(mate)], mates[k])
        for k in range(team - 1)
    ]
    for copy in swap_copies:
        copy.start()
    keep = pltpu.make_async_copy(mine.at[mate], weights_out.at[group, share(mate)], swap_local)
    keep.start()
    small_out[me] = small_ref[...]

    others = [lax.rem(me + k * team, devices) for k in range(1, teams)]
    team_rows = pl.ds(pl.multiple_of(group * team, team), team)
    small_near = [
        small.copy(k, small_out.at[me], small_out.at[me], device) for k, device in enumerate(mates)
    ]
    small_far = [
        small.copy(team + k, small_out.at[team_rows], small_out.at[team_rows], device)
        for k, device in enumerate(others)
    ]
    for copy in small_near:
        copy.start()
    spread = spread_block(
        (1, 2, 4), HALF, tokens_ref, tokens_all, Links(send_sems, recv_sems), local_sem
    )
    for i, member, source, target, columns in ffn_moves:
        both_mine[member, :, target : target + columns] = (gate_ref, up_ref)[i][:, source : source + columns]

    def passed(slot, shard, device):
        return line.copy(slot, weights_out.at[shard], weights_out.at[shard], device)

    steps = teams - 1

    def up(step):
        return passed(step - 1, group - (step - 1), above)

    def down(step):
        return passed(steps + step - 1, group + (step - 1), below)

    def line_start(step):
        pl.when((group < teams - 1) & (group >= step - 1))(lambda: up(step).start())
        pl.when((group > 0) & (group + step - 1 < teams))(lambda: down(step).start())

    def line_wait(step):
        pl.when(group >= step)(lambda: up(step).wait_recv())
        pl.when(group + step < teams)(lambda: down(step).wait_recv())

    def line_sent(step):
        pl.when((group < teams - 1) & (group >= step - 1))(lambda: up(step).wait_send())
        pl.when((group > 0) & (group + step - 1 < teams))(lambda: down(step).wait_send())

    for copy in small_near:
        copy.wait_recv()
    for copy in small_far:
        copy.start()
    own_place = ffn_mates[0][1]
    both_copies = [
        both.copy(k, both_mine.at[ffn_mates[k][1]], both_out.at[own_place], ffn_mates[k][0])
        for k in range(1, team)
    ]
    for copy in both_copies:
        copy.start()
    both_keep = pltpu.make_async_copy(both_mine.at[own_place], both_out.at[own_place], both_local)
    both_keep.start()
    for copy in swap_copies:
        copy.wait_recv()
    keep.wait()
    line_start(1)
    spread[0]()
    for copy in small_far:
        copy.wait_recv()
    spread[1]()
    spread[2]()
    line_wait(1)
    line_start(2)
    spread[3]()
    spread[4]()
    width = tokens_all.shape[1]
    gains = width // devices
    for d in range(devices):
        gain[:, d * gains : (d + 1) * gains] = small_out[d, 0:1, 0:gains]
    for phase in spread[5:]:
        phase()
    block = tokens_ref.shape[0]

    def normed_copy(k):
        span = pl.ds(pl.multiple_of(k * block, block), block)
        return pltpu.make_async_copy(tokens_all.at[span], normed_out.at[span], out_sems.at[k])

    def norm_blocks(first, last):
        @pl.loop(first, last)
        def _(k):
            span = pl.ds(pl.multiple_of(k * block, block), block)
            values = tokens_all[span, :].astype(f32)
            tokens_all[span, :] = (values * row_scale(values) * gain[...]).astype(bf16)
            normed_copy(k).start()

    norm_blocks(0, 2)
    for step in range(2, teams):
        line_wait(step)
        if step < steps:
            line_start(step + 1)
        if step == 2:
            norm_blocks(2, team)
    for k in range(team):
        normed_copy(k).wait()
    for copy in both_copies:
        copy.wait_recv()
    both_keep.wait()
    for copy in swap_copies + both_copies:
        copy.wait_send()
    for step in range(1, teams):
        line_sent(step)
    for copy in small_near + small_far:
        copy.wait_send()


def front(tokens, weights, small, teams, qkv_moves, ffn_moves):
    block, width = tokens.shape
    team = 8
    rows, cols = weights[0].shape[0], 3 * width // team
    both_cols = 2 * weights[3].shape[1] // team
    devices = team * teams
    dma = pltpu.SemaphoreType.DMA
    shape = jax.ShapeDtypeStruct
    return pl.pallas_call(
        functools.partial(front_kernel, team, teams, qkv_moves, ffn_moves),
        out_shape=(
            shape((team * block, width), bf16),
            shape((teams, team * rows, cols), bf16),
            shape((team, rows, both_cols), bf16),
            shape((devices,) + small.shape, f32),
        ),
        in_specs=[vmem] * 7,
        out_specs=(anywhere, anywhere, anywhere, vmem),
        scratch_shapes=[
            pltpu.VMEM((team * block, width), bf16), pltpu.VMEM((team, rows, cols), bf16),
            pltpu.VMEM((team, rows, both_cols), bf16), pltpu.VMEM((1, width), f32),
        ]
        + spread_scratch(block, width)[1:]
        + [dma((team - 1,)), dma((team - 1,)), dma, dma((2 * teams,)), dma((2 * teams,)), dma((team + teams,)), dma((team + teams,))]
        + [dma((team,)), dma((team,)), dma, dma((team,))],
        compiler_params=link_params(1),
        cost_estimate=cost(0, 200e6),
        name="front",
    )(tokens, *weights, small)


def branch_kernel(
    carry, swap_bits, spread_bits, left_ref, right_ref, residual_ref, gain_ref, peak_ref, *refs,
):
    if carry:
        (both_own, both_y, both_z, down_own), refs = refs[:4], refs[4:]
        (h2_ref, out_ref, peak_out, gate_full, up_full, down_full), refs = refs[:6], refs[6:]
        (landed, together, swap_send, swap_recv, own, send_sems, recv_sems, local_sem,
         peak_in, peak_send, peak_recv, carry_send, carry_recv, carry_local) = refs
    else:
        (h2_ref, out_ref, peak_out), refs = refs[:3], refs[3:]
        (landed, together, swap_send, swap_recv, own, send_sems, recv_sems, local_sem,
         peak_in, peak_send, peak_recv) = refs
    me = lax.axis_index(AXIS)
    team, block, _ = landed.shape
    bits = [1 << k for k in range(peak_in.shape[0])]
    mates = [team_mate(me, swap_bits, k) for k in range(team)]
    greet([device for device, _ in mates[1:]] + [flip_bit(me, bit) for bit in bits if bit not in swap_bits])
    own_place = mates[0][1]

    def rows_at(place):
        return pl.ds(pl.multiple_of(place * block, block), block)

    swap_copies = [
        Links(swap_send, swap_recv).copy(k, left_ref.at[rows_at(mates[k][1])], landed.at[own_place], mates[k][0])
        for k in range(1, team)
    ]
    for copy in swap_copies:
        copy.start()
    peaks = Links(peak_send, peak_recv)

    def peak_copy(k):
        return peaks.copy(k, peak_out, peak_in.at[k], flip_bit(me, bits[k]))

    def peak_step(k):
        if k:
            peak_copy(k - 1).wait()
            peak_out[...] = jnp.maximum(peak_out[...], peak_in[k - 1])
        if k < len(bits):
            peak_copy(k).start()

    if carry:
        carried = Links(carry_send, carry_recv)
        high, middle = bit_of(me, 16), bit_of(me, 4)
        by_y, by_z = flip_bit(me, 4), flip_bit(me, 16)

        def rows_of(part, flip_z, flip_y):
            z, y = lax.rem(high + flip_z, 2), lax.rem(middle + flip_y, 2)
            return pl.ds(pl.multiple_of(z * 16 + part * 8 + y * 4, 4), 4)

        cols, early = both_own.shape[2] // 2, both_z.shape[2]

        def piece(source, part, first, last):
            return source.at[pl.ds(part * 4, 4), :, pl.ds(first, last - first)]

        def placed(part, flips, first, last):
            full, start = (gate_full, first) if last <= cols else (up_full, first - cols)
            return full.at[rows_of(part, *flips), :, pl.ds(start, last - first)]

        def unit(flip_z, flip_y):
            return lax.rem(high + flip_z, 2) * 2 + lax.rem(middle + flip_y, 2)

        spans = ((0, cols), (cols, 2 * cols))
        early_spans = ((0, cols), (cols, early))
        kept = []
        for source, flips, columns in ((both_own, (0, 0), spans), (both_y, (0, 1), spans), (both_z, (1, 0), early_spans)):
            for span in columns:
                for part in range(2):
                    kept.append((piece(source, part, *span), placed(part, flips, *span)))
        kept.append((down_own, down_full.at[unit(0, 0)]))
        kept = [pltpu.make_async_copy(a, b, carry_local.at[i]) for i, (a, b) in enumerate(kept)]
        late = (early, 2 * cols)
        up_z = [
            carried.copy(part, piece(both_own, part, *late), placed(part, (0, 0), *late), by_z) for part in range(2)
        ]
        early_yz = [
            carried.copy(2 + 2 * i + part, piece(both_z, part, *span), placed(part, (1, 0), *span), by_y)
            for i, span in enumerate(early_spans) for part in range(2)
        ]
        up_yz = [
            carried.copy(6 + part, placed(part, (1, 0), *late), placed(part, (1, 0), *late), by_y)
            for part in range(2)
        ]
        down_z = carried.copy(8, down_own, down_full.at[unit(0, 0)], by_z)
        down_y = carried.copy(9, down_own, down_full.at[unit(0, 0)], by_y)
        for copy in up_z + [down_y] + kept:
            copy.start()

    peak_out[...] = peak_ref[...]
    peak_step(0)
    landed[own_place] = left_ref[rows_at(own_place), :]
    for copy in swap_copies:
        copy.wait_recv()
    heads = landed.shape[2] // HEAD_DIM
    for b in range(team):
        for g in range(heads):
            first = (g * team + b) * HEAD_DIM
            together[:, first : first + HEAD_DIM] = landed[b, :, g * HEAD_DIM : (g + 1) * HEAD_DIM]
    tile = 512

    @pl.loop(0, own.shape[1] // tile)
    def _(column):
        columns = pl.ds(pl.multiple_of(column * tile, tile), tile)
        h2_ref[:, columns] = residual_ref[:, columns].astype(f32) + contract(
            together[...], right_ref[:, columns], 1, 0
        )

    h2 = h2_ref[...]
    own[...] = (h2 * row_scale(h2) * gain_ref[...]).astype(bf16)
    spread = spread_block(spread_bits, BRANCH_CUT, own, out_ref, Links(send_sems, recv_sems), local_sem)
    spread[0]()
    if carry:
        for copy in early_yz:
            copy.start()
        for part in range(2):
            up_z[part].wait_recv()
            up_yz[part].start()
        down_z.start()
    for k, phase in enumerate(spread[1:-1]):
        phase()
        if k < len(bits):
            peak_step(k + 1)
    for k in range(len(spread) - 2, len(bits)):
        peak_step(k + 1)
    spread[-1]()
    for copy in swap_copies:
        copy.wait_send()
    if carry:
        for copy in kept:
            copy.wait()
        for copy in early_yz + up_yz + [down_y, down_z]:
            copy.wait_recv()
        for copy in up_z + early_yz + up_yz + [down_y, down_z]:
            copy.wait_send()


def branch(left, right, residual, gain, peak, carry, swap_bits, spread_bits, bit_count):
    block, width = residual.shape
    dma = pltpu.SemaphoreType.DMA
    shape = jax.ShapeDtypeStruct
    out_shape = [shape((block, width), f32), shape((8 * block, width), bf16), shape((8, 128), f32)]
    scratch = [pltpu.VMEM((8, block, left.shape[1]), bf16), pltpu.VMEM((block, width), bf16), dma((8,)), dma((8,))]
    scratch += spread_scratch(block, width)
    scratch += [pltpu.VMEM((bit_count, 8, 128), f32), dma((bit_count,)), dma((bit_count,))]
    if carry:
        out_shape += [
            shape((32, carry[0].shape[1], carry[0].shape[2] // 2), bf16),
            shape((32, carry[0].shape[1], carry[0].shape[2] // 2), bf16),
            shape((4,) + carry[3].shape, bf16),
        ]
        scratch += [dma((10,)), dma((10,)), dma((13,))]
    return pl.pallas_call(
        functools.partial(branch_kernel, bool(carry), swap_bits, spread_bits),
        out_shape=tuple(out_shape),
        in_specs=[vmem] * (5 + len(carry)),
        out_specs=tuple([vmem, anywhere, vmem] + [anywhere] * (len(out_shape) - 3)),
        scratch_shapes=scratch,
        compiler_params=link_params(2),
        cost_estimate=cost(16 * block * left.shape[1] * width, 300e6),
        name="attention_branch",
    )(left, right, residual, gain, peak, *carry)


def norm_back(values, gain, upstream):
    scaled = upstream * gain
    scale = row_scale(values)
    inner = jnp.mean(scaled * values, -1, keepdims=True)
    return scale * scaled - scale * scale * scale * values * inner


def ffn_back_kernel(
    sum_bits, swap_bits, gate_ref, up_ref, gate_w_ref, up_w_ref, normed_ref, out_w_ref, h2_ref, cot_ref, gain_ref,
    residual_ref, branch_ref, heads_out, d_gate_out, d_up_out,
    total, to_core, from_core, chip_sum, arrived, sum_send, sum_recv,
    swap_send, swap_recv, local_sem, stage, stage_sems,
):
    me = lax.axis_index(AXIS)
    block, width = total.shape
    team = 1 << len(swap_bits)
    mates = [team_mate(me, swap_bits, k) for k in range(team)]
    greet(
        [device for device, _ in mates[1:]] + [flip_bit(me, bit) for bit in sum_bits if bit not in swap_bits]
    )

    def product(place, columns):
        rows = pl.ds(pl.multiple_of(place * block, block), block)
        return contract(gate_ref[rows, :], gate_w_ref[columns, :], 1, 1) + contract(
            up_ref[rows, :], up_w_ref[columns, :], 1, 1
        )

    side = stage.shape[2]
    count = width // side
    outs = (d_gate_out, d_up_out)

    def stage_copy(k, which):
        span = pl.ds(pl.multiple_of(k * side, side), side)
        slot = lax.rem(k, 2)
        return pltpu.make_async_copy(stage.at[slot, which], outs[which].at[span], stage_sems.at[slot, which])

    def gradients(first, last):
        @pl.loop(first, last)
        def _(k):
            @pl.when(k >= 2)
            def _():
                for which in range(2):
                    stage_copy(k - 2, which).wait()

            columns = normed_ref[:, pl.ds(pl.multiple_of(k * side, side), side)]
            slot = lax.rem(k, 2)
            stage[slot, 0] = contract(columns, gate_ref[...], 0, 0).astype(bf16)
            stage[slot, 1] = contract(columns, up_ref[...], 0, 0).astype(bf16)
            for which in range(2):
                stage_copy(k, which).start()

    for_sibling, for_chip, hand_on, finish = sum_block(
        sum_bits, HALF, product, total, to_core, from_core, chip_sum, arrived, Links(sum_send, sum_recv)
    )
    for_sibling()
    for_chip()
    gradients(0, 1)
    hand_on()
    gradients(1, count - 2)
    finish()
    residual = cot_ref[...].astype(f32) + norm_back(h2_ref[...], gain_ref[...], total[...])
    residual_ref[...] = residual
    branch_ref[...] = residual.astype(bf16)
    tile, share = team * HEAD_DIM, width // team
    for g in range(width // tile):
        heads = contract(branch_ref[...], out_w_ref[g * tile : (g + 1) * tile, :], 1, 1).astype(bf16)
        for b in range(team):
            first = b * share + g * HEAD_DIM
            to_core[0, :, first : first + HEAD_DIM] = heads[:, b * HEAD_DIM : (b + 1) * HEAD_DIM]
    own_place = mates[0][1]
    own_rows = pl.ds(pl.multiple_of(own_place * block, block), block)
    def heads_of(place):
        return to_core.at[0, :, pl.ds(pl.multiple_of(place * share, share), share)]

    swap_copies = [
        Links(swap_send, swap_recv).copy(k, heads_of(mates[k][1]), heads_out.at[own_rows], mates[k][0])
        for k in range(1, team)
    ]
    keep = pltpu.make_async_copy(heads_of(own_place), heads_out.at[own_rows], local_sem)
    for copy in swap_copies + [keep]:
        copy.start()
    gradients(count - 2, count)
    for copy in swap_copies:
        copy.wait_recv()
    for copy in swap_copies:
        copy.wait_send()
    keep.wait()
    for k in range(count - 2, count):
        for which in range(2):
            stage_copy(k, which).wait()


def ffn_back(gate, up, gate_w, up_w, normed, out_w, h2, cot, gain, sum_bits, swap_bits):
    block, width = h2.shape
    shape = jax.ShapeDtypeStruct
    dma = pltpu.SemaphoreType.DMA
    ff_cols = gate.shape[1]
    return pl.pallas_call(
        functools.partial(ffn_back_kernel, sum_bits, swap_bits),
        out_shape=(
            shape((block, width), f32), shape((block, width), bf16), shape((8 * block, width // 8), bf16),
            shape((width, ff_cols), bf16), shape((width, ff_cols), bf16),
        ),
        in_specs=[vmem] * 9,
        out_specs=(vmem, vmem, anywhere, anywhere, anywhere),
        scratch_shapes=sum_scratch(block, width, HALF)
        + [dma((8,)), dma((8,)), dma]
        + [pltpu.VMEM((2, 2, 256, ff_cols), bf16), dma((2, 2))],
        compiler_params=link_params(3),
        cost_estimate=cost(96 * block * ff_cols * width, 200e6),
        name="ffn_back",
    )(gate, up, gate_w, up_w, normed, out_w, h2, cot, gain)


def last_sums_kernel(
    sum_bits, ffn_bits, left_ref, other_ref, right_ref, tokens_ref, gain_ref, residual_ref, hidden_ref, down_ref, h2_ref,
    gate_ref, out_ref, mixed_ref, gate_out, *scratch,
):
    (swap_send, swap_recv, swap_local), scratch = scratch[-3:], scratch[:-3]
    count = len(scratch) // 2
    me = lax.axis_index(AXIS)
    total, ffn_total = scratch[0], scratch[count]
    block = total.shape[0]
    mates = [team_mate(me, ffn_bits, k) for k in range(8)]
    partners = [flip_bit(me, bit) for bit in sum_bits if bit not in ffn_bits]
    greet(partners + [device for device, _ in mates[1:]])
    swaps, own_place = Links(swap_send, swap_recv), mates[0][1]
    swap_copies = [
        swaps.copy(k, gate_ref.at[mates[k][1]], gate_out.at[own_place], mates[k][0]) for k in range(1, 8)
    ]
    keep = pltpu.make_async_copy(gate_ref.at[own_place], gate_out.at[own_place], swap_local)

    def rows_of(place):
        return pl.ds(pl.multiple_of(place * block, block), block)

    def product(place, columns):
        rows = rows_of(place)
        middle = left_ref.shape[1]
        return contract(left_ref[rows, :], right_ref[columns, 0:middle], 1, 1) + contract(
            other_ref[rows, :], right_ref[columns, middle : 2 * middle], 1, 1
        )

    def ffn_product(place, columns):
        return contract(hidden_ref[rows_of(place), :], down_ref[:, columns], 1, 0)

    first = sum_block(sum_bits, LAST_CUT, product, *scratch[: count - 2], Links(*scratch[count - 2 : count]))
    second = sum_block(ffn_bits, LAST_CUT, ffn_product, *scratch[count:-2], Links(*scratch[-2:]))
    run(first[:2])
    run(second[:2])
    for copy in swap_copies + [keep]:
        copy.start()
    for one, other in zip(first[2:], second[2:]):
        one()
        other()
    out_ref[...] = residual_ref[...] + norm_back(
        tokens_ref[...].astype(f32), gain_ref[...], total[...]
    )
    mixed_ref[...] = (h2_ref[...] + ffn_total[...]).astype(bf16)
    for copy in swap_copies:
        copy.wait_recv()
    for copy in swap_copies:
        copy.wait_send()
    keep.wait()


def last_sums(left, other, right, tokens, gain, residual, hidden, down, h2, d_gate, sum_bits, ffn_bits):
    block, width = tokens.shape
    return pl.pallas_call(
        functools.partial(last_sums_kernel, sum_bits, ffn_bits),
        out_shape=(
            jax.ShapeDtypeStruct((block, width), f32), jax.ShapeDtypeStruct((block, width), bf16),
            jax.ShapeDtypeStruct(d_gate.shape, bf16),
        ),
        in_specs=[vmem] * 9 + [anywhere],
        out_specs=(vmem, vmem, anywhere),
        scratch_shapes=sum_scratch(block, width, LAST_CUT) * 2
        + [pltpu.SemaphoreType.DMA((8,)), pltpu.SemaphoreType.DMA((8,)), pltpu.SemaphoreType.DMA],
        compiler_params=link_params(4),
        cost_estimate=cost(16 * block * right.size // 8, 300e6),
        name="last_sums",
    )(left, other, right, tokens, gain, residual, hidden, down, h2, d_gate)


def home_kernel(teams, places, gain_of, sources, *refs):
    count = len(places)
    kinds = max(gain_of) + 1
    mine, refs = refs[:sources], refs[sources:]
    weights, refs = refs[:count], refs[count:]
    gains, refs = refs[:kinds], refs[kinds:]
    outs, refs = refs[:count], refs[count:]
    gain_outs, refs = refs[:kinds], refs[kinds:]
    landed, (send_sems, recv_sems, local_sems) = list(refs[:-3]), refs[-3:]
    me = lax.axis_index(AXIS)
    members = mine[0].shape[0]
    links = Links(send_sems, recv_sems)
    greeted = {}
    for bits in teams:
        for k in range(1, members) if bits else ():
            device, _ = team_mate(me, bits, k)
            greeted[tuple(sorted(bit for j, bit in enumerate(bits) if (k >> j) % 2))] = device
    greet(list(greeted.values()))
    copies, kept, arrived = [], [], []
    for i, (source, bits) in enumerate(zip(mine, teams)):
        if not bits:
            arrived.append(source)
            continue
        target = landed.pop(0)
        arrived.append(target)
        own = team_mate(me, bits, 0)[1]
        kept.append(pltpu.make_async_copy(source.at[own], target.at[own], local_sems.at[i]))
        for k in range(1, members):
            device, place = team_mate(me, bits, k)
            copies.append(links.copy(i * members + k, source.at[place], target.at[own], device))
    for copy in copies + kept:
        copy.start()
    totals = [jnp.zeros(gain.shape, f32) for gain in gains]

    def settle(i):
        out, weight = outs[i], weights[i]
        for source, member, first, target, columns in places[i]:
            out[:, target : target + columns] = arrived[source][member, :, first : first + columns].astype(f32)
        for first in range(0, out.shape[1], 1024):
            product = out[:, first : first + 1024] * weight[:, first : first + 1024].astype(f32)
            totals[gain_of[i]] += jnp.sum(product, 1, keepdims=True)

    ready = [i for i in range(count) if all(not teams[move[0]] for move in places[i])]
    for i in ready:
        settle(i)
    for copy in copies:
        copy.wait_recv()
    for copy in kept:
        copy.wait()
    for i in range(count):
        if i not in ready:
            settle(i)
    for gain, total, out in zip(gains, totals, gain_outs):
        out[...] = total / gain[...]
    for copy in copies:
        copy.wait_send()


def home(parts, teams, weights, gains, gain_of, places):
    shape = jax.ShapeDtypeStruct
    dma = pltpu.SemaphoreType.DMA
    count, slots = len(weights), len(parts) * parts[0].shape[0]
    gains = [gain.astype(f32).reshape(-1, 1) for gain in gains]
    return pl.pallas_call(
        functools.partial(home_kernel, teams, places, gain_of, len(parts)),
        out_shape=tuple(shape(w.shape, f32) for w in weights) + tuple(shape(g.shape, f32) for g in gains),
        in_specs=[vmem] * (len(parts) + count + len(gains)),
        out_specs=tuple([vmem] * (count + len(gains))),
        scratch_shapes=[pltpu.VMEM(part.shape, bf16) for part, bits in zip(parts, teams) if bits]
        + [dma((slots,)), dma((slots,)), dma((len(parts),))],
        compiler_params=link_params(5),
        cost_estimate=cost(1e6, 60e6),
        name="home",
    )(*parts, *weights, *gains)


def body(
    tokens, block_of, clip_limit, norm_attn, w_query, w_key, w_value, w_out,
    norm_ffn, w_gate, w_up, w_down, cotangent,
):
    tok_rows, width = tokens.shape
    devices = lax.axis_size(AXIS)
    team = SEQ // tok_rows
    teams = devices // team
    head_total = width // HEAD_DIM
    heads = head_total // team
    head_cols = heads * HEAD_DIM
    ff_rows = w_down.shape[0]
    weight_rows = w_gate.shape[0]
    ff_cols = w_gate.shape[1] // team
    device = lax.axis_index(AXIS)
    mate = device % team
    bit_count = devices.bit_length() - 1
    attn_bits, ffn_bits = (1, 2, 4), (1, 2, 8)
    data_bits = [4] + [1 << k for k in range(4, bit_count)]
    in_team = [[g * team + b for b in range(team)] for g in range(teams)]
    across = [[g * team + b for g in range(teams)] for b in range(team)]
    ffn_team = [
        [g * 16 + z * 8 + y * 4 + c for z in range(2) for c in range(4)]
        for g in range(devices // 16)
        for y in range(2)
    ]

    def flip(x, bit):
        return lax.ppermute(x, AXIS, [(i, i ^ bit) for i in range(devices)])

    def gather_across(x):
        return lax.all_gather(x, AXIS, axis=0, tiled=True, axis_index_groups=across)

    def scatter_across(x):
        return lax.psum_scatter(
            x.astype(bf16), AXIS, scatter_dimension=0, tiled=True, axis_index_groups=across
        )

    def dim_of(bit):
        return bit_count - bit.bit_length()

    def data_pieces(x):
        pieces = {0: x}
        for bit in reversed(data_bits):
            for key in list(pieces):
                pieces[key | bit] = flip(pieces[key], bit)
        return pieces

    def place_pieces(pieces, dims, shape):
        total = jnp.zeros(shape, bf16)
        for key, piece in pieces.items():
            start = [0] * len(shape)
            size = list(shape)
            for bit in data_bits:
                start[dims[bit]] = ((device // bit) + (1 if key & bit else 0)) % 2
                size[dims[bit]] = 1
            total = lax.dynamic_update_slice(total, piece.reshape(size), start)
        return total

    def after_bit(dims, bit):
        return {b: d - (d > dims[bit]) for b, d in dims.items() if b != bit}

    def data_sum(x, dims, bits):
        for bit in bits:
            mine = (device // bit) % 2
            keep = lax.dynamic_index_in_dim(x, mine, dims[bit], False)
            sent = flip(lax.dynamic_index_in_dim(x, 1 - mine, dims[bit], False), bit)
            x = (keep.astype(f32) + sent.astype(f32)).astype(bf16)
            dims = after_bit(dims, bit)
        return x

    row_dims = {bit: dim_of(bit) for bit in data_bits}
    row_shape = (2,) * bit_count
    unit_dims = {bit: i for i, bit in enumerate(reversed(data_bits))}
    unit_shape = (2,) * len(data_bits)

    def tie(*values):
        return lax.optimization_barrier(values)

    qkv_moves = tuple(
        (i, b, (g * team + b) * HEAD_DIM, (3 * (g // 2) + i) * PAIR + (g % 2) * HEAD_DIM, HEAD_DIM)
        for i in range(3) for g in range(heads) for b in range(team)
    )
    ffn_units = tuple(
        (z * 4 + c, (2 * h + y) * ff_rows, (h * 16 + z * 8 + y * 4 + c) * ff_rows)
        for h in range(devices // 16) for z in range(2) for y in range(2) for c in range(4)
    )
    ffn_moves = tuple(
        (i, member, source, i * ff_cols + target, ff_rows)
        for i in range(2) for member, target, source in ffn_units
    )
    out_w = lax.all_gather(w_out, AXIS, axis=0, tiled=True)
    gain_row = jnp.concatenate([norm_attn, norm_ffn]).astype(f32)
    gain_row = jnp.pad(gain_row, (0, 128 - 2 * weight_rows)).reshape(1, 128)
    block_rows = block_of.astype(f32).reshape(tok_rows // 128, 128)
    small = jnp.concatenate([gain_row, block_rows, jnp.zeros((7 - tok_rows // 128, 128), f32)])
    normed_attn, qkv_w, both_mine, gathered = front(
        tokens, (w_query, w_key, w_value, w_gate, w_up), small, teams, qkv_moves, ffn_moves
    )
    qkv_w = qkv_w.reshape(width, 3 * head_cols)
    gain_attn = gathered[:, 0, :weight_rows].reshape(1, width)
    gain_ffn = gathered[:, 0, weight_rows : 2 * weight_rows].reshape(1, width)
    blocks = lax.dynamic_slice_in_dim(gathered, device - mate, team, 0)
    blocks = blocks[:, 1 : 1 + tok_rows // 128].astype(jnp.int32).reshape(SEQ)
    row_blocks, col_blocks = blocks.reshape(1, SEQ), blocks.reshape(SEQ, 1)
    both_mine, down_mine, qkv_w = tie(both_mine, w_down, qkv_w)

    def whole_rows(mine):
        shape = row_shape + (weight_rows, ff_cols)
        return place_pieces(data_pieces(mine), row_dims, shape).reshape(width, ff_cols)

    qkv = contract(normed_attn, qkv_w, 1, 0)
    cosine, sine = rope_tables(SEQ, PAIR)
    qkv, cot_mine = tie(qkv, cotangent)
    if data_bits == [4, 16]:
        early = ff_cols + EARLY_UP
        carry = [both_mine, flip(both_mine, 4), flip(both_mine[:, :, :early], 16), down_mine]
    else:
        carry = []
    query, key, value, attended, lse, peak = attend_forward(qkv, cosine, sine, row_blocks, col_blocks)
    peaks = jnp.where(
        (jnp.arange(head_total) % team) == mate, jnp.repeat(peak[0, :heads], team), -jnp.inf
    )
    peaks = jnp.broadcast_to(jnp.pad(peaks, (0, 128 - head_total))[None], (8, 128))
    after_attn, normed_ffn, peaks, *full = branch(
        attended, out_w, tokens, gain_ffn, peaks, carry, attn_bits, ffn_bits, bit_count
    )
    head_peak = peaks[0, :head_total]
    if carry:
        gate_w, up_w = (w.reshape(width, ff_cols) for w in full[:2])
        z_side, y_side = (device // 16) % 2, (device // 4) % 2
        passed = lax.dynamic_index_in_dim(full[2], (1 - z_side) * 2 + y_side, 0, True)
        down_w = lax.dynamic_update_slice(
            full[2], flip(passed, 4), ((1 - z_side) * 2 + 1 - y_side, 0, 0)
        ).reshape(ff_cols, width)
    else:
        gate_w, up_w = whole_rows(both_mine[:, :, :ff_cols]), whole_rows(both_mine[:, :, ff_cols:])
        down_w = place_pieces(
            data_pieces(down_mine), unit_dims, unit_shape + (ff_rows, width)
        ).reshape(ff_cols, width)
    gate_pre = contract(normed_ffn, gate_w, 1, 0)
    up_pre = contract(normed_ffn, up_w, 1, 0)
    sigmoid_gate = jax.nn.sigmoid(gate_pre)
    silu_gate = gate_pre * sigmoid_gate
    hidden = (silu_gate * up_pre).astype(bf16)

    team_cot = lax.all_gather(cot_mine, AXIS, axis=0, tiled=True, axis_index_groups=ffn_team)
    d_down = contract(hidden, team_cot, 0, 0).astype(bf16).reshape(unit_shape + (ff_rows, width))
    team_cot, d_down = tie(team_cot, d_down)
    d_hidden = contract(team_cot, down_w, 1, 1)
    grad_gate = (d_hidden * up_pre * sigmoid_gate * (1.0 + gate_pre * (1.0 - sigmoid_gate))).astype(bf16)
    grad_up = (d_hidden * silu_gate).astype(bf16)

    d_down = data_sum(d_down, unit_dims, data_bits[:1])
    unit_rest, row_rest = after_bit(unit_dims, data_bits[0]), after_bit(row_dims, data_bits[0])
    grad_gate, d_down = tie(grad_gate, d_down)
    d_residual, branch_mine, grad_attended, d_gate, d_up = ffn_back(
        grad_gate, grad_up, gate_w, up_w, normed_ffn, out_w, after_attn, cotangent, gain_ffn, ffn_bits, attn_bits
    )
    d_gate, d_up = (d.reshape(row_shape + (weight_rows, ff_cols)) for d in (d_gate, d_up))
    branch_grad = lax.all_gather(branch_mine, AXIS, axis=0, tiled=True, axis_index_groups=in_team)
    d_down = data_sum(d_down, unit_rest, data_bits[1:]).astype(f32)

    def heads_back(pair):
        return attend_backward(
            pair, query, key, value, grad_attended, lse, cosine, sine, row_blocks, col_blocks
        )

    grad_pairs, shares = [None] * (heads // 2), [None] * (heads // 2)
    grad_pairs[0] = heads_back(0)
    shares[0] = scatter_across(contract(normed_attn, grad_pairs[0], 0, 0))
    d_gate = data_sum(d_gate, row_dims, data_bits[:1])
    grad_attended, d_gate, d_up, d_down, _ = tie(grad_attended, d_gate, d_up, d_down, grad_pairs[0])
    d_gate = data_sum(d_gate, row_rest, data_bits[1:])
    d_up = data_sum(d_up, row_dims, data_bits[:1])
    for p in range(1, heads // 2):
        grad_pairs[p], d_up, d_gate = tie(heads_back(p), d_up, d_gate)
        shares[p] = scatter_across(contract(normed_attn, grad_pairs[p], 0, 0))
    d_up = data_sum(d_up, row_rest, data_bits[1:])
    d_gate = d_gate.reshape(team, weight_rows, ff_cols)
    out_part = contract(attended, branch_grad, 0, 0)
    if weight_rows == HEAD_DIM:
        d_out = scatter_across(out_part).astype(f32)
    else:
        spread = jnp.where(
            (jnp.arange(team) == mate)[None, :, None, None],
            out_part.reshape(heads, 1, HEAD_DIM, width), 0.0,
        ).reshape(width, width)
        d_out = lax.psum_scatter(spread, AXIS, scatter_dimension=0, tiled=True)
    d_tokens, mixed, d_gate = last_sums(
        *grad_pairs, qkv_w, tokens, gain_attn, d_residual, hidden, down_w, after_attn, d_gate, attn_bits, ffn_bits
    )
    places = [[], [], []]
    for i, b, source, target, columns in qkv_moves:
        places[i].append((target // (3 * PAIR), b, target % (3 * PAIR), source, columns))
    places += [
        [(heads // 2 + i, member, target, source, ff_rows) for member, target, source in ffn_units] for i in range(2)
    ]
    shares = [share.reshape(team, weight_rows, 3 * PAIR) for share in shares]
    d_query, d_key, d_value, d_gate, d_up, d_norm_attn, d_norm_ffn = home(
        shares + [d_gate, d_up.reshape(team, weight_rows, ff_cols)],
        (attn_bits,) * (heads // 2) + (None, ffn_bits),
        (w_query, w_key, w_value, w_gate, w_up), (norm_attn, norm_ffn), (0, 0, 0, 1, 1),
        tuple(tuple(p) for p in places),
    )
    d_norm_attn, d_norm_ffn = d_norm_attn[:, 0], d_norm_ffn[:, 0]
    clip_value = clip_limit.astype(f32)
    factor = jnp.sqrt(clip_value / jnp.maximum(head_peak, clip_value))
    factors = jnp.repeat(factor, HEAD_DIM)[None, :]
    clipped_query = (w_query.astype(f32) * factors).astype(bf16)
    clipped_key = (w_key.astype(f32) * factors).astype(bf16)
    return (
        mixed, d_tokens, d_norm_attn, d_query, d_key, d_value, d_out, d_norm_ffn,
        d_gate, d_up, d_down, head_peak, clipped_query, clipped_key,
    )


def solution(mesh):
    rows, whole = P(AXIS, None), P(AXIS)
    return jax.shard_map(
        body,
        mesh=mesh,
        in_specs=(rows, whole, P(), whole, rows, rows, rows, rows, whole, rows, rows, rows, rows),
        out_specs=(
            rows, rows, whole, rows, rows, rows, rows, whole, rows, rows, rows, P(), rows, rows,
        ),
        check_vma=False,
    )
```

```python
import functools

import jax
import jax.numpy as jnp
import numpy as np
from jax import lax
from jax.experimental import pallas as pl
from jax.experimental.pallas import tpu as pltpu
from jax.sharding import PartitionSpec as P

HEAD_DIM = 64
SEQ = 2048
BLOCK = 256
HALF = 128
LAST_CUT = 0
EARLY_HALVES = 3
BRANCH_CUT = 128
AXIS = "fsdp"
MESH = pl.DeviceIdType.MESH

epsilon = 1e-05
rope_base = 130000.0
bf16 = jnp.bfloat16
f32 = jnp.float32
vmem = pl.BlockSpec(memory_space=pltpu.VMEM)
anywhere = pl.BlockSpec(memory_space=pl.ANY)


def contract(left, right, left_dim, right_dim):
    return lax.dot_general(
        left, right, (((left_dim,), (right_dim,)), ((), ())), preferred_element_type=f32
    )


def rope_tables(length, width):
    half_dim = HEAD_DIM // 2
    inverse = rope_base ** (-np.arange(half_dim) * 2.0 / HEAD_DIM)
    angles = (np.arange(length, dtype=np.float32)[:, None] * inverse.astype(np.float32)).astype(np.float64)
    cosine, sine = np.cos(angles).astype(np.float32), np.sin(angles).astype(np.float32)
    repeats = width // HEAD_DIM
    return (
        jnp.asarray(np.tile(np.concatenate([cosine, cosine], 1), (1, repeats))),
        jnp.asarray(np.tile(np.concatenate([-sine, sine], 1), (1, repeats))),
    )


def swap_halves(rows):
    width = rows.shape[1]
    half = HEAD_DIM // 2
    lane = lax.broadcasted_iota(jnp.int32, rows.shape, 1)
    return jnp.where(
        lane % HEAD_DIM < half, pltpu.roll(rows, width - half, 1), pltpu.roll(rows, half, 1)
    )


PAIR = 2 * HEAD_DIM


def head_mask(shape, head):
    lane = lax.broadcasted_iota(jnp.int32, shape, 1)
    return (lane >= head * HEAD_DIM) & (lane < (head + 1) * HEAD_DIM)


def masked_scores(query, key_ref, row_ref, col_ref, q0, cols):
    tail = min(2 * BLOCK, cols)
    scores = contract(query, key_ref[0:cols, :], 1, 1)
    shown = row_ref[:, pl.ds(cols - tail, tail)] <= col_ref[pl.ds(q0, BLOCK), :]
    hidden = jnp.where(shown, scores[:, cols - tail :], -jnp.inf)
    return jnp.concatenate([scores[:, : cols - tail], hidden], 1) if tail < cols else hidden


def attend_forward_kernel(
    qkv_ref, cos_ref, sin_ref, row_ref, col_ref, q_ref, k_ref, v_ref, out_ref, lse_ref, peak_ref
):
    pairs, length, _ = q_ref.shape
    for t in range(length // BLOCK):
        rows = pl.ds(t * BLOCK, BLOCK)
        cosine, sine = cos_ref[rows, :], sin_ref[rows, :]
        for pair in range(pairs):
            first = 3 * pair * PAIR
            query = qkv_ref[rows, first : first + PAIR]
            query = (query * cosine + swap_halves(query) * sine).astype(bf16)
            q_ref[pair, rows, :] = (query.astype(f32) * HEAD_DIM ** (-0.5)).astype(bf16)
            key = qkv_ref[rows, first + PAIR : first + 2 * PAIR]
            k_ref[pair, rows, :] = (key * cosine + swap_halves(key) * sine).astype(bf16)
            v_ref[pair, rows, :] = qkv_ref[rows, first + 2 * PAIR : first + 3 * PAIR].astype(bf16)
    peak_ref[...] = jnp.full(peak_ref.shape, -jnp.inf, f32)
    lane = lax.broadcasted_iota(jnp.int32, (BLOCK, 128), 1)
    for t in range(length // BLOCK):
        q0 = t * BLOCK
        rows = pl.ds(q0, BLOCK)
        cols = min(q0 + 2 * BLOCK, length)

        @pl.loop(0, pairs)
        def _(pair):
            total = jnp.zeros((BLOCK, PAIR), f32)
            for sub in range(2):
                head = 2 * pair + sub
                mask = head_mask((BLOCK, PAIR), sub)
                query = jnp.where(mask, q_ref[pair, rows, :], 0).astype(bf16)
                scores = masked_scores(query, k_ref.at[pair], row_ref, col_ref, q0, cols)
                row_max = jnp.max(scores, 1, keepdims=True)
                numerators = jnp.exp(scores - row_max)
                totals = jnp.sum(numerators, 1, keepdims=True)
                mixed = contract(numerators.astype(bf16), v_ref[pair, 0:cols, :], 1, 0) / totals
                total = jnp.where(mask, mixed, total)
                lse_ref[rows, :] = jnp.where(lane == head, row_max + jnp.log(totals), lse_ref[rows, :])
                peak_ref[...] = jnp.where(
                    lax.broadcasted_iota(jnp.int32, peak_ref.shape, 1) == head,
                    jnp.maximum(peak_ref[...], jnp.max(row_max)),
                    peak_ref[...],
                )
            out_ref[rows, pl.ds(pl.multiple_of(pair * PAIR, PAIR), PAIR)] = total.astype(bf16)


def attend_forward(qkv, cosine, sine, row_blocks, col_blocks):
    length = qkv.shape[0]
    pairs = qkv.shape[1] // (3 * PAIR)
    shape = jax.ShapeDtypeStruct
    return pl.pallas_call(
        attend_forward_kernel,
        out_shape=(
            shape((pairs, length, PAIR), bf16),
            shape((pairs, length, PAIR), bf16),
            shape((pairs, length, PAIR), bf16),
            shape((length, pairs * PAIR), bf16),
            shape((length, 128), f32),
            shape((8, 128), f32),
        ),
        in_specs=[vmem] * 5,
        out_specs=tuple([vmem] * 6),
        compiler_params=pltpu.CompilerParams(vmem_limit_bytes=56 * 1024 * 1024),
        cost_estimate=pl.CostEstimate(
            flops=16 * pairs * length * length * PAIR, bytes_accessed=length * PAIR * pairs * 24,
            transcendentals=2 * pairs * length * length,
        ),
        name="attend_forward",
    )(qkv, cosine, sine, row_blocks, col_blocks)


def attend_backward_kernel(
    first_head, q_ref, k_ref, v_ref, grad_ref, lse_ref, cos_ref, sin_ref, row_ref, col_ref, normed_ref,
    out_ref, weight_ref, dk_ref, dv_ref,
):
    length = q_ref.shape[0]
    dk_ref[...] = jnp.zeros_like(dk_ref)
    dv_ref[...] = jnp.zeros_like(dv_ref)
    lane = lax.broadcasted_iota(jnp.int32, (BLOCK, 128), 1)
    for t in range(length // BLOCK):
        q0 = t * BLOCK
        rows = pl.ds(q0, BLOCK)
        cols = min(q0 + 2 * BLOCK, length)

        def one_head(sub, dq):
            mask = head_mask((BLOCK, PAIR), sub)
            query = jnp.where(mask, q_ref[rows, :], 0).astype(bf16)
            grad = jnp.where(mask, grad_ref[rows, :], 0).astype(bf16)
            lse = jnp.sum(
                jnp.where(lane == first_head + sub, lse_ref[rows, :], 0.0), 1, keepdims=True
            )
            scores = masked_scores(query, k_ref, row_ref, col_ref, q0, cols)
            attention = jnp.exp(scores - lse)
            grad_attention = contract(grad, v_ref[0:cols, :], 1, 1)
            weighted = attention * grad_attention
            centre = jnp.sum(weighted, 1, keepdims=True)
            grad_scores = (weighted - attention * centre).astype(bf16)
            dv_ref[0:cols, :] += contract(attention.astype(bf16), grad, 0, 0)
            dk_ref[0:cols, :] += contract(grad_scores, query, 0, 0)
            return jnp.where(mask, contract(grad_scores, k_ref[0:cols, :], 1, 0), dq)

        dq = lax.fori_loop(0, 2, one_head, jnp.zeros((BLOCK, PAIR), f32)) * HEAD_DIM ** (-0.5)
        out_ref[rows, 0:PAIR] = (dq * cos_ref[rows, :] - swap_halves(dq) * sin_ref[rows, :]).astype(bf16)
    for t in range(length // BLOCK):
        rows = pl.ds(t * BLOCK, BLOCK)
        dk = dk_ref[rows, :]
        out_ref[rows, PAIR : 2 * PAIR] = (
            dk * cos_ref[rows, :] - swap_halves(dk) * sin_ref[rows, :]
        ).astype(bf16)
        out_ref[rows, 2 * PAIR : 3 * PAIR] = dv_ref[rows, :].astype(bf16)
    side = 256

    @pl.loop(0, normed_ref.shape[1] // side)
    def _(k):
        span = pl.ds(pl.multiple_of(k * side, side), side)
        weight_ref[span, :] = contract(normed_ref[:, span], out_ref[...], 0, 0).astype(bf16)


def attend_backward(pair, query, key, value, grad, lse, cosine, sine, row_blocks, col_blocks, normed):
    length, width = normed.shape
    heads = pl.BlockSpec((None, length, PAIR), lambda _: (pair, 0, 0))
    return pl.pallas_call(
        functools.partial(attend_backward_kernel, 2 * pair),
        grid=(1,),
        out_shape=(
            jax.ShapeDtypeStruct((length, 3 * PAIR), bf16), jax.ShapeDtypeStruct((width, 3 * PAIR), bf16),
        ),
        in_specs=[heads] * 3 + [pl.BlockSpec((length, PAIR), lambda _: (0, pair))] + [vmem] * 6,
        out_specs=(vmem, vmem),
        scratch_shapes=[pltpu.VMEM((length, PAIR), f32), pltpu.VMEM((length, PAIR), f32)],
        compiler_params=pltpu.CompilerParams(vmem_limit_bytes=56 * 1024 * 1024),
        cost_estimate=pl.CostEstimate(
            flops=40 * length * length * PAIR + 6 * length * width * PAIR, bytes_accessed=100_000_000,
            transcendentals=2 * length * length,
        ),
        name="attend_backward",
    )(query, key, value, grad, lse, cosine, sine, row_blocks, col_blocks, normed)


def bit_of(index, bit):
    return lax.rem(lax.div(index, bit), 2)


def flip_bit(index, bit):
    return index + bit - 2 * bit * bit_of(index, bit)


def team_mate(me, bits, offset):
    device, place = me, 0
    for k, bit in enumerate(bits):
        moved = (offset >> k) % 2
        place = place + lax.rem(bit_of(me, bit) + moved, 2) * (1 << k)
        device = flip_bit(device, bit) if moved else device
    return device, place


class Links:

    def __init__(self, send_sems, recv_sems):
        self.send_sems, self.recv_sems = send_sems, recv_sems

    def copy(self, slot, src, dst, device):
        return pltpu.make_async_remote_copy(
            src_ref=src, dst_ref=dst, send_sem=self.send_sems.at[slot],
            recv_sem=self.recv_sems.at[slot], device_id=(device,), device_id_type=MESH,
        )


def greet(partners):
    barrier = pltpu.get_barrier_semaphore()
    for partner in partners:
        pl.semaphore_signal(barrier, inc=1, device_id=(partner,), device_id_type=MESH)
    pl.semaphore_wait(barrier, len(partners))


def spread_block(bits, cut, own_ref, out_ref, links, local_sem):
    core, first, second = bits
    me = lax.axis_index(AXIS)
    sibling, next_a, next_b = (flip_bit(me, bit) for bit in bits)
    block = own_ref.shape[0]
    in_a, in_b = bit_of(me, first), bit_of(me, second)
    spans = {None: (0, block), 0: (0, cut), 1: (cut, block - cut)}

    def rows(flip_a, flip_b, part):
        place = bit_of(me, core)
        place = place + 2 * lax.rem(in_a + flip_a, 2) + 4 * lax.rem(in_b + flip_b, 2)
        start, size = spans[part]
        return pl.ds(pl.multiple_of(place * block + start, 16), size)

    def passed(slot, where, device):
        return links.copy(slot, out_ref.at[where], out_ref.at[where], device)

    def first_hand(slot, part, device):
        start, size = spans[part]
        return links.copy(slot, own_ref.at[pl.ds(start, size)], out_ref.at[rows(0, 0, part)], device)

    makers = {
        0: lambda: first_hand(0, 0, next_a),
        1: lambda: first_hand(1, 1, next_b),
        2: lambda: first_hand(2, 1, next_a),
        3: lambda: first_hand(3, 0, next_b),
        4: lambda: links.copy(4, own_ref, out_ref.at[rows(0, 0, None)], sibling),
        5: lambda: passed(5, rows(1, 0, 0), next_b),
        6: lambda: passed(6, rows(1, 0, 0), sibling),
        7: lambda: passed(7, rows(0, 1, 1), next_a),
        8: lambda: passed(8, rows(0, 1, 1), sibling),
        9: lambda: passed(9, rows(1, 0, 1), sibling),
        10: lambda: passed(10, rows(0, 1, 0), sibling),
        11: lambda: passed(11, rows(1, 1, 0), sibling),
        12: lambda: passed(12, rows(1, 1, 1), sibling),
    }
    needs = {0: 0, 1: 1, 2: 1, 3: 0, 4: None, 5: 0, 6: 0, 7: 1, 8: 1, 9: 1, 10: 0, 11: 0, 12: 1}
    copies = {slot: make() for slot, make in makers.items() if spans[needs[slot]][1]}
    keep = pltpu.make_async_copy(own_ref, out_ref.at[rows(0, 0, None)], local_sem)

    def begin():
        for slot in range(5):
            if slot in copies:
                copies[slot].start()
        keep.start()

    def hand_on(arrived, *sent):
        def phase():
            if arrived in copies:
                copies[arrived].wait_recv()
                for slot in sent:
                    copies[slot].start()

        return phase

    def finish():
        for slot in (4, 6, 8, 9, 10, 11, 12):
            if slot in copies:
                copies[slot].wait_recv()
        keep.wait()
        for slot in copies:
            copies[slot].wait_send()

    return [
        begin, hand_on(0, 5, 6), hand_on(1, 7, 8), hand_on(2, 9), hand_on(3, 10),
        hand_on(5, 11), hand_on(7, 12), finish,
    ]


def run(phases):
    for phase in phases:
        phase()


SPREAD_COPIES = 13
SUM_COPIES = 10


def sum_block(bits, cut, swapped, product, total, to_core, from_core, chip_sum, arrived, links):
    core = bits[0]
    (first, weight_a), (second, weight_b) = ((bits[2], 4), (bits[1], 2)) if swapped else ((bits[1], 2), (bits[2], 4))
    me = lax.axis_index(AXIS)
    sibling, next_a, next_b = flip_bit(me, core), flip_bit(me, first), flip_bit(me, second)
    block, width = total.shape
    tile = 512

    def place(step, other_core):
        flip_a, flip_b = 1 - step // 2, 1 - step % 2
        return (
            lax.rem(bit_of(me, core) + other_core, 2)
            + weight_a * lax.rem(bit_of(me, first) + flip_a, 2)
            + weight_b * lax.rem(bit_of(me, second) + flip_b, 2)
        )

    low, high = (0, cut), (cut, block - cut)
    landing = range(6) if cut else {1: 0, 3: 1, 4: 2}

    def link(slot, step, span, device):
        return links.copy(slot, chip_sum.at[step, pl.ds(*span)], arrived.at[landing[slot - 4], pl.ds(0, span[1])], device)

    diag_a, diag_b = (link(4, 0, low, next_a) if cut else None), link(5, 0, high, next_b)
    plain_a, plain_b = (link(6, 1, low, next_a) if cut else None), link(7, 2, high, next_b)
    last_a, last_b = link(8, 1, high, next_a), (link(9, 2, low, next_b) if cut else None)

    def core_copy(step):
        return links.copy(step, to_core.at[step], from_core.at[step], sibling)

    def for_sibling():
        @pl.loop(0, 4)
        def _(step):
            @pl.loop(0, width // tile)
            def _(column):
                columns = pl.ds(pl.multiple_of(column * tile, tile), tile)
                to_core[step, :, columns] = product(place(step, 1), columns).astype(bf16)

            core_copy(step).start()

    def for_chip():
        @pl.loop(0, 4)
        def _(step):
            core_copy(step).wait_recv()

            @pl.loop(0, width // tile)
            def _(column):
                columns = pl.ds(pl.multiple_of(column * tile, tile), tile)
                summed = product(place(step, 0), columns) + from_core[step, :, columns].astype(f32)
                total[:, columns] = summed

                @pl.when(step < 3)
                def _():
                    chip_sum[step, :, columns] = summed.astype(bf16)

            @pl.when(step == 0)
            def _():
                if cut:
                    diag_a.start()
                diag_b.start()

            @pl.when(step == 1)
            def _():
                if cut:
                    plain_a.start()

            @pl.when(step == 2)
            def _():
                plain_b.start()

    def add(step, span, slot):
        rows = pl.ds(*span)
        chip_sum[step, rows, :] = (
            chip_sum[step, rows, :].astype(f32) + arrived[landing[slot], 0 : span[1], :].astype(f32)
        ).astype(bf16)

    def take(span, slot):
        total[pl.ds(*span), :] += arrived[landing[slot], 0 : span[1], :].astype(f32)

    def hand_on():
        if cut:
            diag_a.wait_recv()
            add(2, low, 0)
            last_b.start()
        diag_b.wait_recv()
        add(1, high, 1)
        last_a.start()

    def finish():
        if cut:
            plain_a.wait_recv()
            take(low, 2)
        plain_b.wait_recv()
        take(high, 3)
        if cut:
            last_b.wait_recv()
            take(low, 5)
        last_a.wait_recv()
        take(high, 4)

        @pl.loop(0, 4)
        def _(step):
            core_copy(step).wait_send()

        for copy in (diag_a, diag_b, plain_a, plain_b, last_a, last_b):
            if copy is not None:
                copy.wait_send()

    return for_sibling, for_chip, hand_on, finish


def sum_scratch(block, width, cut):
    return [
        pltpu.VMEM((block, width), f32),
        pltpu.VMEM((4, block, width), bf16),
        pltpu.VMEM((4, block, width), bf16),
        pltpu.VMEM((3, block, width), bf16),
        pltpu.VMEM((6 if cut else 3, block - cut, width), bf16),
        pltpu.SemaphoreType.DMA((SUM_COPIES,)),
        pltpu.SemaphoreType.DMA((SUM_COPIES,)),
    ]


def spread_scratch(block, width):
    return [
        pltpu.VMEM((block, width), bf16),
        pltpu.SemaphoreType.DMA((SPREAD_COPIES,)),
        pltpu.SemaphoreType.DMA((SPREAD_COPIES,)),
        pltpu.SemaphoreType.DMA,
    ]


def link_params(collective_id):
    return pltpu.CompilerParams(
        collective_id=collective_id, has_side_effects=True, vmem_limit_bytes=60 * 1024 * 1024
    )


def cost(flops, size):
    return pl.CostEstimate(flops=int(flops), bytes_accessed=int(size), transcendentals=0)


def row_scale(values):
    return lax.rsqrt(jnp.mean(values * values, -1, keepdims=True) + epsilon)


def front_kernel(
    team, teams, qkv_moves, ffn_moves, carry_bits, tokens_ref, query_ref, key_ref, value_ref, gate_ref, up_ref, small_ref, *refs,
):
    moved = len(carry_bits)
    (carried, refs) = (refs[0], refs[1:]) if moved else (None, refs)
    (normed_out, weights_out, both_out, small_out), refs = refs[:4], refs[4:]
    carried_out, refs = refs[:moved], refs[moved:]
    (tokens_all, mine, both_mine, gain,
    send_sems, recv_sems, local_sem, swap_send, swap_recv, swap_local, line_send, line_recv, small_send, small_recv,
    both_send, both_recv, both_local, out_sems, *carry_sems) = refs
    me = lax.axis_index(AXIS)
    mate, group = lax.rem(me, team), lax.div(me, team)
    devices = team * teams
    mates = [group * team + lax.rem(mate + k, team) for k in range(1, team)]
    above, below = lax.rem(me + team, devices), lax.rem(me + devices - team, devices)
    ffn_mates = [team_mate(me, (1, 2, 8), k) for k in range(team)]
    rows = mine.shape[1]
    swaps, line, small = Links(swap_send, swap_recv), Links(line_send, line_recv), Links(small_send, small_recv)
    both = Links(both_send, both_recv)
    for i, member, source, target, columns in qkv_moves:
        weight = (query_ref, key_ref, value_ref)[i]
        mine[member, :, target : target + columns] = weight[:, source : source + columns]
    greet(
        mates + [lax.rem(me + k * team, devices) for k in range(1, teams)]
        + [device for device, _ in ffn_mates[4:]]
    )

    def share(place):
        return pl.ds(pl.multiple_of(place * rows, rows), rows)

    swap_copies = [
        swaps.copy(k, mine.at[lax.rem(mate + k + 1, team)], weights_out.at[group, share(mate)], mates[k])
        for k in range(team - 1)
    ]
    crossing = [
        Links(*carry_sems).copy(i, carried, carried_out[i], flip_bit(me, bit)) for i, bit in enumerate(carry_bits)
    ]
    for copy in swap_copies:
        copy.start()
    keep = pltpu.make_async_copy(mine.at[mate], weights_out.at[group, share(mate)], swap_local)
    keep.start()
    small_out[me] = small_ref[...]

    others = [lax.rem(me + k * team, devices) for k in range(1, teams)]
    team_rows = pl.ds(pl.multiple_of(group * team, team), team)
    small_near = [
        small.copy(k, small_out.at[me], small_out.at[me], device) for k, device in enumerate(mates)
    ]
    small_far = [
        small.copy(team + k, small_out.at[team_rows], small_out.at[team_rows], device)
        for k, device in enumerate(others)
    ]
    for copy in small_near:
        copy.start()
    spread = spread_block(
        (1, 2, 4), HALF, tokens_ref, tokens_all, Links(send_sems, recv_sems), local_sem
    )
    for i, member, source, target, columns in ffn_moves:
        both_mine[i * team + member, :, target : target + columns] = (gate_ref, up_ref)[i][:, source : source + columns]

    def passed(slot, shard, device):
        return line.copy(slot, weights_out.at[shard], weights_out.at[shard], device)

    steps = teams - 1

    def up(step):
        return passed(step - 1, group - (step - 1), above)

    def down(step):
        return passed(steps + step - 1, group + (step - 1), below)

    def line_start(step):
        pl.when((group < teams - 1) & (group >= step - 1))(lambda: up(step).start())
        pl.when((group > 0) & (group + step - 1 < teams))(lambda: down(step).start())

    def line_wait(step):
        pl.when(group >= step)(lambda: up(step).wait_recv())
        pl.when(group + step < teams)(lambda: down(step).wait_recv())

    def line_sent(step):
        pl.when((group < teams - 1) & (group >= step - 1))(lambda: up(step).wait_send())
        pl.when((group > 0) & (group + step - 1 < teams))(lambda: down(step).wait_send())

    for copy in small_near:
        copy.wait_recv()
    for copy in small_far:
        copy.start()
    own_place = ffn_mates[0][1]
    both_copies = [
        both.copy(
            i * team + k, both_mine.at[i * team + ffn_mates[k][1]], both_out.at[i * team + own_place], ffn_mates[k][0]
        )
        for i in range(2) for k in range(1, team)
    ]
    for copy in both_copies:
        copy.start()
    both_keep = [
        pltpu.make_async_copy(both_mine.at[i * team + own_place], both_out.at[i * team + own_place], both_local.at[i])
        for i in range(2)
    ]
    for copy in both_keep:
        copy.start()
    for copy in swap_copies:
        copy.wait_recv()
    keep.wait()
    line_start(1)
    spread[0]()
    for copy in crossing:
        copy.start()
    for copy in small_far:
        copy.wait_recv()
    spread[1]()
    spread[2]()
    line_wait(1)
    line_start(2)
    spread[3]()
    spread[4]()
    width = tokens_all.shape[1]
    gains = width // devices
    for d in range(devices):
        gain[:, d * gains : (d + 1) * gains] = small_out[d, 0:1, 0:gains]
    for phase in spread[5:]:
        phase()
    block = tokens_ref.shape[0]

    def normed_copy(k):
        span = pl.ds(pl.multiple_of(k * block, block), block)
        return pltpu.make_async_copy(tokens_all.at[span], normed_out.at[span], out_sems.at[k])

    def norm_blocks(first, last):
        @pl.loop(first, last)
        def _(k):
            span = pl.ds(pl.multiple_of(k * block, block), block)
            values = tokens_all[span, :].astype(f32)
            tokens_all[span, :] = (values * row_scale(values) * gain[...]).astype(bf16)
            normed_copy(k).start()

    norm_blocks(0, 2)
    for step in range(2, teams):
        line_wait(step)
        if step < steps:
            line_start(step + 1)
        if step == 2:
            norm_blocks(2, team)
    for k in range(team):
        normed_copy(k).wait()
    for copy in both_copies:
        copy.wait_recv()
    for copy in both_keep:
        copy.wait()
    for copy in swap_copies + both_copies:
        copy.wait_send()
    for step in range(1, teams):
        line_sent(step)
    for copy in small_near + small_far:
        copy.wait_send()
    for copy in crossing:
        copy.wait()


def front(tokens, weights, small, teams, qkv_moves, ffn_moves, carried, carry_bits):
    block, width = tokens.shape
    team = 8
    rows, cols = weights[0].shape[0], 3 * width // team
    both_cols = weights[3].shape[1] // team
    devices = team * teams
    dma = pltpu.SemaphoreType.DMA
    shape = jax.ShapeDtypeStruct
    return pl.pallas_call(
        functools.partial(front_kernel, team, teams, qkv_moves, ffn_moves, carry_bits),
        out_shape=(
            shape((team * block, width), bf16),
            shape((teams, team * rows, cols), bf16),
            shape((2 * team, rows, both_cols), bf16),
            shape((devices,) + small.shape, f32),
        ) + tuple(shape(carried[0].shape, bf16) for _ in carry_bits),
        in_specs=[vmem] * 7 + [anywhere] * len(carried),
        out_specs=(anywhere, anywhere, anywhere, vmem) + (anywhere,) * len(carry_bits),
        scratch_shapes=[
            pltpu.VMEM((team * block, width), bf16), pltpu.VMEM((team, rows, cols), bf16),
            pltpu.VMEM((2 * team, rows, both_cols), bf16), pltpu.VMEM((1, width), f32),
        ]
        + spread_scratch(block, width)[1:]
        + [dma((team - 1,)), dma((team - 1,)), dma, dma((2 * teams,)), dma((2 * teams,)), dma((team + teams,)), dma((team + teams,))]
        + [dma((2 * team,)), dma((2 * team,)), dma((2,)), dma((team,))]
        + [dma((1,))] * (2 * len(carried)),
        compiler_params=link_params(1),
        cost_estimate=cost(0, 200e6),
        name="front",
    )(tokens, *weights, small, *carried)


def branch_kernel(
    carry, swap_bits, spread_bits, left_ref, right_ref, residual_ref, gain_ref, peak_ref, *refs,
):
    if carry:
        (both_own, both_y, both_z, down_own, down_y), refs = refs[:5], refs[5:]
        (h2_ref, out_ref, peak_out, gate_full, up_full, down_full), refs = refs[:6], refs[6:]
        (landed, together, swap_send, swap_recv, own, send_sems, recv_sems, local_sem,
         peak_in, peak_send, peak_recv, carry_send, carry_recv, carry_local) = refs
    else:
        (h2_ref, out_ref, peak_out), refs = refs[:3], refs[3:]
        (landed, together, swap_send, swap_recv, own, send_sems, recv_sems, local_sem,
         peak_in, peak_send, peak_recv) = refs
    me = lax.axis_index(AXIS)
    team, block, _ = landed.shape
    bits = [1 << k for k in range(peak_in.shape[0])]
    mates = [team_mate(me, swap_bits, k) for k in range(team)]
    greet([device for device, _ in mates[1:]] + [flip_bit(me, bit) for bit in bits if bit not in swap_bits])
    own_place = mates[0][1]

    def rows_at(place):
        return pl.ds(pl.multiple_of(place * block, block), block)

    swap_copies = [
        Links(swap_send, swap_recv).copy(k, left_ref.at[rows_at(mates[k][1])], landed.at[own_place], mates[k][0])
        for k in range(1, team)
    ]
    for copy in swap_copies:
        copy.start()
    peaks = Links(peak_send, peak_recv)

    def peak_copy(k):
        return peaks.copy(k, peak_out, peak_in.at[k], flip_bit(me, bits[k]))

    def peak_step(k):
        if k:
            peak_copy(k - 1).wait()
            peak_out[...] = jnp.maximum(peak_out[...], peak_in[k - 1])
        if k < len(bits):
            peak_copy(k).start()

    if carry:
        carried = Links(carry_send, carry_recv)
        high, middle = bit_of(me, 16), bit_of(me, 4)
        by_y, by_z = flip_bit(me, 4), flip_bit(me, 16)

        def rows_of(part, flip_z, flip_y):
            z, y = lax.rem(high + flip_z, 2), lax.rem(middle + flip_y, 2)
            return pl.ds(pl.multiple_of(z * 16 + part * 8 + y * 4, 4), 4)

        early = both_z.shape[0] // 4

        def piece(source, half):
            return source.at[pl.ds(half * 4, 4)]

        def placed(half, flips):
            return (gate_full, up_full)[half // 2].at[rows_of(half % 2, *flips)]

        def unit(flip_z, flip_y):
            return lax.rem(high + flip_z, 2) * 2 + lax.rem(middle + flip_y, 2)

        kept = []
        for source, flips, halves in ((both_own, (0, 0), 4), (both_y, (0, 1), 4), (both_z, (1, 0), early)):
            for half in range(halves):
                kept.append((piece(source, half), placed(half, flips)))
        kept.append((down_own, down_full.at[unit(0, 0)]))
        kept.append((down_y, down_full.at[unit(0, 1)]))
        kept = [pltpu.make_async_copy(a, b, carry_local.at[i]) for i, (a, b) in enumerate(kept)]
        up_z = [
            carried.copy(half, piece(both_own, half), placed(half, (0, 0)), by_z) for half in range(early, 4)
        ]
        early_yz = [
            carried.copy(4 + half, piece(both_z, half), placed(half, (1, 0)), by_y) for half in range(early)
        ]
        up_yz = [
            carried.copy(4 + half, placed(half, (1, 0)), placed(half, (1, 0)), by_y) for half in range(early, 4)
        ]
        down_z = carried.copy(8, down_own, down_full.at[unit(0, 0)], by_z)
        for copy in up_z + kept:
            copy.start()

    peak_out[...] = peak_ref[...]
    peak_step(0)
    landed[own_place] = left_ref[rows_at(own_place), :]
    for copy in swap_copies:
        copy.wait_recv()
    if carry:
        for copy in early_yz:
            copy.start()
    heads = landed.shape[2] // HEAD_DIM
    for b in range(team):
        for g in range(heads):
            first = (g * team + b) * HEAD_DIM
            together[:, first : first + HEAD_DIM] = landed[b, :, g * HEAD_DIM : (g + 1) * HEAD_DIM]
    tile = 512

    @pl.loop(0, own.shape[1] // tile)
    def _(column):
        columns = pl.ds(pl.multiple_of(column * tile, tile), tile)
        h2_ref[:, columns] = residual_ref[:, columns].astype(f32) + contract(
            together[...], right_ref[:, columns], 1, 0
        )

    h2 = h2_ref[...]
    own[...] = (h2 * row_scale(h2) * gain_ref[...]).astype(bf16)
    spread = spread_block(spread_bits, BRANCH_CUT, own, out_ref, Links(send_sems, recv_sems), local_sem)
    spread[0]()
    if carry:
        for over, on in zip(up_z, up_yz):
            over.wait_recv()
            on.start()
        down_z.start()
    for k, phase in enumerate(spread[1:-1]):
        phase()
        if k < len(bits):
            peak_step(k + 1)
    for k in range(len(spread) - 2, len(bits)):
        peak_step(k + 1)
    spread[-1]()
    for copy in swap_copies:
        copy.wait_send()
    if carry:
        for copy in kept:
            copy.wait()
        for copy in early_yz + up_yz + [down_z]:
            copy.wait_recv()
        for copy in up_z + early_yz + up_yz + [down_z]:
            copy.wait_send()


def branch(left, right, residual, gain, peak, carry, swap_bits, spread_bits, bit_count):
    block, width = residual.shape
    dma = pltpu.SemaphoreType.DMA
    shape = jax.ShapeDtypeStruct
    out_shape = [shape((block, width), f32), shape((8 * block, width), bf16), shape((8, 128), f32)]
    scratch = [pltpu.VMEM((8, block, left.shape[1]), bf16), pltpu.VMEM((block, width), bf16), dma((8,)), dma((8,))]
    scratch += spread_scratch(block, width)
    scratch += [pltpu.VMEM((bit_count, 8, 128), f32), dma((bit_count,)), dma((bit_count,))]
    if carry:
        out_shape += [
            shape((32,) + carry[0].shape[1:], bf16), shape((32,) + carry[0].shape[1:], bf16),
            shape((4,) + carry[3].shape, bf16),
        ]
        scratch += [dma((9,)), dma((9,)), dma((14,))]
    return pl.pallas_call(
        functools.partial(branch_kernel, bool(carry), swap_bits, spread_bits),
        out_shape=tuple(out_shape),
        in_specs=[vmem] * (5 + len(carry)),
        out_specs=tuple([vmem, anywhere, vmem] + [anywhere] * (len(out_shape) - 3)),
        scratch_shapes=scratch,
        compiler_params=link_params(2),
        cost_estimate=cost(16 * block * left.shape[1] * width, 300e6),
        name="attention_branch",
    )(left, right, residual, gain, peak, *carry)


def norm_back(values, gain, upstream):
    scaled = upstream * gain
    scale = row_scale(values)
    inner = jnp.mean(scaled * values, -1, keepdims=True)
    return scale * scaled - scale * scale * scale * values * inner


def ffn_back_kernel(
    cross, sum_bits, swap_bits, gate_ref, up_ref, gate_w_ref, up_w_ref, normed_ref, out_w_ref, h2_ref, cot_ref, gain_ref, *refs,
):
    (part_ref, refs) = (refs[0], refs[1:]) if cross else (None, refs)
    (residual_ref, branch_ref, heads_out, d_up_out, d_gate_own), refs = refs[:5], refs[5:]
    (d_gate_in, part_in, refs) = (refs[0], refs[1], refs[2:]) if cross else (None, None, refs)
    (total, to_core, from_core, chip_sum, arrived, sum_send, sum_recv,
     swap_send, swap_recv, local_sem, stage, stage_sems, own_sems, *more) = refs
    if cross:
        cross_send, cross_recv = more
        crossing = Links(cross_send, cross_recv)
    else:
        (stage_gate,) = more
    me = lax.axis_index(AXIS)
    block, width = total.shape
    team = 1 << len(swap_bits)
    mates = [team_mate(me, swap_bits, k) for k in range(team)]
    greet(
        [device for device, _ in mates[1:]] + [flip_bit(me, bit) for bit in sum_bits if bit not in swap_bits]
    )

    def product(place, columns):
        rows = pl.ds(pl.multiple_of(place * block, block), block)
        return contract(gate_ref[rows, :], gate_w_ref[columns, :], 1, 1) + contract(
            up_ref[rows, :], up_w_ref[columns, :], 1, 1
        )

    side, columns_ff = stage.shape[1:]
    count = width // side
    y_side, by_y = bit_of(me, 4), flip_bit(me, 4)
    if cross:
        part_copy = crossing.copy(count // 2, part_ref, part_in, by_y)
        part_copy.start()

    def parked(i, part):
        row = i * side
        rows = pl.ds(pl.multiple_of(lax.rem(row, block), 16), side)
        return from_core.at[lax.div(row, block), rows, pl.ds(part * columns_ff, columns_ff)]

    def cross_copy(i):
        return crossing.copy(i, parked(i, 0), d_gate_in.at[i], by_y)

    def own_copy(i):
        return pltpu.make_async_copy(parked(i, 1), d_gate_own.at[i], own_sems.at[i])

    def tile_of(step):
        if not cross:
            return step
        theirs = step < count // 2
        return jnp.where(theirs, 2 * step + 1 - y_side, 2 * step - count + y_side)

    def up_copy(step):
        span = pl.ds(pl.multiple_of(tile_of(step) * side, side), side)
        slot = lax.rem(step, 2)
        return pltpu.make_async_copy(stage.at[slot], d_up_out.at[span], stage_sems.at[slot])

    def gate_copy(step):
        span = pl.ds(pl.multiple_of(step * side, side), side)
        slot = lax.rem(step, 2)
        return pltpu.make_async_copy(stage_gate.at[slot], d_gate_own.at[span], own_sems.at[slot])

    def gradients(first, last):
        @pl.loop(first, last)
        def _(step):
            @pl.when(step >= 2)
            def _():
                up_copy(step - 2).wait()
                if not cross:
                    gate_copy(step - 2).wait()

            columns = normed_ref[:, pl.ds(pl.multiple_of(tile_of(step) * side, side), side)]
            stage[lax.rem(step, 2)] = contract(columns, up_ref[...], 0, 0).astype(bf16)
            up_copy(step).start()
            tile = contract(columns, gate_ref[...], 0, 0).astype(bf16)
            if not cross:
                stage_gate[lax.rem(step, 2)] = tile
                gate_copy(step).start()
                return

            @pl.when(step < count // 2)
            def _():
                parked(step, 0)[...] = tile
                cross_copy(step).start()

            @pl.when(step >= count // 2)
            def _():
                parked(step - count // 2, 1)[...] = tile
                own_copy(step - count // 2).start()

    for_sibling, for_chip, hand_on, finish = sum_block(
        sum_bits, HALF, False, product, total, to_core, from_core, chip_sum, arrived, Links(sum_send, sum_recv)
    )
    for_sibling()
    for_chip()
    gradients(0, 1)
    hand_on()
    gradients(1, count - 2)
    finish()
    residual = cot_ref[...].astype(f32) + norm_back(h2_ref[...], gain_ref[...], total[...])
    residual_ref[...] = residual
    branch_ref[...] = residual.astype(bf16)
    tile, share = team * HEAD_DIM, width // team
    for g in range(width // tile):
        heads = contract(branch_ref[...], out_w_ref[g * tile : (g + 1) * tile, :], 1, 1).astype(bf16)
        for b in range(team):
            first = b * share + g * HEAD_DIM
            to_core[0, :, first : first + HEAD_DIM] = heads[:, b * HEAD_DIM : (b + 1) * HEAD_DIM]
    own_place = mates[0][1]
    own_rows = pl.ds(pl.multiple_of(own_place * block, block), block)
    def heads_of(place):
        return to_core.at[0, :, pl.ds(pl.multiple_of(place * share, share), share)]

    swap_copies = [
        Links(swap_send, swap_recv).copy(k, heads_of(mates[k][1]), heads_out.at[own_rows], mates[k][0])
        for k in range(1, team)
    ]
    keep = pltpu.make_async_copy(heads_of(own_place), heads_out.at[own_rows], local_sem)
    for copy in swap_copies + [keep]:
        copy.start()
    gradients(count - 2, count)
    for copy in swap_copies:
        copy.wait_recv()
    for copy in swap_copies:
        copy.wait_send()
    keep.wait()
    for step in range(count - 2, count):
        up_copy(step).wait()
        if not cross:
            gate_copy(step).wait()
    if cross:
        part_copy.wait()

        @pl.loop(0, count // 2)
        def _(i):
            own_copy(i).wait()
            cross_copy(i).wait()


def ffn_back(gate, up, gate_w, up_w, normed, out_w, h2, cot, gain, part, side, sum_bits, swap_bits):
    block, width = h2.shape
    shape = jax.ShapeDtypeStruct
    dma = pltpu.SemaphoreType.DMA
    ff_cols, cross = gate.shape[1], side % 128 == 0
    side = side if cross else 256
    tiles = width // side // 2
    if cross:
        d_gate = (shape((tiles, side, ff_cols), bf16),) * 2 + (shape(part[0].shape, bf16),)
        more = [dma((tiles + 1,)), dma((tiles + 1,))]
    else:
        d_gate, more = (shape((width, ff_cols), bf16),), [pltpu.VMEM((2, side, ff_cols), bf16)]
    return pl.pallas_call(
        functools.partial(ffn_back_kernel, cross, sum_bits, swap_bits),
        out_shape=(
            shape((block, width), f32), shape((block, width), bf16), shape((8 * block, width // 8), bf16),
            shape((width, ff_cols), bf16),
        ) + d_gate,
        in_specs=[vmem] * 9 + [anywhere] * len(part),
        out_specs=(vmem, vmem) + (anywhere,) * (2 + len(d_gate)),
        scratch_shapes=sum_scratch(block, width, HALF)
        + [dma((8,)), dma((8,)), dma]
        + [pltpu.VMEM((2, side, ff_cols), bf16), dma((2,)), dma((tiles,))]
        + more,
        compiler_params=link_params(3),
        cost_estimate=cost(96 * block * ff_cols * width, 200e6),
        name="ffn_back",
    )(gate, up, gate_w, up_w, normed, out_w, h2, cot, gain, *part)


def last_sums_kernel(
    sum_bits, ffn_bits, left_ref, other_ref, right_ref, tokens_ref, gain_ref, residual_ref, hidden_ref, down_ref, h2_ref,
    gate_ref, out_ref, mixed_ref, gate_out, *scratch,
):
    (swap_send, swap_recv, swap_local), scratch = scratch[-3:], scratch[:-3]
    count = len(scratch) // 2
    me = lax.axis_index(AXIS)
    total, ffn_total = scratch[0], scratch[count]
    block = total.shape[0]
    mates = [team_mate(me, ffn_bits, k) for k in range(8)]
    partners = [flip_bit(me, bit) for bit in sum_bits if bit not in ffn_bits]
    greet(partners + [device for device, _ in mates[1:]])
    swaps, own_place = Links(swap_send, swap_recv), mates[0][1]
    swap_copies = [
        swaps.copy(k, gate_ref.at[mates[k][1]], gate_out.at[own_place], mates[k][0]) for k in range(1, 8)
    ]
    keep = pltpu.make_async_copy(gate_ref.at[own_place], gate_out.at[own_place], swap_local)

    def rows_of(place):
        return pl.ds(pl.multiple_of(place * block, block), block)

    def product(place, columns):
        rows = rows_of(place)
        middle = left_ref.shape[1]
        return contract(left_ref[rows, :], right_ref[columns, 0:middle], 1, 1) + contract(
            other_ref[rows, :], right_ref[columns, middle : 2 * middle], 1, 1
        )

    def ffn_product(place, columns):
        return contract(hidden_ref[rows_of(place), :], down_ref[:, columns], 1, 0)

    first = sum_block(sum_bits, LAST_CUT, False, product, *scratch[: count - 2], Links(*scratch[count - 2 : count]))
    second = sum_block(ffn_bits, LAST_CUT, False, ffn_product, *scratch[count:-2], Links(*scratch[-2:]))
    run(first[:2])
    run(second[:2])
    for copy in swap_copies + [keep]:
        copy.start()
    for one, other in zip(first[2:], second[2:]):
        one()
        other()
    out_ref[...] = residual_ref[...] + norm_back(
        tokens_ref[...].astype(f32), gain_ref[...], total[...]
    )
    mixed_ref[...] = (h2_ref[...] + ffn_total[...]).astype(bf16)
    for copy in swap_copies:
        copy.wait_recv()
    for copy in swap_copies:
        copy.wait_send()
    keep.wait()


def last_sums(left, other, right, tokens, gain, residual, hidden, down, h2, d_gate, sum_bits, ffn_bits):
    block, width = tokens.shape
    return pl.pallas_call(
        functools.partial(last_sums_kernel, sum_bits, ffn_bits),
        out_shape=(
            jax.ShapeDtypeStruct((block, width), f32), jax.ShapeDtypeStruct((block, width), bf16),
            jax.ShapeDtypeStruct(d_gate.shape, bf16),
        ),
        in_specs=[vmem] * 9 + [anywhere],
        out_specs=(vmem, vmem, anywhere),
        scratch_shapes=sum_scratch(block, width, LAST_CUT) * 2
        + [pltpu.SemaphoreType.DMA((8,)), pltpu.SemaphoreType.DMA((8,)), pltpu.SemaphoreType.DMA],
        compiler_params=link_params(4),
        cost_estimate=cost(16 * block * right.size // 8, 300e6),
        name="last_sums",
    )(left, other, right, tokens, gain, residual, hidden, down, h2, d_gate)


def exchange_kernel(teams, sources, *refs):
    mine, landed, (send_sems, recv_sems, local_sems) = refs[:sources], refs[sources : 2 * sources], refs[2 * sources :]
    me = lax.axis_index(AXIS)
    members = mine[0].shape[0]
    links = Links(send_sems, recv_sems)
    greeted = {}
    for bits in teams:
        for k in range(1, members):
            device, _ = team_mate(me, bits, k)
            greeted[tuple(sorted(bit for j, bit in enumerate(bits) if (k >> j) % 2))] = device
    greet(list(greeted.values()))
    copies, kept = [], []
    for i, (source, target, bits) in enumerate(zip(mine, landed, teams)):
        own = team_mate(me, bits, 0)[1]
        kept.append(pltpu.make_async_copy(source.at[own], target.at[own], local_sems.at[i]))
        for k in range(1, members):
            device, place = team_mate(me, bits, k)
            copies.append(links.copy(i * members + k, source.at[place], target.at[own], device))
    for copy in copies + kept:
        copy.start()
    for copy in copies:
        copy.wait()
    for copy in kept:
        copy.wait()


def exchange(parts, teams):
    dma = pltpu.SemaphoreType.DMA
    slots = len(parts) * parts[0].shape[0]
    return pl.pallas_call(
        functools.partial(exchange_kernel, teams, len(parts)),
        out_shape=tuple(jax.ShapeDtypeStruct(part.shape, part.dtype) for part in parts),
        in_specs=[vmem] * len(parts),
        out_specs=tuple([vmem] * len(parts)),
        scratch_shapes=[dma((slots,)), dma((slots,)), dma((len(parts),))],
        compiler_params=link_params(5),
        cost_estimate=cost(1e6, 40e6),
        name="exchange",
    )(*parts)


def home_kernel(places, gain_of, sources, *refs):
    count = len(places)
    kinds = max(gain_of) + 1
    parts, weights, gains = refs[:sources], refs[sources : sources + count], refs[sources + count : sources + count + kinds]
    outs, gain_outs = refs[-count - kinds : -kinds], refs[-kinds:]
    totals = [jnp.zeros(gain.shape, f32) for gain in gains]
    for i, (out, weight) in enumerate(zip(outs, weights)):
        for source, member, first, target, columns in places[i]:
            out[:, target : target + columns] = parts[source][member, :, first : first + columns].astype(f32)
        for first in range(0, out.shape[1], 1024):
            product = out[:, first : first + 1024] * weight[:, first : first + 1024].astype(f32)
            totals[gain_of[i]] += jnp.sum(product, 1, keepdims=True)
    for gain, total, out in zip(gains, totals, gain_outs):
        out[...] = jnp.broadcast_to(total / gain[...], (out.shape[1], 128)).T[0:1, :]


def home(parts, weights, gains, gain_of, places):
    shape = jax.ShapeDtypeStruct
    count = len(weights)
    gains = [gain.astype(f32).reshape(-1, 1) for gain in gains]
    return pl.pallas_call(
        functools.partial(home_kernel, places, gain_of, len(parts)),
        out_shape=tuple(shape(w.shape, f32) for w in weights) + tuple(shape((1, g.shape[0]), f32) for g in gains),
        in_specs=[vmem] * (len(parts) + count + len(gains)),
        out_specs=tuple([vmem] * (count + len(gains))),
        compiler_params=pltpu.CompilerParams(vmem_limit_bytes=40 * 1024 * 1024),
        cost_estimate=cost(1e6, 30e6),
        name="home",
    )(*parts, *weights, *gains)


def body(
    tokens, block_of, clip_limit, norm_attn, w_query, w_key, w_value, w_out,
    norm_ffn, w_gate, w_up, w_down, cotangent,
):
    tok_rows, width = tokens.shape
    devices = lax.axis_size(AXIS)
    team = SEQ // tok_rows
    teams = devices // team
    head_total = width // HEAD_DIM
    heads = head_total // team
    head_cols = heads * HEAD_DIM
    ff_rows = w_down.shape[0]
    weight_rows = w_gate.shape[0]
    ff_cols = w_gate.shape[1] // team
    device = lax.axis_index(AXIS)
    mate = device % team
    bit_count = devices.bit_length() - 1
    attn_bits, ffn_bits = (1, 2, 4), (1, 2, 8)
    data_bits = [4] + [1 << k for k in range(4, bit_count)]
    in_team = [[g * team + b for b in range(team)] for g in range(teams)]
    across = [[g * team + b for g in range(teams)] for b in range(team)]
    ffn_team = [
        [g * 16 + z * 8 + y * 4 + c for z in range(2) for c in range(4)]
        for g in range(devices // 16)
        for y in range(2)
    ]

    def flip(x, bit):
        return lax.ppermute(x, AXIS, [(i, i ^ bit) for i in range(devices)])

    def gather_across(x):
        return lax.all_gather(x, AXIS, axis=0, tiled=True, axis_index_groups=across)

    def scatter_across(x):
        return lax.psum_scatter(
            x.astype(bf16), AXIS, scatter_dimension=0, tiled=True, axis_index_groups=across
        )

    def dim_of(bit):
        return bit_count - bit.bit_length()

    def data_pieces(x):
        pieces = {0: x}
        for bit in reversed(data_bits):
            for key in list(pieces):
                pieces[key | bit] = flip(pieces[key], bit)
        return pieces

    def place_pieces(pieces, dims, shape):
        total = jnp.zeros(shape, bf16)
        for key, piece in pieces.items():
            start = [0] * len(shape)
            size = list(shape)
            for bit in data_bits:
                start[dims[bit]] = ((device // bit) + (1 if key & bit else 0)) % 2
                size[dims[bit]] = 1
            total = lax.dynamic_update_slice(total, piece.reshape(size), start)
        return total

    def after_bit(dims, bit):
        return {b: d - (d > dims[bit]) for b, d in dims.items() if b != bit}

    def data_sum(x, dims, bits):
        for bit in bits:
            mine = (device // bit) % 2
            keep = lax.dynamic_index_in_dim(x, mine, dims[bit], False)
            sent = flip(lax.dynamic_index_in_dim(x, 1 - mine, dims[bit], False), bit)
            x = (keep.astype(f32) + sent.astype(f32)).astype(bf16)
            dims = after_bit(dims, bit)
        return x

    row_dims = {bit: dim_of(bit) for bit in data_bits}
    row_shape = (2,) * bit_count
    unit_dims = {bit: i for i, bit in enumerate(reversed(data_bits))}
    unit_shape = (2,) * len(data_bits)

    def tie(*values):
        return lax.optimization_barrier(values)

    qkv_moves = tuple(
        (i, b, (g * team + b) * HEAD_DIM, (3 * (g // 2) + i) * PAIR + (g % 2) * HEAD_DIM, HEAD_DIM)
        for i in range(3) for g in range(heads) for b in range(team)
    )
    ffn_units = tuple(
        (z * 4 + c, (2 * h + y) * ff_rows, (h * 16 + z * 8 + y * 4 + c) * ff_rows)
        for h in range(devices // 16) for z in range(2) for y in range(2) for c in range(4)
    )
    ffn_moves = tuple(
        (i, member, source, target, ff_rows)
        for i in range(2) for member, target, source in ffn_units
    )
    out_w = lax.all_gather(w_out, AXIS, axis=0, tiled=True)
    gain_row = jnp.concatenate([norm_attn, norm_ffn]).astype(f32)
    gain_row = jnp.pad(gain_row, (0, 128 - 2 * weight_rows)).reshape(1, 128)
    block_rows = block_of.astype(f32).reshape(tok_rows // 128, 128)
    small = jnp.concatenate([gain_row, block_rows, jnp.zeros((7 - tok_rows // 128, 128), f32)])
    ahead = data_bits == [4, 16]
    normed_attn, qkv_w, both_mine, gathered, *down_moved = front(
        tokens, (w_query, w_key, w_value, w_gate, w_up), small, teams, qkv_moves, ffn_moves,
        [w_down] if ahead else [], (4,) if ahead else (),
    )
    qkv_w = qkv_w.reshape(width, 3 * head_cols)
    gain_attn = gathered[:, 0, :weight_rows].reshape(1, width)
    gain_ffn = gathered[:, 0, weight_rows : 2 * weight_rows].reshape(1, width)
    blocks = lax.dynamic_slice_in_dim(gathered, device - mate, team, 0)
    blocks = blocks[:, 1 : 1 + tok_rows // 128].astype(jnp.int32).reshape(SEQ)
    row_blocks, col_blocks = blocks.reshape(1, SEQ), blocks.reshape(SEQ, 1)
    both_mine, qkv_w = tie(both_mine, qkv_w)

    def whole_rows(mine):
        shape = row_shape + (weight_rows, ff_cols)
        return place_pieces(data_pieces(mine), row_dims, shape).reshape(width, ff_cols)

    qkv = contract(normed_attn, qkv_w, 1, 0)
    cosine, sine = rope_tables(SEQ, PAIR)
    qkv, cot_mine = tie(qkv, cotangent)
    if data_bits == [4, 16]:
        carry = [both_mine, flip(both_mine, 4), flip(both_mine[: 4 * EARLY_HALVES], 16), w_down, *down_moved]
    else:
        carry = []
    query, key, value, attended, lse, peak = attend_forward(qkv, cosine, sine, row_blocks, col_blocks)
    peaks = jnp.where(
        (jnp.arange(head_total) % team) == mate, jnp.repeat(peak[0, :heads], team), -jnp.inf
    )
    peaks = jnp.broadcast_to(jnp.pad(peaks, (0, 128 - head_total))[None], (8, 128))
    after_attn, normed_ffn, peaks, *full = branch(
        attended, out_w, tokens, gain_ffn, peaks, carry, attn_bits, ffn_bits, bit_count
    )
    head_peak = peaks[0, :head_total]
    if carry:
        gate_w, up_w = (w.reshape(width, ff_cols) for w in full[:2])
        z_side, y_side = (device // 16) % 2, (device // 4) % 2
        passed = lax.dynamic_index_in_dim(full[2], (1 - z_side) * 2 + y_side, 0, True)
        down_w = lax.dynamic_update_slice(
            full[2], flip(passed, 4), ((1 - z_side) * 2 + 1 - y_side, 0, 0)
        ).reshape(ff_cols, width)
    else:
        gate_w, up_w = whole_rows(both_mine[:team]), whole_rows(both_mine[team:])
        down_w = place_pieces(
            data_pieces(w_down), unit_dims, unit_shape + (ff_rows, width)
        ).reshape(ff_cols, width)
    gate_pre = contract(normed_ffn, gate_w, 1, 0)
    up_pre = contract(normed_ffn, up_w, 1, 0)
    sigmoid_gate = jax.nn.sigmoid(gate_pre)
    silu_gate = gate_pre * sigmoid_gate
    hidden = (silu_gate * up_pre).astype(bf16)

    team_cot = lax.all_gather(cot_mine, AXIS, axis=0, tiled=True, axis_index_groups=ffn_team)
    d_down = contract(hidden, team_cot, 0, 0).astype(bf16).reshape(unit_shape + (ff_rows, width))
    team_cot, d_down = tie(team_cot, d_down)
    d_hidden = contract(team_cot, down_w, 1, 1)
    grad_gate = (d_hidden * up_pre * sigmoid_gate * (1.0 + gate_pre * (1.0 - sigmoid_gate))).astype(bf16)
    grad_up = (d_hidden * silu_gate).astype(bf16)

    unit_rest, row_rest = after_bit(unit_dims, data_bits[0]), after_bit(row_dims, data_bits[0])
    row_values = (weight_rows, ff_cols)
    crosses = data_bits == [4, 16]
    if crosses:
        y_side = (device // 4) % 2
        kept = lax.dynamic_index_in_dim(d_down, y_side, unit_dims[4], False)
        sent = lax.dynamic_index_in_dim(d_down, 1 - y_side, unit_dims[4], False)
        ahead = flip(sent[0], 4)
        grad_gate, ahead = tie(grad_gate, ahead)
        beside = [sent[1]]
    else:
        beside = []
    d_residual, branch_mine, grad_attended, d_up, *d_gate = ffn_back(
        grad_gate, grad_up, gate_w, up_w, normed_ffn, out_w, after_attn, cotangent, gain_ffn, beside, 4 * weight_rows,
        ffn_bits, attn_bits,
    )
    if crosses:
        d_down = (kept.astype(f32) + jnp.stack([ahead, d_gate[2]]).astype(f32)).astype(bf16)
        d_gate = (d_gate[0].astype(f32) + d_gate[1].astype(f32)).astype(bf16)
        d_gate = d_gate.reshape((2,) * (bit_count - 1) + row_values)
    else:
        d_down = data_sum(d_down, unit_dims, data_bits[:1])
        d_gate = data_sum(d_gate[0].reshape(row_shape + row_values), row_dims, data_bits[:1])
    grad_attended, d_down, d_gate = tie(grad_attended, d_down, d_gate)
    d_gate = data_sum(d_gate, row_rest, data_bits[1:])
    branch_grad = lax.all_gather(branch_mine, AXIS, axis=0, tiled=True, axis_index_groups=in_team)

    def heads_back(pair):
        return attend_backward(
            pair, query, key, value, grad_attended, lse, cosine, sine, row_blocks, col_blocks, normed_attn
        )

    grad_pairs, shares = [None] * (heads // 2), [None] * (heads // 2)
    grad_pairs[0], share = heads_back(0)
    grad_attended, d_down, d_gate, d_up, share = tie(grad_attended, d_down, d_gate, d_up, share)
    shares[0] = scatter_across(share)
    d_down = data_sum(d_down, unit_rest, data_bits[1:]).astype(f32)
    d_up = data_sum(d_up.reshape(row_shape + row_values), row_dims, data_bits[:1])
    for p in range(1, heads // 2):
        grad_pairs[p], share = heads_back(p)
        grad_pairs[p], share, d_down, d_up, branch_grad = tie(grad_pairs[p], share, d_down, d_up, branch_grad)
        shares[p] = scatter_across(share)
    d_up = data_sum(d_up, row_rest, data_bits[1:])
    d_gate = d_gate.reshape(team, weight_rows, ff_cols)
    out_part = contract(attended, branch_grad, 0, 0)
    if weight_rows == HEAD_DIM:
        d_out = scatter_across(out_part).astype(f32)
    else:
        spread = jnp.where(
            (jnp.arange(team) == mate)[None, :, None, None],
            out_part.reshape(heads, 1, HEAD_DIM, width), 0.0,
        ).reshape(width, width)
        d_out = lax.psum_scatter(spread, AXIS, scatter_dimension=0, tiled=True)
    d_tokens, mixed, d_gate = last_sums(
        *grad_pairs, qkv_w, tokens, gain_attn, d_residual, hidden, down_w, after_attn, d_gate, attn_bits, ffn_bits
    )
    places = [[], [], []]
    for i, b, source, target, columns in qkv_moves:
        places[i].append((target // (3 * PAIR), b, target % (3 * PAIR), source, columns))
    places += [
        [(heads // 2 + i, member, target, source, ff_rows) for member, target, source in ffn_units] for i in range(2)
    ]
    shares = [share.reshape(team, weight_rows, 3 * PAIR) for share in shares]
    *shares, d_up = exchange(
        shares + [d_up.reshape(team, weight_rows, ff_cols)], (attn_bits,) * (heads // 2) + (ffn_bits,)
    )
    d_query, d_key, d_value, d_gate, d_up, d_norm_attn, d_norm_ffn = home(
        shares + [d_gate, d_up], (w_query, w_key, w_value, w_gate, w_up), (norm_attn, norm_ffn), (0, 0, 0, 1, 1),
        tuple(tuple(p) for p in places),
    )
    d_norm_attn, d_norm_ffn = d_norm_attn[0], d_norm_ffn[0]
    clip_value = clip_limit.astype(f32)
    factor = jnp.sqrt(clip_value / jnp.maximum(head_peak, clip_value))
    factors = jnp.repeat(factor, HEAD_DIM)[None, :]
    clipped_query = (w_query.astype(f32) * factors).astype(bf16)
    clipped_key = (w_key.astype(f32) * factors).astype(bf16)
    return (
        mixed, d_tokens, d_norm_attn, d_query, d_key, d_value, d_out, d_norm_ffn,
        d_gate, d_up, d_down, head_peak, clipped_query, clipped_key,
    )


def solution(mesh):
    rows, whole = P(AXIS, None), P(AXIS)
    return jax.shard_map(
        body,
        mesh=mesh,
        in_specs=(rows, whole, P(), whole, rows, rows, rows, rows, whole, rows, rows, rows, rows),
        out_specs=(
            rows, rows, whole, rows, rows, rows, rows, whole, rows, rows, rows, P(), rows, rows,
        ),
        check_vma=False,
    )
```

```python
import functools

import jax
import jax.numpy as jnp
import numpy as np
from jax import lax
from jax.experimental import pallas as pl
from jax.experimental.pallas import tpu as pltpu
from jax.sharding import PartitionSpec as P

HEAD_DIM = 64
SEQ = 2048
BLOCK = 256
HALF = 128
LAST_CUT = 0
EARLY_HALVES = 3
BRANCH_CUT = 128
AXIS = "fsdp"
MESH = pl.DeviceIdType.MESH

epsilon = 1e-05
rope_base = 130000.0
bf16 = jnp.bfloat16
f32 = jnp.float32
vmem = pl.BlockSpec(memory_space=pltpu.VMEM)
anywhere = pl.BlockSpec(memory_space=pl.ANY)


def contract(left, right, left_dim, right_dim):
    return lax.dot_general(
        left, right, (((left_dim,), (right_dim,)), ((), ())), preferred_element_type=f32
    )


def rope_tables(length, width):
    half_dim = HEAD_DIM // 2
    inverse = rope_base ** (-np.arange(half_dim) * 2.0 / HEAD_DIM)
    angles = (np.arange(length, dtype=np.float32)[:, None] * inverse.astype(np.float32)).astype(np.float64)
    cosine, sine = np.cos(angles).astype(np.float32), np.sin(angles).astype(np.float32)
    repeats = width // HEAD_DIM
    return (
        jnp.asarray(np.tile(np.concatenate([cosine, cosine], 1), (1, repeats))),
        jnp.asarray(np.tile(np.concatenate([-sine, sine], 1), (1, repeats))),
    )


def swap_halves(rows):
    width = rows.shape[1]
    half = HEAD_DIM // 2
    lane = lax.broadcasted_iota(jnp.int32, rows.shape, 1)
    return jnp.where(
        lane % HEAD_DIM < half, pltpu.roll(rows, width - half, 1), pltpu.roll(rows, half, 1)
    )


PAIR = 2 * HEAD_DIM


def head_mask(shape, head):
    lane = lax.broadcasted_iota(jnp.int32, shape, 1)
    return (lane >= head * HEAD_DIM) & (lane < (head + 1) * HEAD_DIM)


def masked_scores(query, key_ref, row_ref, col_ref, q0, cols):
    tail = min(2 * BLOCK, cols)
    scores = contract(query, key_ref[0:cols, :], 1, 1)
    shown = row_ref[:, pl.ds(cols - tail, tail)] <= col_ref[pl.ds(q0, BLOCK), :]
    hidden = jnp.where(shown, scores[:, cols - tail :], -jnp.inf)
    return jnp.concatenate([scores[:, : cols - tail], hidden], 1) if tail < cols else hidden


def attend_forward_kernel(
    qkv_ref, cos_ref, sin_ref, row_ref, col_ref, q_ref, k_ref, v_ref, out_ref, lse_ref, peak_ref
):
    pairs, length, _ = q_ref.shape
    for t in range(length // BLOCK):
        rows = pl.ds(t * BLOCK, BLOCK)
        cosine, sine = cos_ref[rows, :], sin_ref[rows, :]
        for pair in range(pairs):
            first = 3 * pair * PAIR
            query = qkv_ref[rows, first : first + PAIR]
            query = (query * cosine + swap_halves(query) * sine).astype(bf16)
            q_ref[pair, rows, :] = (query.astype(f32) * HEAD_DIM ** (-0.5)).astype(bf16)
            key = qkv_ref[rows, first + PAIR : first + 2 * PAIR]
            k_ref[pair, rows, :] = (key * cosine + swap_halves(key) * sine).astype(bf16)
            v_ref[pair, rows, :] = qkv_ref[rows, first + 2 * PAIR : first + 3 * PAIR].astype(bf16)
    peak_ref[...] = jnp.full(peak_ref.shape, -jnp.inf, f32)
    lane = lax.broadcasted_iota(jnp.int32, (BLOCK, 128), 1)
    for t in range(length // BLOCK):
        q0 = t * BLOCK
        rows = pl.ds(q0, BLOCK)
        cols = min(q0 + 2 * BLOCK, length)

        @pl.loop(0, pairs)
        def _(pair):
            total = jnp.zeros((BLOCK, PAIR), f32)
            for sub in range(2):
                head = 2 * pair + sub
                mask = head_mask((BLOCK, PAIR), sub)
                query = jnp.where(mask, q_ref[pair, rows, :], 0).astype(bf16)
                scores = masked_scores(query, k_ref.at[pair], row_ref, col_ref, q0, cols)
                row_max = jnp.max(scores, 1, keepdims=True)
                numerators = jnp.exp(scores - row_max)
                totals = jnp.sum(numerators, 1, keepdims=True)
                mixed = contract(numerators.astype(bf16), v_ref[pair, 0:cols, :], 1, 0) / totals
                total = jnp.where(mask, mixed, total)
                lse_ref[rows, :] = jnp.where(lane == head, row_max + jnp.log(totals), lse_ref[rows, :])
                peak_ref[...] = jnp.where(
                    lax.broadcasted_iota(jnp.int32, peak_ref.shape, 1) == head,
                    jnp.maximum(peak_ref[...], jnp.max(row_max)),
                    peak_ref[...],
                )
            out_ref[rows, pl.ds(pl.multiple_of(pair * PAIR, PAIR), PAIR)] = total.astype(bf16)


def attend_forward(qkv, cosine, sine, row_blocks, col_blocks):
    length = qkv.shape[0]
    pairs = qkv.shape[1] // (3 * PAIR)
    shape = jax.ShapeDtypeStruct
    return pl.pallas_call(
        attend_forward_kernel,
        out_shape=(
            shape((pairs, length, PAIR), bf16),
            shape((pairs, length, PAIR), bf16),
            shape((pairs, length, PAIR), bf16),
            shape((length, pairs * PAIR), bf16),
            shape((length, 128), f32),
            shape((8, 128), f32),
        ),
        in_specs=[vmem] * 5,
        out_specs=tuple([vmem] * 6),
        compiler_params=pltpu.CompilerParams(vmem_limit_bytes=56 * 1024 * 1024),
        cost_estimate=pl.CostEstimate(
            flops=16 * pairs * length * length * PAIR, bytes_accessed=length * PAIR * pairs * 24,
            transcendentals=2 * pairs * length * length,
        ),
        name="attend_forward",
    )(qkv, cosine, sine, row_blocks, col_blocks)


def attend_backward_kernel(
    first_head, q_ref, k_ref, v_ref, grad_ref, lse_ref, cos_ref, sin_ref, row_ref, col_ref, normed_ref,
    out_ref, weight_ref, dk_ref, dv_ref,
):
    length = q_ref.shape[0]
    dk_ref[...] = jnp.zeros_like(dk_ref)
    dv_ref[...] = jnp.zeros_like(dv_ref)
    lane = lax.broadcasted_iota(jnp.int32, (BLOCK, 128), 1)
    for t in range(length // BLOCK):
        q0 = t * BLOCK
        rows = pl.ds(q0, BLOCK)
        cols = min(q0 + 2 * BLOCK, length)

        def one_head(sub, dq):
            mask = head_mask((BLOCK, PAIR), sub)
            query = jnp.where(mask, q_ref[rows, :], 0).astype(bf16)
            grad = jnp.where(mask, grad_ref[rows, :], 0).astype(bf16)
            lse = jnp.sum(
                jnp.where(lane == first_head + sub, lse_ref[rows, :], 0.0), 1, keepdims=True
            )
            scores = masked_scores(query, k_ref, row_ref, col_ref, q0, cols)
            attention = jnp.exp(scores - lse)
            grad_attention = contract(grad, v_ref[0:cols, :], 1, 1)
            weighted = attention * grad_attention
            centre = jnp.sum(weighted, 1, keepdims=True)
            grad_scores = (weighted - attention * centre).astype(bf16)
            dv_ref[0:cols, :] += contract(attention.astype(bf16), grad, 0, 0)
            dk_ref[0:cols, :] += contract(grad_scores, query, 0, 0)
            return jnp.where(mask, contract(grad_scores, k_ref[0:cols, :], 1, 0), dq)

        dq = lax.fori_loop(0, 2, one_head, jnp.zeros((BLOCK, PAIR), f32)) * HEAD_DIM ** (-0.5)
        out_ref[rows, 0:PAIR] = (dq * cos_ref[rows, :] - swap_halves(dq) * sin_ref[rows, :]).astype(bf16)
    for t in range(length // BLOCK):
        rows = pl.ds(t * BLOCK, BLOCK)
        dk = dk_ref[rows, :]
        out_ref[rows, PAIR : 2 * PAIR] = (
            dk * cos_ref[rows, :] - swap_halves(dk) * sin_ref[rows, :]
        ).astype(bf16)
        out_ref[rows, 2 * PAIR : 3 * PAIR] = dv_ref[rows, :].astype(bf16)
    side = 256

    @pl.loop(0, normed_ref.shape[1] // side)
    def _(k):
        span = pl.ds(pl.multiple_of(k * side, side), side)
        weight_ref[span, :] = contract(normed_ref[:, span], out_ref[...], 0, 0).astype(bf16)


def attend_backward(pair, query, key, value, grad, lse, cosine, sine, row_blocks, col_blocks, normed):
    length, width = normed.shape
    heads = pl.BlockSpec((None, length, PAIR), lambda _: (pair, 0, 0))
    return pl.pallas_call(
        functools.partial(attend_backward_kernel, 2 * pair),
        grid=(1,),
        out_shape=(
            jax.ShapeDtypeStruct((length, 3 * PAIR), bf16), jax.ShapeDtypeStruct((width, 3 * PAIR), bf16),
        ),
        in_specs=[heads] * 3 + [pl.BlockSpec((length, PAIR), lambda _: (0, pair))] + [vmem] * 6,
        out_specs=(vmem, vmem),
        scratch_shapes=[pltpu.VMEM((length, PAIR), f32), pltpu.VMEM((length, PAIR), f32)],
        compiler_params=pltpu.CompilerParams(vmem_limit_bytes=56 * 1024 * 1024),
        cost_estimate=pl.CostEstimate(
            flops=40 * length * length * PAIR + 6 * length * width * PAIR, bytes_accessed=100_000_000,
            transcendentals=2 * length * length,
        ),
        name="attend_backward",
    )(query, key, value, grad, lse, cosine, sine, row_blocks, col_blocks, normed)


def bit_of(index, bit):
    return lax.rem(lax.div(index, bit), 2)


def flip_bit(index, bit):
    return index + bit - 2 * bit * bit_of(index, bit)


def team_mate(me, bits, offset):
    device, place = me, 0
    for k, bit in enumerate(bits):
        moved = (offset >> k) % 2
        place = place + lax.rem(bit_of(me, bit) + moved, 2) * (1 << k)
        device = flip_bit(device, bit) if moved else device
    return device, place


class Links:

    def __init__(self, send_sems, recv_sems):
        self.send_sems, self.recv_sems = send_sems, recv_sems

    def copy(self, slot, src, dst, device):
        return pltpu.make_async_remote_copy(
            src_ref=src, dst_ref=dst, send_sem=self.send_sems.at[slot],
            recv_sem=self.recv_sems.at[slot], device_id=(device,), device_id_type=MESH,
        )


def greet(partners):
    barrier = pltpu.get_barrier_semaphore()
    for partner in partners:
        pl.semaphore_signal(barrier, inc=1, device_id=(partner,), device_id_type=MESH)
    pl.semaphore_wait(barrier, len(partners))


def spread_block(bits, cut, own_ref, out_ref, links, local_sem):
    core, first, second = bits
    me = lax.axis_index(AXIS)
    sibling, next_a, next_b = (flip_bit(me, bit) for bit in bits)
    block = own_ref.shape[0]
    in_a, in_b = bit_of(me, first), bit_of(me, second)
    spans = {None: (0, block), 0: (0, cut), 1: (cut, block - cut)}

    def rows(flip_a, flip_b, part):
        place = bit_of(me, core)
        place = place + 2 * lax.rem(in_a + flip_a, 2) + 4 * lax.rem(in_b + flip_b, 2)
        start, size = spans[part]
        return pl.ds(pl.multiple_of(place * block + start, 16), size)

    def passed(slot, where, device):
        return links.copy(slot, out_ref.at[where], out_ref.at[where], device)

    def first_hand(slot, part, device):
        start, size = spans[part]
        return links.copy(slot, own_ref.at[pl.ds(start, size)], out_ref.at[rows(0, 0, part)], device)

    makers = {
        0: lambda: first_hand(0, 0, next_a),
        1: lambda: first_hand(1, 1, next_b),
        2: lambda: first_hand(2, 1, next_a),
        3: lambda: first_hand(3, 0, next_b),
        4: lambda: links.copy(4, own_ref, out_ref.at[rows(0, 0, None)], sibling),
        5: lambda: passed(5, rows(1, 0, 0), next_b),
        6: lambda: passed(6, rows(1, 0, 0), sibling),
        7: lambda: passed(7, rows(0, 1, 1), next_a),
        8: lambda: passed(8, rows(0, 1, 1), sibling),
        9: lambda: passed(9, rows(1, 0, 1), sibling),
        10: lambda: passed(10, rows(0, 1, 0), sibling),
        11: lambda: passed(11, rows(1, 1, 0), sibling),
        12: lambda: passed(12, rows(1, 1, 1), sibling),
    }
    needs = {0: 0, 1: 1, 2: 1, 3: 0, 4: None, 5: 0, 6: 0, 7: 1, 8: 1, 9: 1, 10: 0, 11: 0, 12: 1}
    copies = {slot: make() for slot, make in makers.items() if spans[needs[slot]][1]}
    keep = pltpu.make_async_copy(own_ref, out_ref.at[rows(0, 0, None)], local_sem)

    def begin():
        for slot in range(5):
            if slot in copies:
                copies[slot].start()
        keep.start()

    def hand_on(arrived, *sent):
        def phase():
            if arrived in copies:
                copies[arrived].wait_recv()
                for slot in sent:
                    copies[slot].start()

        return phase

    def finish():
        for slot in (4, 6, 8, 9, 10, 11, 12):
            if slot in copies:
                copies[slot].wait_recv()
        keep.wait()
        for slot in copies:
            copies[slot].wait_send()

    return [
        begin, hand_on(0, 5, 6), hand_on(1, 7, 8), hand_on(2, 9), hand_on(3, 10),
        hand_on(5, 11), hand_on(7, 12), finish,
    ]


def run(phases):
    for phase in phases:
        phase()


SPREAD_COPIES = 13
SUM_COPIES = 10


def sum_block(bits, cut, swapped, product, total, to_core, from_core, chip_sum, arrived, links):
    core = bits[0]
    (first, weight_a), (second, weight_b) = ((bits[2], 4), (bits[1], 2)) if swapped else ((bits[1], 2), (bits[2], 4))
    me = lax.axis_index(AXIS)
    sibling, next_a, next_b = flip_bit(me, core), flip_bit(me, first), flip_bit(me, second)
    block, width = total.shape
    tile = 512

    def place(step, other_core):
        flip_a, flip_b = 1 - step // 2, 1 - step % 2
        return (
            lax.rem(bit_of(me, core) + other_core, 2)
            + weight_a * lax.rem(bit_of(me, first) + flip_a, 2)
            + weight_b * lax.rem(bit_of(me, second) + flip_b, 2)
        )

    low, high = (0, cut), (cut, block - cut)
    landing = range(6) if cut else {1: 0, 3: 1, 4: 2}

    def link(slot, step, span, device):
        return links.copy(slot, chip_sum.at[step, pl.ds(*span)], arrived.at[landing[slot - 4], pl.ds(0, span[1])], device)

    diag_a, diag_b = (link(4, 0, low, next_a) if cut else None), link(5, 0, high, next_b)
    plain_a, plain_b = (link(6, 1, low, next_a) if cut else None), link(7, 2, high, next_b)
    last_a, last_b = link(8, 1, high, next_a), (link(9, 2, low, next_b) if cut else None)

    def core_copy(step):
        return links.copy(step, to_core.at[step], from_core.at[step], sibling)

    def for_sibling():
        @pl.loop(0, 4)
        def _(step):
            @pl.loop(0, width // tile)
            def _(column):
                columns = pl.ds(pl.multiple_of(column * tile, tile), tile)
                to_core[step, :, columns] = product(place(step, 1), columns).astype(bf16)

            core_copy(step).start()

    def for_chip():
        @pl.loop(0, 4)
        def _(step):
            core_copy(step).wait_recv()

            @pl.loop(0, width // tile)
            def _(column):
                columns = pl.ds(pl.multiple_of(column * tile, tile), tile)
                summed = product(place(step, 0), columns) + from_core[step, :, columns].astype(f32)
                total[:, columns] = summed

                @pl.when(step < 3)
                def _():
                    chip_sum[step, :, columns] = summed.astype(bf16)

            @pl.when(step == 0)
            def _():
                if cut:
                    diag_a.start()
                diag_b.start()

            @pl.when(step == 1)
            def _():
                if cut:
                    plain_a.start()

            @pl.when(step == 2)
            def _():
                plain_b.start()

    def add(step, span, slot):
        rows = pl.ds(*span)
        chip_sum[step, rows, :] = (
            chip_sum[step, rows, :].astype(f32) + arrived[landing[slot], 0 : span[1], :].astype(f32)
        ).astype(bf16)

    def take(span, slot):
        total[pl.ds(*span), :] += arrived[landing[slot], 0 : span[1], :].astype(f32)

    def hand_on():
        if cut:
            diag_a.wait_recv()
            add(2, low, 0)
            last_b.start()
        diag_b.wait_recv()
        add(1, high, 1)
        last_a.start()

    def finish():
        if cut:
            plain_a.wait_recv()
            take(low, 2)
        plain_b.wait_recv()
        take(high, 3)
        if cut:
            last_b.wait_recv()
            take(low, 5)
        last_a.wait_recv()
        take(high, 4)

        @pl.loop(0, 4)
        def _(step):
            core_copy(step).wait_send()

        for copy in (diag_a, diag_b, plain_a, plain_b, last_a, last_b):
            if copy is not None:
                copy.wait_send()

    return for_sibling, for_chip, hand_on, finish


def sum_scratch(block, width, cut):
    return [
        pltpu.VMEM((block, width), f32),
        pltpu.VMEM((4, block, width), bf16),
        pltpu.VMEM((4, block, width), bf16),
        pltpu.VMEM((3, block, width), bf16),
        pltpu.VMEM((6 if cut else 3, block - cut, width), bf16),
        pltpu.SemaphoreType.DMA((SUM_COPIES,)),
        pltpu.SemaphoreType.DMA((SUM_COPIES,)),
    ]


def spread_scratch(block, width):
    return [
        pltpu.VMEM((block, width), bf16),
        pltpu.SemaphoreType.DMA((SPREAD_COPIES,)),
        pltpu.SemaphoreType.DMA((SPREAD_COPIES,)),
        pltpu.SemaphoreType.DMA,
    ]


def link_params(collective_id):
    return pltpu.CompilerParams(
        collective_id=collective_id, has_side_effects=True, vmem_limit_bytes=60 * 1024 * 1024
    )


def cost(flops, size):
    return pl.CostEstimate(flops=int(flops), bytes_accessed=int(size), transcendentals=0)


def row_scale(values):
    return lax.rsqrt(jnp.mean(values * values, -1, keepdims=True) + epsilon)


def front_kernel(
    team, teams, qkv_moves, ffn_moves, carry_bits, tokens_ref, query_ref, key_ref, value_ref, gate_ref, up_ref, small_ref, *refs,
):
    moved = len(carry_bits)
    (carried, refs) = (refs[0], refs[1:]) if moved else (None, refs)
    (normed_out, weights_out, both_out, small_out), refs = refs[:4], refs[4:]
    carried_out, refs = refs[:moved], refs[moved:]
    (tokens_all, mine, both_mine, gain,
    send_sems, recv_sems, local_sem, swap_send, swap_recv, swap_local, line_send, line_recv, small_send, small_recv,
    both_send, both_recv, both_local, out_sems, *carry_sems) = refs
    me = lax.axis_index(AXIS)
    mate, group = lax.rem(me, team), lax.div(me, team)
    devices = team * teams
    mates = [group * team + lax.rem(mate + k, team) for k in range(1, team)]
    above, below = lax.rem(me + team, devices), lax.rem(me + devices - team, devices)
    ffn_mates = [team_mate(me, (1, 2, 8), k) for k in range(team)]
    rows = mine.shape[1]
    swaps, line, small = Links(swap_send, swap_recv), Links(line_send, line_recv), Links(small_send, small_recv)
    both = Links(both_send, both_recv)
    for i, member, source, target, columns in qkv_moves:
        weight = (query_ref, key_ref, value_ref)[i]
        mine[member, :, target : target + columns] = weight[:, source : source + columns]
    greet(
        mates + [lax.rem(me + k * team, devices) for k in range(1, teams)]
        + [device for device, _ in ffn_mates[4:]]
    )

    def share(place):
        return pl.ds(pl.multiple_of(place * rows, rows), rows)

    swap_copies = [
        swaps.copy(k, mine.at[lax.rem(mate + k + 1, team)], weights_out.at[group, share(mate)], mates[k])
        for k in range(team - 1)
    ]
    crossing = [
        Links(*carry_sems).copy(i, carried, carried_out[i], flip_bit(me, bit)) for i, bit in enumerate(carry_bits)
    ]
    for copy in swap_copies:
        copy.start()
    keep = pltpu.make_async_copy(mine.at[mate], weights_out.at[group, share(mate)], swap_local)
    keep.start()
    small_out[me] = small_ref[...]

    others = [lax.rem(me + k * team, devices) for k in range(1, teams)]
    team_rows = pl.ds(pl.multiple_of(group * team, team), team)
    small_near = [
        small.copy(k, small_out.at[me], small_out.at[me], device) for k, device in enumerate(mates)
    ]
    small_far = [
        small.copy(team + k, small_out.at[team_rows], small_out.at[team_rows], device)
        for k, device in enumerate(others)
    ]
    for copy in small_near:
        copy.start()
    spread = spread_block(
        (1, 2, 4), HALF, tokens_ref, tokens_all, Links(send_sems, recv_sems), local_sem
    )
    for i, member, source, target, columns in ffn_moves:
        both_mine[i * team + member, :, target : target + columns] = (gate_ref, up_ref)[i][:, source : source + columns]

    def passed(slot, shard, device):
        return line.copy(slot, weights_out.at[shard], weights_out.at[shard], device)

    steps = teams - 1

    def up(step):
        return passed(step - 1, group - (step - 1), above)

    def down(step):
        return passed(steps + step - 1, group + (step - 1), below)

    def line_start(step):
        pl.when((group < teams - 1) & (group >= step - 1))(lambda: up(step).start())
        pl.when((group > 0) & (group + step - 1 < teams))(lambda: down(step).start())

    def line_wait(step):
        pl.when(group >= step)(lambda: up(step).wait_recv())
        pl.when(group + step < teams)(lambda: down(step).wait_recv())

    def line_sent(step):
        pl.when((group < teams - 1) & (group >= step - 1))(lambda: up(step).wait_send())
        pl.when((group > 0) & (group + step - 1 < teams))(lambda: down(step).wait_send())

    for copy in small_near:
        copy.wait_recv()
    for copy in small_far:
        copy.start()
    own_place = ffn_mates[0][1]
    both_copies = [
        both.copy(
            i * team + k, both_mine.at[i * team + ffn_mates[k][1]], both_out.at[i * team + own_place], ffn_mates[k][0]
        )
        for i in range(2) for k in range(1, team)
    ]
    for copy in both_copies:
        copy.start()
    both_keep = [
        pltpu.make_async_copy(both_mine.at[i * team + own_place], both_out.at[i * team + own_place], both_local.at[i])
        for i in range(2)
    ]
    for copy in both_keep:
        copy.start()
    for copy in swap_copies:
        copy.wait_recv()
    keep.wait()
    line_start(1)
    spread[0]()
    for copy in crossing:
        copy.start()
    for copy in small_far:
        copy.wait_recv()
    spread[1]()
    spread[2]()
    line_wait(1)
    line_start(2)
    spread[3]()
    spread[4]()
    width = tokens_all.shape[1]
    gains = width // devices
    for d in range(devices):
        gain[:, d * gains : (d + 1) * gains] = small_out[d, 0:1, 0:gains]
    for phase in spread[5:]:
        phase()
    block = tokens_ref.shape[0]

    def normed_copy(k):
        span = pl.ds(pl.multiple_of(k * block, block), block)
        return pltpu.make_async_copy(tokens_all.at[span], normed_out.at[span], out_sems.at[k])

    def norm_blocks(first, last):
        @pl.loop(first, last)
        def _(k):
            span = pl.ds(pl.multiple_of(k * block, block), block)
            values = tokens_all[span, :].astype(f32)
            tokens_all[span, :] = (values * row_scale(values) * gain[...]).astype(bf16)
            normed_copy(k).start()

    norm_blocks(0, 2)
    for step in range(2, teams):
        line_wait(step)
        if step < steps:
            line_start(step + 1)
        if step == 2:
            norm_blocks(2, team)
    for k in range(team):
        normed_copy(k).wait()
    for copy in both_copies:
        copy.wait_recv()
    for copy in both_keep:
        copy.wait()
    for copy in swap_copies + both_copies:
        copy.wait_send()
    for step in range(1, teams):
        line_sent(step)
    for copy in small_near + small_far:
        copy.wait_send()
    for copy in crossing:
        copy.wait()


def front(tokens, weights, small, teams, qkv_moves, ffn_moves, carried, carry_bits):
    block, width = tokens.shape
    team = 8
    rows, cols = weights[0].shape[0], 3 * width // team
    both_cols = weights[3].shape[1] // team
    devices = team * teams
    dma = pltpu.SemaphoreType.DMA
    shape = jax.ShapeDtypeStruct
    return pl.pallas_call(
        functools.partial(front_kernel, team, teams, qkv_moves, ffn_moves, carry_bits),
        out_shape=(
            shape((team * block, width), bf16),
            shape((teams, team * rows, cols), bf16),
            shape((2 * team, rows, both_cols), bf16),
            shape((devices,) + small.shape, f32),
        ) + tuple(shape(carried[0].shape, bf16) for _ in carry_bits),
        in_specs=[vmem] * 7 + [anywhere] * len(carried),
        out_specs=(anywhere, anywhere, anywhere, vmem) + (anywhere,) * len(carry_bits),
        scratch_shapes=[
            pltpu.VMEM((team * block, width), bf16), pltpu.VMEM((team, rows, cols), bf16),
            pltpu.VMEM((2 * team, rows, both_cols), bf16), pltpu.VMEM((1, width), f32),
        ]
        + spread_scratch(block, width)[1:]
        + [dma((team - 1,)), dma((team - 1,)), dma, dma((2 * teams,)), dma((2 * teams,)), dma((team + teams,)), dma((team + teams,))]
        + [dma((2 * team,)), dma((2 * team,)), dma((2,)), dma((team,))]
        + [dma((1,))] * (2 * len(carried)),
        compiler_params=link_params(1),
        cost_estimate=cost(0, 200e6),
        name="front",
    )(tokens, *weights, small, *carried)


def branch_kernel(
    carry, swap_bits, spread_bits, left_ref, right_ref, residual_ref, gain_ref, peak_ref, *refs,
):
    if carry:
        (both_own, both_y, both_z, down_own, down_y), refs = refs[:5], refs[5:]
        (h2_ref, out_ref, peak_out, gate_full, up_full, down_full), refs = refs[:6], refs[6:]
        (landed, together, swap_send, swap_recv, own, send_sems, recv_sems, local_sem,
         peak_in, peak_send, peak_recv, carry_send, carry_recv, carry_local) = refs
    else:
        (h2_ref, out_ref, peak_out), refs = refs[:3], refs[3:]
        (landed, together, swap_send, swap_recv, own, send_sems, recv_sems, local_sem,
         peak_in, peak_send, peak_recv) = refs
    me = lax.axis_index(AXIS)
    team, block, _ = landed.shape
    bits = [1 << k for k in range(peak_in.shape[0])]
    mates = [team_mate(me, swap_bits, k) for k in range(team)]
    greet([device for device, _ in mates[1:]] + [flip_bit(me, bit) for bit in bits if bit not in swap_bits])
    own_place = mates[0][1]

    def rows_at(place):
        return pl.ds(pl.multiple_of(place * block, block), block)

    swap_copies = [
        Links(swap_send, swap_recv).copy(k, left_ref.at[rows_at(mates[k][1])], landed.at[own_place], mates[k][0])
        for k in range(1, team)
    ]
    for copy in swap_copies:
        copy.start()
    peaks = Links(peak_send, peak_recv)

    def peak_copy(k):
        return peaks.copy(k, peak_out, peak_in.at[k], flip_bit(me, bits[k]))

    def peak_step(k):
        if k:
            peak_copy(k - 1).wait()
            peak_out[...] = jnp.maximum(peak_out[...], peak_in[k - 1])
        if k < len(bits):
            peak_copy(k).start()

    if carry:
        carried = Links(carry_send, carry_recv)
        high, middle = bit_of(me, 16), bit_of(me, 4)
        by_y, by_z = flip_bit(me, 4), flip_bit(me, 16)

        def rows_of(part, flip_z, flip_y):
            z, y = lax.rem(high + flip_z, 2), lax.rem(middle + flip_y, 2)
            return pl.ds(pl.multiple_of(z * 16 + part * 8 + y * 4, 4), 4)

        early = both_z.shape[0] // 4

        def piece(source, half):
            return source.at[pl.ds(half * 4, 4)]

        def placed(half, flips):
            return (gate_full, up_full)[half // 2].at[rows_of(half % 2, *flips)]

        def unit(flip_z, flip_y):
            return lax.rem(high + flip_z, 2) * 2 + lax.rem(middle + flip_y, 2)

        kept = []
        for source, flips, halves in ((both_own, (0, 0), 4), (both_y, (0, 1), 4), (both_z, (1, 0), early)):
            for half in range(halves):
                kept.append((piece(source, half), placed(half, flips)))
        kept.append((down_own, down_full.at[unit(0, 0)]))
        kept.append((down_y, down_full.at[unit(0, 1)]))
        kept = [pltpu.make_async_copy(a, b, carry_local.at[i]) for i, (a, b) in enumerate(kept)]
        up_z = [
            carried.copy(half, piece(both_own, half), placed(half, (0, 0)), by_z) for half in range(early, 4)
        ]
        early_yz = [
            carried.copy(4 + half, piece(both_z, half), placed(half, (1, 0)), by_y) for half in range(early)
        ]
        up_yz = [
            carried.copy(4 + half, placed(half, (1, 0)), placed(half, (1, 0)), by_y) for half in range(early, 4)
        ]
        for copy in up_z + kept:
            copy.start()

    peak_out[...] = peak_ref[...]
    peak_step(0)
    landed[own_place] = left_ref[rows_at(own_place), :]
    for copy in swap_copies:
        copy.wait_recv()
    if carry:
        for copy in early_yz:
            copy.start()
    heads = landed.shape[2] // HEAD_DIM
    for b in range(team):
        for g in range(heads):
            first = (g * team + b) * HEAD_DIM
            together[:, first : first + HEAD_DIM] = landed[b, :, g * HEAD_DIM : (g + 1) * HEAD_DIM]
    tile = 512

    @pl.loop(0, own.shape[1] // tile)
    def _(column):
        columns = pl.ds(pl.multiple_of(column * tile, tile), tile)
        h2_ref[:, columns] = residual_ref[:, columns].astype(f32) + contract(
            together[...], right_ref[:, columns], 1, 0
        )

    h2 = h2_ref[...]
    own[...] = (h2 * row_scale(h2) * gain_ref[...]).astype(bf16)
    spread = spread_block(spread_bits, BRANCH_CUT, own, out_ref, Links(send_sems, recv_sems), local_sem)
    spread[0]()
    if carry:
        for over, on in zip(up_z, up_yz):
            over.wait_recv()
            on.start()
    for k, phase in enumerate(spread[1:-1]):
        phase()
        if k < len(bits):
            peak_step(k + 1)
    for k in range(len(spread) - 2, len(bits)):
        peak_step(k + 1)
    spread[-1]()
    for copy in swap_copies:
        copy.wait_send()
    if carry:
        for copy in kept:
            copy.wait()
        for copy in early_yz + up_yz:
            copy.wait_recv()
        for copy in up_z + early_yz + up_yz:
            copy.wait_send()


def branch(left, right, residual, gain, peak, carry, swap_bits, spread_bits, bit_count):
    block, width = residual.shape
    dma = pltpu.SemaphoreType.DMA
    shape = jax.ShapeDtypeStruct
    out_shape = [shape((block, width), f32), shape((8 * block, width), bf16), shape((8, 128), f32)]
    scratch = [pltpu.VMEM((8, block, left.shape[1]), bf16), pltpu.VMEM((block, width), bf16), dma((8,)), dma((8,))]
    scratch += spread_scratch(block, width)
    scratch += [pltpu.VMEM((bit_count, 8, 128), f32), dma((bit_count,)), dma((bit_count,))]
    if carry:
        out_shape += [
            shape((32,) + carry[0].shape[1:], bf16), shape((32,) + carry[0].shape[1:], bf16),
            shape((4,) + carry[3].shape, bf16),
        ]
        scratch += [dma((8,)), dma((8,)), dma((14,))]
    return pl.pallas_call(
        functools.partial(branch_kernel, bool(carry), swap_bits, spread_bits),
        out_shape=tuple(out_shape),
        in_specs=[vmem] * (5 + len(carry)),
        out_specs=tuple([vmem, anywhere, vmem] + [anywhere] * (len(out_shape) - 3)),
        scratch_shapes=scratch,
        compiler_params=link_params(2),
        cost_estimate=cost(16 * block * left.shape[1] * width, 300e6),
        name="attention_branch",
    )(left, right, residual, gain, peak, *carry)


def norm_back(values, gain, upstream):
    scaled = upstream * gain
    scale = row_scale(values)
    inner = jnp.mean(scaled * values, -1, keepdims=True)
    return scale * scaled - scale * scale * scale * values * inner


def ffn_back_kernel(
    cross, sum_bits, swap_bits, gate_ref, up_ref, gate_w_ref, up_w_ref, normed_ref, out_w_ref, h2_ref, cot_ref, gain_ref, *refs,
):
    (part_ref, refs) = (refs[0], refs[1:]) if cross else (None, refs)
    (residual_ref, branch_ref, heads_out, d_up_out, d_gate_own), refs = refs[:5], refs[5:]
    (d_gate_in, part_in, refs) = (refs[0], refs[1], refs[2:]) if cross else (None, None, refs)
    (total, to_core, from_core, chip_sum, arrived, sum_send, sum_recv,
     swap_send, swap_recv, local_sem, stage, stage_sems, own_sems, *more) = refs
    if cross:
        cross_send, cross_recv = more
        crossing = Links(cross_send, cross_recv)
    else:
        (stage_gate,) = more
    me = lax.axis_index(AXIS)
    block, width = total.shape
    team = 1 << len(swap_bits)
    mates = [team_mate(me, swap_bits, k) for k in range(team)]
    greet(
        [device for device, _ in mates[1:]] + [flip_bit(me, bit) for bit in sum_bits if bit not in swap_bits]
    )

    def product(place, columns):
        rows = pl.ds(pl.multiple_of(place * block, block), block)
        return contract(gate_ref[rows, :], gate_w_ref[columns, :], 1, 1) + contract(
            up_ref[rows, :], up_w_ref[columns, :], 1, 1
        )

    side, columns_ff = stage.shape[1:]
    count = width // side
    y_side, by_y = bit_of(me, 4), flip_bit(me, 4)
    if cross:
        part_copy = crossing.copy(count // 2, part_ref, part_in, by_y)
        part_copy.start()

    def parked(i, part):
        row = i * side
        rows = pl.ds(pl.multiple_of(lax.rem(row, block), 16), side)
        return from_core.at[lax.div(row, block), rows, pl.ds(part * columns_ff, columns_ff)]

    def cross_copy(i):
        return crossing.copy(i, parked(i, 0), d_gate_in.at[i], by_y)

    def own_copy(i):
        return pltpu.make_async_copy(parked(i, 1), d_gate_own.at[i], own_sems.at[i])

    def tile_of(step):
        if not cross:
            return step
        theirs = step < count // 2
        return jnp.where(theirs, 2 * step + 1 - y_side, 2 * step - count + y_side)

    def up_copy(step):
        span = pl.ds(pl.multiple_of(tile_of(step) * side, side), side)
        slot = lax.rem(step, 2)
        return pltpu.make_async_copy(stage.at[slot], d_up_out.at[span], stage_sems.at[slot])

    def gate_copy(step):
        span = pl.ds(pl.multiple_of(step * side, side), side)
        slot = lax.rem(step, 2)
        return pltpu.make_async_copy(stage_gate.at[slot], d_gate_own.at[span], own_sems.at[slot])

    def gradients(first, last):
        @pl.loop(first, last)
        def _(step):
            @pl.when(step >= 2)
            def _():
                up_copy(step - 2).wait()
                if not cross:
                    gate_copy(step - 2).wait()

            columns = normed_ref[:, pl.ds(pl.multiple_of(tile_of(step) * side, side), side)]
            stage[lax.rem(step, 2)] = contract(columns, up_ref[...], 0, 0).astype(bf16)
            up_copy(step).start()
            tile = contract(columns, gate_ref[...], 0, 0).astype(bf16)
            if not cross:
                stage_gate[lax.rem(step, 2)] = tile
                gate_copy(step).start()
                return

            @pl.when(step < count // 2)
            def _():
                parked(step, 0)[...] = tile
                cross_copy(step).start()

            @pl.when(step >= count // 2)
            def _():
                parked(step - count // 2, 1)[...] = tile
                own_copy(step - count // 2).start()

    for_sibling, for_chip, hand_on, finish = sum_block(
        sum_bits, HALF, False, product, total, to_core, from_core, chip_sum, arrived, Links(sum_send, sum_recv)
    )
    for_sibling()
    for_chip()
    gradients(0, 1)
    hand_on()
    gradients(1, count - 2)
    finish()
    residual = cot_ref[...].astype(f32) + norm_back(h2_ref[...], gain_ref[...], total[...])
    residual_ref[...] = residual
    branch_ref[...] = residual.astype(bf16)
    tile, share = team * HEAD_DIM, width // team
    for g in range(width // tile):
        heads = contract(branch_ref[...], out_w_ref[g * tile : (g + 1) * tile, :], 1, 1).astype(bf16)
        for b in range(team):
            first = b * share + g * HEAD_DIM
            to_core[0, :, first : first + HEAD_DIM] = heads[:, b * HEAD_DIM : (b + 1) * HEAD_DIM]
    own_place = mates[0][1]
    own_rows = pl.ds(pl.multiple_of(own_place * block, block), block)
    def heads_of(place):
        return to_core.at[0, :, pl.ds(pl.multiple_of(place * share, share), share)]

    swap_copies = [
        Links(swap_send, swap_recv).copy(k, heads_of(mates[k][1]), heads_out.at[own_rows], mates[k][0])
        for k in range(1, team)
    ]
    keep = pltpu.make_async_copy(heads_of(own_place), heads_out.at[own_rows], local_sem)
    for copy in swap_copies + [keep]:
        copy.start()
    gradients(count - 2, count)
    for copy in swap_copies:
        copy.wait_recv()
    for copy in swap_copies:
        copy.wait_send()
    keep.wait()
    for step in range(count - 2, count):
        up_copy(step).wait()
        if not cross:
            gate_copy(step).wait()
    if cross:
        part_copy.wait()

        @pl.loop(0, count // 2)
        def _(i):
            own_copy(i).wait()
            cross_copy(i).wait()


def ffn_back(gate, up, gate_w, up_w, normed, out_w, h2, cot, gain, part, side, sum_bits, swap_bits):
    block, width = h2.shape
    shape = jax.ShapeDtypeStruct
    dma = pltpu.SemaphoreType.DMA
    ff_cols, cross = gate.shape[1], side % 128 == 0
    side = side if cross else 256
    tiles = width // side // 2
    if cross:
        d_gate = (shape((tiles, side, ff_cols), bf16),) * 2 + (shape(part[0].shape, bf16),)
        more = [dma((tiles + 1,)), dma((tiles + 1,))]
    else:
        d_gate, more = (shape((width, ff_cols), bf16),), [pltpu.VMEM((2, side, ff_cols), bf16)]
    return pl.pallas_call(
        functools.partial(ffn_back_kernel, cross, sum_bits, swap_bits),
        out_shape=(
            shape((block, width), f32), shape((block, width), bf16), shape((8 * block, width // 8), bf16),
            shape((width, ff_cols), bf16),
        ) + d_gate,
        in_specs=[vmem] * 9 + [anywhere] * len(part),
        out_specs=(vmem, vmem) + (anywhere,) * (2 + len(d_gate)),
        scratch_shapes=sum_scratch(block, width, HALF)
        + [dma((8,)), dma((8,)), dma]
        + [pltpu.VMEM((2, side, ff_cols), bf16), dma((2,)), dma((tiles,))]
        + more,
        compiler_params=link_params(3),
        cost_estimate=cost(96 * block * ff_cols * width, 200e6),
        name="ffn_back",
    )(gate, up, gate_w, up_w, normed, out_w, h2, cot, gain, *part)


def last_sums_kernel(
    sum_bits, ffn_bits, left_ref, other_ref, right_ref, tokens_ref, gain_ref, residual_ref, hidden_ref, down_ref, h2_ref,
    gate_ref, out_ref, mixed_ref, gate_out, *scratch,
):
    (swap_send, swap_recv, swap_local), scratch = scratch[-3:], scratch[:-3]
    count = len(scratch) // 2
    me = lax.axis_index(AXIS)
    total, ffn_total = scratch[0], scratch[count]
    block = total.shape[0]
    mates = [team_mate(me, ffn_bits, k) for k in range(8)]
    partners = [flip_bit(me, bit) for bit in sum_bits if bit not in ffn_bits]
    greet(partners + [device for device, _ in mates[1:]])
    swaps, own_place = Links(swap_send, swap_recv), mates[0][1]
    swap_copies = [
        swaps.copy(k, gate_ref.at[mates[k][1]], gate_out.at[own_place], mates[k][0]) for k in range(1, 8)
    ]
    keep = pltpu.make_async_copy(gate_ref.at[own_place], gate_out.at[own_place], swap_local)

    def rows_of(place):
        return pl.ds(pl.multiple_of(place * block, block), block)

    def product(place, columns):
        rows = rows_of(place)
        middle = left_ref.shape[1]
        return contract(left_ref[rows, :], right_ref[columns, 0:middle], 1, 1) + contract(
            other_ref[rows, :], right_ref[columns, middle : 2 * middle], 1, 1
        )

    def ffn_product(place, columns):
        return contract(hidden_ref[rows_of(place), :], down_ref[:, columns], 1, 0)

    first = sum_block(sum_bits, LAST_CUT, False, product, *scratch[: count - 2], Links(*scratch[count - 2 : count]))
    second = sum_block(ffn_bits, LAST_CUT, True, ffn_product, *scratch[count:-2], Links(*scratch[-2:]))
    run(first[:2])
    run(second[:2])
    for copy in swap_copies + [keep]:
        copy.start()
    for one, other in zip(first[2:], second[2:]):
        one()
        other()
    out_ref[...] = residual_ref[...] + norm_back(
        tokens_ref[...].astype(f32), gain_ref[...], total[...]
    )
    mixed_ref[...] = (h2_ref[...] + ffn_total[...]).astype(bf16)
    for copy in swap_copies:
        copy.wait_recv()
    for copy in swap_copies:
        copy.wait_send()
    keep.wait()


def last_sums(left, other, right, tokens, gain, residual, hidden, down, h2, d_gate, sum_bits, ffn_bits):
    block, width = tokens.shape
    return pl.pallas_call(
        functools.partial(last_sums_kernel, sum_bits, ffn_bits),
        out_shape=(
            jax.ShapeDtypeStruct((block, width), f32), jax.ShapeDtypeStruct((block, width), bf16),
            jax.ShapeDtypeStruct(d_gate.shape, bf16),
        ),
        in_specs=[vmem] * 9 + [anywhere],
        out_specs=(vmem, vmem, anywhere),
        scratch_shapes=sum_scratch(block, width, LAST_CUT) * 2
        + [pltpu.SemaphoreType.DMA((8,)), pltpu.SemaphoreType.DMA((8,)), pltpu.SemaphoreType.DMA],
        compiler_params=link_params(4),
        cost_estimate=cost(16 * block * right.size // 8, 300e6),
        name="last_sums",
    )(left, other, right, tokens, gain, residual, hidden, down, h2, d_gate)


def exchange_kernel(teams, sources, *refs):
    mine, landed, (send_sems, recv_sems, local_sems) = refs[:sources], refs[sources : 2 * sources], refs[2 * sources :]
    me = lax.axis_index(AXIS)
    members = mine[0].shape[0]
    links = Links(send_sems, recv_sems)
    greeted = {}
    for bits in teams:
        for k in range(1, members):
            device, _ = team_mate(me, bits, k)
            greeted[tuple(sorted(bit for j, bit in enumerate(bits) if (k >> j) % 2))] = device
    greet(list(greeted.values()))
    copies, kept = [], []
    for i, (source, target, bits) in enumerate(zip(mine, landed, teams)):
        own = team_mate(me, bits, 0)[1]
        kept.append(pltpu.make_async_copy(source.at[own], target.at[own], local_sems.at[i]))
        for k in range(1, members):
            device, place = team_mate(me, bits, k)
            copies.append(links.copy(i * members + k, source.at[place], target.at[own], device))
    for copy in copies + kept:
        copy.start()
    for copy in copies:
        copy.wait()
    for copy in kept:
        copy.wait()


def exchange(parts, teams):
    dma = pltpu.SemaphoreType.DMA
    slots = len(parts) * parts[0].shape[0]
    return pl.pallas_call(
        functools.partial(exchange_kernel, teams, len(parts)),
        out_shape=tuple(jax.ShapeDtypeStruct(part.shape, part.dtype) for part in parts),
        in_specs=[vmem] * len(parts),
        out_specs=tuple([vmem] * len(parts)),
        scratch_shapes=[dma((slots,)), dma((slots,)), dma((len(parts),))],
        compiler_params=link_params(5),
        cost_estimate=cost(1e6, 40e6),
        name="exchange",
    )(*parts)


def home_kernel(places, gain_of, sources, *refs):
    count = len(places)
    kinds = max(gain_of) + 1
    parts, weights, gains = refs[:sources], refs[sources : sources + count], refs[sources + count : sources + count + kinds]
    outs, gain_outs = refs[-count - kinds : -kinds], refs[-kinds:]
    totals = [jnp.zeros(gain.shape, f32) for gain in gains]
    for i, (out, weight) in enumerate(zip(outs, weights)):
        for source, member, first, target, columns in places[i]:
            out[:, target : target + columns] = parts[source][member, :, first : first + columns].astype(f32)
        for first in range(0, out.shape[1], 1024):
            product = out[:, first : first + 1024] * weight[:, first : first + 1024].astype(f32)
            totals[gain_of[i]] += jnp.sum(product, 1, keepdims=True)
    for gain, total, out in zip(gains, totals, gain_outs):
        out[...] = jnp.broadcast_to(total / gain[...], (out.shape[1], 128)).T[0:1, :]


def home(parts, weights, gains, gain_of, places):
    shape = jax.ShapeDtypeStruct
    count = len(weights)
    gains = [gain.astype(f32).reshape(-1, 1) for gain in gains]
    return pl.pallas_call(
        functools.partial(home_kernel, places, gain_of, len(parts)),
        out_shape=tuple(shape(w.shape, f32) for w in weights) + tuple(shape((1, g.shape[0]), f32) for g in gains),
        in_specs=[vmem] * (len(parts) + count + len(gains)),
        out_specs=tuple([vmem] * (count + len(gains))),
        compiler_params=pltpu.CompilerParams(vmem_limit_bytes=40 * 1024 * 1024),
        cost_estimate=cost(1e6, 30e6),
        name="home",
    )(*parts, *weights, *gains)


def body(
    tokens, block_of, clip_limit, norm_attn, w_query, w_key, w_value, w_out,
    norm_ffn, w_gate, w_up, w_down, cotangent,
):
    tok_rows, width = tokens.shape
    devices = lax.axis_size(AXIS)
    team = SEQ // tok_rows
    teams = devices // team
    head_total = width // HEAD_DIM
    heads = head_total // team
    head_cols = heads * HEAD_DIM
    ff_rows = w_down.shape[0]
    weight_rows = w_gate.shape[0]
    ff_cols = w_gate.shape[1] // team
    device = lax.axis_index(AXIS)
    mate = device % team
    bit_count = devices.bit_length() - 1
    attn_bits, ffn_bits = (1, 2, 4), (1, 2, 8)
    data_bits = [4] + [1 << k for k in range(4, bit_count)]
    in_team = [[g * team + b for b in range(team)] for g in range(teams)]
    across = [[g * team + b for g in range(teams)] for b in range(team)]
    ffn_team = [
        [g * 16 + z * 8 + y * 4 + c for z in range(2) for c in range(4)]
        for g in range(devices // 16)
        for y in range(2)
    ]

    def flip(x, bit):
        return lax.ppermute(x, AXIS, [(i, i ^ bit) for i in range(devices)])

    def gather_across(x):
        return lax.all_gather(x, AXIS, axis=0, tiled=True, axis_index_groups=across)

    def scatter_across(x):
        return lax.psum_scatter(
            x.astype(bf16), AXIS, scatter_dimension=0, tiled=True, axis_index_groups=across
        )

    def dim_of(bit):
        return bit_count - bit.bit_length()

    def data_pieces(x):
        pieces = {0: x}
        for bit in reversed(data_bits):
            for key in list(pieces):
                pieces[key | bit] = flip(pieces[key], bit)
        return pieces

    def place_pieces(pieces, dims, shape):
        total = jnp.zeros(shape, bf16)
        for key, piece in pieces.items():
            start = [0] * len(shape)
            size = list(shape)
            for bit in data_bits:
                start[dims[bit]] = ((device // bit) + (1 if key & bit else 0)) % 2
                size[dims[bit]] = 1
            total = lax.dynamic_update_slice(total, piece.reshape(size), start)
        return total

    def after_bit(dims, bit):
        return {b: d - (d > dims[bit]) for b, d in dims.items() if b != bit}

    def data_sum(x, dims, bits):
        for bit in bits:
            mine = (device // bit) % 2
            keep = lax.dynamic_index_in_dim(x, mine, dims[bit], False)
            sent = flip(lax.dynamic_index_in_dim(x, 1 - mine, dims[bit], False), bit)
            x = (keep.astype(f32) + sent.astype(f32)).astype(bf16)
            dims = after_bit(dims, bit)
        return x

    row_dims = {bit: dim_of(bit) for bit in data_bits}
    row_shape = (2,) * bit_count
    unit_dims = {bit: i for i, bit in enumerate(reversed(data_bits))}
    unit_shape = (2,) * len(data_bits)

    def tie(*values):
        return lax.optimization_barrier(values)

    qkv_moves = tuple(
        (i, b, (g * team + b) * HEAD_DIM, (3 * (g // 2) + i) * PAIR + (g % 2) * HEAD_DIM, HEAD_DIM)
        for i in range(3) for g in range(heads) for b in range(team)
    )
    ffn_units = tuple(
        (z * 4 + c, (2 * h + y) * ff_rows, (h * 16 + z * 8 + y * 4 + c) * ff_rows)
        for h in range(devices // 16) for z in range(2) for y in range(2) for c in range(4)
    )
    ffn_moves = tuple(
        (i, member, source, target, ff_rows)
        for i in range(2) for member, target, source in ffn_units
    )
    out_w = lax.all_gather(w_out, AXIS, axis=0, tiled=True)
    gain_row = jnp.concatenate([norm_attn, norm_ffn]).astype(f32)
    gain_row = jnp.pad(gain_row, (0, 128 - 2 * weight_rows)).reshape(1, 128)
    block_rows = block_of.astype(f32).reshape(tok_rows // 128, 128)
    small = jnp.concatenate([gain_row, block_rows, jnp.zeros((7 - tok_rows // 128, 128), f32)])
    ahead = data_bits == [4, 16]
    normed_attn, qkv_w, both_mine, gathered, *down_moved = front(
        tokens, (w_query, w_key, w_value, w_gate, w_up), small, teams, qkv_moves, ffn_moves,
        [w_down] if ahead else [], (4,) if ahead else (),
    )
    qkv_w = qkv_w.reshape(width, 3 * head_cols)
    gain_attn = gathered[:, 0, :weight_rows].reshape(1, width)
    gain_ffn = gathered[:, 0, weight_rows : 2 * weight_rows].reshape(1, width)
    blocks = lax.dynamic_slice_in_dim(gathered, device - mate, team, 0)
    blocks = blocks[:, 1 : 1 + tok_rows // 128].astype(jnp.int32).reshape(SEQ)
    row_blocks, col_blocks = blocks.reshape(1, SEQ), blocks.reshape(SEQ, 1)
    both_mine, qkv_w = tie(both_mine, qkv_w)

    def whole_rows(mine):
        shape = row_shape + (weight_rows, ff_cols)
        return place_pieces(data_pieces(mine), row_dims, shape).reshape(width, ff_cols)

    qkv = contract(normed_attn, qkv_w, 1, 0)
    cosine, sine = rope_tables(SEQ, PAIR)
    qkv, cot_mine = tie(qkv, cotangent)
    if data_bits == [4, 16]:
        carry = [both_mine, flip(both_mine, 4), flip(both_mine[: 4 * EARLY_HALVES], 16), w_down, *down_moved]
    else:
        carry = []
    query, key, value, attended, lse, peak = attend_forward(qkv, cosine, sine, row_blocks, col_blocks)
    peaks = jnp.where(
        (jnp.arange(head_total) % team) == mate, jnp.repeat(peak[0, :heads], team), -jnp.inf
    )
    peaks = jnp.broadcast_to(jnp.pad(peaks, (0, 128 - head_total))[None], (8, 128))
    if carry:
        carry[2], down_sent = tie(carry[2], w_down)
        over = flip(down_sent, 16)
    after_attn, normed_ffn, peaks, *full = branch(
        attended, out_w, tokens, gain_ffn, peaks, carry, attn_bits, ffn_bits, bit_count
    )
    head_peak = peaks[0, :head_total]
    if carry:
        normed_ffn, over = tie(normed_ffn, over)
    if carry:
        gate_w, up_w = (w.reshape(width, ff_cols) for w in full[:2])
        z_side, y_side = (device // 16) % 2, (device // 4) % 2
        full_down = lax.dynamic_update_slice(full[2], over[None], ((1 - z_side) * 2 + y_side, 0, 0))
        down_w = lax.dynamic_update_slice(
            full_down, flip(over, 4)[None], ((1 - z_side) * 2 + 1 - y_side, 0, 0)
        ).reshape(ff_cols, width)
    else:
        gate_w, up_w = whole_rows(both_mine[:team]), whole_rows(both_mine[team:])
        down_w = place_pieces(
            data_pieces(w_down), unit_dims, unit_shape + (ff_rows, width)
        ).reshape(ff_cols, width)
    gate_pre = contract(normed_ffn, gate_w, 1, 0)
    up_pre = contract(normed_ffn, up_w, 1, 0)
    sigmoid_gate = jax.nn.sigmoid(gate_pre)
    silu_gate = gate_pre * sigmoid_gate
    hidden = (silu_gate * up_pre).astype(bf16)

    team_cot = lax.all_gather(cot_mine, AXIS, axis=0, tiled=True, axis_index_groups=ffn_team)
    d_down = contract(hidden, team_cot, 0, 0).astype(bf16).reshape(unit_shape + (ff_rows, width))
    team_cot, d_down = tie(team_cot, d_down)
    d_hidden = contract(team_cot, down_w, 1, 1)
    grad_gate = (d_hidden * up_pre * sigmoid_gate * (1.0 + gate_pre * (1.0 - sigmoid_gate))).astype(bf16)
    grad_up = (d_hidden * silu_gate).astype(bf16)

    unit_rest, row_rest = after_bit(unit_dims, data_bits[0]), after_bit(row_dims, data_bits[0])
    row_values = (weight_rows, ff_cols)
    crosses = data_bits == [4, 16]
    if crosses:
        y_side = (device // 4) % 2
        kept = lax.dynamic_index_in_dim(d_down, y_side, unit_dims[4], False)
        sent = lax.dynamic_index_in_dim(d_down, 1 - y_side, unit_dims[4], False)
        ahead = flip(sent[0], 4)
        grad_gate, ahead = tie(grad_gate, ahead)
        beside = [sent[1]]
    else:
        beside = []
    d_residual, branch_mine, grad_attended, d_up, *d_gate = ffn_back(
        grad_gate, grad_up, gate_w, up_w, normed_ffn, out_w, after_attn, cotangent, gain_ffn, beside, 4 * weight_rows,
        ffn_bits, attn_bits,
    )
    if crosses:
        d_down = (kept.astype(f32) + jnp.stack([ahead, d_gate[2]]).astype(f32)).astype(bf16)
        d_gate = (d_gate[0].astype(f32) + d_gate[1].astype(f32)).astype(bf16)
        d_gate = d_gate.reshape((2,) * (bit_count - 1) + row_values)
    else:
        d_down = data_sum(d_down, unit_dims, data_bits[:1])
        d_gate = data_sum(d_gate[0].reshape(row_shape + row_values), row_dims, data_bits[:1])
    grad_attended, d_down, d_gate = tie(grad_attended, d_down, d_gate)
    d_gate = data_sum(d_gate, row_rest, data_bits[1:])
    branch_grad = lax.all_gather(branch_mine, AXIS, axis=0, tiled=True, axis_index_groups=in_team)

    def heads_back(pair):
        return attend_backward(
            pair, query, key, value, grad_attended, lse, cosine, sine, row_blocks, col_blocks, normed_attn
        )

    grad_pairs, shares = [None] * (heads // 2), [None] * (heads // 2)
    grad_pairs[0], share = heads_back(0)
    grad_attended, d_down, d_gate, d_up, share, branch_grad = tie(
        grad_attended, d_down, d_gate, d_up, share, branch_grad
    )
    shares[0] = scatter_across(share)
    d_down = data_sum(d_down, unit_rest, data_bits[1:]).astype(f32)
    d_up = data_sum(d_up.reshape(row_shape + row_values), row_dims, data_bits[:1])
    for p in range(1, heads // 2):
        grad_pairs[p], share = heads_back(p)
        grad_pairs[p], share, d_down, d_up, branch_grad = tie(grad_pairs[p], share, d_down, d_up, branch_grad)
        shares[p] = scatter_across(share)
    d_up = data_sum(d_up, row_rest, data_bits[1:])
    grad_pairs[0], shares[0] = tie(grad_pairs[0], shares[0])
    d_gate = d_gate.reshape(team, weight_rows, ff_cols)
    out_part = contract(attended, branch_grad, 0, 0)
    if weight_rows == HEAD_DIM:
        d_out = scatter_across(out_part).astype(f32)
    else:
        spread = jnp.where(
            (jnp.arange(team) == mate)[None, :, None, None],
            out_part.reshape(heads, 1, HEAD_DIM, width), 0.0,
        ).reshape(width, width)
        d_out = lax.psum_scatter(spread, AXIS, scatter_dimension=0, tiled=True)
    d_tokens, mixed, d_gate = last_sums(
        *grad_pairs, qkv_w, tokens, gain_attn, d_residual, hidden, down_w, after_attn, d_gate, attn_bits, ffn_bits
    )
    places = [[], [], []]
    for i, b, source, target, columns in qkv_moves:
        places[i].append((target // (3 * PAIR), b, target % (3 * PAIR), source, columns))
    places += [
        [(heads // 2 + i, member, target, source, ff_rows) for member, target, source in ffn_units] for i in range(2)
    ]
    shares = [share.reshape(team, weight_rows, 3 * PAIR) for share in shares]
    *shares, d_up = exchange(
        shares + [d_up.reshape(team, weight_rows, ff_cols)], (attn_bits,) * (heads // 2) + (ffn_bits,)
    )
    d_query, d_key, d_value, d_gate, d_up, d_norm_attn, d_norm_ffn = home(
        shares + [d_gate, d_up], (w_query, w_key, w_value, w_gate, w_up), (norm_attn, norm_ffn), (0, 0, 0, 1, 1),
        tuple(tuple(p) for p in places),
    )
    d_norm_attn, d_norm_ffn = d_norm_attn[0], d_norm_ffn[0]
    clip_value = clip_limit.astype(f32)
    factor = jnp.sqrt(clip_value / jnp.maximum(head_peak, clip_value))
    factors = jnp.repeat(factor, HEAD_DIM)[None, :]
    clipped_query = (w_query.astype(f32) * factors).astype(bf16)
    clipped_key = (w_key.astype(f32) * factors).astype(bf16)
    return (
        mixed, d_tokens, d_norm_attn, d_query, d_key, d_value, d_out, d_norm_ffn,
        d_gate, d_up, d_down, head_peak, clipped_query, clipped_key,
    )


def solution(mesh):
    rows, whole = P(AXIS, None), P(AXIS)
    return jax.shard_map(
        body,
        mesh=mesh,
        in_specs=(rows, whole, P(), whole, rows, rows, rows, rows, whole, rows, rows, rows, rows),
        out_specs=(
            rows, rows, whole, rows, rows, rows, rows, whole, rows, rows, rows, P(), rows, rows,
        ),
        check_vma=False,
    )
```

```python
import functools

import jax
import jax.numpy as jnp
import numpy as np
from jax import lax
from jax.experimental import pallas as pl
from jax.experimental.pallas import tpu as pltpu
from jax.sharding import PartitionSpec as P

HEAD_DIM = 64
SEQ = 2048
BLOCK = 256
HALF = 128
LAST_CUT = 0
EARLY_HALVES = 3
BRANCH_CUT = 128
AXIS = "fsdp"
MESH = pl.DeviceIdType.MESH

epsilon = 1e-05
rope_base = 130000.0
bf16 = jnp.bfloat16
f32 = jnp.float32
vmem = pl.BlockSpec(memory_space=pltpu.VMEM)
anywhere = pl.BlockSpec(memory_space=pl.ANY)


def contract(left, right, left_dim, right_dim):
    return lax.dot_general(
        left, right, (((left_dim,), (right_dim,)), ((), ())), preferred_element_type=f32
    )


def rope_tables(length, width):
    half_dim = HEAD_DIM // 2
    inverse = rope_base ** (-np.arange(half_dim) * 2.0 / HEAD_DIM)
    angles = (np.arange(length, dtype=np.float32)[:, None] * inverse.astype(np.float32)).astype(np.float64)
    cosine, sine = np.cos(angles).astype(np.float32), np.sin(angles).astype(np.float32)
    repeats = width // HEAD_DIM
    return (
        jnp.asarray(np.tile(np.concatenate([cosine, cosine], 1), (1, repeats))),
        jnp.asarray(np.tile(np.concatenate([-sine, sine], 1), (1, repeats))),
    )


def swap_halves(rows):
    width = rows.shape[1]
    half = HEAD_DIM // 2
    lane = lax.broadcasted_iota(jnp.int32, rows.shape, 1)
    return jnp.where(
        lane % HEAD_DIM < half, pltpu.roll(rows, width - half, 1), pltpu.roll(rows, half, 1)
    )


PAIR = 2 * HEAD_DIM


def head_mask(shape, head):
    lane = lax.broadcasted_iota(jnp.int32, shape, 1)
    return (lane >= head * HEAD_DIM) & (lane < (head + 1) * HEAD_DIM)


def masked_scores(query, key_ref, row_ref, col_ref, q0, cols):
    tail = min(2 * BLOCK, cols)
    scores = contract(query, key_ref[0:cols, :], 1, 1)
    shown = row_ref[:, pl.ds(cols - tail, tail)] <= col_ref[pl.ds(q0, BLOCK), :]
    hidden = jnp.where(shown, scores[:, cols - tail :], -jnp.inf)
    return jnp.concatenate([scores[:, : cols - tail], hidden], 1) if tail < cols else hidden


def attend_forward_kernel(
    qkv_ref, cos_ref, sin_ref, row_ref, col_ref, q_ref, k_ref, v_ref, out_ref, lse_ref, peak_ref
):
    pairs, length, _ = q_ref.shape
    for t in range(length // BLOCK):
        rows = pl.ds(t * BLOCK, BLOCK)
        cosine, sine = cos_ref[rows, :], sin_ref[rows, :]
        for pair in range(pairs):
            first = 3 * pair * PAIR
            query = qkv_ref[rows, first : first + PAIR]
            query = (query * cosine + swap_halves(query) * sine).astype(bf16)
            q_ref[pair, rows, :] = (query.astype(f32) * HEAD_DIM ** (-0.5)).astype(bf16)
            key = qkv_ref[rows, first + PAIR : first + 2 * PAIR]
            k_ref[pair, rows, :] = (key * cosine + swap_halves(key) * sine).astype(bf16)
            v_ref[pair, rows, :] = qkv_ref[rows, first + 2 * PAIR : first + 3 * PAIR].astype(bf16)
    peak_ref[...] = jnp.full(peak_ref.shape, -jnp.inf, f32)
    lane = lax.broadcasted_iota(jnp.int32, (BLOCK, 128), 1)
    for t in range(length // BLOCK):
        q0 = t * BLOCK
        rows = pl.ds(q0, BLOCK)
        cols = min(q0 + 2 * BLOCK, length)

        @pl.loop(0, pairs)
        def _(pair):
            total = jnp.zeros((BLOCK, PAIR), f32)
            for sub in range(2):
                head = 2 * pair + sub
                mask = head_mask((BLOCK, PAIR), sub)
                query = jnp.where(mask, q_ref[pair, rows, :], 0).astype(bf16)
                scores = masked_scores(query, k_ref.at[pair], row_ref, col_ref, q0, cols)
                row_max = jnp.max(scores, 1, keepdims=True)
                numerators = jnp.exp(scores - row_max)
                totals = jnp.sum(numerators, 1, keepdims=True)
                mixed = contract(numerators.astype(bf16), v_ref[pair, 0:cols, :], 1, 0) / totals
                total = jnp.where(mask, mixed, total)
                lse_ref[rows, :] = jnp.where(lane == head, row_max + jnp.log(totals), lse_ref[rows, :])
                peak_ref[...] = jnp.where(
                    lax.broadcasted_iota(jnp.int32, peak_ref.shape, 1) == head,
                    jnp.maximum(peak_ref[...], jnp.max(row_max)),
                    peak_ref[...],
                )
            out_ref[rows, pl.ds(pl.multiple_of(pair * PAIR, PAIR), PAIR)] = total.astype(bf16)


def attend_forward(qkv, cosine, sine, row_blocks, col_blocks):
    length = qkv.shape[0]
    pairs = qkv.shape[1] // (3 * PAIR)
    shape = jax.ShapeDtypeStruct
    return pl.pallas_call(
        attend_forward_kernel,
        out_shape=(
            shape((pairs, length, PAIR), bf16),
            shape((pairs, length, PAIR), bf16),
            shape((pairs, length, PAIR), bf16),
            shape((length, pairs * PAIR), bf16),
            shape((length, 128), f32),
            shape((8, 128), f32),
        ),
        in_specs=[vmem] * 5,
        out_specs=tuple([vmem] * 6),
        compiler_params=pltpu.CompilerParams(vmem_limit_bytes=56 * 1024 * 1024),
        cost_estimate=pl.CostEstimate(
            flops=16 * pairs * length * length * PAIR, bytes_accessed=length * PAIR * pairs * 24,
            transcendentals=2 * pairs * length * length,
        ),
        name="attend_forward",
    )(qkv, cosine, sine, row_blocks, col_blocks)


def attend_backward_kernel(
    first_head, q_ref, k_ref, v_ref, grad_ref, lse_ref, cos_ref, sin_ref, row_ref, col_ref, normed_ref,
    out_ref, weight_ref, dk_ref, dv_ref,
):
    length = q_ref.shape[0]
    dk_ref[...] = jnp.zeros_like(dk_ref)
    dv_ref[...] = jnp.zeros_like(dv_ref)
    lane = lax.broadcasted_iota(jnp.int32, (BLOCK, 128), 1)
    for t in range(length // BLOCK):
        q0 = t * BLOCK
        rows = pl.ds(q0, BLOCK)
        cols = min(q0 + 2 * BLOCK, length)

        def one_head(sub, dq):
            mask = head_mask((BLOCK, PAIR), sub)
            query = jnp.where(mask, q_ref[rows, :], 0).astype(bf16)
            grad = jnp.where(mask, grad_ref[rows, :], 0).astype(bf16)
            lse = jnp.sum(
                jnp.where(lane == first_head + sub, lse_ref[rows, :], 0.0), 1, keepdims=True
            )
            scores = masked_scores(query, k_ref, row_ref, col_ref, q0, cols)
            attention = jnp.exp(scores - lse)
            grad_attention = contract(grad, v_ref[0:cols, :], 1, 1)
            weighted = attention * grad_attention
            centre = jnp.sum(weighted, 1, keepdims=True)
            grad_scores = (weighted - attention * centre).astype(bf16)
            dv_ref[0:cols, :] += contract(attention.astype(bf16), grad, 0, 0)
            dk_ref[0:cols, :] += contract(grad_scores, query, 0, 0)
            return jnp.where(mask, contract(grad_scores, k_ref[0:cols, :], 1, 0), dq)

        dq = lax.fori_loop(0, 2, one_head, jnp.zeros((BLOCK, PAIR), f32)) * HEAD_DIM ** (-0.5)
        out_ref[rows, 0:PAIR] = (dq * cos_ref[rows, :] - swap_halves(dq) * sin_ref[rows, :]).astype(bf16)
    for t in range(length // BLOCK):
        rows = pl.ds(t * BLOCK, BLOCK)
        dk = dk_ref[rows, :]
        out_ref[rows, PAIR : 2 * PAIR] = (
            dk * cos_ref[rows, :] - swap_halves(dk) * sin_ref[rows, :]
        ).astype(bf16)
        out_ref[rows, 2 * PAIR : 3 * PAIR] = dv_ref[rows, :].astype(bf16)
    side = 256

    @pl.loop(0, normed_ref.shape[1] // side)
    def _(k):
        span = pl.ds(pl.multiple_of(k * side, side), side)
        weight_ref[span, :] = contract(normed_ref[:, span], out_ref[...], 0, 0).astype(bf16)


def attend_backward(pair, query, key, value, grad, lse, cosine, sine, row_blocks, col_blocks, normed):
    length, width = normed.shape
    heads = pl.BlockSpec((None, length, PAIR), lambda _: (pair, 0, 0))
    return pl.pallas_call(
        functools.partial(attend_backward_kernel, 2 * pair),
        grid=(1,),
        out_shape=(
            jax.ShapeDtypeStruct((length, 3 * PAIR), bf16), jax.ShapeDtypeStruct((width, 3 * PAIR), bf16),
        ),
        in_specs=[heads] * 3 + [pl.BlockSpec((length, PAIR), lambda _: (0, pair))] + [vmem] * 6,
        out_specs=(vmem, vmem),
        scratch_shapes=[pltpu.VMEM((length, PAIR), f32), pltpu.VMEM((length, PAIR), f32)],
        compiler_params=pltpu.CompilerParams(vmem_limit_bytes=56 * 1024 * 1024),
        cost_estimate=pl.CostEstimate(
            flops=40 * length * length * PAIR + 6 * length * width * PAIR, bytes_accessed=100_000_000,
            transcendentals=2 * length * length,
        ),
        name="attend_backward",
    )(query, key, value, grad, lse, cosine, sine, row_blocks, col_blocks, normed)


def bit_of(index, bit):
    return lax.rem(lax.div(index, bit), 2)


def flip_bit(index, bit):
    return index + bit - 2 * bit * bit_of(index, bit)


def team_mate(me, bits, offset):
    device, place = me, 0
    for k, bit in enumerate(bits):
        moved = (offset >> k) % 2
        place = place + lax.rem(bit_of(me, bit) + moved, 2) * (1 << k)
        device = flip_bit(device, bit) if moved else device
    return device, place


class Links:

    def __init__(self, send_sems, recv_sems):
        self.send_sems, self.recv_sems = send_sems, recv_sems

    def copy(self, slot, src, dst, device):
        return pltpu.make_async_remote_copy(
            src_ref=src, dst_ref=dst, send_sem=self.send_sems.at[slot],
            recv_sem=self.recv_sems.at[slot], device_id=(device,), device_id_type=MESH,
        )


def greet(partners):
    barrier = pltpu.get_barrier_semaphore()
    for partner in partners:
        pl.semaphore_signal(barrier, inc=1, device_id=(partner,), device_id_type=MESH)
    pl.semaphore_wait(barrier, len(partners))


def spread_block(bits, cut, own_ref, out_ref, links, local_sem):
    core, first, second = bits
    me = lax.axis_index(AXIS)
    sibling, next_a, next_b = (flip_bit(me, bit) for bit in bits)
    block = own_ref.shape[0]
    in_a, in_b = bit_of(me, first), bit_of(me, second)
    spans = {None: (0, block), 0: (0, cut), 1: (cut, block - cut)}

    def rows(flip_a, flip_b, part):
        place = bit_of(me, core)
        place = place + 2 * lax.rem(in_a + flip_a, 2) + 4 * lax.rem(in_b + flip_b, 2)
        start, size = spans[part]
        return pl.ds(pl.multiple_of(place * block + start, 16), size)

    def passed(slot, where, device):
        return links.copy(slot, out_ref.at[where], out_ref.at[where], device)

    def first_hand(slot, part, device):
        start, size = spans[part]
        return links.copy(slot, own_ref.at[pl.ds(start, size)], out_ref.at[rows(0, 0, part)], device)

    makers = {
        0: lambda: first_hand(0, 0, next_a),
        1: lambda: first_hand(1, 1, next_b),
        2: lambda: first_hand(2, 1, next_a),
        3: lambda: first_hand(3, 0, next_b),
        4: lambda: links.copy(4, own_ref, out_ref.at[rows(0, 0, None)], sibling),
        5: lambda: passed(5, rows(1, 0, 0), next_b),
        6: lambda: passed(6, rows(1, 0, 0), sibling),
        7: lambda: passed(7, rows(0, 1, 1), next_a),
        8: lambda: passed(8, rows(0, 1, 1), sibling),
        9: lambda: passed(9, rows(1, 0, 1), sibling),
        10: lambda: passed(10, rows(0, 1, 0), sibling),
        11: lambda: passed(11, rows(1, 1, 0), sibling),
        12: lambda: passed(12, rows(1, 1, 1), sibling),
    }
    needs = {0: 0, 1: 1, 2: 1, 3: 0, 4: None, 5: 0, 6: 0, 7: 1, 8: 1, 9: 1, 10: 0, 11: 0, 12: 1}
    copies = {slot: make() for slot, make in makers.items() if spans[needs[slot]][1]}
    keep = pltpu.make_async_copy(own_ref, out_ref.at[rows(0, 0, None)], local_sem)

    def begin():
        for slot in range(5):
            if slot in copies:
                copies[slot].start()
        keep.start()

    def hand_on(arrived, *sent):
        def phase():
            if arrived in copies:
                copies[arrived].wait_recv()
                for slot in sent:
                    copies[slot].start()

        return phase

    def finish():
        for slot in (4, 6, 8, 9, 10, 11, 12):
            if slot in copies:
                copies[slot].wait_recv()
        keep.wait()
        for slot in copies:
            copies[slot].wait_send()

    return [
        begin, hand_on(0, 5, 6), hand_on(1, 7, 8), hand_on(2, 9), hand_on(3, 10),
        hand_on(5, 11), hand_on(7, 12), finish,
    ]


def run(phases):
    for phase in phases:
        phase()


SPREAD_COPIES = 13
SUM_COPIES = 10


def sum_block(bits, cut, swapped, product, total, to_core, from_core, chip_sum, arrived, links):
    core = bits[0]
    (first, weight_a), (second, weight_b) = ((bits[2], 4), (bits[1], 2)) if swapped else ((bits[1], 2), (bits[2], 4))
    me = lax.axis_index(AXIS)
    sibling, next_a, next_b = flip_bit(me, core), flip_bit(me, first), flip_bit(me, second)
    block, width = total.shape
    tile = 512

    def place(step, other_core):
        flip_a, flip_b = 1 - step // 2, 1 - step % 2
        return (
            lax.rem(bit_of(me, core) + other_core, 2)
            + weight_a * lax.rem(bit_of(me, first) + flip_a, 2)
            + weight_b * lax.rem(bit_of(me, second) + flip_b, 2)
        )

    low, high = (0, cut), (cut, block - cut)
    landing = range(6) if cut else {1: 0, 3: 1, 4: 2}

    def link(slot, step, span, device):
        return links.copy(slot, chip_sum.at[step, pl.ds(*span)], arrived.at[landing[slot - 4], pl.ds(0, span[1])], device)

    diag_a, diag_b = (link(4, 0, low, next_a) if cut else None), link(5, 0, high, next_b)
    plain_a, plain_b = (link(6, 1, low, next_a) if cut else None), link(7, 2, high, next_b)
    last_a, last_b = link(8, 1, high, next_a), (link(9, 2, low, next_b) if cut else None)

    def core_copy(step):
        return links.copy(step, to_core.at[step], from_core.at[step], sibling)

    def for_sibling():
        @pl.loop(0, 4)
        def _(step):
            @pl.loop(0, width // tile)
            def _(column):
                columns = pl.ds(pl.multiple_of(column * tile, tile), tile)
                to_core[step, :, columns] = product(place(step, 1), columns).astype(bf16)

            core_copy(step).start()

    def for_chip():
        @pl.loop(0, 4)
        def _(step):
            core_copy(step).wait_recv()

            @pl.loop(0, width // tile)
            def _(column):
                columns = pl.ds(pl.multiple_of(column * tile, tile), tile)
                summed = product(place(step, 0), columns) + from_core[step, :, columns].astype(f32)
                total[:, columns] = summed

                @pl.when(step < 3)
                def _():
                    chip_sum[step, :, columns] = summed.astype(bf16)

            @pl.when(step == 0)
            def _():
                if cut:
                    diag_a.start()
                diag_b.start()

            @pl.when(step == 1)
            def _():
                if cut:
                    plain_a.start()

            @pl.when(step == 2)
            def _():
                plain_b.start()

    def add(step, span, slot):
        rows = pl.ds(*span)
        chip_sum[step, rows, :] = (
            chip_sum[step, rows, :].astype(f32) + arrived[landing[slot], 0 : span[1], :].astype(f32)
        ).astype(bf16)

    def take(span, slot):
        total[pl.ds(*span), :] += arrived[landing[slot], 0 : span[1], :].astype(f32)

    def hand_on():
        if cut:
            diag_a.wait_recv()
            add(2, low, 0)
            last_b.start()
        diag_b.wait_recv()
        add(1, high, 1)
        last_a.start()

    def finish():
        if cut:
            plain_a.wait_recv()
            take(low, 2)
        plain_b.wait_recv()
        take(high, 3)
        if cut:
            last_b.wait_recv()
            take(low, 5)
        last_a.wait_recv()
        take(high, 4)

        @pl.loop(0, 4)
        def _(step):
            core_copy(step).wait_send()

        for copy in (diag_a, diag_b, plain_a, plain_b, last_a, last_b):
            if copy is not None:
                copy.wait_send()

    return for_sibling, for_chip, hand_on, finish


def sum_scratch(block, width, cut):
    return [
        pltpu.VMEM((block, width), f32),
        pltpu.VMEM((4, block, width), bf16),
        pltpu.VMEM((4, block, width), bf16),
        pltpu.VMEM((3, block, width), bf16),
        pltpu.VMEM((6 if cut else 3, block - cut, width), bf16),
        pltpu.SemaphoreType.DMA((SUM_COPIES,)),
        pltpu.SemaphoreType.DMA((SUM_COPIES,)),
    ]


def spread_scratch(block, width):
    return [
        pltpu.VMEM((block, width), bf16),
        pltpu.SemaphoreType.DMA((SPREAD_COPIES,)),
        pltpu.SemaphoreType.DMA((SPREAD_COPIES,)),
        pltpu.SemaphoreType.DMA,
    ]


def link_params(collective_id):
    return pltpu.CompilerParams(
        collective_id=collective_id, has_side_effects=True, vmem_limit_bytes=60 * 1024 * 1024
    )


def cost(flops, size):
    return pl.CostEstimate(flops=int(flops), bytes_accessed=int(size), transcendentals=0)


def row_scale(values):
    return lax.rsqrt(jnp.mean(values * values, -1, keepdims=True) + epsilon)


def front_kernel(
    team, teams, qkv_moves, ffn_moves, carry_bits, tokens_ref, query_ref, key_ref, value_ref, gate_ref, up_ref, small_ref, *refs,
):
    moved = len(carry_bits)
    (carried, refs) = (refs[0], refs[1:]) if moved else (None, refs)
    (normed_out, weights_out, both_out, small_out), refs = refs[:4], refs[4:]
    carried_out, refs = refs[:moved], refs[moved:]
    (tokens_all, mine, both_mine, gain,
    send_sems, recv_sems, local_sem, swap_send, swap_recv, swap_local, line_send, line_recv, small_send, small_recv,
    both_send, both_recv, both_local, out_sems, *carry_sems) = refs
    me = lax.axis_index(AXIS)
    mate, group = lax.rem(me, team), lax.div(me, team)
    devices = team * teams
    mates = [group * team + lax.rem(mate + k, team) for k in range(1, team)]
    above, below = lax.rem(me + team, devices), lax.rem(me + devices - team, devices)
    ffn_mates = [team_mate(me, (1, 2, 8), k) for k in range(team)]
    rows = mine.shape[1]
    swaps, line, small = Links(swap_send, swap_recv), Links(line_send, line_recv), Links(small_send, small_recv)
    both = Links(both_send, both_recv)
    for i, member, source, target, columns in qkv_moves:
        weight = (query_ref, key_ref, value_ref)[i]
        mine[member, :, target : target + columns] = weight[:, source : source + columns]
    greet(
        mates + [lax.rem(me + k * team, devices) for k in range(1, teams)]
        + [device for device, _ in ffn_mates[4:]]
    )

    def share(place):
        return pl.ds(pl.multiple_of(place * rows, rows), rows)

    swap_copies = [
        swaps.copy(k, mine.at[lax.rem(mate + k + 1, team)], weights_out.at[group, share(mate)], mates[k])
        for k in range(team - 1)
    ]
    crossing = [
        Links(*carry_sems).copy(i, carried, carried_out[i], flip_bit(me, bit)) for i, bit in enumerate(carry_bits)
    ]
    for copy in swap_copies:
        copy.start()
    keep = pltpu.make_async_copy(mine.at[mate], weights_out.at[group, share(mate)], swap_local)
    keep.start()
    small_out[me] = small_ref[...]

    others = [lax.rem(me + k * team, devices) for k in range(1, teams)]
    team_rows = pl.ds(pl.multiple_of(group * team, team), team)
    small_near = [
        small.copy(k, small_out.at[me], small_out.at[me], device) for k, device in enumerate(mates)
    ]
    small_far = [
        small.copy(team + k, small_out.at[team_rows], small_out.at[team_rows], device)
        for k, device in enumerate(others)
    ]
    for copy in small_near:
        copy.start()
    spread = spread_block(
        (1, 2, 4), HALF, tokens_ref, tokens_all, Links(send_sems, recv_sems), local_sem
    )
    for i, member, source, target, columns in ffn_moves:
        both_mine[i * team + member, :, target : target + columns] = (gate_ref, up_ref)[i][:, source : source + columns]

    def passed(slot, shard, device):
        return line.copy(slot, weights_out.at[shard], weights_out.at[shard], device)

    steps = teams - 1

    def up(step):
        return passed(step - 1, group - (step - 1), above)

    def down(step):
        return passed(steps + step - 1, group + (step - 1), below)

    def line_start(step):
        pl.when((group < teams - 1) & (group >= step - 1))(lambda: up(step).start())
        pl.when((group > 0) & (group + step - 1 < teams))(lambda: down(step).start())

    def line_wait(step):
        pl.when(group >= step)(lambda: up(step).wait_recv())
        pl.when(group + step < teams)(lambda: down(step).wait_recv())

    def line_sent(step):
        pl.when((group < teams - 1) & (group >= step - 1))(lambda: up(step).wait_send())
        pl.when((group > 0) & (group + step - 1 < teams))(lambda: down(step).wait_send())

    for copy in small_near:
        copy.wait_recv()
    for copy in small_far:
        copy.start()
    own_place = ffn_mates[0][1]
    both_copies = [
        both.copy(
            i * team + k, both_mine.at[i * team + ffn_mates[k][1]], both_out.at[i * team + own_place], ffn_mates[k][0]
        )
        for i in range(2) for k in range(1, team)
    ]
    for copy in both_copies:
        copy.start()
    both_keep = [
        pltpu.make_async_copy(both_mine.at[i * team + own_place], both_out.at[i * team + own_place], both_local.at[i])
        for i in range(2)
    ]
    for copy in both_keep:
        copy.start()
    for copy in swap_copies:
        copy.wait_recv()
    keep.wait()
    line_start(1)
    spread[0]()
    for copy in crossing:
        copy.start()
    for copy in small_far:
        copy.wait_recv()
    spread[1]()
    spread[2]()
    line_wait(1)
    line_start(2)
    spread[3]()
    spread[4]()
    width = tokens_all.shape[1]
    gains = width // devices
    for d in range(devices):
        gain[:, d * gains : (d + 1) * gains] = small_out[d, 0:1, 0:gains]
    for phase in spread[5:]:
        phase()
    block = tokens_ref.shape[0]

    def normed_copy(k):
        span = pl.ds(pl.multiple_of(k * block, block), block)
        return pltpu.make_async_copy(tokens_all.at[span], normed_out.at[span], out_sems.at[k])

    def norm_blocks(first, last):
        @pl.loop(first, last)
        def _(k):
            span = pl.ds(pl.multiple_of(k * block, block), block)
            values = tokens_all[span, :].astype(f32)
            tokens_all[span, :] = (values * row_scale(values) * gain[...]).astype(bf16)
            normed_copy(k).start()

    norm_blocks(0, 2)
    for step in range(2, teams):
        line_wait(step)
        if step < steps:
            line_start(step + 1)
        if step == 2:
            norm_blocks(2, team)
    for k in range(team):
        normed_copy(k).wait()
    for copy in both_copies:
        copy.wait_recv()
    for copy in both_keep:
        copy.wait()
    for copy in swap_copies + both_copies:
        copy.wait_send()
    for step in range(1, teams):
        line_sent(step)
    for copy in small_near + small_far:
        copy.wait_send()
    for copy in crossing:
        copy.wait()


def front(tokens, weights, small, teams, qkv_moves, ffn_moves, carried, carry_bits):
    block, width = tokens.shape
    team = 8
    rows, cols = weights[0].shape[0], 3 * width // team
    both_cols = weights[3].shape[1] // team
    devices = team * teams
    dma = pltpu.SemaphoreType.DMA
    shape = jax.ShapeDtypeStruct
    return pl.pallas_call(
        functools.partial(front_kernel, team, teams, qkv_moves, ffn_moves, carry_bits),
        out_shape=(
            shape((team * block, width), bf16),
            shape((teams, team * rows, cols), bf16),
            shape((2 * team, rows, both_cols), bf16),
            shape((devices,) + small.shape, f32),
        ) + tuple(shape(carried[0].shape, bf16) for _ in carry_bits),
        in_specs=[vmem] * 7 + [anywhere] * len(carried),
        out_specs=(anywhere, anywhere, anywhere, vmem) + (anywhere,) * len(carry_bits),
        scratch_shapes=[
            pltpu.VMEM((team * block, width), bf16), pltpu.VMEM((team, rows, cols), bf16),
            pltpu.VMEM((2 * team, rows, both_cols), bf16), pltpu.VMEM((1, width), f32),
        ]
        + spread_scratch(block, width)[1:]
        + [dma((team - 1,)), dma((team - 1,)), dma, dma((2 * teams,)), dma((2 * teams,)), dma((team + teams,)), dma((team + teams,))]
        + [dma((2 * team,)), dma((2 * team,)), dma((2,)), dma((team,))]
        + [dma((1,))] * (2 * len(carried)),
        compiler_params=link_params(1),
        cost_estimate=cost(0, 200e6),
        name="front",
    )(tokens, *weights, small, *carried)


def branch_kernel(
    carry, swap_bits, spread_bits, left_ref, right_ref, residual_ref, gain_ref, peak_ref, *refs,
):
    if carry:
        (both_own, both_y, both_z, down_own, down_y), refs = refs[:5], refs[5:]
        (h2_ref, out_ref, peak_out, gate_full, up_full, down_full), refs = refs[:6], refs[6:]
        (landed, together, swap_send, swap_recv, own, send_sems, recv_sems, local_sem,
         peak_in, peak_send, peak_recv, carry_send, carry_recv, carry_local) = refs
    else:
        (h2_ref, out_ref, peak_out), refs = refs[:3], refs[3:]
        (landed, together, swap_send, swap_recv, own, send_sems, recv_sems, local_sem,
         peak_in, peak_send, peak_recv) = refs
    me = lax.axis_index(AXIS)
    team, block, _ = landed.shape
    bits = [1 << k for k in range(peak_in.shape[0])]
    mates = [team_mate(me, swap_bits, k) for k in range(team)]
    greet([device for device, _ in mates[1:]] + [flip_bit(me, bit) for bit in bits if bit not in swap_bits])
    own_place = mates[0][1]

    def rows_at(place):
        return pl.ds(pl.multiple_of(place * block, block), block)

    swap_copies = [
        Links(swap_send, swap_recv).copy(k, left_ref.at[rows_at(mates[k][1])], landed.at[own_place], mates[k][0])
        for k in range(1, team)
    ]
    for copy in swap_copies:
        copy.start()
    peaks = Links(peak_send, peak_recv)

    def peak_copy(k):
        return peaks.copy(k, peak_out, peak_in.at[k], flip_bit(me, bits[k]))

    def peak_step(k):
        if k:
            peak_copy(k - 1).wait()
            peak_out[...] = jnp.maximum(peak_out[...], peak_in[k - 1])
        if k < len(bits):
            peak_copy(k).start()

    if carry:
        carried = Links(carry_send, carry_recv)
        high, middle = bit_of(me, 16), bit_of(me, 4)
        by_y, by_z = flip_bit(me, 4), flip_bit(me, 16)

        def rows_of(part, flip_z, flip_y):
            z, y = lax.rem(high + flip_z, 2), lax.rem(middle + flip_y, 2)
            return pl.ds(pl.multiple_of(z * 16 + part * 8 + y * 4, 4), 4)

        early = both_z.shape[0] // 4

        def piece(source, half):
            return source.at[pl.ds(half * 4, 4)]

        def placed(half, flips):
            return (gate_full, up_full)[half // 2].at[rows_of(half % 2, *flips)]

        def unit(flip_z, flip_y):
            return lax.rem(high + flip_z, 2) * 2 + lax.rem(middle + flip_y, 2)

        kept = []
        for source, flips, halves in ((both_own, (0, 0), 4), (both_y, (0, 1), 4), (both_z, (1, 0), early)):
            for half in range(halves):
                kept.append((piece(source, half), placed(half, flips)))
        kept.append((down_own, down_full.at[unit(0, 0)]))
        kept.append((down_y, down_full.at[unit(0, 1)]))
        kept = [pltpu.make_async_copy(a, b, carry_local.at[i]) for i, (a, b) in enumerate(kept)]
        up_z = [
            carried.copy(half, piece(both_own, half), placed(half, (0, 0)), by_z) for half in range(early, 4)
        ]
        early_yz = [
            carried.copy(4 + half, piece(both_z, half), placed(half, (1, 0)), by_y) for half in range(early)
        ]
        up_yz = [
            carried.copy(4 + half, placed(half, (1, 0)), placed(half, (1, 0)), by_y) for half in range(early, 4)
        ]
        for copy in up_z + kept:
            copy.start()

    peak_out[...] = peak_ref[...]
    peak_step(0)
    landed[own_place] = left_ref[rows_at(own_place), :]
    for copy in swap_copies:
        copy.wait_recv()
    if carry:
        for copy in early_yz:
            copy.start()
    heads = landed.shape[2] // HEAD_DIM
    for b in range(team):
        for g in range(heads):
            first = (g * team + b) * HEAD_DIM
            together[:, first : first + HEAD_DIM] = landed[b, :, g * HEAD_DIM : (g + 1) * HEAD_DIM]
    tile = 512

    @pl.loop(0, own.shape[1] // tile)
    def _(column):
        columns = pl.ds(pl.multiple_of(column * tile, tile), tile)
        h2_ref[:, columns] = residual_ref[:, columns].astype(f32) + contract(
            together[...], right_ref[:, columns], 1, 0
        )

    h2 = h2_ref[...]
    own[...] = (h2 * row_scale(h2) * gain_ref[...]).astype(bf16)
    spread = spread_block(spread_bits, BRANCH_CUT, own, out_ref, Links(send_sems, recv_sems), local_sem)
    spread[0]()
    if carry:
        for over, on in zip(up_z, up_yz):
            over.wait_recv()
            on.start()
    for k, phase in enumerate(spread[1:-1]):
        phase()
        if k < len(bits):
            peak_step(k + 1)
    for k in range(len(spread) - 2, len(bits)):
        peak_step(k + 1)
    spread[-1]()
    for copy in swap_copies:
        copy.wait_send()
    if carry:
        for copy in kept:
            copy.wait()
        for copy in early_yz + up_yz:
            copy.wait_recv()
        for copy in up_z + early_yz + up_yz:
            copy.wait_send()


def branch(left, right, residual, gain, peak, carry, swap_bits, spread_bits, bit_count):
    block, width = residual.shape
    dma = pltpu.SemaphoreType.DMA
    shape = jax.ShapeDtypeStruct
    out_shape = [shape((block, width), f32), shape((8 * block, width), bf16), shape((8, 128), f32)]
    scratch = [pltpu.VMEM((8, block, left.shape[1]), bf16), pltpu.VMEM((block, width), bf16), dma((8,)), dma((8,))]
    scratch += spread_scratch(block, width)
    scratch += [pltpu.VMEM((bit_count, 8, 128), f32), dma((bit_count,)), dma((bit_count,))]
    if carry:
        out_shape += [
            shape((32,) + carry[0].shape[1:], bf16), shape((32,) + carry[0].shape[1:], bf16),
            shape((4,) + carry[3].shape, bf16),
        ]
        scratch += [dma((8,)), dma((8,)), dma((14,))]
    return pl.pallas_call(
        functools.partial(branch_kernel, bool(carry), swap_bits, spread_bits),
        out_shape=tuple(out_shape),
        in_specs=[vmem] * (5 + len(carry)),
        out_specs=tuple([vmem, anywhere, vmem] + [anywhere] * (len(out_shape) - 3)),
        scratch_shapes=scratch,
        compiler_params=link_params(2),
        cost_estimate=cost(16 * block * left.shape[1] * width, 300e6),
        name="attention_branch",
    )(left, right, residual, gain, peak, *carry)


def norm_back(values, gain, upstream):
    scaled = upstream * gain
    scale = row_scale(values)
    inner = jnp.mean(scaled * values, -1, keepdims=True)
    return scale * scaled - scale * scale * scale * values * inner


def ffn_back_kernel(
    cross, sum_bits, swap_bits, gate_ref, up_ref, gate_w_ref, up_w_ref, normed_ref, out_w_ref, h2_ref, cot_ref, gain_ref, *refs,
):
    (part_ref, over_ref, refs) = (refs[0], refs[1], refs[2:]) if cross else (None, None, refs)
    (residual_ref, branch_ref, heads_out, d_up_out, d_gate_own), refs = refs[:5], refs[5:]
    (d_gate_in, part_in, over_in), refs = (refs[:3], refs[3:]) if cross else ((None,) * 3, refs)
    (total, to_core, from_core, chip_sum, arrived, sum_send, sum_recv,
     swap_send, swap_recv, local_sem, stage, stage_sems, own_sems, *more) = refs
    if cross:
        cross_send, cross_recv = more
        crossing = Links(cross_send, cross_recv)
    else:
        (stage_gate,) = more
    me = lax.axis_index(AXIS)
    block, width = total.shape
    team = 1 << len(swap_bits)
    mates = [team_mate(me, swap_bits, k) for k in range(team)]
    greet(
        [device for device, _ in mates[1:]] + [flip_bit(me, bit) for bit in sum_bits if bit not in swap_bits]
        + ([flip_bit(me, 16)] if cross else [])
    )

    def product(place, columns):
        rows = pl.ds(pl.multiple_of(place * block, block), block)
        return contract(gate_ref[rows, :], gate_w_ref[columns, :], 1, 1) + contract(
            up_ref[rows, :], up_w_ref[columns, :], 1, 1
        )

    side, columns_ff = stage.shape[1:]
    count = width // side
    y_side, by_y = bit_of(me, 4), flip_bit(me, 4)
    if cross:
        part_copy = crossing.copy(count // 2, part_ref, part_in, by_y)
        over_copy = crossing.copy(count // 2 + 1, over_ref, over_in, flip_bit(me, 16))
        part_copy.start()

    def parked(i, part):
        row = i * side
        rows = pl.ds(pl.multiple_of(lax.rem(row, block), 16), side)
        return from_core.at[lax.div(row, block), rows, pl.ds(part * columns_ff, columns_ff)]

    def cross_copy(i):
        return crossing.copy(i, parked(i, 0), d_gate_in.at[i], by_y)

    def own_copy(i):
        return pltpu.make_async_copy(parked(i, 1), d_gate_own.at[i], own_sems.at[i])

    def tile_of(step):
        if not cross:
            return step
        theirs = step < count // 2
        return jnp.where(theirs, 2 * step + 1 - y_side, 2 * step - count + y_side)

    def up_copy(step):
        span = pl.ds(pl.multiple_of(tile_of(step) * side, side), side)
        slot = lax.rem(step, 2)
        return pltpu.make_async_copy(stage.at[slot], d_up_out.at[span], stage_sems.at[slot])

    def gate_copy(step):
        span = pl.ds(pl.multiple_of(step * side, side), side)
        slot = lax.rem(step, 2)
        return pltpu.make_async_copy(stage_gate.at[slot], d_gate_own.at[span], own_sems.at[slot])

    def gradients(first, last):
        @pl.loop(first, last)
        def _(step):
            @pl.when(step >= 2)
            def _():
                up_copy(step - 2).wait()
                if not cross:
                    gate_copy(step - 2).wait()

            columns = normed_ref[:, pl.ds(pl.multiple_of(tile_of(step) * side, side), side)]
            stage[lax.rem(step, 2)] = contract(columns, up_ref[...], 0, 0).astype(bf16)
            up_copy(step).start()
            tile = contract(columns, gate_ref[...], 0, 0).astype(bf16)
            if not cross:
                stage_gate[lax.rem(step, 2)] = tile
                gate_copy(step).start()
                return

            @pl.when(step < count // 2)
            def _():
                parked(step, 0)[...] = tile
                cross_copy(step).start()

            @pl.when(step >= count // 2)
            def _():
                parked(step - count // 2, 1)[...] = tile
                own_copy(step - count // 2).start()

    for_sibling, for_chip, hand_on, finish = sum_block(
        sum_bits, HALF, False, product, total, to_core, from_core, chip_sum, arrived, Links(sum_send, sum_recv)
    )
    for_sibling()
    for_chip()
    gradients(0, 1)
    hand_on()
    gradients(1, count - 2)
    finish()
    if cross:
        over_copy.start()
    residual = cot_ref[...].astype(f32) + norm_back(h2_ref[...], gain_ref[...], total[...])
    residual_ref[...] = residual
    branch_ref[...] = residual.astype(bf16)
    tile, share = team * HEAD_DIM, width // team
    for g in range(width // tile):
        heads = contract(branch_ref[...], out_w_ref[g * tile : (g + 1) * tile, :], 1, 1).astype(bf16)
        for b in range(team):
            first = b * share + g * HEAD_DIM
            to_core[0, :, first : first + HEAD_DIM] = heads[:, b * HEAD_DIM : (b + 1) * HEAD_DIM]
    own_place = mates[0][1]
    own_rows = pl.ds(pl.multiple_of(own_place * block, block), block)
    def heads_of(place):
        return to_core.at[0, :, pl.ds(pl.multiple_of(place * share, share), share)]

    swap_copies = [
        Links(swap_send, swap_recv).copy(k, heads_of(mates[k][1]), heads_out.at[own_rows], mates[k][0])
        for k in range(1, team)
    ]
    keep = pltpu.make_async_copy(heads_of(own_place), heads_out.at[own_rows], local_sem)
    for copy in swap_copies + [keep]:
        copy.start()
    gradients(count - 2, count)
    for copy in swap_copies:
        copy.wait_recv()
    for copy in swap_copies:
        copy.wait_send()
    keep.wait()
    for step in range(count - 2, count):
        up_copy(step).wait()
        if not cross:
            gate_copy(step).wait()
    if cross:
        part_copy.wait()
        over_copy.wait()

        @pl.loop(0, count // 2)
        def _(i):
            own_copy(i).wait()
            cross_copy(i).wait()


def ffn_back(gate, up, gate_w, up_w, normed, out_w, h2, cot, gain, part, side, sum_bits, swap_bits):
    block, width = h2.shape
    shape = jax.ShapeDtypeStruct
    dma = pltpu.SemaphoreType.DMA
    ff_cols, cross = gate.shape[1], side % 128 == 0
    side = side if cross else 256
    tiles = width // side // 2
    if cross:
        d_gate = (shape((tiles, side, ff_cols), bf16),) * 2 + (shape(part[0].shape, bf16),) * 2
        more = [dma((tiles + 2,)), dma((tiles + 2,))]
    else:
        d_gate, more = (shape((width, ff_cols), bf16),), [pltpu.VMEM((2, side, ff_cols), bf16)]
    return pl.pallas_call(
        functools.partial(ffn_back_kernel, cross, sum_bits, swap_bits),
        out_shape=(
            shape((block, width), f32), shape((block, width), bf16), shape((8 * block, width // 8), bf16),
            shape((width, ff_cols), bf16),
        ) + d_gate,
        in_specs=[vmem] * 9 + [anywhere] * len(part),
        out_specs=(vmem, vmem) + (anywhere,) * (2 + len(d_gate)),
        scratch_shapes=sum_scratch(block, width, HALF)
        + [dma((8,)), dma((8,)), dma]
        + [pltpu.VMEM((2, side, ff_cols), bf16), dma((2,)), dma((tiles,))]
        + more,
        compiler_params=link_params(3),
        cost_estimate=cost(96 * block * ff_cols * width, 200e6),
        name="ffn_back",
    )(gate, up, gate_w, up_w, normed, out_w, h2, cot, gain, *part)


def last_sums_kernel(
    carry_bits, sum_bits, ffn_bits, left_ref, other_ref, right_ref, tokens_ref, gain_ref, residual_ref, hidden_ref,
    down_ref, h2_ref, gate_ref, *refs,
):
    moved = len(carry_bits)
    carried, (out_ref, mixed_ref, gate_out), refs = refs[:moved], refs[moved : moved + 3], refs[moved + 3 :]
    carried_out, scratch = refs[:moved], refs[moved:]
    if moved:
        carry_sems, scratch = scratch[-2:], scratch[:-2]
    (swap_send, swap_recv, swap_local), scratch = scratch[-3:], scratch[:-3]
    count = len(scratch) // 2
    me = lax.axis_index(AXIS)
    total, ffn_total = scratch[0], scratch[count]
    block = total.shape[0]
    mates = [team_mate(me, ffn_bits, k) for k in range(8)]
    partners = [flip_bit(me, bit) for bit in sum_bits if bit not in ffn_bits]
    greet(partners + [device for device, _ in mates[1:]] + [flip_bit(me, bit) for bit in carry_bits])
    crossing = [
        Links(*carry_sems).copy(i, carried[i], carried_out[i], flip_bit(me, bit)) for i, bit in enumerate(carry_bits)
    ]
    for copy in crossing:
        copy.start()
    swaps, own_place = Links(swap_send, swap_recv), mates[0][1]
    swap_copies = [
        swaps.copy(k, gate_ref.at[mates[k][1]], gate_out.at[own_place], mates[k][0]) for k in range(1, 8)
    ]
    keep = pltpu.make_async_copy(gate_ref.at[own_place], gate_out.at[own_place], swap_local)

    def rows_of(place):
        return pl.ds(pl.multiple_of(place * block, block), block)

    def product(place, columns):
        rows = rows_of(place)
        middle = left_ref.shape[1]
        return contract(left_ref[rows, :], right_ref[columns, 0:middle], 1, 1) + contract(
            other_ref[rows, :], right_ref[columns, middle : 2 * middle], 1, 1
        )

    def ffn_product(place, columns):
        return contract(hidden_ref[rows_of(place), :], down_ref[:, columns], 1, 0)

    first = sum_block(sum_bits, LAST_CUT, False, product, *scratch[: count - 2], Links(*scratch[count - 2 : count]))
    second = sum_block(ffn_bits, LAST_CUT, True, ffn_product, *scratch[count:-2], Links(*scratch[-2:]))
    run(first[:2])
    run(second[:2])
    for copy in swap_copies + [keep]:
        copy.start()
    for one, other in zip(first[2:], second[2:]):
        one()
        other()
    out_ref[...] = residual_ref[...] + norm_back(
        tokens_ref[...].astype(f32), gain_ref[...], total[...]
    )
    mixed_ref[...] = (h2_ref[...] + ffn_total[...]).astype(bf16)
    for copy in swap_copies:
        copy.wait_recv()
    for copy in swap_copies:
        copy.wait_send()
    keep.wait()
    for copy in crossing:
        copy.wait()


def last_sums(left, other, right, tokens, gain, residual, hidden, down, h2, d_gate, carry, carry_bits, sum_bits, ffn_bits):
    block, width = tokens.shape
    return pl.pallas_call(
        functools.partial(last_sums_kernel, carry_bits, sum_bits, ffn_bits),
        out_shape=(
            jax.ShapeDtypeStruct((block, width), f32), jax.ShapeDtypeStruct((block, width), bf16),
            jax.ShapeDtypeStruct(d_gate.shape, bf16),
        ) + tuple(jax.ShapeDtypeStruct(x.shape, x.dtype) for x in carry),
        in_specs=[vmem] * 9 + [anywhere] * (1 + len(carry)),
        out_specs=(vmem, vmem, anywhere) + (anywhere,) * len(carry),
        scratch_shapes=sum_scratch(block, width, LAST_CUT) * 2
        + [pltpu.SemaphoreType.DMA((8,)), pltpu.SemaphoreType.DMA((8,)), pltpu.SemaphoreType.DMA]
        + [pltpu.SemaphoreType.DMA((1,))] * (2 * len(carry)),
        compiler_params=link_params(4),
        cost_estimate=cost(16 * block * right.size // 8, 300e6),
        name="last_sums",
    )(left, other, right, tokens, gain, residual, hidden, down, h2, d_gate, *carry)


def exchange_kernel(teams, sources, *refs):
    mine, landed, (send_sems, recv_sems, local_sems) = refs[:sources], refs[sources : 2 * sources], refs[2 * sources :]
    me = lax.axis_index(AXIS)
    members = mine[0].shape[0]
    links = Links(send_sems, recv_sems)
    greeted = {}
    for bits in teams:
        for k in range(1, members):
            device, _ = team_mate(me, bits, k)
            greeted[tuple(sorted(bit for j, bit in enumerate(bits) if (k >> j) % 2))] = device
    greet(list(greeted.values()))
    copies, kept = [], []
    for i, (source, target, bits) in enumerate(zip(mine, landed, teams)):
        own = team_mate(me, bits, 0)[1]
        kept.append(pltpu.make_async_copy(source.at[own], target.at[own], local_sems.at[i]))
        for k in range(1, members):
            device, place = team_mate(me, bits, k)
            copies.append(links.copy(i * members + k, source.at[place], target.at[own], device))
    for copy in copies + kept:
        copy.start()
    for copy in copies:
        copy.wait()
    for copy in kept:
        copy.wait()


def exchange(parts, teams):
    dma = pltpu.SemaphoreType.DMA
    slots = len(parts) * parts[0].shape[0]
    return pl.pallas_call(
        functools.partial(exchange_kernel, teams, len(parts)),
        out_shape=tuple(jax.ShapeDtypeStruct(part.shape, part.dtype) for part in parts),
        in_specs=[vmem] * len(parts),
        out_specs=tuple([vmem] * len(parts)),
        scratch_shapes=[dma((slots,)), dma((slots,)), dma((len(parts),))],
        compiler_params=link_params(5),
        cost_estimate=cost(1e6, 40e6),
        name="exchange",
    )(*parts)


def home_kernel(places, gain_of, sources, *refs):
    count = len(places)
    kinds = max(gain_of) + 1
    parts, weights, gains = refs[:sources], refs[sources : sources + count], refs[sources + count : sources + count + kinds]
    outs, gain_outs = refs[-count - kinds : -kinds], refs[-kinds:]
    totals = [jnp.zeros(gain.shape, f32) for gain in gains]
    for i, (out, weight) in enumerate(zip(outs, weights)):
        for source, member, first, target, columns in places[i]:
            out[:, target : target + columns] = parts[source][member, :, first : first + columns].astype(f32)
        for first in range(0, out.shape[1], 1024):
            product = out[:, first : first + 1024] * weight[:, first : first + 1024].astype(f32)
            totals[gain_of[i]] += jnp.sum(product, 1, keepdims=True)
    for gain, total, out in zip(gains, totals, gain_outs):
        out[...] = jnp.broadcast_to(total / gain[...], (out.shape[1], 128)).T[0:1, :]


def home(parts, weights, gains, gain_of, places):
    shape = jax.ShapeDtypeStruct
    count = len(weights)
    gains = [gain.astype(f32).reshape(-1, 1) for gain in gains]
    return pl.pallas_call(
        functools.partial(home_kernel, places, gain_of, len(parts)),
        out_shape=tuple(shape(w.shape, f32) for w in weights) + tuple(shape((1, g.shape[0]), f32) for g in gains),
        in_specs=[vmem] * (len(parts) + count + len(gains)),
        out_specs=tuple([vmem] * (count + len(gains))),
        compiler_params=pltpu.CompilerParams(vmem_limit_bytes=40 * 1024 * 1024),
        cost_estimate=cost(1e6, 30e6),
        name="home",
    )(*parts, *weights, *gains)


def body(
    tokens, block_of, clip_limit, norm_attn, w_query, w_key, w_value, w_out,
    norm_ffn, w_gate, w_up, w_down, cotangent,
):
    tok_rows, width = tokens.shape
    devices = lax.axis_size(AXIS)
    team = SEQ // tok_rows
    teams = devices // team
    head_total = width // HEAD_DIM
    heads = head_total // team
    head_cols = heads * HEAD_DIM
    ff_rows = w_down.shape[0]
    weight_rows = w_gate.shape[0]
    ff_cols = w_gate.shape[1] // team
    device = lax.axis_index(AXIS)
    mate = device % team
    bit_count = devices.bit_length() - 1
    attn_bits, ffn_bits = (1, 2, 4), (1, 2, 8)
    data_bits = [4] + [1 << k for k in range(4, bit_count)]
    in_team = [[g * team + b for b in range(team)] for g in range(teams)]
    across = [[g * team + b for g in range(teams)] for b in range(team)]
    ffn_team = [
        [g * 16 + z * 8 + y * 4 + c for z in range(2) for c in range(4)]
        for g in range(devices // 16)
        for y in range(2)
    ]

    def flip(x, bit):
        return lax.ppermute(x, AXIS, [(i, i ^ bit) for i in range(devices)])

    def gather_across(x):
        return lax.all_gather(x, AXIS, axis=0, tiled=True, axis_index_groups=across)

    def scatter_across(x):
        return lax.psum_scatter(
            x.astype(bf16), AXIS, scatter_dimension=0, tiled=True, axis_index_groups=across
        )

    def dim_of(bit):
        return bit_count - bit.bit_length()

    def data_pieces(x):
        pieces = {0: x}
        for bit in reversed(data_bits):
            for key in list(pieces):
                pieces[key | bit] = flip(pieces[key], bit)
        return pieces

    def place_pieces(pieces, dims, shape):
        total = jnp.zeros(shape, bf16)
        for key, piece in pieces.items():
            start = [0] * len(shape)
            size = list(shape)
            for bit in data_bits:
                start[dims[bit]] = ((device // bit) + (1 if key & bit else 0)) % 2
                size[dims[bit]] = 1
            total = lax.dynamic_update_slice(total, piece.reshape(size), start)
        return total

    def after_bit(dims, bit):
        return {b: d - (d > dims[bit]) for b, d in dims.items() if b != bit}

    def data_sum(x, dims, bits):
        for bit in bits:
            mine = (device // bit) % 2
            keep = lax.dynamic_index_in_dim(x, mine, dims[bit], False)
            sent = flip(lax.dynamic_index_in_dim(x, 1 - mine, dims[bit], False), bit)
            x = (keep.astype(f32) + sent.astype(f32)).astype(bf16)
            dims = after_bit(dims, bit)
        return x

    row_dims = {bit: dim_of(bit) for bit in data_bits}
    row_shape = (2,) * bit_count
    unit_dims = {bit: i for i, bit in enumerate(reversed(data_bits))}
    unit_shape = (2,) * len(data_bits)

    def tie(*values):
        return lax.optimization_barrier(values)

    qkv_moves = tuple(
        (i, b, (g * team + b) * HEAD_DIM, (3 * (g // 2) + i) * PAIR + (g % 2) * HEAD_DIM, HEAD_DIM)
        for i in range(3) for g in range(heads) for b in range(team)
    )
    ffn_units = tuple(
        (z * 4 + c, (2 * h + y) * ff_rows, (h * 16 + z * 8 + y * 4 + c) * ff_rows)
        for h in range(devices // 16) for z in range(2) for y in range(2) for c in range(4)
    )
    ffn_moves = tuple(
        (i, member, source, target, ff_rows)
        for i in range(2) for member, target, source in ffn_units
    )
    out_w = lax.all_gather(w_out, AXIS, axis=0, tiled=True)
    gain_row = jnp.concatenate([norm_attn, norm_ffn]).astype(f32)
    gain_row = jnp.pad(gain_row, (0, 128 - 2 * weight_rows)).reshape(1, 128)
    block_rows = block_of.astype(f32).reshape(tok_rows // 128, 128)
    small = jnp.concatenate([gain_row, block_rows, jnp.zeros((7 - tok_rows // 128, 128), f32)])
    ahead = data_bits == [4, 16]
    normed_attn, qkv_w, both_mine, gathered, *down_moved = front(
        tokens, (w_query, w_key, w_value, w_gate, w_up), small, teams, qkv_moves, ffn_moves,
        [w_down] if ahead else [], (4,) if ahead else (),
    )
    qkv_w = qkv_w.reshape(width, 3 * head_cols)
    gain_attn = gathered[:, 0, :weight_rows].reshape(1, width)
    gain_ffn = gathered[:, 0, weight_rows : 2 * weight_rows].reshape(1, width)
    blocks = lax.dynamic_slice_in_dim(gathered, device - mate, team, 0)
    blocks = blocks[:, 1 : 1 + tok_rows // 128].astype(jnp.int32).reshape(SEQ)
    row_blocks, col_blocks = blocks.reshape(1, SEQ), blocks.reshape(SEQ, 1)
    both_mine, qkv_w = tie(both_mine, qkv_w)

    def whole_rows(mine):
        shape = row_shape + (weight_rows, ff_cols)
        return place_pieces(data_pieces(mine), row_dims, shape).reshape(width, ff_cols)

    qkv = contract(normed_attn, qkv_w, 1, 0)
    cosine, sine = rope_tables(SEQ, PAIR)
    qkv, cot_mine = tie(qkv, cotangent)
    if data_bits == [4, 16]:
        carry = [both_mine, flip(both_mine, 4), flip(both_mine[: 4 * EARLY_HALVES], 16), w_down, *down_moved]
    else:
        carry = []
    query, key, value, attended, lse, peak = attend_forward(qkv, cosine, sine, row_blocks, col_blocks)
    peaks = jnp.where(
        (jnp.arange(head_total) % team) == mate, jnp.repeat(peak[0, :heads], team), -jnp.inf
    )
    peaks = jnp.broadcast_to(jnp.pad(peaks, (0, 128 - head_total))[None], (8, 128))
    if carry:
        carry[2], attended, down_sent = tie(carry[2], attended, w_down)
        over = flip(down_sent, 16)
    after_attn, normed_ffn, peaks, *full = branch(
        attended, out_w, tokens, gain_ffn, peaks, carry, attn_bits, ffn_bits, bit_count
    )
    head_peak = peaks[0, :head_total]
    if carry:
        normed_ffn, over = tie(normed_ffn, over)
    if carry:
        gate_w, up_w = (w.reshape(width, ff_cols) for w in full[:2])
        z_side, y_side = (device // 16) % 2, (device // 4) % 2
        full_down = lax.dynamic_update_slice(full[2], over[None], ((1 - z_side) * 2 + y_side, 0, 0))
        down_w = lax.dynamic_update_slice(
            full_down, flip(over, 4)[None], ((1 - z_side) * 2 + 1 - y_side, 0, 0)
        ).reshape(ff_cols, width)
    else:
        gate_w, up_w = whole_rows(both_mine[:team]), whole_rows(both_mine[team:])
        down_w = place_pieces(
            data_pieces(w_down), unit_dims, unit_shape + (ff_rows, width)
        ).reshape(ff_cols, width)
    gate_pre = contract(normed_ffn, gate_w, 1, 0)
    up_pre = contract(normed_ffn, up_w, 1, 0)
    sigmoid_gate = jax.nn.sigmoid(gate_pre)
    silu_gate = gate_pre * sigmoid_gate
    hidden = (silu_gate * up_pre).astype(bf16)

    team_cot = lax.all_gather(cot_mine, AXIS, axis=0, tiled=True, axis_index_groups=ffn_team)
    d_down = contract(hidden, team_cot, 0, 0).astype(bf16).reshape(unit_shape + (ff_rows, width))
    team_cot, d_down = tie(team_cot, d_down)
    d_hidden = contract(team_cot, down_w, 1, 1)
    grad_gate = (d_hidden * up_pre * sigmoid_gate * (1.0 + gate_pre * (1.0 - sigmoid_gate))).astype(bf16)
    grad_up = (d_hidden * silu_gate).astype(bf16)

    unit_rest, row_rest = after_bit(unit_dims, data_bits[0]), after_bit(row_dims, data_bits[0])
    row_values = (weight_rows, ff_cols)
    crosses = data_bits == [4, 16]
    if crosses:
        y_side, z_side = (device // 4) % 2, (device // 16) % 2
        kept = lax.dynamic_index_in_dim(d_down, y_side, unit_dims[4], False)
        sent = lax.dynamic_index_in_dim(d_down, 1 - y_side, unit_dims[4], False)
        mine, theirs = (lax.dynamic_index_in_dim(kept, z, 0, False) for z in (z_side, 1 - z_side))
        to_mine, to_theirs = (lax.dynamic_index_in_dim(sent, z, 0, False) for z in (z_side, 1 - z_side))
        theirs = (theirs.astype(f32) + flip(to_theirs, 4).astype(f32)).astype(bf16)
        grad_gate, theirs = tie(grad_gate, theirs)
        beside = [to_mine, theirs]
    else:
        beside = []
    d_residual, branch_mine, grad_attended, d_up, *d_gate = ffn_back(
        grad_gate, grad_up, gate_w, up_w, normed_ffn, out_w, after_attn, cotangent, gain_ffn, beside, 4 * weight_rows,
        ffn_bits, attn_bits,
    )
    if crosses:
        d_down = mine.astype(f32) + d_gate[2].astype(f32) + d_gate[3].astype(f32)
        d_gate = (d_gate[0].astype(f32) + d_gate[1].astype(f32)).astype(bf16)
        d_gate = d_gate.reshape((2,) * (bit_count - 1) + row_values)
    else:
        d_down = data_sum(d_down, unit_dims, data_bits[:1])
        d_gate = data_sum(d_gate[0].reshape(row_shape + row_values), row_dims, data_bits[:1])
    if not crosses:
        d_down = data_sum(d_down, unit_rest, data_bits[1:]).astype(f32)
    grad_attended, d_gate = tie(grad_attended, d_gate)
    d_gate = data_sum(d_gate, row_rest, data_bits[1:])
    branch_grad = lax.all_gather(branch_mine, AXIS, axis=0, tiled=True, axis_index_groups=in_team)

    def heads_back(pair):
        return attend_backward(
            pair, query, key, value, grad_attended, lse, cosine, sine, row_blocks, col_blocks, normed_attn
        )

    grad_pairs, shares = [None] * (heads // 2), [None] * (heads // 2)
    grad_pairs[0], share = heads_back(0)
    grad_attended, d_gate, d_up, share, branch_grad = tie(grad_attended, d_gate, d_up, share, branch_grad)
    shares[0] = scatter_across(share)
    d_up = data_sum(d_up.reshape(row_shape + row_values), row_dims, data_bits[:1])
    for p in range(1, heads // 2):
        grad_pairs[p], share = heads_back(p)
        grad_pairs[p], share, d_up = tie(grad_pairs[p], share, d_up)
        shares[p] = scatter_across(share)
    sent, sent_bits = [], ()
    if crosses:
        kept_up = lax.dynamic_index_in_dim(d_up, z_side, row_rest[16], False)
        sent, sent_bits = [lax.dynamic_index_in_dim(d_up, 1 - z_side, row_rest[16], False)], (16,)
        kept_up, sent[0] = (d.reshape(team, weight_rows, ff_cols) for d in (kept_up, sent[0]))
    else:
        d_up = data_sum(d_up, row_rest, data_bits[1:])
    grad_pairs[0], shares[0] = tie(grad_pairs[0], shares[0])
    d_gate = d_gate.reshape(team, weight_rows, ff_cols)
    d_tokens, mixed, d_gate, *landed = last_sums(
        *grad_pairs, qkv_w, tokens, gain_attn, d_residual, hidden, down_w, after_attn, d_gate, sent, sent_bits,
        attn_bits, ffn_bits,
    )
    if crosses:
        d_up = (kept_up.astype(f32) + landed[0].astype(f32)).astype(bf16)
    d_tokens, attended = tie(d_tokens, attended)
    out_part = contract(attended, branch_grad, 0, 0)
    if weight_rows == HEAD_DIM:
        d_out = scatter_across(out_part).astype(f32)
    else:
        spread = jnp.where(
            (jnp.arange(team) == mate)[None, :, None, None],
            out_part.reshape(heads, 1, HEAD_DIM, width), 0.0,
        ).reshape(width, width)
        d_out = lax.psum_scatter(spread, AXIS, scatter_dimension=0, tiled=True)
    places = [[], [], []]
    for i, b, source, target, columns in qkv_moves:
        places[i].append((target // (3 * PAIR), b, target % (3 * PAIR), source, columns))
    places += [
        [(heads // 2 + i, member, target, source, ff_rows) for member, target, source in ffn_units] for i in range(2)
    ]
    shares = [share.reshape(team, weight_rows, 3 * PAIR) for share in shares]
    *shares, d_up = exchange(
        shares + [d_up.reshape(team, weight_rows, ff_cols)], (attn_bits,) * (heads // 2) + (ffn_bits,)
    )
    d_query, d_key, d_value, d_gate, d_up, d_norm_attn, d_norm_ffn = home(
        shares + [d_gate, d_up], (w_query, w_key, w_value, w_gate, w_up), (norm_attn, norm_ffn), (0, 0, 0, 1, 1),
        tuple(tuple(p) for p in places),
    )
    d_norm_attn, d_norm_ffn = d_norm_attn[0], d_norm_ffn[0]
    clip_value = clip_limit.astype(f32)
    factor = jnp.sqrt(clip_value / jnp.maximum(head_peak, clip_value))
    factors = jnp.repeat(factor, HEAD_DIM)[None, :]
    clipped_query = (w_query.astype(f32) * factors).astype(bf16)
    clipped_key = (w_key.astype(f32) * factors).astype(bf16)
    return (
        mixed, d_tokens, d_norm_attn, d_query, d_key, d_value, d_out, d_norm_ffn,
        d_gate, d_up, d_down, head_peak, clipped_query, clipped_key,
    )


def solution(mesh):
    rows, whole = P(AXIS, None), P(AXIS)
    return jax.shard_map(
        body,
        mesh=mesh,
        in_specs=(rows, whole, P(), whole, rows, rows, rows, rows, whole, rows, rows, rows, rows),
        out_specs=(
            rows, rows, whole, rows, rows, rows, rows, whole, rows, rows, rows, P(), rows, rows,
        ),
        check_vma=False,
    )
```

```python
import functools

import jax
import jax.numpy as jnp
import numpy as np
from jax import lax
from jax.experimental import pallas as pl
from jax.experimental.pallas import tpu as pltpu
from jax.sharding import PartitionSpec as P

HEAD_DIM = 64
SEQ = 2048
BLOCK = 256
HALF = 128
LAST_CUT = 0
EARLY_HALVES = 3
BRANCH_CUT = 128
AXIS = "fsdp"
MESH = pl.DeviceIdType.MESH

epsilon = 1e-05
rope_base = 130000.0
bf16 = jnp.bfloat16
f32 = jnp.float32
vmem = pl.BlockSpec(memory_space=pltpu.VMEM)
anywhere = pl.BlockSpec(memory_space=pl.ANY)


def contract(left, right, left_dim, right_dim):
    return lax.dot_general(
        left, right, (((left_dim,), (right_dim,)), ((), ())), preferred_element_type=f32
    )


def rope_tables(length, width):
    half_dim = HEAD_DIM // 2
    inverse = rope_base ** (-np.arange(half_dim) * 2.0 / HEAD_DIM)
    angles = (np.arange(length, dtype=np.float32)[:, None] * inverse.astype(np.float32)).astype(np.float64)
    cosine, sine = np.cos(angles).astype(np.float32), np.sin(angles).astype(np.float32)
    repeats = width // HEAD_DIM
    return (
        jnp.asarray(np.tile(np.concatenate([cosine, cosine], 1), (1, repeats))),
        jnp.asarray(np.tile(np.concatenate([-sine, sine], 1), (1, repeats))),
    )


def swap_halves(rows):
    width = rows.shape[1]
    half = HEAD_DIM // 2
    lane = lax.broadcasted_iota(jnp.int32, rows.shape, 1)
    return jnp.where(
        lane % HEAD_DIM < half, pltpu.roll(rows, width - half, 1), pltpu.roll(rows, half, 1)
    )


PAIR = 2 * HEAD_DIM


def head_mask(shape, head):
    lane = lax.broadcasted_iota(jnp.int32, shape, 1)
    return (lane >= head * HEAD_DIM) & (lane < (head + 1) * HEAD_DIM)


def masked_scores(query, key_ref, row_ref, col_ref, q0, cols):
    tail = min(2 * BLOCK, cols)
    scores = contract(query, key_ref[0:cols, :], 1, 1)
    shown = row_ref[:, pl.ds(cols - tail, tail)] <= col_ref[pl.ds(q0, BLOCK), :]
    hidden = jnp.where(shown, scores[:, cols - tail :], -jnp.inf)
    return jnp.concatenate([scores[:, : cols - tail], hidden], 1) if tail < cols else hidden


def attend_forward_kernel(
    normed_ref, qkv_w_ref, cos_ref, sin_ref, row_ref, col_ref, q_ref, k_ref, v_ref, out_ref, lse_ref, peak_ref
):
    pairs, length, _ = q_ref.shape

    @pl.loop(0, length // BLOCK)
    def _(t):
        rows = pl.ds(pl.multiple_of(t * BLOCK, BLOCK), BLOCK)
        cosine, sine = cos_ref[rows, :], sin_ref[rows, :]
        for pair in range(pairs):
            first = 3 * pair * PAIR
            qkv = contract(normed_ref[rows, :], qkv_w_ref[:, first : first + 3 * PAIR], 1, 0)
            query = qkv[:, 0:PAIR]
            query = (query * cosine + swap_halves(query) * sine).astype(bf16)
            q_ref[pair, rows, :] = (query.astype(f32) * HEAD_DIM ** (-0.5)).astype(bf16)
            key = qkv[:, PAIR : 2 * PAIR]
            k_ref[pair, rows, :] = (key * cosine + swap_halves(key) * sine).astype(bf16)
            v_ref[pair, rows, :] = qkv[:, 2 * PAIR : 3 * PAIR].astype(bf16)

    peak_ref[...] = jnp.full(peak_ref.shape, -jnp.inf, f32)
    lane = lax.broadcasted_iota(jnp.int32, (BLOCK, 128), 1)
    for t in range(length // BLOCK):
        q0 = t * BLOCK
        rows = pl.ds(q0, BLOCK)
        cols = min(q0 + 2 * BLOCK, length)

        @pl.loop(0, pairs)
        def _(pair):
            total = jnp.zeros((BLOCK, PAIR), f32)
            for sub in range(2):
                head = 2 * pair + sub
                mask = head_mask((BLOCK, PAIR), sub)
                query = jnp.where(mask, q_ref[pair, rows, :], 0).astype(bf16)
                scores = masked_scores(query, k_ref.at[pair], row_ref, col_ref, q0, cols)
                row_max = jnp.max(scores, 1, keepdims=True)
                numerators = jnp.exp(scores - row_max)
                totals = jnp.sum(numerators, 1, keepdims=True)
                mixed = contract(numerators.astype(bf16), v_ref[pair, 0:cols, :], 1, 0) / totals
                total = jnp.where(mask, mixed, total)
                lse_ref[rows, :] = jnp.where(lane == head, row_max + jnp.log(totals), lse_ref[rows, :])
                peak_ref[...] = jnp.where(
                    lax.broadcasted_iota(jnp.int32, peak_ref.shape, 1) == head,
                    jnp.maximum(peak_ref[...], jnp.max(row_max)),
                    peak_ref[...],
                )
            out_ref[rows, pl.ds(pl.multiple_of(pair * PAIR, PAIR), PAIR)] = total.astype(bf16)


def attend_forward(normed, qkv_w, cosine, sine, row_blocks, col_blocks):
    length = normed.shape[0]
    pairs = qkv_w.shape[1] // (3 * PAIR)
    shape = jax.ShapeDtypeStruct
    return pl.pallas_call(
        attend_forward_kernel,
        out_shape=(
            shape((pairs, length, PAIR), bf16),
            shape((pairs, length, PAIR), bf16),
            shape((pairs, length, PAIR), bf16),
            shape((length, pairs * PAIR), bf16),
            shape((length, 128), f32),
            shape((8, 128), f32),
        ),
        in_specs=[vmem] * 6,
        out_specs=tuple([vmem] * 6),
        compiler_params=pltpu.CompilerParams(vmem_limit_bytes=56 * 1024 * 1024),
        cost_estimate=pl.CostEstimate(
            flops=16 * pairs * length * length * PAIR + 2 * normed.size * qkv_w.shape[1], bytes_accessed=100_000_000,
            transcendentals=2 * pairs * length * length,
        ),
        name="attend_forward",
    )(normed, qkv_w, cosine, sine, row_blocks, col_blocks)


def attend_backward_kernel(
    first_head, q_ref, k_ref, v_ref, grad_ref, lse_ref, cos_ref, sin_ref, row_ref, col_ref, normed_ref,
    out_ref, weight_ref, dk_ref, dv_ref,
):
    length = q_ref.shape[0]
    dk_ref[...] = jnp.zeros_like(dk_ref)
    dv_ref[...] = jnp.zeros_like(dv_ref)
    lane = lax.broadcasted_iota(jnp.int32, (BLOCK, 128), 1)
    for t in range(length // BLOCK):
        q0 = t * BLOCK
        rows = pl.ds(q0, BLOCK)
        cols = min(q0 + 2 * BLOCK, length)

        def one_head(sub, dq):
            mask = head_mask((BLOCK, PAIR), sub)
            query = jnp.where(mask, q_ref[rows, :], 0).astype(bf16)
            grad = jnp.where(mask, grad_ref[rows, :], 0).astype(bf16)
            lse = jnp.sum(
                jnp.where(lane == first_head + sub, lse_ref[rows, :], 0.0), 1, keepdims=True
            )
            scores = masked_scores(query, k_ref, row_ref, col_ref, q0, cols)
            attention = jnp.exp(scores - lse)
            grad_attention = contract(grad, v_ref[0:cols, :], 1, 1)
            weighted = attention * grad_attention
            centre = jnp.sum(weighted, 1, keepdims=True)
            grad_scores = (weighted - attention * centre).astype(bf16)
            dv_ref[0:cols, :] += contract(attention.astype(bf16), grad, 0, 0)
            dk_ref[0:cols, :] += contract(grad_scores, query, 0, 0)
            return jnp.where(mask, contract(grad_scores, k_ref[0:cols, :], 1, 0), dq)

        dq = lax.fori_loop(0, 2, one_head, jnp.zeros((BLOCK, PAIR), f32)) * HEAD_DIM ** (-0.5)
        out_ref[rows, 0:PAIR] = (dq * cos_ref[rows, :] - swap_halves(dq) * sin_ref[rows, :]).astype(bf16)
    for t in range(length // BLOCK):
        rows = pl.ds(t * BLOCK, BLOCK)
        dk = dk_ref[rows, :]
        out_ref[rows, PAIR : 2 * PAIR] = (
            dk * cos_ref[rows, :] - swap_halves(dk) * sin_ref[rows, :]
        ).astype(bf16)
        out_ref[rows, 2 * PAIR : 3 * PAIR] = dv_ref[rows, :].astype(bf16)
    side = 256

    @pl.loop(0, normed_ref.shape[1] // side)
    def _(k):
        span = pl.ds(pl.multiple_of(k * side, side), side)
        weight_ref[span, :] = contract(normed_ref[:, span], out_ref[...], 0, 0).astype(bf16)


def attend_backward(pair, query, key, value, grad, lse, cosine, sine, row_blocks, col_blocks, normed):
    length, width = normed.shape
    heads = pl.BlockSpec((None, length, PAIR), lambda _: (pair, 0, 0))
    return pl.pallas_call(
        functools.partial(attend_backward_kernel, 2 * pair),
        grid=(1,),
        out_shape=(
            jax.ShapeDtypeStruct((length, 3 * PAIR), bf16), jax.ShapeDtypeStruct((width, 3 * PAIR), bf16),
        ),
        in_specs=[heads] * 3 + [pl.BlockSpec((length, PAIR), lambda _: (0, pair))] + [vmem] * 6,
        out_specs=(vmem, vmem),
        scratch_shapes=[pltpu.VMEM((length, PAIR), f32), pltpu.VMEM((length, PAIR), f32)],
        compiler_params=pltpu.CompilerParams(vmem_limit_bytes=56 * 1024 * 1024),
        cost_estimate=pl.CostEstimate(
            flops=40 * length * length * PAIR + 6 * length * width * PAIR, bytes_accessed=100_000_000,
            transcendentals=2 * length * length,
        ),
        name="attend_backward",
    )(query, key, value, grad, lse, cosine, sine, row_blocks, col_blocks, normed)


def bit_of(index, bit):
    return lax.rem(lax.div(index, bit), 2)


def flip_bit(index, bit):
    return index + bit - 2 * bit * bit_of(index, bit)


def team_mate(me, bits, offset):
    device, place = me, 0
    for k, bit in enumerate(bits):
        moved = (offset >> k) % 2
        place = place + lax.rem(bit_of(me, bit) + moved, 2) * (1 << k)
        device = flip_bit(device, bit) if moved else device
    return device, place


class Links:

    def __init__(self, send_sems, recv_sems):
        self.send_sems, self.recv_sems = send_sems, recv_sems

    def copy(self, slot, src, dst, device):
        return pltpu.make_async_remote_copy(
            src_ref=src, dst_ref=dst, send_sem=self.send_sems.at[slot],
            recv_sem=self.recv_sems.at[slot], device_id=(device,), device_id_type=MESH,
        )


def greet(partners):
    barrier = pltpu.get_barrier_semaphore()
    for partner in partners:
        pl.semaphore_signal(barrier, inc=1, device_id=(partner,), device_id_type=MESH)
    pl.semaphore_wait(barrier, len(partners))


def spread_block(bits, cut, own_ref, out_ref, links, local_sem):
    core, first, second = bits
    me = lax.axis_index(AXIS)
    sibling, next_a, next_b = (flip_bit(me, bit) for bit in bits)
    block = own_ref.shape[0]
    in_a, in_b = bit_of(me, first), bit_of(me, second)
    spans = {None: (0, block), 0: (0, cut), 1: (cut, block - cut)}

    def rows(flip_a, flip_b, part):
        place = bit_of(me, core)
        place = place + 2 * lax.rem(in_a + flip_a, 2) + 4 * lax.rem(in_b + flip_b, 2)
        start, size = spans[part]
        return pl.ds(pl.multiple_of(place * block + start, 16), size)

    def passed(slot, where, device):
        return links.copy(slot, out_ref.at[where], out_ref.at[where], device)

    def first_hand(slot, part, device):
        start, size = spans[part]
        return links.copy(slot, own_ref.at[pl.ds(start, size)], out_ref.at[rows(0, 0, part)], device)

    makers = {
        0: lambda: first_hand(0, 0, next_a),
        1: lambda: first_hand(1, 1, next_b),
        2: lambda: first_hand(2, 1, next_a),
        3: lambda: first_hand(3, 0, next_b),
        4: lambda: links.copy(4, own_ref, out_ref.at[rows(0, 0, None)], sibling),
        5: lambda: passed(5, rows(1, 0, 0), next_b),
        6: lambda: passed(6, rows(1, 0, 0), sibling),
        7: lambda: passed(7, rows(0, 1, 1), next_a),
        8: lambda: passed(8, rows(0, 1, 1), sibling),
        9: lambda: passed(9, rows(1, 0, 1), sibling),
        10: lambda: passed(10, rows(0, 1, 0), sibling),
        11: lambda: passed(11, rows(1, 1, 0), sibling),
        12: lambda: passed(12, rows(1, 1, 1), sibling),
    }
    needs = {0: 0, 1: 1, 2: 1, 3: 0, 4: None, 5: 0, 6: 0, 7: 1, 8: 1, 9: 1, 10: 0, 11: 0, 12: 1}
    copies = {slot: make() for slot, make in makers.items() if spans[needs[slot]][1]}
    keep = pltpu.make_async_copy(own_ref, out_ref.at[rows(0, 0, None)], local_sem)

    def begin():
        for slot in range(5):
            if slot in copies:
                copies[slot].start()
        keep.start()

    def hand_on(arrived, *sent):
        def phase():
            if arrived in copies:
                copies[arrived].wait_recv()
                for slot in sent:
                    copies[slot].start()

        return phase

    def finish():
        for slot in (4, 6, 8, 9, 10, 11, 12):
            if slot in copies:
                copies[slot].wait_recv()
        keep.wait()
        for slot in copies:
            copies[slot].wait_send()

    return [
        begin, hand_on(0, 5, 6), hand_on(1, 7, 8), hand_on(2, 9), hand_on(3, 10),
        hand_on(5, 11), hand_on(7, 12), finish,
    ]


def run(phases):
    for phase in phases:
        phase()


SPREAD_COPIES = 13
SUM_COPIES = 10


def sum_block(bits, cut, swapped, product, total, to_core, from_core, chip_sum, arrived, links):
    core = bits[0]
    (first, weight_a), (second, weight_b) = ((bits[2], 4), (bits[1], 2)) if swapped else ((bits[1], 2), (bits[2], 4))
    me = lax.axis_index(AXIS)
    sibling, next_a, next_b = flip_bit(me, core), flip_bit(me, first), flip_bit(me, second)
    block, width = total.shape
    tile = 512

    def place(step, other_core):
        flip_a, flip_b = 1 - step // 2, 1 - step % 2
        return (
            lax.rem(bit_of(me, core) + other_core, 2)
            + weight_a * lax.rem(bit_of(me, first) + flip_a, 2)
            + weight_b * lax.rem(bit_of(me, second) + flip_b, 2)
        )

    low, high = (0, cut), (cut, block - cut)
    landing = range(6) if cut else {1: 0, 3: 1, 4: 2}

    def link(slot, step, span, device):
        return links.copy(slot, chip_sum.at[step, pl.ds(*span)], arrived.at[landing[slot - 4], pl.ds(0, span[1])], device)

    diag_a, diag_b = (link(4, 0, low, next_a) if cut else None), link(5, 0, high, next_b)
    plain_a, plain_b = (link(6, 1, low, next_a) if cut else None), link(7, 2, high, next_b)
    last_a, last_b = link(8, 1, high, next_a), (link(9, 2, low, next_b) if cut else None)

    def core_copy(step):
        return links.copy(step, to_core.at[step], from_core.at[step], sibling)

    def for_sibling():
        @pl.loop(0, 4)
        def _(step):
            @pl.loop(0, width // tile)
            def _(column):
                columns = pl.ds(pl.multiple_of(column * tile, tile), tile)
                to_core[step, :, columns] = product(place(step, 1), columns).astype(bf16)

            core_copy(step).start()

    def for_chip():
        @pl.loop(0, 4)
        def _(step):
            core_copy(step).wait_recv()

            @pl.loop(0, width // tile)
            def _(column):
                columns = pl.ds(pl.multiple_of(column * tile, tile), tile)
                summed = product(place(step, 0), columns) + from_core[step, :, columns].astype(f32)
                total[:, columns] = summed

                @pl.when(step < 3)
                def _():
                    chip_sum[step, :, columns] = summed.astype(bf16)

            @pl.when(step == 0)
            def _():
                if cut:
                    diag_a.start()
                diag_b.start()

            @pl.when(step == 1)
            def _():
                if cut:
                    plain_a.start()

            @pl.when(step == 2)
            def _():
                plain_b.start()

    def add(step, span, slot):
        rows = pl.ds(*span)
        chip_sum[step, rows, :] = (
            chip_sum[step, rows, :].astype(f32) + arrived[landing[slot], 0 : span[1], :].astype(f32)
        ).astype(bf16)

    def take(span, slot):
        total[pl.ds(*span), :] += arrived[landing[slot], 0 : span[1], :].astype(f32)

    def hand_on():
        if cut:
            diag_a.wait_recv()
            add(2, low, 0)
            last_b.start()
        diag_b.wait_recv()
        add(1, high, 1)
        last_a.start()

    def finish():
        if cut:
            plain_a.wait_recv()
            take(low, 2)
        plain_b.wait_recv()
        take(high, 3)
        if cut:
            last_b.wait_recv()
            take(low, 5)
        last_a.wait_recv()
        take(high, 4)

        @pl.loop(0, 4)
        def _(step):
            core_copy(step).wait_send()

        for copy in (diag_a, diag_b, plain_a, plain_b, last_a, last_b):
            if copy is not None:
                copy.wait_send()

    return for_sibling, for_chip, hand_on, finish


def sum_scratch(block, width, cut):
    return [
        pltpu.VMEM((block, width), f32),
        pltpu.VMEM((4, block, width), bf16),
        pltpu.VMEM((4, block, width), bf16),
        pltpu.VMEM((3, block, width), bf16),
        pltpu.VMEM((6 if cut else 3, block - cut, width), bf16),
        pltpu.SemaphoreType.DMA((SUM_COPIES,)),
        pltpu.SemaphoreType.DMA((SUM_COPIES,)),
    ]


def spread_scratch(block, width):
    return [
        pltpu.VMEM((block, width), bf16),
        pltpu.SemaphoreType.DMA((SPREAD_COPIES,)),
        pltpu.SemaphoreType.DMA((SPREAD_COPIES,)),
        pltpu.SemaphoreType.DMA,
    ]


def link_params(collective_id):
    return pltpu.CompilerParams(
        collective_id=collective_id, has_side_effects=True, vmem_limit_bytes=60 * 1024 * 1024
    )


def cost(flops, size):
    return pl.CostEstimate(flops=int(flops), bytes_accessed=int(size), transcendentals=0)


def row_scale(values):
    return lax.rsqrt(jnp.mean(values * values, -1, keepdims=True) + epsilon)


def front_kernel(
    team, teams, qkv_moves, ffn_moves, carry_bits, tokens_ref, query_ref, key_ref, value_ref, gate_ref, up_ref, small_ref, *refs,
):
    moved = len(carry_bits)
    (carried, refs) = (refs[0], refs[1:]) if moved else (None, refs)
    (normed_out, weights_out, both_out, small_out), refs = refs[:4], refs[4:]
    carried_out, refs = refs[:moved], refs[moved:]
    (tokens_all, mine, both_mine, gain,
    send_sems, recv_sems, local_sem, swap_send, swap_recv, swap_local, line_send, line_recv, small_send, small_recv,
    both_send, both_recv, both_local, out_sems, *carry_sems) = refs
    me = lax.axis_index(AXIS)
    mate, group = lax.rem(me, team), lax.div(me, team)
    devices = team * teams
    mates = [group * team + lax.rem(mate + k, team) for k in range(1, team)]
    above, below = lax.rem(me + team, devices), lax.rem(me + devices - team, devices)
    ffn_mates = [team_mate(me, (1, 2, 8), k) for k in range(team)]
    rows = mine.shape[1]
    swaps, line, small = Links(swap_send, swap_recv), Links(line_send, line_recv), Links(small_send, small_recv)
    both = Links(both_send, both_recv)
    for i, member, source, target, columns in qkv_moves:
        weight = (query_ref, key_ref, value_ref)[i]
        mine[member, :, target : target + columns] = weight[:, source : source + columns]
    greet(
        mates + [lax.rem(me + k * team, devices) for k in range(1, teams)]
        + [device for device, _ in ffn_mates[4:]]
    )

    def share(place):
        return pl.ds(pl.multiple_of(place * rows, rows), rows)

    swap_copies = [
        swaps.copy(k, mine.at[lax.rem(mate + k + 1, team)], weights_out.at[group, share(mate)], mates[k])
        for k in range(team - 1)
    ]
    crossing = [
        Links(*carry_sems).copy(i, carried, carried_out[i], flip_bit(me, bit)) for i, bit in enumerate(carry_bits)
    ]
    for copy in swap_copies:
        copy.start()
    keep = pltpu.make_async_copy(mine.at[mate], weights_out.at[group, share(mate)], swap_local)
    keep.start()
    small_out[me] = small_ref[...]

    others = [lax.rem(me + k * team, devices) for k in range(1, teams)]
    team_rows = pl.ds(pl.multiple_of(group * team, team), team)
    small_near = [
        small.copy(k, small_out.at[me], small_out.at[me], device) for k, device in enumerate(mates)
    ]
    small_far = [
        small.copy(team + k, small_out.at[team_rows], small_out.at[team_rows], device)
        for k, device in enumerate(others)
    ]
    for copy in small_near:
        copy.start()
    spread = spread_block(
        (1, 2, 4), HALF, tokens_ref, tokens_all, Links(send_sems, recv_sems), local_sem
    )
    for i, member, source, target, columns in ffn_moves:
        both_mine[i * team + member, :, target : target + columns] = (gate_ref, up_ref)[i][:, source : source + columns]

    def passed(slot, shard, device):
        return line.copy(slot, weights_out.at[shard], weights_out.at[shard], device)

    steps = teams - 1

    def up(step):
        return passed(step - 1, group - (step - 1), above)

    def down(step):
        return passed(steps + step - 1, group + (step - 1), below)

    def line_start(step):
        pl.when((group < teams - 1) & (group >= step - 1))(lambda: up(step).start())
        pl.when((group > 0) & (group + step - 1 < teams))(lambda: down(step).start())

    def line_wait(step):
        pl.when(group >= step)(lambda: up(step).wait_recv())
        pl.when(group + step < teams)(lambda: down(step).wait_recv())

    def line_sent(step):
        pl.when((group < teams - 1) & (group >= step - 1))(lambda: up(step).wait_send())
        pl.when((group > 0) & (group + step - 1 < teams))(lambda: down(step).wait_send())

    for copy in small_near:
        copy.wait_recv()
    for copy in small_far:
        copy.start()
    own_place = ffn_mates[0][1]
    both_copies = [
        both.copy(
            i * team + k, both_mine.at[i * team + ffn_mates[k][1]], both_out.at[i * team + own_place], ffn_mates[k][0]
        )
        for i in range(2) for k in range(1, team)
    ]
    for copy in both_copies:
        copy.start()
    both_keep = [
        pltpu.make_async_copy(both_mine.at[i * team + own_place], both_out.at[i * team + own_place], both_local.at[i])
        for i in range(2)
    ]
    for copy in both_keep:
        copy.start()
    for copy in swap_copies:
        copy.wait_recv()
    keep.wait()
    line_start(1)
    spread[0]()
    for copy in crossing:
        copy.start()
    for copy in small_far:
        copy.wait_recv()
    spread[1]()
    spread[2]()
    line_wait(1)
    line_start(2)
    spread[3]()
    spread[4]()
    width = tokens_all.shape[1]
    gains = width // devices
    for d in range(devices):
        gain[:, d * gains : (d + 1) * gains] = small_out[d, 0:1, 0:gains]
    for phase in spread[5:]:
        phase()
    block = tokens_ref.shape[0]

    def normed_copy(k):
        span = pl.ds(pl.multiple_of(k * block, block), block)
        return pltpu.make_async_copy(tokens_all.at[span], normed_out.at[span], out_sems.at[k])

    def norm_blocks(first, last):
        @pl.loop(first, last)
        def _(k):
            span = pl.ds(pl.multiple_of(k * block, block), block)
            values = tokens_all[span, :].astype(f32)
            tokens_all[span, :] = (values * row_scale(values) * gain[...]).astype(bf16)
            normed_copy(k).start()

    norm_blocks(0, 2)
    for step in range(2, teams):
        line_wait(step)
        if step < steps:
            line_start(step + 1)
        if step == 2:
            norm_blocks(2, team)
    for k in range(team):
        normed_copy(k).wait()
    for copy in both_copies:
        copy.wait_recv()
    for copy in both_keep:
        copy.wait()
    for copy in swap_copies + both_copies:
        copy.wait_send()
    for step in range(1, teams):
        line_sent(step)
    for copy in small_near + small_far:
        copy.wait_send()
    for copy in crossing:
        copy.wait()


def front(tokens, weights, small, teams, qkv_moves, ffn_moves, carried, carry_bits):
    block, width = tokens.shape
    team = 8
    rows, cols = weights[0].shape[0], 3 * width // team
    both_cols = weights[3].shape[1] // team
    devices = team * teams
    dma = pltpu.SemaphoreType.DMA
    shape = jax.ShapeDtypeStruct
    return pl.pallas_call(
        functools.partial(front_kernel, team, teams, qkv_moves, ffn_moves, carry_bits),
        out_shape=(
            shape((team * block, width), bf16),
            shape((teams, team * rows, cols), bf16),
            shape((2 * team, rows, both_cols), bf16),
            shape((devices,) + small.shape, f32),
        ) + tuple(shape(carried[0].shape, bf16) for _ in carry_bits),
        in_specs=[vmem] * 7 + [anywhere] * len(carried),
        out_specs=(anywhere, anywhere, anywhere, vmem) + (anywhere,) * len(carry_bits),
        scratch_shapes=[
            pltpu.VMEM((team * block, width), bf16), pltpu.VMEM((team, rows, cols), bf16),
            pltpu.VMEM((2 * team, rows, both_cols), bf16), pltpu.VMEM((1, width), f32),
        ]
        + spread_scratch(block, width)[1:]
        + [dma((team - 1,)), dma((team - 1,)), dma, dma((2 * teams,)), dma((2 * teams,)), dma((team + teams,)), dma((team + teams,))]
        + [dma((2 * team,)), dma((2 * team,)), dma((2,)), dma((team,))]
        + [dma((1,))] * (2 * len(carried)),
        compiler_params=link_params(1),
        cost_estimate=cost(0, 200e6),
        name="front",
    )(tokens, *weights, small, *carried)


def branch_kernel(
    carry, swap_bits, spread_bits, left_ref, right_ref, residual_ref, gain_ref, peak_ref, *refs,
):
    if carry:
        (both_own, both_y, both_z, down_own, down_y), refs = refs[:5], refs[5:]
        (h2_ref, out_ref, peak_out, gate_full, up_full, down_full), refs = refs[:6], refs[6:]
        (landed, together, swap_send, swap_recv, own, send_sems, recv_sems, local_sem,
         peak_in, peak_send, peak_recv, carry_send, carry_recv, carry_local) = refs
    else:
        (h2_ref, out_ref, peak_out), refs = refs[:3], refs[3:]
        (landed, together, swap_send, swap_recv, own, send_sems, recv_sems, local_sem,
         peak_in, peak_send, peak_recv) = refs
    me = lax.axis_index(AXIS)
    team, block, _ = landed.shape
    bits = [1 << k for k in range(peak_in.shape[0])]
    mates = [team_mate(me, swap_bits, k) for k in range(team)]
    greet([device for device, _ in mates[1:]] + [flip_bit(me, bit) for bit in bits if bit not in swap_bits])
    own_place = mates[0][1]

    def rows_at(place):
        return pl.ds(pl.multiple_of(place * block, block), block)

    swap_copies = [
        Links(swap_send, swap_recv).copy(k, left_ref.at[rows_at(mates[k][1])], landed.at[own_place], mates[k][0])
        for k in range(1, team)
    ]
    for copy in swap_copies:
        copy.start()
    peaks = Links(peak_send, peak_recv)

    def peak_copy(k):
        return peaks.copy(k, peak_out, peak_in.at[k], flip_bit(me, bits[k]))

    def peak_step(k):
        if k:
            peak_copy(k - 1).wait()
            peak_out[...] = jnp.maximum(peak_out[...], peak_in[k - 1])
        if k < len(bits):
            peak_copy(k).start()

    if carry:
        carried = Links(carry_send, carry_recv)
        high, middle = bit_of(me, 16), bit_of(me, 4)
        by_y, by_z = flip_bit(me, 4), flip_bit(me, 16)

        def rows_of(part, flip_z, flip_y):
            z, y = lax.rem(high + flip_z, 2), lax.rem(middle + flip_y, 2)
            return pl.ds(pl.multiple_of(z * 16 + part * 8 + y * 4, 4), 4)

        early = both_z.shape[0] // 4

        def piece(source, half):
            return source.at[pl.ds(half * 4, 4)]

        def placed(half, flips):
            return (gate_full, up_full)[half // 2].at[rows_of(half % 2, *flips)]

        def unit(flip_z, flip_y):
            return lax.rem(high + flip_z, 2) * 2 + lax.rem(middle + flip_y, 2)

        kept = []
        for source, flips, halves in ((both_own, (0, 0), 4), (both_y, (0, 1), 4), (both_z, (1, 0), early)):
            for half in range(halves):
                kept.append((piece(source, half), placed(half, flips)))
        kept.append((down_own, down_full.at[unit(0, 0)]))
        kept.append((down_y, down_full.at[unit(0, 1)]))
        kept = [pltpu.make_async_copy(a, b, carry_local.at[i]) for i, (a, b) in enumerate(kept)]
        up_z = [
            carried.copy(half, piece(both_own, half), placed(half, (0, 0)), by_z) for half in range(early, 4)
        ]
        early_yz = [
            carried.copy(4 + half, piece(both_z, half), placed(half, (1, 0)), by_y) for half in range(early)
        ]
        up_yz = [
            carried.copy(4 + half, placed(half, (1, 0)), placed(half, (1, 0)), by_y) for half in range(early, 4)
        ]
        for copy in up_z + kept:
            copy.start()

    peak_out[...] = peak_ref[...]
    peak_step(0)
    landed[own_place] = left_ref[rows_at(own_place), :]
    for copy in swap_copies:
        copy.wait_recv()
    if carry:
        for copy in early_yz:
            copy.start()
    heads = landed.shape[2] // HEAD_DIM
    for b in range(team):
        for g in range(heads):
            first = (g * team + b) * HEAD_DIM
            together[:, first : first + HEAD_DIM] = landed[b, :, g * HEAD_DIM : (g + 1) * HEAD_DIM]
    tile = 512

    @pl.loop(0, own.shape[1] // tile)
    def _(column):
        columns = pl.ds(pl.multiple_of(column * tile, tile), tile)
        h2_ref[:, columns] = residual_ref[:, columns].astype(f32) + contract(
            together[...], right_ref[:, columns], 1, 0
        )

    h2 = h2_ref[...]
    own[...] = (h2 * row_scale(h2) * gain_ref[...]).astype(bf16)
    spread = spread_block(spread_bits, BRANCH_CUT, own, out_ref, Links(send_sems, recv_sems), local_sem)
    spread[0]()
    if carry:
        for over, on in zip(up_z, up_yz):
            over.wait_recv()
            on.start()
    for k, phase in enumerate(spread[1:-1]):
        phase()
        if k < len(bits):
            peak_step(k + 1)
    for k in range(len(spread) - 2, len(bits)):
        peak_step(k + 1)
    spread[-1]()
    for copy in swap_copies:
        copy.wait_send()
    if carry:
        for copy in kept:
            copy.wait()
        for copy in early_yz + up_yz:
            copy.wait_recv()
        for copy in up_z + early_yz + up_yz:
            copy.wait_send()


def branch(left, right, residual, gain, peak, carry, swap_bits, spread_bits, bit_count):
    block, width = residual.shape
    dma = pltpu.SemaphoreType.DMA
    shape = jax.ShapeDtypeStruct
    out_shape = [shape((block, width), f32), shape((8 * block, width), bf16), shape((8, 128), f32)]
    scratch = [pltpu.VMEM((8, block, left.shape[1]), bf16), pltpu.VMEM((block, width), bf16), dma((8,)), dma((8,))]
    scratch += spread_scratch(block, width)
    scratch += [pltpu.VMEM((bit_count, 8, 128), f32), dma((bit_count,)), dma((bit_count,))]
    if carry:
        out_shape += [
            shape((32,) + carry[0].shape[1:], bf16), shape((32,) + carry[0].shape[1:], bf16),
            shape((4,) + carry[3].shape, bf16),
        ]
        scratch += [dma((8,)), dma((8,)), dma((14,))]
    return pl.pallas_call(
        functools.partial(branch_kernel, bool(carry), swap_bits, spread_bits),
        out_shape=tuple(out_shape),
        in_specs=[vmem] * (5 + len(carry)),
        out_specs=tuple([vmem, anywhere, vmem] + [anywhere] * (len(out_shape) - 3)),
        scratch_shapes=scratch,
        compiler_params=link_params(2),
        cost_estimate=cost(16 * block * left.shape[1] * width, 300e6),
        name="attention_branch",
    )(left, right, residual, gain, peak, *carry)


def norm_back(values, gain, upstream):
    scaled = upstream * gain
    scale = row_scale(values)
    inner = jnp.mean(scaled * values, -1, keepdims=True)
    return scale * scaled - scale * scale * scale * values * inner


def ffn_back_kernel(
    cross, sum_bits, swap_bits, gate_ref, up_ref, gate_w_ref, up_w_ref, normed_ref, out_w_ref, h2_ref, cot_ref, gain_ref, *refs,
):
    (part_ref, over_ref, refs) = (refs[0], refs[1], refs[2:]) if cross else (None, None, refs)
    (residual_ref, branch_ref, heads_out, d_up_out, d_gate_own), refs = refs[:5], refs[5:]
    (d_gate_in, part_in, over_in), refs = (refs[:3], refs[3:]) if cross else ((None,) * 3, refs)
    (total, to_core, from_core, chip_sum, arrived, sum_send, sum_recv,
     swap_send, swap_recv, local_sem, stage, stage_sems, own_sems, *more) = refs
    if cross:
        cross_send, cross_recv = more
        crossing = Links(cross_send, cross_recv)
    else:
        (stage_gate,) = more
    me = lax.axis_index(AXIS)
    block, width = total.shape
    team = 1 << len(swap_bits)
    mates = [team_mate(me, swap_bits, k) for k in range(team)]
    greet(
        [device for device, _ in mates[1:]] + [flip_bit(me, bit) for bit in sum_bits if bit not in swap_bits]
        + ([flip_bit(me, 16)] if cross else [])
    )

    def product(place, columns):
        rows = pl.ds(pl.multiple_of(place * block, block), block)
        return contract(gate_ref[rows, :], gate_w_ref[columns, :], 1, 1) + contract(
            up_ref[rows, :], up_w_ref[columns, :], 1, 1
        )

    side, columns_ff = stage.shape[1:]
    count = width // side
    y_side, by_y = bit_of(me, 4), flip_bit(me, 4)
    if cross:
        part_copy = crossing.copy(count // 2, part_ref, part_in, by_y)
        over_copy = crossing.copy(count // 2 + 1, over_ref, over_in, flip_bit(me, 16))
        part_copy.start()

    def parked(i, part):
        row = i * side
        rows = pl.ds(pl.multiple_of(lax.rem(row, block), 16), side)
        return from_core.at[lax.div(row, block), rows, pl.ds(part * columns_ff, columns_ff)]

    def cross_copy(i):
        return crossing.copy(i, parked(i, 0), d_gate_in.at[i], by_y)

    def own_copy(i):
        return pltpu.make_async_copy(parked(i, 1), d_gate_own.at[i], own_sems.at[i])

    def tile_of(step):
        if not cross:
            return step
        theirs = step < count // 2
        return jnp.where(theirs, 2 * step + 1 - y_side, 2 * step - count + y_side)

    def up_copy(step):
        span = pl.ds(pl.multiple_of(tile_of(step) * side, side), side)
        slot = lax.rem(step, 2)
        return pltpu.make_async_copy(stage.at[slot], d_up_out.at[span], stage_sems.at[slot])

    def gate_copy(step):
        span = pl.ds(pl.multiple_of(step * side, side), side)
        slot = lax.rem(step, 2)
        return pltpu.make_async_copy(stage_gate.at[slot], d_gate_own.at[span], own_sems.at[slot])

    def gradients(first, last):
        @pl.loop(first, last)
        def _(step):
            @pl.when(step >= 2)
            def _():
                up_copy(step - 2).wait()
                if not cross:
                    gate_copy(step - 2).wait()

            columns = normed_ref[:, pl.ds(pl.multiple_of(tile_of(step) * side, side), side)]
            stage[lax.rem(step, 2)] = contract(columns, up_ref[...], 0, 0).astype(bf16)
            up_copy(step).start()
            tile = contract(columns, gate_ref[...], 0, 0).astype(bf16)
            if not cross:
                stage_gate[lax.rem(step, 2)] = tile
                gate_copy(step).start()
                return

            @pl.when(step < count // 2)
            def _():
                parked(step, 0)[...] = tile
                cross_copy(step).start()

            @pl.when(step >= count // 2)
            def _():
                parked(step - count // 2, 1)[...] = tile
                own_copy(step - count // 2).start()

    for_sibling, for_chip, hand_on, finish = sum_block(
        sum_bits, HALF, False, product, total, to_core, from_core, chip_sum, arrived, Links(sum_send, sum_recv)
    )
    for_sibling()
    for_chip()
    if cross:
        over_copy.start()
    gradients(0, 1)
    hand_on()
    gradients(1, count - 2)
    finish()
    residual = cot_ref[...].astype(f32) + norm_back(h2_ref[...], gain_ref[...], total[...])
    residual_ref[...] = residual
    branch_ref[...] = residual.astype(bf16)
    tile, share = team * HEAD_DIM, width // team
    for g in range(width // tile):
        heads = contract(branch_ref[...], out_w_ref[g * tile : (g + 1) * tile, :], 1, 1).astype(bf16)
        for b in range(team):
            first = b * share + g * HEAD_DIM
            to_core[0, :, first : first + HEAD_DIM] = heads[:, b * HEAD_DIM : (b + 1) * HEAD_DIM]
    own_place = mates[0][1]
    own_rows = pl.ds(pl.multiple_of(own_place * block, block), block)
    def heads_of(place):
        return to_core.at[0, :, pl.ds(pl.multiple_of(place * share, share), share)]

    swap_copies = [
        Links(swap_send, swap_recv).copy(k, heads_of(mates[k][1]), heads_out.at[own_rows], mates[k][0])
        for k in range(1, team)
    ]
    keep = pltpu.make_async_copy(heads_of(own_place), heads_out.at[own_rows], local_sem)
    for copy in swap_copies + [keep]:
        copy.start()
    gradients(count - 2, count)
    for copy in swap_copies:
        copy.wait_recv()
    for copy in swap_copies:
        copy.wait_send()
    keep.wait()
    for step in range(count - 2, count):
        up_copy(step).wait()
        if not cross:
            gate_copy(step).wait()
    if cross:
        part_copy.wait()
        over_copy.wait()

        @pl.loop(0, count // 2)
        def _(i):
            own_copy(i).wait()
            cross_copy(i).wait()


def ffn_back(gate, up, gate_w, up_w, normed, out_w, h2, cot, gain, part, side, sum_bits, swap_bits):
    block, width = h2.shape
    shape = jax.ShapeDtypeStruct
    dma = pltpu.SemaphoreType.DMA
    ff_cols, cross = gate.shape[1], side % 128 == 0
    side = side if cross else 256
    tiles = width // side // 2
    if cross:
        d_gate = (shape((tiles, side, ff_cols), bf16),) * 2 + (shape(part[0].shape, bf16),) * 2
        more = [dma((tiles + 2,)), dma((tiles + 2,))]
    else:
        d_gate, more = (shape((width, ff_cols), bf16),), [pltpu.VMEM((2, side, ff_cols), bf16)]
    return pl.pallas_call(
        functools.partial(ffn_back_kernel, cross, sum_bits, swap_bits),
        out_shape=(
            shape((block, width), f32), shape((block, width), bf16), shape((8 * block, width // 8), bf16),
            shape((width, ff_cols), bf16),
        ) + d_gate,
        in_specs=[vmem] * 9 + [anywhere] * len(part),
        out_specs=(vmem, vmem) + (anywhere,) * (2 + len(d_gate)),
        scratch_shapes=sum_scratch(block, width, HALF)
        + [dma((8,)), dma((8,)), dma]
        + [pltpu.VMEM((2, side, ff_cols), bf16), dma((2,)), dma((tiles,))]
        + more,
        compiler_params=link_params(3),
        cost_estimate=cost(96 * block * ff_cols * width, 200e6),
        name="ffn_back",
    )(gate, up, gate_w, up_w, normed, out_w, h2, cot, gain, *part)


def last_sums_kernel(
    carry_bits, sum_bits, ffn_bits, left_ref, other_ref, right_ref, tokens_ref, gain_ref, residual_ref, hidden_ref,
    down_ref, h2_ref, gate_ref, *refs,
):
    moved = len(carry_bits)
    carried, (out_ref, mixed_ref, gate_out), refs = refs[:moved], refs[moved : moved + 3], refs[moved + 3 :]
    carried_out, scratch = refs[:moved], refs[moved:]
    if moved:
        carry_sems, scratch = scratch[-2:], scratch[:-2]
    (swap_send, swap_recv, swap_local), scratch = scratch[-3:], scratch[:-3]
    count = len(scratch) // 2
    me = lax.axis_index(AXIS)
    total, ffn_total = scratch[0], scratch[count]
    block = total.shape[0]
    mates = [team_mate(me, ffn_bits, k) for k in range(8)]
    partners = [flip_bit(me, bit) for bit in sum_bits if bit not in ffn_bits]
    greet(partners + [device for device, _ in mates[1:]] + [flip_bit(me, bit) for bit in carry_bits])
    crossing = [
        Links(*carry_sems).copy(i, carried[i], carried_out[i], flip_bit(me, bit)) for i, bit in enumerate(carry_bits)
    ]
    for copy in crossing:
        copy.start()
    swaps, own_place = Links(swap_send, swap_recv), mates[0][1]
    swap_copies = [
        swaps.copy(k, gate_ref.at[mates[k][1]], gate_out.at[own_place], mates[k][0]) for k in range(1, 8)
    ]
    keep = pltpu.make_async_copy(gate_ref.at[own_place], gate_out.at[own_place], swap_local)

    def rows_of(place):
        return pl.ds(pl.multiple_of(place * block, block), block)

    def product(place, columns):
        rows = rows_of(place)
        middle = left_ref.shape[1]
        return contract(left_ref[rows, :], right_ref[columns, 0:middle], 1, 1) + contract(
            other_ref[rows, :], right_ref[columns, middle : 2 * middle], 1, 1
        )

    def ffn_product(place, columns):
        return contract(hidden_ref[rows_of(place), :], down_ref[:, columns], 1, 0)

    first = sum_block(sum_bits, LAST_CUT, False, product, *scratch[: count - 2], Links(*scratch[count - 2 : count]))
    second = sum_block(ffn_bits, HALF, True, ffn_product, *scratch[count:-2], Links(*scratch[-2:]))
    run(first[:2])
    run(second[:2])
    for copy in swap_copies + [keep]:
        copy.start()
    for one, other in zip(first[2:], second[2:]):
        one()
        other()
    out_ref[...] = residual_ref[...] + norm_back(
        tokens_ref[...].astype(f32), gain_ref[...], total[...]
    )
    mixed_ref[...] = (h2_ref[...] + ffn_total[...]).astype(bf16)
    for copy in swap_copies:
        copy.wait_recv()
    for copy in swap_copies:
        copy.wait_send()
    keep.wait()
    for copy in crossing:
        copy.wait()


def last_sums(left, other, right, tokens, gain, residual, hidden, down, h2, d_gate, carry, carry_bits, sum_bits, ffn_bits):
    block, width = tokens.shape
    return pl.pallas_call(
        functools.partial(last_sums_kernel, carry_bits, sum_bits, ffn_bits),
        out_shape=(
            jax.ShapeDtypeStruct((block, width), f32), jax.ShapeDtypeStruct((block, width), bf16),
            jax.ShapeDtypeStruct(d_gate.shape, bf16),
        ) + tuple(jax.ShapeDtypeStruct(x.shape, x.dtype) for x in carry),
        in_specs=[vmem] * 9 + [anywhere] * (1 + len(carry)),
        out_specs=(vmem, vmem, anywhere) + (anywhere,) * len(carry),
        scratch_shapes=sum_scratch(block, width, LAST_CUT) + sum_scratch(block, width, HALF)
        + [pltpu.SemaphoreType.DMA((8,)), pltpu.SemaphoreType.DMA((8,)), pltpu.SemaphoreType.DMA]
        + [pltpu.SemaphoreType.DMA((1,))] * (2 * len(carry)),
        compiler_params=link_params(4),
        cost_estimate=cost(16 * block * right.size // 8, 300e6),
        name="last_sums",
    )(left, other, right, tokens, gain, residual, hidden, down, h2, d_gate, *carry)


def exchange_kernel(teams, sources, *refs):
    mine, landed, (send_sems, recv_sems, local_sems) = refs[:sources], refs[sources : 2 * sources], refs[2 * sources :]
    me = lax.axis_index(AXIS)
    members = mine[0].shape[0]
    links = Links(send_sems, recv_sems)
    greeted = {}
    for bits in teams:
        for k in range(1, members):
            device, _ = team_mate(me, bits, k)
            greeted[tuple(sorted(bit for j, bit in enumerate(bits) if (k >> j) % 2))] = device
    greet(list(greeted.values()))
    copies, kept = [], []
    for i, (source, target, bits) in enumerate(zip(mine, landed, teams)):
        own = team_mate(me, bits, 0)[1]
        kept.append(pltpu.make_async_copy(source.at[own], target.at[own], local_sems.at[i]))
        for k in range(1, members):
            device, place = team_mate(me, bits, k)
            copies.append(links.copy(i * members + k, source.at[place], target.at[own], device))
    for copy in copies + kept:
        copy.start()
    for copy in copies:
        copy.wait()
    for copy in kept:
        copy.wait()


def exchange(parts, teams):
    dma = pltpu.SemaphoreType.DMA
    slots = len(parts) * parts[0].shape[0]
    return pl.pallas_call(
        functools.partial(exchange_kernel, teams, len(parts)),
        out_shape=tuple(jax.ShapeDtypeStruct(part.shape, part.dtype) for part in parts),
        in_specs=[vmem] * len(parts),
        out_specs=tuple([vmem] * len(parts)),
        scratch_shapes=[dma((slots,)), dma((slots,)), dma((len(parts),))],
        compiler_params=link_params(5),
        cost_estimate=cost(1e6, 40e6),
        name="exchange",
    )(*parts)


def home_kernel(places, gain_of, sources, *refs):
    count = len(places)
    kinds = max(gain_of) + 1
    parts, weights, gains = refs[:sources], refs[sources : sources + count], refs[sources + count : sources + count + kinds]
    outs, gain_outs = refs[-count - kinds : -kinds], refs[-kinds:]
    totals = [jnp.zeros(gain.shape, f32) for gain in gains]
    for i, (out, weight) in enumerate(zip(outs, weights)):
        for source, member, first, target, columns in places[i]:
            out[:, target : target + columns] = parts[source][member, :, first : first + columns].astype(f32)
        for first in range(0, out.shape[1], 1024):
            product = out[:, first : first + 1024] * weight[:, first : first + 1024].astype(f32)
            totals[gain_of[i]] += jnp.sum(product, 1, keepdims=True)
    for gain, total, out in zip(gains, totals, gain_outs):
        out[...] = jnp.broadcast_to(total / gain[...], (out.shape[1], 128)).T[0:1, :]


def home(parts, weights, gains, gain_of, places):
    shape = jax.ShapeDtypeStruct
    count = len(weights)
    gains = [gain.astype(f32).reshape(-1, 1) for gain in gains]
    return pl.pallas_call(
        functools.partial(home_kernel, places, gain_of, len(parts)),
        out_shape=tuple(shape(w.shape, f32) for w in weights) + tuple(shape((1, g.shape[0]), f32) for g in gains),
        in_specs=[vmem] * (len(parts) + count + len(gains)),
        out_specs=tuple([vmem] * (count + len(gains))),
        compiler_params=pltpu.CompilerParams(vmem_limit_bytes=40 * 1024 * 1024),
        cost_estimate=cost(1e6, 30e6),
        name="home",
    )(*parts, *weights, *gains)


def body(
    tokens, block_of, clip_limit, norm_attn, w_query, w_key, w_value, w_out,
    norm_ffn, w_gate, w_up, w_down, cotangent,
):
    tok_rows, width = tokens.shape
    devices = lax.axis_size(AXIS)
    team = SEQ // tok_rows
    teams = devices // team
    head_total = width // HEAD_DIM
    heads = head_total // team
    head_cols = heads * HEAD_DIM
    ff_rows = w_down.shape[0]
    weight_rows = w_gate.shape[0]
    ff_cols = w_gate.shape[1] // team
    device = lax.axis_index(AXIS)
    mate = device % team
    bit_count = devices.bit_length() - 1
    attn_bits, ffn_bits = (1, 2, 4), (1, 2, 8)
    data_bits = [4] + [1 << k for k in range(4, bit_count)]
    in_team = [[g * team + b for b in range(team)] for g in range(teams)]
    across = [[g * team + b for g in range(teams)] for b in range(team)]
    ffn_team = [
        [g * 16 + z * 8 + y * 4 + c for z in range(2) for c in range(4)]
        for g in range(devices // 16)
        for y in range(2)
    ]

    def flip(x, bit):
        return lax.ppermute(x, AXIS, [(i, i ^ bit) for i in range(devices)])

    def gather_across(x):
        return lax.all_gather(x, AXIS, axis=0, tiled=True, axis_index_groups=across)

    def scatter_across(x):
        return lax.psum_scatter(
            x.astype(bf16), AXIS, scatter_dimension=0, tiled=True, axis_index_groups=across
        )

    def dim_of(bit):
        return bit_count - bit.bit_length()

    def data_pieces(x):
        pieces = {0: x}
        for bit in reversed(data_bits):
            for key in list(pieces):
                pieces[key | bit] = flip(pieces[key], bit)
        return pieces

    def place_pieces(pieces, dims, shape):
        total = jnp.zeros(shape, bf16)
        for key, piece in pieces.items():
            start = [0] * len(shape)
            size = list(shape)
            for bit in data_bits:
                start[dims[bit]] = ((device // bit) + (1 if key & bit else 0)) % 2
                size[dims[bit]] = 1
            total = lax.dynamic_update_slice(total, piece.reshape(size), start)
        return total

    def after_bit(dims, bit):
        return {b: d - (d > dims[bit]) for b, d in dims.items() if b != bit}

    def data_sum(x, dims, bits):
        for bit in bits:
            mine = (device // bit) % 2
            keep = lax.dynamic_index_in_dim(x, mine, dims[bit], False)
            sent = flip(lax.dynamic_index_in_dim(x, 1 - mine, dims[bit], False), bit)
            x = (keep.astype(f32) + sent.astype(f32)).astype(bf16)
            dims = after_bit(dims, bit)
        return x

    row_dims = {bit: dim_of(bit) for bit in data_bits}
    row_shape = (2,) * bit_count
    unit_dims = {bit: i for i, bit in enumerate(reversed(data_bits))}
    unit_shape = (2,) * len(data_bits)

    def tie(*values):
        return lax.optimization_barrier(values)

    qkv_moves = tuple(
        (i, b, (g * team + b) * HEAD_DIM, (3 * (g // 2) + i) * PAIR + (g % 2) * HEAD_DIM, HEAD_DIM)
        for i in range(3) for g in range(heads) for b in range(team)
    )
    ffn_units = tuple(
        (z * 4 + c, (2 * h + y) * ff_rows, (h * 16 + z * 8 + y * 4 + c) * ff_rows)
        for h in range(devices // 16) for z in range(2) for y in range(2) for c in range(4)
    )
    ffn_moves = tuple(
        (i, member, source, target, ff_rows)
        for i in range(2) for member, target, source in ffn_units
    )
    gain_row = jnp.concatenate([norm_attn, norm_ffn]).astype(f32)
    gain_row = jnp.pad(gain_row, (0, 128 - 2 * weight_rows)).reshape(1, 128)
    block_rows = block_of.astype(f32).reshape(tok_rows // 128, 128)
    small = jnp.concatenate([gain_row, block_rows, jnp.zeros((7 - tok_rows // 128, 128), f32)])
    ahead = data_bits == [4, 16]
    normed_attn, qkv_w, both_mine, gathered, *down_moved = front(
        tokens, (w_query, w_key, w_value, w_gate, w_up), small, teams, qkv_moves, ffn_moves,
        [w_down] if ahead else [], (4,) if ahead else (),
    )
    qkv_w = qkv_w.reshape(width, 3 * head_cols)
    gain_attn = gathered[:, 0, :weight_rows].reshape(1, width)
    gain_ffn = gathered[:, 0, weight_rows : 2 * weight_rows].reshape(1, width)
    blocks = lax.dynamic_slice_in_dim(gathered, device - mate, team, 0)
    blocks = blocks[:, 1 : 1 + tok_rows // 128].astype(jnp.int32).reshape(SEQ)
    row_blocks, col_blocks = blocks.reshape(1, SEQ), blocks.reshape(SEQ, 1)
    both_mine, qkv_w, out_mine = tie(both_mine, qkv_w, w_out)
    out_w = lax.all_gather(out_mine, AXIS, axis=0, tiled=True)

    def whole_rows(mine):
        shape = row_shape + (weight_rows, ff_cols)
        return place_pieces(data_pieces(mine), row_dims, shape).reshape(width, ff_cols)

    cosine, sine = rope_tables(SEQ, PAIR)
    if data_bits == [4, 16]:
        carry = [both_mine, flip(both_mine, 4), flip(both_mine[: 4 * EARLY_HALVES], 16), w_down, *down_moved]
    else:
        carry = []
    query, key, value, attended, lse, peak = attend_forward(
        normed_attn, qkv_w, cosine, sine, row_blocks, col_blocks
    )
    cot_mine = cotangent
    peaks = jnp.where(
        (jnp.arange(head_total) % team) == mate, jnp.repeat(peak[0, :heads], team), -jnp.inf
    )
    peaks = jnp.broadcast_to(jnp.pad(peaks, (0, 128 - head_total))[None], (8, 128))
    if carry:
        carry[1], carry[2], attended, down_sent, cot_mine = tie(carry[1], carry[2], attended, w_down, cotangent)
        over = flip(down_sent, 16)
    after_attn, normed_ffn, peaks, *full = branch(
        attended, out_w, tokens, gain_ffn, peaks, carry, attn_bits, ffn_bits, bit_count
    )
    head_peak = peaks[0, :head_total]
    if carry:
        normed_ffn, over = tie(normed_ffn, over)
    if carry:
        gate_w, up_w = (w.reshape(width, ff_cols) for w in full[:2])
        z_side, y_side = (device // 16) % 2, (device // 4) % 2
        full_down = lax.dynamic_update_slice(full[2], over[None], ((1 - z_side) * 2 + y_side, 0, 0))
        down_w = lax.dynamic_update_slice(
            full_down, flip(over, 4)[None], ((1 - z_side) * 2 + 1 - y_side, 0, 0)
        ).reshape(ff_cols, width)
    else:
        gate_w, up_w = whole_rows(both_mine[:team]), whole_rows(both_mine[team:])
        down_w = place_pieces(
            data_pieces(w_down), unit_dims, unit_shape + (ff_rows, width)
        ).reshape(ff_cols, width)
    gate_pre = contract(normed_ffn, gate_w, 1, 0)
    up_pre = contract(normed_ffn, up_w, 1, 0)
    sigmoid_gate = jax.nn.sigmoid(gate_pre)
    silu_gate = gate_pre * sigmoid_gate
    hidden = (silu_gate * up_pre).astype(bf16)

    team_cot = lax.all_gather(cot_mine, AXIS, axis=0, tiled=True, axis_index_groups=ffn_team)
    d_down = contract(hidden, team_cot, 0, 0).astype(bf16).reshape(unit_shape + (ff_rows, width))
    team_cot, d_down = tie(team_cot, d_down)
    d_hidden = contract(team_cot, down_w, 1, 1)
    grad_gate = (d_hidden * up_pre * sigmoid_gate * (1.0 + gate_pre * (1.0 - sigmoid_gate))).astype(bf16)
    grad_up = (d_hidden * silu_gate).astype(bf16)

    unit_rest, row_rest = after_bit(unit_dims, data_bits[0]), after_bit(row_dims, data_bits[0])
    row_values = (weight_rows, ff_cols)
    crosses = data_bits == [4, 16]
    if crosses:
        y_side, z_side = (device // 4) % 2, (device // 16) % 2
        kept = lax.dynamic_index_in_dim(d_down, y_side, unit_dims[4], False)
        sent = lax.dynamic_index_in_dim(d_down, 1 - y_side, unit_dims[4], False)
        mine, theirs = (lax.dynamic_index_in_dim(kept, z, 0, False) for z in (z_side, 1 - z_side))
        to_mine, to_theirs = (lax.dynamic_index_in_dim(sent, z, 0, False) for z in (z_side, 1 - z_side))
        theirs = (theirs.astype(f32) + flip(to_theirs, 4).astype(f32)).astype(bf16)
        grad_gate, theirs = tie(grad_gate, theirs)
        beside = [to_mine, theirs]
    else:
        beside = []
    d_residual, branch_mine, grad_attended, d_up, *d_gate = ffn_back(
        grad_gate, grad_up, gate_w, up_w, normed_ffn, out_w, after_attn, cotangent, gain_ffn, beside, 4 * weight_rows,
        ffn_bits, attn_bits,
    )
    if crosses:
        d_down = mine.astype(f32) + d_gate[2].astype(f32) + d_gate[3].astype(f32)
        d_gate = (d_gate[0].astype(f32) + d_gate[1].astype(f32)).astype(bf16)
        d_gate = d_gate.reshape((2,) * (bit_count - 1) + row_values)
    else:
        d_down = data_sum(d_down, unit_dims, data_bits[:1])
        d_gate = data_sum(d_gate[0].reshape(row_shape + row_values), row_dims, data_bits[:1])
    if not crosses:
        d_down = data_sum(d_down, unit_rest, data_bits[1:]).astype(f32)
    grad_attended, d_gate = tie(grad_attended, d_gate)
    d_gate = data_sum(d_gate, row_rest, data_bits[1:])
    branch_grad = lax.all_gather(branch_mine, AXIS, axis=0, tiled=True, axis_index_groups=in_team)

    def heads_back(pair):
        return attend_backward(
            pair, query, key, value, grad_attended, lse, cosine, sine, row_blocks, col_blocks, normed_attn
        )

    grad_pairs, shares = [None] * (heads // 2), [None] * (heads // 2)
    grad_pairs[0], share = heads_back(0)
    grad_attended, d_gate, d_up, share, branch_grad = tie(grad_attended, d_gate, d_up, share, branch_grad)
    shares[0] = scatter_across(share)
    d_up = data_sum(d_up.reshape(row_shape + row_values), row_dims, data_bits[:1])
    for p in range(1, heads // 2):
        grad_pairs[p], share = heads_back(p)
        grad_pairs[p], share, d_up = tie(grad_pairs[p], share, d_up)
        shares[p] = scatter_across(share)
    sent, sent_bits = [], ()
    if crosses:
        kept_up = lax.dynamic_index_in_dim(d_up, z_side, row_rest[16], False)
        sent, sent_bits = [lax.dynamic_index_in_dim(d_up, 1 - z_side, row_rest[16], False)], (16,)
        kept_up, sent[0] = (d.reshape(team, weight_rows, ff_cols) for d in (kept_up, sent[0]))
    else:
        d_up = data_sum(d_up, row_rest, data_bits[1:])
    grad_pairs[0], shares[0] = tie(grad_pairs[0], shares[0])
    d_gate = d_gate.reshape(team, weight_rows, ff_cols)
    d_tokens, mixed, d_gate, *landed = last_sums(
        *grad_pairs, qkv_w, tokens, gain_attn, d_residual, hidden, down_w, after_attn, d_gate, sent, sent_bits,
        attn_bits, ffn_bits,
    )
    if crosses:
        d_up = (kept_up.astype(f32) + landed[0].astype(f32)).astype(bf16)
    d_tokens, attended = tie(d_tokens, attended)
    out_part = contract(attended, branch_grad, 0, 0)
    if weight_rows == HEAD_DIM:
        d_out = scatter_across(out_part).astype(f32)
    else:
        spread = jnp.where(
            (jnp.arange(team) == mate)[None, :, None, None],
            out_part.reshape(heads, 1, HEAD_DIM, width), 0.0,
        ).reshape(width, width)
        d_out = lax.psum_scatter(spread, AXIS, scatter_dimension=0, tiled=True)
    places = [[], [], []]
    for i, b, source, target, columns in qkv_moves:
        places[i].append((target // (3 * PAIR), b, target % (3 * PAIR), source, columns))
    places += [
        [(heads // 2 + i, member, target, source, ff_rows) for member, target, source in ffn_units] for i in range(2)
    ]
    shares = [share.reshape(team, weight_rows, 3 * PAIR) for share in shares]
    *shares, d_up = exchange(
        shares + [d_up.reshape(team, weight_rows, ff_cols)], (attn_bits,) * (heads // 2) + (ffn_bits,)
    )
    d_query, d_key, d_value, d_gate, d_up, d_norm_attn, d_norm_ffn = home(
        shares + [d_gate, d_up], (w_query, w_key, w_value, w_gate, w_up), (norm_attn, norm_ffn), (0, 0, 0, 1, 1),
        tuple(tuple(p) for p in places),
    )
    d_norm_attn, d_norm_ffn = d_norm_attn[0], d_norm_ffn[0]
    clip_value = clip_limit.astype(f32)
    factor = jnp.sqrt(clip_value / jnp.maximum(head_peak, clip_value))
    factors = jnp.repeat(factor, HEAD_DIM)[None, :]
    clipped_query = (w_query.astype(f32) * factors).astype(bf16)
    clipped_key = (w_key.astype(f32) * factors).astype(bf16)
    return (
        mixed, d_tokens, d_norm_attn, d_query, d_key, d_value, d_out, d_norm_ffn,
        d_gate, d_up, d_down, head_peak, clipped_query, clipped_key,
    )


def solution(mesh):
    rows, whole = P(AXIS, None), P(AXIS)
    return jax.shard_map(
        body,
        mesh=mesh,
        in_specs=(rows, whole, P(), whole, rows, rows, rows, rows, whole, rows, rows, rows, rows),
        out_specs=(
            rows, rows, whole, rows, rows, rows, rows, whole, rows, rows, rows, P(), rows, rows,
        ),
        check_vma=False,
    )
```

```python
import functools

import jax
import jax.numpy as jnp
import numpy as np
from jax import lax
from jax.experimental import pallas as pl
from jax.experimental.pallas import tpu as pltpu
from jax.sharding import PartitionSpec as P

HEAD_DIM = 64
SEQ = 2048
BLOCK = 256
HALF = 128
LAST_CUT = 0
EARLY_HALVES = 3
BRANCH_CUT = 128
AXIS = "fsdp"
MESH = pl.DeviceIdType.MESH

epsilon = 1e-05
rope_base = 130000.0
bf16 = jnp.bfloat16
f32 = jnp.float32
vmem = pl.BlockSpec(memory_space=pltpu.VMEM)
anywhere = pl.BlockSpec(memory_space=pl.ANY)


def contract(left, right, left_dim, right_dim):
    return lax.dot_general(
        left, right, (((left_dim,), (right_dim,)), ((), ())), preferred_element_type=f32
    )


def rope_tables(length, width):
    half_dim = HEAD_DIM // 2
    inverse = rope_base ** (-np.arange(half_dim) * 2.0 / HEAD_DIM)
    angles = (np.arange(length, dtype=np.float32)[:, None] * inverse.astype(np.float32)).astype(np.float64)
    cosine, sine = np.cos(angles).astype(np.float32), np.sin(angles).astype(np.float32)
    repeats = width // HEAD_DIM
    return (
        jnp.asarray(np.tile(np.concatenate([cosine, cosine], 1), (1, repeats))),
        jnp.asarray(np.tile(np.concatenate([-sine, sine], 1), (1, repeats))),
    )


def swap_halves(rows):
    width = rows.shape[1]
    half = HEAD_DIM // 2
    lane = lax.broadcasted_iota(jnp.int32, rows.shape, 1)
    return jnp.where(
        lane % HEAD_DIM < half, pltpu.roll(rows, width - half, 1), pltpu.roll(rows, half, 1)
    )


PAIR = 2 * HEAD_DIM


def head_mask(shape, head):
    lane = lax.broadcasted_iota(jnp.int32, shape, 1)
    return (lane >= head * HEAD_DIM) & (lane < (head + 1) * HEAD_DIM)


def masked_scores(query, key_ref, row_ref, col_ref, q0, cols):
    tail = min(2 * BLOCK, cols)
    scores = contract(query, key_ref[0:cols, :], 1, 1)
    shown = row_ref[:, pl.ds(cols - tail, tail)] <= col_ref[pl.ds(q0, BLOCK), :]
    hidden = jnp.where(shown, scores[:, cols - tail :], -jnp.inf)
    return jnp.concatenate([scores[:, : cols - tail], hidden], 1) if tail < cols else hidden


def attend_forward_kernel(
    normed_ref, qkv_w_ref, cos_ref, sin_ref, row_ref, col_ref, q_ref, k_ref, v_ref, out_ref, lse_ref, peak_ref
):
    pairs, length, _ = q_ref.shape

    @pl.loop(0, length // BLOCK)
    def _(t):
        rows = pl.ds(pl.multiple_of(t * BLOCK, BLOCK), BLOCK)
        cosine, sine = cos_ref[rows, :], sin_ref[rows, :]
        for pair in range(pairs):
            first = 3 * pair * PAIR
            qkv = contract(normed_ref[rows, :], qkv_w_ref[:, first : first + 3 * PAIR], 1, 0)
            query = qkv[:, 0:PAIR]
            query = (query * cosine + swap_halves(query) * sine).astype(bf16)
            q_ref[pair, rows, :] = (query.astype(f32) * HEAD_DIM ** (-0.5)).astype(bf16)
            key = qkv[:, PAIR : 2 * PAIR]
            k_ref[pair, rows, :] = (key * cosine + swap_halves(key) * sine).astype(bf16)
            v_ref[pair, rows, :] = qkv[:, 2 * PAIR : 3 * PAIR].astype(bf16)

    peak_ref[...] = jnp.full(peak_ref.shape, -jnp.inf, f32)
    lane = lax.broadcasted_iota(jnp.int32, (BLOCK, 128), 1)
    for t in range(length // BLOCK):
        q0 = t * BLOCK
        rows = pl.ds(q0, BLOCK)
        cols = min(q0 + 2 * BLOCK, length)

        @pl.loop(0, pairs)
        def _(pair):
            total = jnp.zeros((BLOCK, PAIR), f32)
            for sub in range(2):
                head = 2 * pair + sub
                mask = head_mask((BLOCK, PAIR), sub)
                query = jnp.where(mask, q_ref[pair, rows, :], 0).astype(bf16)
                scores = masked_scores(query, k_ref.at[pair], row_ref, col_ref, q0, cols)
                row_max = jnp.max(scores, 1, keepdims=True)
                numerators = jnp.exp(scores - row_max)
                totals = jnp.sum(numerators, 1, keepdims=True)
                mixed = contract(numerators.astype(bf16), v_ref[pair, 0:cols, :], 1, 0) / totals
                total = jnp.where(mask, mixed, total)
                lse_ref[rows, :] = jnp.where(lane == head, row_max + jnp.log(totals), lse_ref[rows, :])
                peak_ref[...] = jnp.where(
                    lax.broadcasted_iota(jnp.int32, peak_ref.shape, 1) == head,
                    jnp.maximum(peak_ref[...], jnp.max(row_max)),
                    peak_ref[...],
                )
            out_ref[rows, pl.ds(pl.multiple_of(pair * PAIR, PAIR), PAIR)] = total.astype(bf16)


def attend_forward(normed, qkv_w, cosine, sine, row_blocks, col_blocks):
    length = normed.shape[0]
    pairs = qkv_w.shape[1] // (3 * PAIR)
    shape = jax.ShapeDtypeStruct
    return pl.pallas_call(
        attend_forward_kernel,
        out_shape=(
            shape((pairs, length, PAIR), bf16),
            shape((pairs, length, PAIR), bf16),
            shape((pairs, length, PAIR), bf16),
            shape((length, pairs * PAIR), bf16),
            shape((length, 128), f32),
            shape((8, 128), f32),
        ),
        in_specs=[vmem] * 6,
        out_specs=tuple([vmem] * 6),
        compiler_params=pltpu.CompilerParams(vmem_limit_bytes=56 * 1024 * 1024),
        cost_estimate=pl.CostEstimate(
            flops=16 * pairs * length * length * PAIR + 2 * normed.size * qkv_w.shape[1], bytes_accessed=100_000_000,
            transcendentals=2 * pairs * length * length,
        ),
        name="attend_forward",
    )(normed, qkv_w, cosine, sine, row_blocks, col_blocks)


def attend_backward_kernel(
    first_head, q_ref, k_ref, v_ref, grad_ref, lse_ref, cos_ref, sin_ref, row_ref, col_ref, normed_ref,
    out_ref, weight_ref, dk_ref, dv_ref,
):
    length = q_ref.shape[0]
    dk_ref[...] = jnp.zeros_like(dk_ref)
    dv_ref[...] = jnp.zeros_like(dv_ref)
    lane = lax.broadcasted_iota(jnp.int32, (BLOCK, 128), 1)
    for t in range(length // BLOCK):
        q0 = t * BLOCK
        rows = pl.ds(q0, BLOCK)
        cols = min(q0 + 2 * BLOCK, length)

        def one_head(sub, dq):
            mask = head_mask((BLOCK, PAIR), sub)
            query = jnp.where(mask, q_ref[rows, :], 0).astype(bf16)
            grad = jnp.where(mask, grad_ref[rows, :], 0).astype(bf16)
            lse = jnp.sum(
                jnp.where(lane == first_head + sub, lse_ref[rows, :], 0.0), 1, keepdims=True
            )
            scores = masked_scores(query, k_ref, row_ref, col_ref, q0, cols)
            attention = jnp.exp(scores - lse)
            grad_attention = contract(grad, v_ref[0:cols, :], 1, 1)
            weighted = attention * grad_attention
            centre = jnp.sum(weighted, 1, keepdims=True)
            grad_scores = (weighted - attention * centre).astype(bf16)
            dv_ref[0:cols, :] += contract(attention.astype(bf16), grad, 0, 0)
            dk_ref[0:cols, :] += contract(grad_scores, query, 0, 0)
            return jnp.where(mask, contract(grad_scores, k_ref[0:cols, :], 1, 0), dq)

        dq = lax.fori_loop(0, 2, one_head, jnp.zeros((BLOCK, PAIR), f32)) * HEAD_DIM ** (-0.5)
        out_ref[rows, 0:PAIR] = (dq * cos_ref[rows, :] - swap_halves(dq) * sin_ref[rows, :]).astype(bf16)
    for t in range(length // BLOCK):
        rows = pl.ds(t * BLOCK, BLOCK)
        dk = dk_ref[rows, :]
        out_ref[rows, PAIR : 2 * PAIR] = (
            dk * cos_ref[rows, :] - swap_halves(dk) * sin_ref[rows, :]
        ).astype(bf16)
        out_ref[rows, 2 * PAIR : 3 * PAIR] = dv_ref[rows, :].astype(bf16)
    side = 256

    @pl.loop(0, normed_ref.shape[1] // side)
    def _(k):
        span = pl.ds(pl.multiple_of(k * side, side), side)
        weight_ref[span, :] = contract(normed_ref[:, span], out_ref[...], 0, 0).astype(bf16)


def attend_backward(pair, query, key, value, grad, lse, cosine, sine, row_blocks, col_blocks, normed):
    length, width = normed.shape
    heads = pl.BlockSpec((None, length, PAIR), lambda _: (pair, 0, 0))
    return pl.pallas_call(
        functools.partial(attend_backward_kernel, 2 * pair),
        grid=(1,),
        out_shape=(
            jax.ShapeDtypeStruct((length, 3 * PAIR), bf16), jax.ShapeDtypeStruct((width, 3 * PAIR), bf16),
        ),
        in_specs=[heads] * 3 + [pl.BlockSpec((length, PAIR), lambda _: (0, pair))] + [vmem] * 6,
        out_specs=(vmem, vmem),
        scratch_shapes=[pltpu.VMEM((length, PAIR), f32), pltpu.VMEM((length, PAIR), f32)],
        compiler_params=pltpu.CompilerParams(vmem_limit_bytes=56 * 1024 * 1024),
        cost_estimate=pl.CostEstimate(
            flops=40 * length * length * PAIR + 6 * length * width * PAIR, bytes_accessed=100_000_000,
            transcendentals=2 * length * length,
        ),
        name="attend_backward",
    )(query, key, value, grad, lse, cosine, sine, row_blocks, col_blocks, normed)


def bit_of(index, bit):
    return lax.rem(lax.div(index, bit), 2)


def flip_bit(index, bit):
    return index + bit - 2 * bit * bit_of(index, bit)


def team_mate(me, bits, offset):
    device, place = me, 0
    for k, bit in enumerate(bits):
        moved = (offset >> k) % 2
        place = place + lax.rem(bit_of(me, bit) + moved, 2) * (1 << k)
        device = flip_bit(device, bit) if moved else device
    return device, place


class Links:

    def __init__(self, send_sems, recv_sems):
        self.send_sems, self.recv_sems = send_sems, recv_sems

    def copy(self, slot, src, dst, device):
        return pltpu.make_async_remote_copy(
            src_ref=src, dst_ref=dst, send_sem=self.send_sems.at[slot],
            recv_sem=self.recv_sems.at[slot], device_id=(device,), device_id_type=MESH,
        )


def greet(partners):
    barrier = pltpu.get_barrier_semaphore()
    for partner in partners:
        pl.semaphore_signal(barrier, inc=1, device_id=(partner,), device_id_type=MESH)
    pl.semaphore_wait(barrier, len(partners))


def spread_block(bits, cut, own_ref, out_ref, links, local_sem):
    core, first, second = bits
    me = lax.axis_index(AXIS)
    sibling, next_a, next_b = (flip_bit(me, bit) for bit in bits)
    block = own_ref.shape[0]
    in_a, in_b = bit_of(me, first), bit_of(me, second)
    spans = {None: (0, block), 0: (0, cut), 1: (cut, block - cut)}

    def rows(flip_a, flip_b, part):
        place = bit_of(me, core)
        place = place + 2 * lax.rem(in_a + flip_a, 2) + 4 * lax.rem(in_b + flip_b, 2)
        start, size = spans[part]
        return pl.ds(pl.multiple_of(place * block + start, 16), size)

    def passed(slot, where, device):
        return links.copy(slot, out_ref.at[where], out_ref.at[where], device)

    def first_hand(slot, part, device):
        start, size = spans[part]
        return links.copy(slot, own_ref.at[pl.ds(start, size)], out_ref.at[rows(0, 0, part)], device)

    makers = {
        0: lambda: first_hand(0, 0, next_a),
        1: lambda: first_hand(1, 1, next_b),
        2: lambda: first_hand(2, 1, next_a),
        3: lambda: first_hand(3, 0, next_b),
        4: lambda: links.copy(4, own_ref, out_ref.at[rows(0, 0, None)], sibling),
        5: lambda: passed(5, rows(1, 0, 0), next_b),
        6: lambda: passed(6, rows(1, 0, 0), sibling),
        7: lambda: passed(7, rows(0, 1, 1), next_a),
        8: lambda: passed(8, rows(0, 1, 1), sibling),
        9: lambda: passed(9, rows(1, 0, 1), sibling),
        10: lambda: passed(10, rows(0, 1, 0), sibling),
        11: lambda: passed(11, rows(1, 1, 0), sibling),
        12: lambda: passed(12, rows(1, 1, 1), sibling),
    }
    needs = {0: 0, 1: 1, 2: 1, 3: 0, 4: None, 5: 0, 6: 0, 7: 1, 8: 1, 9: 1, 10: 0, 11: 0, 12: 1}
    copies = {slot: make() for slot, make in makers.items() if spans[needs[slot]][1]}
    keep = pltpu.make_async_copy(own_ref, out_ref.at[rows(0, 0, None)], local_sem)

    def begin():
        for slot in range(5):
            if slot in copies:
                copies[slot].start()
        keep.start()

    def hand_on(arrived, *sent):
        def phase():
            if arrived in copies:
                copies[arrived].wait_recv()
                for slot in sent:
                    copies[slot].start()

        return phase

    def finish():
        for slot in (4, 6, 8, 9, 10, 11, 12):
            if slot in copies:
                copies[slot].wait_recv()
        keep.wait()
        for slot in copies:
            copies[slot].wait_send()

    return [
        begin, hand_on(0, 5, 6), hand_on(1, 7, 8), hand_on(2, 9), hand_on(3, 10),
        hand_on(5, 11), hand_on(7, 12), finish,
    ]


def run(phases):
    for phase in phases:
        phase()


SPREAD_COPIES = 13
SUM_COPIES = 10


def sum_block(bits, cut, swapped, product, total, to_core, from_core, chip_sum, arrived, links):
    core = bits[0]
    (first, weight_a), (second, weight_b) = ((bits[2], 4), (bits[1], 2)) if swapped else ((bits[1], 2), (bits[2], 4))
    me = lax.axis_index(AXIS)
    sibling, next_a, next_b = flip_bit(me, core), flip_bit(me, first), flip_bit(me, second)
    block, width = total.shape
    tile = 512

    def place(step, other_core):
        flip_a, flip_b = 1 - step // 2, 1 - step % 2
        return (
            lax.rem(bit_of(me, core) + other_core, 2)
            + weight_a * lax.rem(bit_of(me, first) + flip_a, 2)
            + weight_b * lax.rem(bit_of(me, second) + flip_b, 2)
        )

    low, high = (0, cut), (cut, block - cut)
    landing = range(6) if cut else {1: 0, 3: 1, 4: 2}

    def link(slot, step, span, device):
        return links.copy(slot, chip_sum.at[step, pl.ds(*span)], arrived.at[landing[slot - 4], pl.ds(0, span[1])], device)

    diag_a, diag_b = (link(4, 0, low, next_a) if cut else None), link(5, 0, high, next_b)
    plain_a, plain_b = (link(6, 1, low, next_a) if cut else None), link(7, 2, high, next_b)
    last_a, last_b = link(8, 1, high, next_a), (link(9, 2, low, next_b) if cut else None)

    def core_copy(step):
        return links.copy(step, to_core.at[step], from_core.at[step], sibling)

    def for_sibling():
        @pl.loop(0, 4)
        def _(step):
            @pl.loop(0, width // tile)
            def _(column):
                columns = pl.ds(pl.multiple_of(column * tile, tile), tile)
                to_core[step, :, columns] = product(place(step, 1), columns).astype(bf16)

            core_copy(step).start()

    def for_chip():
        @pl.loop(0, 4)
        def _(step):
            core_copy(step).wait_recv()

            @pl.loop(0, width // tile)
            def _(column):
                columns = pl.ds(pl.multiple_of(column * tile, tile), tile)
                summed = product(place(step, 0), columns) + from_core[step, :, columns].astype(f32)
                total[:, columns] = summed

                @pl.when(step < 3)
                def _():
                    chip_sum[step, :, columns] = summed.astype(bf16)

            @pl.when(step == 0)
            def _():
                if cut:
                    diag_a.start()
                diag_b.start()

            @pl.when(step == 1)
            def _():
                if cut:
                    plain_a.start()

            @pl.when(step == 2)
            def _():
                plain_b.start()

    def add(step, span, slot):
        rows = pl.ds(*span)
        chip_sum[step, rows, :] = (
            chip_sum[step, rows, :].astype(f32) + arrived[landing[slot], 0 : span[1], :].astype(f32)
        ).astype(bf16)

    def take(span, slot):
        total[pl.ds(*span), :] += arrived[landing[slot], 0 : span[1], :].astype(f32)

    def hand_on():
        if cut:
            diag_a.wait_recv()
            add(2, low, 0)
            last_b.start()
        diag_b.wait_recv()
        add(1, high, 1)
        last_a.start()

    def finish():
        if cut:
            plain_a.wait_recv()
            take(low, 2)
        plain_b.wait_recv()
        take(high, 3)
        if cut:
            last_b.wait_recv()
            take(low, 5)
        last_a.wait_recv()
        take(high, 4)

        @pl.loop(0, 4)
        def _(step):
            core_copy(step).wait_send()

        for copy in (diag_a, diag_b, plain_a, plain_b, last_a, last_b):
            if copy is not None:
                copy.wait_send()

    return for_sibling, for_chip, hand_on, finish


def sum_scratch(block, width, cut):
    return [
        pltpu.VMEM((block, width), f32),
        pltpu.VMEM((4, block, width), bf16),
        pltpu.VMEM((4, block, width), bf16),
        pltpu.VMEM((3, block, width), bf16),
        pltpu.VMEM((6 if cut else 3, block - cut, width), bf16),
        pltpu.SemaphoreType.DMA((SUM_COPIES,)),
        pltpu.SemaphoreType.DMA((SUM_COPIES,)),
    ]


def spread_scratch(block, width):
    return [
        pltpu.VMEM((block, width), bf16),
        pltpu.SemaphoreType.DMA((SPREAD_COPIES,)),
        pltpu.SemaphoreType.DMA((SPREAD_COPIES,)),
        pltpu.SemaphoreType.DMA,
    ]


def link_params(collective_id):
    return pltpu.CompilerParams(
        collective_id=collective_id, has_side_effects=True, vmem_limit_bytes=60 * 1024 * 1024
    )


def cost(flops, size):
    return pl.CostEstimate(flops=int(flops), bytes_accessed=int(size), transcendentals=0)


def row_scale(values):
    return lax.rsqrt(jnp.mean(values * values, -1, keepdims=True) + epsilon)


def front_kernel(
    team, teams, qkv_moves, ffn_moves, carry_bits, tokens_ref, query_ref, key_ref, value_ref, gate_ref, up_ref, small_ref, *refs,
):
    moved = len(carry_bits)
    (carried, refs) = (refs[0], refs[1:]) if moved else (None, refs)
    (normed_out, weights_out, both_out, small_out), refs = refs[:4], refs[4:]
    carried_out, refs = refs[:moved], refs[moved:]
    (tokens_all, mine, both_mine, gain,
    send_sems, recv_sems, local_sem, swap_send, swap_recv, swap_local, line_send, line_recv, small_send, small_recv,
    both_send, both_recv, both_local, out_sems, *carry_sems) = refs
    me = lax.axis_index(AXIS)
    mate, group = lax.rem(me, team), lax.div(me, team)
    devices = team * teams
    mates = [group * team + lax.rem(mate + k, team) for k in range(1, team)]
    above, below = lax.rem(me + team, devices), lax.rem(me + devices - team, devices)
    ffn_mates = [team_mate(me, (1, 2, 8), k) for k in range(team)]
    rows = mine.shape[1]
    swaps, line, small = Links(swap_send, swap_recv), Links(line_send, line_recv), Links(small_send, small_recv)
    both = Links(both_send, both_recv)
    for i, member, source, target, columns in qkv_moves:
        weight = (query_ref, key_ref, value_ref)[i]
        mine[member, :, target : target + columns] = weight[:, source : source + columns]
    greet(
        mates + [lax.rem(me + k * team, devices) for k in range(1, teams)]
        + [device for device, _ in ffn_mates[4:]]
    )

    def share(place):
        return pl.ds(pl.multiple_of(place * rows, rows), rows)

    swap_copies = [
        swaps.copy(k, mine.at[lax.rem(mate + k + 1, team)], weights_out.at[group, share(mate)], mates[k])
        for k in range(team - 1)
    ]
    crossing = [
        Links(*carry_sems).copy(i, carried, carried_out[i], flip_bit(me, bit)) for i, bit in enumerate(carry_bits)
    ]
    for copy in swap_copies:
        copy.start()
    keep = pltpu.make_async_copy(mine.at[mate], weights_out.at[group, share(mate)], swap_local)
    keep.start()
    small_out[me] = small_ref[...]

    others = [lax.rem(me + k * team, devices) for k in range(1, teams)]
    team_rows = pl.ds(pl.multiple_of(group * team, team), team)
    small_near = [
        small.copy(k, small_out.at[me], small_out.at[me], device) for k, device in enumerate(mates)
    ]
    small_far = [
        small.copy(team + k, small_out.at[team_rows], small_out.at[team_rows], device)
        for k, device in enumerate(others)
    ]
    for copy in small_near:
        copy.start()
    spread = spread_block(
        (1, 2, 4), HALF, tokens_ref, tokens_all, Links(send_sems, recv_sems), local_sem
    )
    for i, member, source, target, columns in ffn_moves:
        both_mine[i * team + member, :, target : target + columns] = (gate_ref, up_ref)[i][:, source : source + columns]

    def passed(slot, shard, device):
        return line.copy(slot, weights_out.at[shard], weights_out.at[shard], device)

    steps = teams - 1

    def up(step):
        return passed(step - 1, group - (step - 1), above)

    def down(step):
        return passed(steps + step - 1, group + (step - 1), below)

    def line_start(step):
        pl.when((group < teams - 1) & (group >= step - 1))(lambda: up(step).start())
        pl.when((group > 0) & (group + step - 1 < teams))(lambda: down(step).start())

    def line_wait(step):
        pl.when(group >= step)(lambda: up(step).wait_recv())
        pl.when(group + step < teams)(lambda: down(step).wait_recv())

    def line_sent(step):
        pl.when((group < teams - 1) & (group >= step - 1))(lambda: up(step).wait_send())
        pl.when((group > 0) & (group + step - 1 < teams))(lambda: down(step).wait_send())

    for copy in small_near:
        copy.wait_recv()
    for copy in small_far:
        copy.start()
    own_place = ffn_mates[0][1]
    both_copies = [
        both.copy(
            i * team + k, both_mine.at[i * team + ffn_mates[k][1]], both_out.at[i * team + own_place], ffn_mates[k][0]
        )
        for i in range(2) for k in range(1, team)
    ]
    for copy in both_copies:
        copy.start()
    both_keep = [
        pltpu.make_async_copy(both_mine.at[i * team + own_place], both_out.at[i * team + own_place], both_local.at[i])
        for i in range(2)
    ]
    for copy in both_keep:
        copy.start()
    for copy in swap_copies:
        copy.wait_recv()
    keep.wait()
    line_start(1)
    spread[0]()
    for copy in crossing:
        copy.start()
    for copy in small_far:
        copy.wait_recv()
    spread[1]()
    spread[2]()
    line_wait(1)
    line_start(2)
    spread[3]()
    spread[4]()
    width = tokens_all.shape[1]
    gains = width // devices
    for d in range(devices):
        gain[:, d * gains : (d + 1) * gains] = small_out[d, 0:1, 0:gains]
    for phase in spread[5:]:
        phase()
    block = tokens_ref.shape[0]

    def normed_copy(k):
        span = pl.ds(pl.multiple_of(k * block, block), block)
        return pltpu.make_async_copy(tokens_all.at[span], normed_out.at[span], out_sems.at[k])

    def norm_blocks(first, last):
        @pl.loop(first, last)
        def _(k):
            span = pl.ds(pl.multiple_of(k * block, block), block)
            values = tokens_all[span, :].astype(f32)
            tokens_all[span, :] = (values * row_scale(values) * gain[...]).astype(bf16)
            normed_copy(k).start()

    norm_blocks(0, 2)
    for step in range(2, teams):
        line_wait(step)
        if step < steps:
            line_start(step + 1)
        if step == 2:
            norm_blocks(2, team)
    for k in range(team):
        normed_copy(k).wait()
    for copy in both_copies:
        copy.wait_recv()
    for copy in both_keep:
        copy.wait()
    for copy in swap_copies + both_copies:
        copy.wait_send()
    for step in range(1, teams):
        line_sent(step)
    for copy in small_near + small_far:
        copy.wait_send()
    for copy in crossing:
        copy.wait()


def front(tokens, weights, small, teams, qkv_moves, ffn_moves, carried, carry_bits):
    block, width = tokens.shape
    team = 8
    rows, cols = weights[0].shape[0], 3 * width // team
    both_cols = weights[3].shape[1] // team
    devices = team * teams
    dma = pltpu.SemaphoreType.DMA
    shape = jax.ShapeDtypeStruct
    return pl.pallas_call(
        functools.partial(front_kernel, team, teams, qkv_moves, ffn_moves, carry_bits),
        out_shape=(
            shape((team * block, width), bf16),
            shape((teams, team * rows, cols), bf16),
            shape((2 * team, rows, both_cols), bf16),
            shape((devices,) + small.shape, f32),
        ) + tuple(shape(carried[0].shape, bf16) for _ in carry_bits),
        in_specs=[vmem] * 7 + [anywhere] * len(carried),
        out_specs=(anywhere, anywhere, anywhere, vmem) + (anywhere,) * len(carry_bits),
        scratch_shapes=[
            pltpu.VMEM((team * block, width), bf16), pltpu.VMEM((team, rows, cols), bf16),
            pltpu.VMEM((2 * team, rows, both_cols), bf16), pltpu.VMEM((1, width), f32),
        ]
        + spread_scratch(block, width)[1:]
        + [dma((team - 1,)), dma((team - 1,)), dma, dma((2 * teams,)), dma((2 * teams,)), dma((team + teams,)), dma((team + teams,))]
        + [dma((2 * team,)), dma((2 * team,)), dma((2,)), dma((team,))]
        + [dma((1,))] * (2 * len(carried)),
        compiler_params=link_params(1),
        cost_estimate=cost(0, 200e6),
        name="front",
    )(tokens, *weights, small, *carried)


def branch_kernel(
    carry, swap_bits, spread_bits, left_ref, right_ref, residual_ref, gain_ref, peak_ref, *refs,
):
    if carry:
        (both_own, both_y, both_z, down_own, down_y), refs = refs[:5], refs[5:]
        (h2_ref, out_ref, peak_out, gate_full, up_full, down_full), refs = refs[:6], refs[6:]
        (landed, together, swap_send, swap_recv, own, send_sems, recv_sems, local_sem,
         peak_in, peak_send, peak_recv, carry_send, carry_recv, carry_local) = refs
    else:
        (h2_ref, out_ref, peak_out), refs = refs[:3], refs[3:]
        (landed, together, swap_send, swap_recv, own, send_sems, recv_sems, local_sem,
         peak_in, peak_send, peak_recv) = refs
    me = lax.axis_index(AXIS)
    team, block, _ = landed.shape
    bits = [1 << k for k in range(peak_in.shape[0])]
    mates = [team_mate(me, swap_bits, k) for k in range(team)]
    greet([device for device, _ in mates[1:]] + [flip_bit(me, bit) for bit in bits if bit not in swap_bits])
    own_place = mates[0][1]

    def rows_at(place):
        return pl.ds(pl.multiple_of(place * block, block), block)

    swap_copies = [
        Links(swap_send, swap_recv).copy(k, left_ref.at[rows_at(mates[k][1])], landed.at[own_place], mates[k][0])
        for k in range(1, team)
    ]
    for copy in swap_copies:
        copy.start()
    peaks = Links(peak_send, peak_recv)

    def peak_copy(k):
        return peaks.copy(k, peak_out, peak_in.at[k], flip_bit(me, bits[k]))

    def peak_step(k):
        if k:
            peak_copy(k - 1).wait()
            peak_out[...] = jnp.maximum(peak_out[...], peak_in[k - 1])
        if k < len(bits):
            peak_copy(k).start()

    if carry:
        carried = Links(carry_send, carry_recv)
        high, middle = bit_of(me, 16), bit_of(me, 4)
        by_y, by_z = flip_bit(me, 4), flip_bit(me, 16)

        def rows_of(part, flip_z, flip_y):
            z, y = lax.rem(high + flip_z, 2), lax.rem(middle + flip_y, 2)
            return pl.ds(pl.multiple_of(z * 16 + part * 8 + y * 4, 4), 4)

        early = both_z.shape[0] // 4

        def piece(source, half):
            return source.at[pl.ds(half * 4, 4)]

        def placed(half, flips):
            return (gate_full, up_full)[half // 2].at[rows_of(half % 2, *flips)]

        def unit(flip_z, flip_y):
            return lax.rem(high + flip_z, 2) * 2 + lax.rem(middle + flip_y, 2)

        kept = []
        for source, flips, halves in ((both_own, (0, 0), 4), (both_y, (0, 1), 4), (both_z, (1, 0), early)):
            for half in range(halves):
                kept.append((piece(source, half), placed(half, flips)))
        kept.append((down_own, down_full.at[unit(0, 0)]))
        kept.append((down_y, down_full.at[unit(0, 1)]))
        kept = [pltpu.make_async_copy(a, b, carry_local.at[i]) for i, (a, b) in enumerate(kept)]
        up_z = [
            carried.copy(half, piece(both_own, half), placed(half, (0, 0)), by_z) for half in range(early, 4)
        ]
        early_yz = [
            carried.copy(4 + half, piece(both_z, half), placed(half, (1, 0)), by_y) for half in range(early)
        ]
        up_yz = [
            carried.copy(4 + half, placed(half, (1, 0)), placed(half, (1, 0)), by_y) for half in range(early, 4)
        ]
        for copy in up_z + kept:
            copy.start()

    peak_out[...] = peak_ref[...]
    peak_step(0)
    landed[own_place] = left_ref[rows_at(own_place), :]
    for copy in swap_copies:
        copy.wait_recv()
    if carry:
        for copy in early_yz:
            copy.start()
    share = landed.shape[2]
    for b in range(team):
        together[:, b * share : (b + 1) * share] = landed[b]
    tile = 512

    @pl.loop(0, own.shape[1] // tile)
    def _(column):
        columns = pl.ds(pl.multiple_of(column * tile, tile), tile)
        h2_ref[:, columns] = residual_ref[:, columns].astype(f32) + contract(
            together[...], right_ref[:, columns], 1, 0
        )

    h2 = h2_ref[...]
    own[...] = (h2 * row_scale(h2) * gain_ref[...]).astype(bf16)
    spread = spread_block(spread_bits, BRANCH_CUT, own, out_ref, Links(send_sems, recv_sems), local_sem)
    spread[0]()
    if carry:
        for over, on in zip(up_z, up_yz):
            over.wait_recv()
            on.start()
    for k, phase in enumerate(spread[1:-1]):
        phase()
        if k < len(bits):
            peak_step(k + 1)
    for k in range(len(spread) - 2, len(bits)):
        peak_step(k + 1)
    spread[-1]()
    for copy in swap_copies:
        copy.wait_send()
    if carry:
        for copy in kept:
            copy.wait()
        for copy in early_yz + up_yz:
            copy.wait_recv()
        for copy in up_z + early_yz + up_yz:
            copy.wait_send()


def branch(left, right, residual, gain, peak, carry, swap_bits, spread_bits, bit_count):
    block, width = residual.shape
    dma = pltpu.SemaphoreType.DMA
    shape = jax.ShapeDtypeStruct
    out_shape = [shape((block, width), f32), shape((8 * block, width), bf16), shape((8, 128), f32)]
    scratch = [pltpu.VMEM((8, block, left.shape[1]), bf16), pltpu.VMEM((block, width), bf16), dma((8,)), dma((8,))]
    scratch += spread_scratch(block, width)
    scratch += [pltpu.VMEM((bit_count, 8, 128), f32), dma((bit_count,)), dma((bit_count,))]
    if carry:
        out_shape += [
            shape((32,) + carry[0].shape[1:], bf16), shape((32,) + carry[0].shape[1:], bf16),
            shape((4,) + carry[3].shape, bf16),
        ]
        scratch += [dma((8,)), dma((8,)), dma((14,))]
    return pl.pallas_call(
        functools.partial(branch_kernel, bool(carry), swap_bits, spread_bits),
        out_shape=tuple(out_shape),
        in_specs=[vmem] * (5 + len(carry)),
        out_specs=tuple([vmem, anywhere, vmem] + [anywhere] * (len(out_shape) - 3)),
        scratch_shapes=scratch,
        compiler_params=link_params(2),
        cost_estimate=cost(16 * block * left.shape[1] * width, 300e6),
        name="attention_branch",
    )(left, right, residual, gain, peak, *carry)


def norm_back(values, gain, upstream):
    scaled = upstream * gain
    scale = row_scale(values)
    inner = jnp.mean(scaled * values, -1, keepdims=True)
    return scale * scaled - scale * scale * scale * values * inner


def ffn_back_kernel(
    cross, sum_bits, swap_bits, gate_ref, up_ref, gate_w_ref, up_w_ref, normed_ref, out_w_ref, h2_ref, cot_ref, gain_ref, *refs,
):
    (part_ref, over_ref, refs) = (refs[0], refs[1], refs[2:]) if cross else (None, None, refs)
    (residual_ref, branch_ref, heads_out, d_up_out, d_gate_own), refs = refs[:5], refs[5:]
    (d_gate_in, part_in, over_in), refs = (refs[:3], refs[3:]) if cross else ((None,) * 3, refs)
    (total, to_core, from_core, chip_sum, arrived, sum_send, sum_recv,
     swap_send, swap_recv, local_sem, stage, stage_sems, own_sems, *more) = refs
    if cross:
        cross_send, cross_recv = more
        crossing = Links(cross_send, cross_recv)
    else:
        (stage_gate,) = more
    me = lax.axis_index(AXIS)
    block, width = total.shape
    team = 1 << len(swap_bits)
    mates = [team_mate(me, swap_bits, k) for k in range(team)]
    greet(
        [device for device, _ in mates[1:]] + [flip_bit(me, bit) for bit in sum_bits if bit not in swap_bits]
        + ([flip_bit(me, 16)] if cross else [])
    )

    def product(place, columns):
        rows = pl.ds(pl.multiple_of(place * block, block), block)
        return contract(gate_ref[rows, :], gate_w_ref[columns, :], 1, 1) + contract(
            up_ref[rows, :], up_w_ref[columns, :], 1, 1
        )

    side, columns_ff = stage.shape[1:]
    count = width // side
    y_side, by_y = bit_of(me, 4), flip_bit(me, 4)
    if cross:
        part_copy = crossing.copy(count // 2, part_ref, part_in, by_y)
        over_copy = crossing.copy(count // 2 + 1, over_ref, over_in, flip_bit(me, 16))
        part_copy.start()

    def parked(i, part):
        row = i * side
        rows = pl.ds(pl.multiple_of(lax.rem(row, block), 16), side)
        return from_core.at[lax.div(row, block), rows, pl.ds(part * columns_ff, columns_ff)]

    def cross_copy(i):
        return crossing.copy(i, parked(i, 0), d_gate_in.at[i], by_y)

    def own_copy(i):
        return pltpu.make_async_copy(parked(i, 1), d_gate_own.at[i], own_sems.at[i])

    def tile_of(step):
        if not cross:
            return step
        theirs = step < count // 2
        return jnp.where(theirs, 2 * step + 1 - y_side, 2 * step - count + y_side)

    def up_copy(step):
        span = pl.ds(pl.multiple_of(tile_of(step) * side, side), side)
        slot = lax.rem(step, 2)
        return pltpu.make_async_copy(stage.at[slot], d_up_out.at[span], stage_sems.at[slot])

    def gate_copy(step):
        span = pl.ds(pl.multiple_of(step * side, side), side)
        slot = lax.rem(step, 2)
        return pltpu.make_async_copy(stage_gate.at[slot], d_gate_own.at[span], own_sems.at[slot])

    def gradients(first, last):
        @pl.loop(first, last)
        def _(step):
            @pl.when(step >= 2)
            def _():
                up_copy(step - 2).wait()
                if not cross:
                    gate_copy(step - 2).wait()

            columns = normed_ref[:, pl.ds(pl.multiple_of(tile_of(step) * side, side), side)]
            stage[lax.rem(step, 2)] = contract(columns, up_ref[...], 0, 0).astype(bf16)
            up_copy(step).start()
            tile = contract(columns, gate_ref[...], 0, 0).astype(bf16)
            if not cross:
                stage_gate[lax.rem(step, 2)] = tile
                gate_copy(step).start()
                return

            @pl.when(step < count // 2)
            def _():
                parked(step, 0)[...] = tile
                cross_copy(step).start()

            @pl.when(step >= count // 2)
            def _():
                parked(step - count // 2, 1)[...] = tile
                own_copy(step - count // 2).start()

    for_sibling, for_chip, hand_on, finish = sum_block(
        sum_bits, HALF, False, product, total, to_core, from_core, chip_sum, arrived, Links(sum_send, sum_recv)
    )
    for_sibling()
    for_chip()
    if cross:
        over_copy.start()
    gradients(0, 1)
    hand_on()
    gradients(1, count - 2)
    finish()
    residual = cot_ref[...].astype(f32) + norm_back(h2_ref[...], gain_ref[...], total[...])
    residual_ref[...] = residual
    branch_ref[...] = residual.astype(bf16)
    share = width // team
    for b in range(team):
        part = slice(b * share, (b + 1) * share)
        to_core[0, :, part] = contract(branch_ref[...], out_w_ref[part, :], 1, 1).astype(bf16)
    own_place = mates[0][1]
    own_rows = pl.ds(pl.multiple_of(own_place * block, block), block)
    def heads_of(place):
        return to_core.at[0, :, pl.ds(pl.multiple_of(place * share, share), share)]

    swap_copies = [
        Links(swap_send, swap_recv).copy(k, heads_of(mates[k][1]), heads_out.at[own_rows], mates[k][0])
        for k in range(1, team)
    ]
    keep = pltpu.make_async_copy(heads_of(own_place), heads_out.at[own_rows], local_sem)
    for copy in swap_copies + [keep]:
        copy.start()
    gradients(count - 2, count)
    for copy in swap_copies:
        copy.wait_recv()
    for copy in swap_copies:
        copy.wait_send()
    keep.wait()
    for step in range(count - 2, count):
        up_copy(step).wait()
        if not cross:
            gate_copy(step).wait()
    if cross:
        part_copy.wait()
        over_copy.wait()

        @pl.loop(0, count // 2)
        def _(i):
            own_copy(i).wait()
            cross_copy(i).wait()


def ffn_back(gate, up, gate_w, up_w, normed, out_w, h2, cot, gain, part, side, sum_bits, swap_bits):
    block, width = h2.shape
    shape = jax.ShapeDtypeStruct
    dma = pltpu.SemaphoreType.DMA
    ff_cols, cross = gate.shape[1], side % 128 == 0
    side = side if cross else 256
    tiles = width // side // 2
    if cross:
        d_gate = (shape((tiles, side, ff_cols), bf16),) * 2 + (shape(part[0].shape, bf16),) * 2
        more = [dma((tiles + 2,)), dma((tiles + 2,))]
    else:
        d_gate, more = (shape((width, ff_cols), bf16),), [pltpu.VMEM((2, side, ff_cols), bf16)]
    return pl.pallas_call(
        functools.partial(ffn_back_kernel, cross, sum_bits, swap_bits),
        out_shape=(
            shape((block, width), f32), shape((block, width), bf16), shape((8 * block, width // 8), bf16),
            shape((width, ff_cols), bf16),
        ) + d_gate,
        in_specs=[vmem] * 9 + [anywhere] * len(part),
        out_specs=(vmem, vmem) + (anywhere,) * (2 + len(d_gate)),
        scratch_shapes=sum_scratch(block, width, HALF)
        + [dma((8,)), dma((8,)), dma]
        + [pltpu.VMEM((2, side, ff_cols), bf16), dma((2,)), dma((tiles,))]
        + more,
        compiler_params=link_params(3),
        cost_estimate=cost(96 * block * ff_cols * width, 200e6),
        name="ffn_back",
    )(gate, up, gate_w, up_w, normed, out_w, h2, cot, gain, *part)


def last_sums_kernel(
    carry_bits, sum_bits, ffn_bits, left_ref, other_ref, right_ref, tokens_ref, gain_ref, residual_ref, hidden_ref,
    down_ref, h2_ref, gate_ref, *refs,
):
    moved = len(carry_bits)
    carried, (out_ref, mixed_ref, gate_out), refs = refs[:moved], refs[moved : moved + 3], refs[moved + 3 :]
    carried_out, scratch = refs[:moved], refs[moved:]
    if moved:
        carry_sems, scratch = scratch[-2:], scratch[:-2]
    (swap_send, swap_recv, swap_local), scratch = scratch[-3:], scratch[:-3]
    count = len(scratch) // 2
    me = lax.axis_index(AXIS)
    total, ffn_total = scratch[0], scratch[count]
    block = total.shape[0]
    mates = [team_mate(me, ffn_bits, k) for k in range(8)]
    partners = [flip_bit(me, bit) for bit in sum_bits if bit not in ffn_bits]
    greet(partners + [device for device, _ in mates[1:]] + [flip_bit(me, bit) for bit in carry_bits])
    crossing = [
        Links(*carry_sems).copy(i, carried[i], carried_out[i], flip_bit(me, bit)) for i, bit in enumerate(carry_bits)
    ]
    for copy in crossing:
        copy.start()
    swaps, own_place = Links(swap_send, swap_recv), mates[0][1]
    swap_copies = [
        swaps.copy(k, gate_ref.at[mates[k][1]], gate_out.at[own_place], mates[k][0]) for k in range(1, 8)
    ]
    keep = pltpu.make_async_copy(gate_ref.at[own_place], gate_out.at[own_place], swap_local)

    def rows_of(place):
        return pl.ds(pl.multiple_of(place * block, block), block)

    def product(place, columns):
        rows = rows_of(place)
        middle = left_ref.shape[1]
        return contract(left_ref[rows, :], right_ref[columns, 0:middle], 1, 1) + contract(
            other_ref[rows, :], right_ref[columns, middle : 2 * middle], 1, 1
        )

    def ffn_product(place, columns):
        return contract(hidden_ref[rows_of(place), :], down_ref[:, columns], 1, 0)

    first = sum_block(sum_bits, LAST_CUT, False, product, *scratch[: count - 2], Links(*scratch[count - 2 : count]))
    second = sum_block(ffn_bits, HALF, True, ffn_product, *scratch[count:-2], Links(*scratch[-2:]))
    run(first[:2])
    run(second[:2])
    for copy in swap_copies + [keep]:
        copy.start()
    for one, other in zip(first[2:], second[2:]):
        one()
        other()
    out_ref[...] = residual_ref[...] + norm_back(
        tokens_ref[...].astype(f32), gain_ref[...], total[...]
    )
    mixed_ref[...] = (h2_ref[...] + ffn_total[...]).astype(bf16)
    for copy in swap_copies:
        copy.wait_recv()
    for copy in swap_copies:
        copy.wait_send()
    keep.wait()
    for copy in crossing:
        copy.wait()


def last_sums(left, other, right, tokens, gain, residual, hidden, down, h2, d_gate, carry, carry_bits, sum_bits, ffn_bits):
    block, width = tokens.shape
    return pl.pallas_call(
        functools.partial(last_sums_kernel, carry_bits, sum_bits, ffn_bits),
        out_shape=(
            jax.ShapeDtypeStruct((block, width), f32), jax.ShapeDtypeStruct((block, width), bf16),
            jax.ShapeDtypeStruct(d_gate.shape, bf16),
        ) + tuple(jax.ShapeDtypeStruct(x.shape, x.dtype) for x in carry),
        in_specs=[vmem] * 9 + [anywhere] * (1 + len(carry)),
        out_specs=(vmem, vmem, anywhere) + (anywhere,) * len(carry),
        scratch_shapes=sum_scratch(block, width, LAST_CUT) + sum_scratch(block, width, HALF)
        + [pltpu.SemaphoreType.DMA((8,)), pltpu.SemaphoreType.DMA((8,)), pltpu.SemaphoreType.DMA]
        + [pltpu.SemaphoreType.DMA((1,))] * (2 * len(carry)),
        compiler_params=link_params(4),
        cost_estimate=cost(16 * block * right.size // 8, 300e6),
        name="last_sums",
    )(left, other, right, tokens, gain, residual, hidden, down, h2, d_gate, *carry)


def exchange_kernel(teams, sources, *refs):
    mine, landed, (send_sems, recv_sems, local_sems) = refs[:sources], refs[sources : 2 * sources], refs[2 * sources :]
    me = lax.axis_index(AXIS)
    members = mine[0].shape[0]
    links = Links(send_sems, recv_sems)
    greeted = {}
    for bits in teams:
        for k in range(1, members):
            device, _ = team_mate(me, bits, k)
            greeted[tuple(sorted(bit for j, bit in enumerate(bits) if (k >> j) % 2))] = device
    greet(list(greeted.values()))
    copies, kept = [], []
    for i, (source, target, bits) in enumerate(zip(mine, landed, teams)):
        own = team_mate(me, bits, 0)[1]
        kept.append(pltpu.make_async_copy(source.at[own], target.at[own], local_sems.at[i]))
        for k in range(1, members):
            device, place = team_mate(me, bits, k)
            copies.append(links.copy(i * members + k, source.at[place], target.at[own], device))
    for copy in copies + kept:
        copy.start()
    for copy in copies:
        copy.wait()
    for copy in kept:
        copy.wait()


def exchange(parts, teams):
    dma = pltpu.SemaphoreType.DMA
    slots = len(parts) * parts[0].shape[0]
    return pl.pallas_call(
        functools.partial(exchange_kernel, teams, len(parts)),
        out_shape=tuple(jax.ShapeDtypeStruct(part.shape, part.dtype) for part in parts),
        in_specs=[vmem] * len(parts),
        out_specs=tuple([vmem] * len(parts)),
        scratch_shapes=[dma((slots,)), dma((slots,)), dma((len(parts),))],
        compiler_params=link_params(5),
        cost_estimate=cost(1e6, 40e6),
        name="exchange",
    )(*parts)


def home_kernel(places, gain_of, sources, *refs):
    count = len(places)
    kinds = max(gain_of) + 1
    parts, weights, gains = refs[:sources], refs[sources : sources + count], refs[sources + count : sources + count + kinds]
    outs, gain_outs = refs[-count - kinds : -kinds], refs[-kinds:]
    totals = [jnp.zeros(gain.shape, f32) for gain in gains]
    for i, (out, weight) in enumerate(zip(outs, weights)):
        for source, member, first, target, columns in places[i]:
            out[:, target : target + columns] = parts[source][member, :, first : first + columns].astype(f32)
        for first in range(0, out.shape[1], 1024):
            product = out[:, first : first + 1024] * weight[:, first : first + 1024].astype(f32)
            totals[gain_of[i]] += jnp.sum(product, 1, keepdims=True)
    for gain, total, out in zip(gains, totals, gain_outs):
        out[...] = jnp.broadcast_to(total / gain[...], (out.shape[1], 128)).T[0:1, :]


def home(parts, weights, gains, gain_of, places):
    shape = jax.ShapeDtypeStruct
    count = len(weights)
    gains = [gain.astype(f32).reshape(-1, 1) for gain in gains]
    return pl.pallas_call(
        functools.partial(home_kernel, places, gain_of, len(parts)),
        out_shape=tuple(shape(w.shape, f32) for w in weights) + tuple(shape((1, g.shape[0]), f32) for g in gains),
        in_specs=[vmem] * (len(parts) + count + len(gains)),
        out_specs=tuple([vmem] * (count + len(gains))),
        compiler_params=pltpu.CompilerParams(vmem_limit_bytes=40 * 1024 * 1024),
        cost_estimate=cost(1e6, 30e6),
        name="home",
    )(*parts, *weights, *gains)


def body(
    tokens, block_of, clip_limit, norm_attn, w_query, w_key, w_value, w_out,
    norm_ffn, w_gate, w_up, w_down, cotangent,
):
    tok_rows, width = tokens.shape
    devices = lax.axis_size(AXIS)
    team = SEQ // tok_rows
    teams = devices // team
    head_total = width // HEAD_DIM
    heads = head_total // team
    head_cols = heads * HEAD_DIM
    ff_rows = w_down.shape[0]
    weight_rows = w_gate.shape[0]
    ff_cols = w_gate.shape[1] // team
    device = lax.axis_index(AXIS)
    mate = device % team
    bit_count = devices.bit_length() - 1
    attn_bits, ffn_bits = (1, 2, 4), (1, 2, 8)
    data_bits = [4] + [1 << k for k in range(4, bit_count)]
    in_team = [[g * team + b for b in range(team)] for g in range(teams)]
    across = [[g * team + b for g in range(teams)] for b in range(team)]
    ffn_team = [
        [g * 16 + z * 8 + y * 4 + c for z in range(2) for c in range(4)]
        for g in range(devices // 16)
        for y in range(2)
    ]

    def flip(x, bit):
        return lax.ppermute(x, AXIS, [(i, i ^ bit) for i in range(devices)])

    def gather_across(x):
        return lax.all_gather(x, AXIS, axis=0, tiled=True, axis_index_groups=across)

    def scatter_across(x):
        return lax.psum_scatter(
            x.astype(bf16), AXIS, scatter_dimension=0, tiled=True, axis_index_groups=across
        )

    def dim_of(bit):
        return bit_count - bit.bit_length()

    def data_pieces(x):
        pieces = {0: x}
        for bit in reversed(data_bits):
            for key in list(pieces):
                pieces[key | bit] = flip(pieces[key], bit)
        return pieces

    def place_pieces(pieces, dims, shape):
        total = jnp.zeros(shape, bf16)
        for key, piece in pieces.items():
            start = [0] * len(shape)
            size = list(shape)
            for bit in data_bits:
                start[dims[bit]] = ((device // bit) + (1 if key & bit else 0)) % 2
                size[dims[bit]] = 1
            total = lax.dynamic_update_slice(total, piece.reshape(size), start)
        return total

    def after_bit(dims, bit):
        return {b: d - (d > dims[bit]) for b, d in dims.items() if b != bit}

    def data_sum(x, dims, bits):
        for bit in bits:
            mine = (device // bit) % 2
            keep = lax.dynamic_index_in_dim(x, mine, dims[bit], False)
            sent = flip(lax.dynamic_index_in_dim(x, 1 - mine, dims[bit], False), bit)
            x = (keep.astype(f32) + sent.astype(f32)).astype(bf16)
            dims = after_bit(dims, bit)
        return x

    row_dims = {bit: dim_of(bit) for bit in data_bits}
    row_shape = (2,) * bit_count
    unit_dims = {bit: i for i, bit in enumerate(reversed(data_bits))}
    unit_shape = (2,) * len(data_bits)

    def tie(*values):
        return lax.optimization_barrier(values)

    qkv_moves = tuple(
        (i, b, (g * team + b) * HEAD_DIM, (3 * (g // 2) + i) * PAIR + (g % 2) * HEAD_DIM, HEAD_DIM)
        for i in range(3) for g in range(heads) for b in range(team)
    )
    ffn_units = tuple(
        (z * 4 + c, (2 * h + y) * ff_rows, (h * 16 + z * 8 + y * 4 + c) * ff_rows)
        for h in range(devices // 16) for z in range(2) for y in range(2) for c in range(4)
    )
    ffn_moves = tuple(
        (i, member, source, target, ff_rows)
        for i in range(2) for member, target, source in ffn_units
    )
    gain_row = jnp.concatenate([norm_attn, norm_ffn]).astype(f32)
    gain_row = jnp.pad(gain_row, (0, 128 - 2 * weight_rows)).reshape(1, 128)
    block_rows = block_of.astype(f32).reshape(tok_rows // 128, 128)
    small = jnp.concatenate([gain_row, block_rows, jnp.zeros((7 - tok_rows // 128, 128), f32)])
    ahead = data_bits == [4, 16]
    normed_attn, qkv_w, both_mine, gathered, *down_moved = front(
        tokens, (w_query, w_key, w_value, w_gate, w_up), small, teams, qkv_moves, ffn_moves,
        [w_down] if ahead else [], (4,) if ahead else (),
    )
    qkv_w = qkv_w.reshape(width, 3 * head_cols)
    gain_attn = gathered[:, 0, :weight_rows].reshape(1, width)
    gain_ffn = gathered[:, 0, weight_rows : 2 * weight_rows].reshape(1, width)
    blocks = lax.dynamic_slice_in_dim(gathered, device - mate, team, 0)
    blocks = blocks[:, 1 : 1 + tok_rows // 128].astype(jnp.int32).reshape(SEQ)
    row_blocks, col_blocks = blocks.reshape(1, SEQ), blocks.reshape(SEQ, 1)
    if weight_rows == HEAD_DIM:
        both_mine, qkv_w, out_mine = tie(both_mine, qkv_w, gather_across(w_out))
        out_w = lax.all_gather(out_mine, AXIS, axis=0, tiled=True, axis_index_groups=in_team)
    else:
        out_w = lax.all_gather(w_out, AXIS, axis=0, tiled=True)
        out_w = out_w.reshape(heads, team, HEAD_DIM, width).transpose(1, 0, 2, 3).reshape(width, width)

    def whole_rows(mine):
        shape = row_shape + (weight_rows, ff_cols)
        return place_pieces(data_pieces(mine), row_dims, shape).reshape(width, ff_cols)

    cosine, sine = rope_tables(SEQ, PAIR)
    if data_bits == [4, 16]:
        carry = [both_mine, flip(both_mine, 4), flip(both_mine[: 4 * EARLY_HALVES], 16), w_down, *down_moved]
    else:
        carry = []
    query, key, value, attended, lse, peak = attend_forward(
        normed_attn, qkv_w, cosine, sine, row_blocks, col_blocks
    )
    cot_mine = cotangent
    peaks = jnp.where(
        (jnp.arange(head_total) % team) == mate, jnp.repeat(peak[0, :heads], team), -jnp.inf
    )
    peaks = jnp.broadcast_to(jnp.pad(peaks, (0, 128 - head_total))[None], (8, 128))
    if carry:
        carry[1], carry[2], attended, down_sent, cot_mine = tie(carry[1], carry[2], attended, w_down, cotangent)
        over = flip(down_sent, 16)
    after_attn, normed_ffn, peaks, *full = branch(
        attended, out_w, tokens, gain_ffn, peaks, carry, attn_bits, ffn_bits, bit_count
    )
    head_peak = peaks[0, :head_total]
    if carry:
        normed_ffn, over = tie(normed_ffn, over)
    if carry:
        gate_w, up_w = (w.reshape(width, ff_cols) for w in full[:2])
        z_side, y_side = (device // 16) % 2, (device // 4) % 2
        full_down = lax.dynamic_update_slice(full[2], over[None], ((1 - z_side) * 2 + y_side, 0, 0))
        down_w = lax.dynamic_update_slice(
            full_down, flip(over, 4)[None], ((1 - z_side) * 2 + 1 - y_side, 0, 0)
        ).reshape(ff_cols, width)
    else:
        gate_w, up_w = whole_rows(both_mine[:team]), whole_rows(both_mine[team:])
        down_w = place_pieces(
            data_pieces(w_down), unit_dims, unit_shape + (ff_rows, width)
        ).reshape(ff_cols, width)
    gate_pre = contract(normed_ffn, gate_w, 1, 0)
    up_pre = contract(normed_ffn, up_w, 1, 0)
    sigmoid_gate = jax.nn.sigmoid(gate_pre)
    silu_gate = gate_pre * sigmoid_gate
    hidden = (silu_gate * up_pre).astype(bf16)

    team_cot = lax.all_gather(cot_mine, AXIS, axis=0, tiled=True, axis_index_groups=ffn_team)
    d_down = contract(hidden, team_cot, 0, 0).astype(bf16).reshape(unit_shape + (ff_rows, width))
    team_cot, d_down = tie(team_cot, d_down)
    d_hidden = contract(team_cot, down_w, 1, 1)
    grad_gate = (d_hidden * up_pre * sigmoid_gate * (1.0 + gate_pre * (1.0 - sigmoid_gate))).astype(bf16)
    grad_up = (d_hidden * silu_gate).astype(bf16)

    unit_rest, row_rest = after_bit(unit_dims, data_bits[0]), after_bit(row_dims, data_bits[0])
    row_values = (weight_rows, ff_cols)
    crosses = data_bits == [4, 16]
    if crosses:
        y_side, z_side = (device // 4) % 2, (device // 16) % 2
        kept = lax.dynamic_index_in_dim(d_down, y_side, unit_dims[4], False)
        sent = lax.dynamic_index_in_dim(d_down, 1 - y_side, unit_dims[4], False)
        mine, theirs = (lax.dynamic_index_in_dim(kept, z, 0, False) for z in (z_side, 1 - z_side))
        to_mine, to_theirs = (lax.dynamic_index_in_dim(sent, z, 0, False) for z in (z_side, 1 - z_side))
        theirs = (theirs.astype(f32) + flip(to_theirs, 4).astype(f32)).astype(bf16)
        grad_gate, theirs = tie(grad_gate, theirs)
        beside = [to_mine, theirs]
    else:
        beside = []
    d_residual, branch_mine, grad_attended, d_up, *d_gate = ffn_back(
        grad_gate, grad_up, gate_w, up_w, normed_ffn, out_w, after_attn, cotangent, gain_ffn, beside, 4 * weight_rows,
        ffn_bits, attn_bits,
    )
    if crosses:
        d_down = mine.astype(f32) + d_gate[2].astype(f32) + d_gate[3].astype(f32)
        d_gate = (d_gate[0].astype(f32) + d_gate[1].astype(f32)).astype(bf16)
        d_gate = d_gate.reshape((2,) * (bit_count - 1) + row_values)
    else:
        d_down = data_sum(d_down, unit_dims, data_bits[:1])
        d_gate = data_sum(d_gate[0].reshape(row_shape + row_values), row_dims, data_bits[:1])
    if not crosses:
        d_down = data_sum(d_down, unit_rest, data_bits[1:]).astype(f32)
    grad_attended, d_gate = tie(grad_attended, d_gate)
    d_gate = data_sum(d_gate, row_rest, data_bits[1:])
    branch_grad = lax.all_gather(branch_mine, AXIS, axis=0, tiled=True, axis_index_groups=in_team)

    def heads_back(pair):
        return attend_backward(
            pair, query, key, value, grad_attended, lse, cosine, sine, row_blocks, col_blocks, normed_attn
        )

    grad_pairs, shares = [None] * (heads // 2), [None] * (heads // 2)
    grad_pairs[0], share = heads_back(0)
    grad_attended, d_gate, d_up, share, branch_grad = tie(grad_attended, d_gate, d_up, share, branch_grad)
    shares[0] = scatter_across(share)
    d_up = data_sum(d_up.reshape(row_shape + row_values), row_dims, data_bits[:1])
    for p in range(1, heads // 2):
        grad_pairs[p], share = heads_back(p)
        grad_pairs[p], share, d_up = tie(grad_pairs[p], share, d_up)
        shares[p] = scatter_across(share)
    sent, sent_bits = [], ()
    if crosses:
        kept_up = lax.dynamic_index_in_dim(d_up, z_side, row_rest[16], False)
        sent, sent_bits = [lax.dynamic_index_in_dim(d_up, 1 - z_side, row_rest[16], False)], (16,)
        kept_up, sent[0] = (d.reshape(team, weight_rows, ff_cols) for d in (kept_up, sent[0]))
    else:
        d_up = data_sum(d_up, row_rest, data_bits[1:])
    grad_pairs[0], shares[0] = tie(grad_pairs[0], shares[0])
    d_gate = d_gate.reshape(team, weight_rows, ff_cols)
    d_tokens, mixed, d_gate, *landed = last_sums(
        *grad_pairs, qkv_w, tokens, gain_attn, d_residual, hidden, down_w, after_attn, d_gate, sent, sent_bits,
        attn_bits, ffn_bits,
    )
    if crosses:
        d_up = (kept_up.astype(f32) + landed[0].astype(f32)).astype(bf16)
    d_tokens, attended = tie(d_tokens, attended)
    out_part = contract(attended, branch_grad, 0, 0)
    if weight_rows == HEAD_DIM:
        d_out = scatter_across(out_part).astype(f32)
    else:
        spread = jnp.where(
            (jnp.arange(team) == mate)[None, :, None, None],
            out_part.reshape(heads, 1, HEAD_DIM, width), 0.0,
        ).reshape(width, width)
        d_out = lax.psum_scatter(spread, AXIS, scatter_dimension=0, tiled=True)
    places = [[], [], []]
    for i, b, source, target, columns in qkv_moves:
        places[i].append((target // (3 * PAIR), b, target % (3 * PAIR), source, columns))
    places += [
        [(heads // 2 + i, member, target, source, ff_rows) for member, target, source in ffn_units] for i in range(2)
    ]
    shares = [share.reshape(team, weight_rows, 3 * PAIR) for share in shares]
    *shares, d_up = exchange(
        shares + [d_up.reshape(team, weight_rows, ff_cols)], (attn_bits,) * (heads // 2) + (ffn_bits,)
    )
    d_query, d_key, d_value, d_gate, d_up, d_norm_attn, d_norm_ffn = home(
        shares + [d_gate, d_up], (w_query, w_key, w_value, w_gate, w_up), (norm_attn, norm_ffn), (0, 0, 0, 1, 1),
        tuple(tuple(p) for p in places),
    )
    d_norm_attn, d_norm_ffn = d_norm_attn[0], d_norm_ffn[0]
    clip_value = clip_limit.astype(f32)
    factor = jnp.sqrt(clip_value / jnp.maximum(head_peak, clip_value))
    factors = jnp.repeat(factor, HEAD_DIM)[None, :]
    clipped_query = (w_query.astype(f32) * factors).astype(bf16)
    clipped_key = (w_key.astype(f32) * factors).astype(bf16)
    return (
        mixed, d_tokens, d_norm_attn, d_query, d_key, d_value, d_out, d_norm_ffn,
        d_gate, d_up, d_down, head_peak, clipped_query, clipped_key,
    )


def solution(mesh):
    rows, whole = P(AXIS, None), P(AXIS)
    return jax.shard_map(
        body,
        mesh=mesh,
        in_specs=(rows, whole, P(), whole, rows, rows, rows, rows, whole, rows, rows, rows, rows),
        out_specs=(
            rows, rows, whole, rows, rows, rows, rows, whole, rows, rows, rows, P(), rows, rows,
        ),
        check_vma=False,
    )
```

```python
import functools

import jax
import jax.numpy as jnp
import numpy as np
from jax import lax
from jax.experimental import pallas as pl
from jax.experimental.pallas import tpu as pltpu
from jax.sharding import PartitionSpec as P

HEAD_DIM = 64
SEQ = 2048
BLOCK = 256
HALF = 128
LAST_CUT = 0
EARLY_HALVES = 3
BRANCH_CUT = 128
AXIS = "fsdp"
MESH = pl.DeviceIdType.MESH

epsilon = 1e-05
rope_base = 130000.0
bf16 = jnp.bfloat16
f32 = jnp.float32
vmem = pl.BlockSpec(memory_space=pltpu.VMEM)
anywhere = pl.BlockSpec(memory_space=pl.ANY)


def contract(left, right, left_dim, right_dim):
    return lax.dot_general(
        left, right, (((left_dim,), (right_dim,)), ((), ())), preferred_element_type=f32
    )


def rope_tables(length, width):
    half_dim = HEAD_DIM // 2
    inverse = rope_base ** (-np.arange(half_dim) * 2.0 / HEAD_DIM)
    angles = (np.arange(length, dtype=np.float32)[:, None] * inverse.astype(np.float32)).astype(np.float64)
    cosine, sine = np.cos(angles).astype(np.float32), np.sin(angles).astype(np.float32)
    repeats = width // HEAD_DIM
    return (
        jnp.asarray(np.tile(np.concatenate([cosine, cosine], 1), (1, repeats))),
        jnp.asarray(np.tile(np.concatenate([-sine, sine], 1), (1, repeats))),
    )


def swap_halves(rows):
    width = rows.shape[1]
    half = HEAD_DIM // 2
    lane = lax.broadcasted_iota(jnp.int32, rows.shape, 1)
    return jnp.where(
        lane % HEAD_DIM < half, pltpu.roll(rows, width - half, 1), pltpu.roll(rows, half, 1)
    )


PAIR = 2 * HEAD_DIM


def head_mask(shape, head):
    lane = lax.broadcasted_iota(jnp.int32, shape, 1)
    return (lane >= head * HEAD_DIM) & (lane < (head + 1) * HEAD_DIM)


def masked_scores(query, key_ref, row_ref, col_ref, q0, cols):
    tail = min(2 * BLOCK, cols)
    scores = contract(query, key_ref[0:cols, :], 1, 1)
    shown = row_ref[:, pl.ds(cols - tail, tail)] <= col_ref[pl.ds(q0, BLOCK), :]
    hidden = jnp.where(shown, scores[:, cols - tail :], -jnp.inf)
    return jnp.concatenate([scores[:, : cols - tail], hidden], 1) if tail < cols else hidden


def attend_forward_kernel(
    normed_ref, qkv_w_ref, cos_ref, sin_ref, row_ref, col_ref, q_ref, k_ref, v_ref, out_ref, lse_ref, peak_ref
):
    pairs, length, _ = q_ref.shape

    @pl.loop(0, length // BLOCK)
    def _(t):
        rows = pl.ds(pl.multiple_of(t * BLOCK, BLOCK), BLOCK)
        cosine, sine = cos_ref[rows, :], sin_ref[rows, :]
        for pair in range(pairs):
            first = 3 * pair * PAIR
            qkv = contract(normed_ref[rows, :], qkv_w_ref[:, first : first + 3 * PAIR], 1, 0)
            query = qkv[:, 0:PAIR]
            query = (query * cosine + swap_halves(query) * sine).astype(bf16)
            q_ref[pair, rows, :] = (query.astype(f32) * HEAD_DIM ** (-0.5)).astype(bf16)
            key = qkv[:, PAIR : 2 * PAIR]
            k_ref[pair, rows, :] = (key * cosine + swap_halves(key) * sine).astype(bf16)
            v_ref[pair, rows, :] = qkv[:, 2 * PAIR : 3 * PAIR].astype(bf16)

    peak_ref[...] = jnp.full(peak_ref.shape, -jnp.inf, f32)
    lane = lax.broadcasted_iota(jnp.int32, (BLOCK, 128), 1)
    for t in range(length // BLOCK):
        q0 = t * BLOCK
        rows = pl.ds(q0, BLOCK)
        cols = min(q0 + 2 * BLOCK, length)

        @pl.loop(0, pairs)
        def _(pair):
            total = jnp.zeros((BLOCK, PAIR), f32)
            for sub in range(2):
                head = 2 * pair + sub
                mask = head_mask((BLOCK, PAIR), sub)
                query = jnp.where(mask, q_ref[pair, rows, :], 0).astype(bf16)
                scores = masked_scores(query, k_ref.at[pair], row_ref, col_ref, q0, cols)
                row_max = jnp.max(scores, 1, keepdims=True)
                numerators = jnp.exp(scores - row_max)
                totals = jnp.sum(numerators, 1, keepdims=True)
                mixed = contract(numerators.astype(bf16), v_ref[pair, 0:cols, :], 1, 0) / totals
                total = jnp.where(mask, mixed, total)
                lse_ref[rows, :] = jnp.where(lane == head, row_max + jnp.log(totals), lse_ref[rows, :])
                peak_ref[...] = jnp.where(
                    lax.broadcasted_iota(jnp.int32, peak_ref.shape, 1) == head,
                    jnp.maximum(peak_ref[...], jnp.max(row_max)),
                    peak_ref[...],
                )
            out_ref[rows, pl.ds(pl.multiple_of(pair * PAIR, PAIR), PAIR)] = total.astype(bf16)


def attend_forward(normed, qkv_w, cosine, sine, row_blocks, col_blocks):
    length = normed.shape[0]
    pairs = qkv_w.shape[1] // (3 * PAIR)
    shape = jax.ShapeDtypeStruct
    return pl.pallas_call(
        attend_forward_kernel,
        out_shape=(
            shape((pairs, length, PAIR), bf16),
            shape((pairs, length, PAIR), bf16),
            shape((pairs, length, PAIR), bf16),
            shape((length, pairs * PAIR), bf16),
            shape((length, 128), f32),
            shape((8, 128), f32),
        ),
        in_specs=[vmem] * 6,
        out_specs=tuple([vmem] * 6),
        compiler_params=pltpu.CompilerParams(vmem_limit_bytes=56 * 1024 * 1024),
        cost_estimate=pl.CostEstimate(
            flops=16 * pairs * length * length * PAIR + 2 * normed.size * qkv_w.shape[1], bytes_accessed=100_000_000,
            transcendentals=2 * pairs * length * length,
        ),
        name="attend_forward",
    )(normed, qkv_w, cosine, sine, row_blocks, col_blocks)


def attend_backward_kernel(
    first_head, q_ref, k_ref, v_ref, grad_ref, lse_ref, cos_ref, sin_ref, row_ref, col_ref, normed_ref,
    out_ref, weight_ref, dk_ref, dv_ref,
):
    length = q_ref.shape[0]
    dk_ref[...] = jnp.zeros_like(dk_ref)
    dv_ref[...] = jnp.zeros_like(dv_ref)
    lane = lax.broadcasted_iota(jnp.int32, (BLOCK, 128), 1)
    for t in range(length // BLOCK):
        q0 = t * BLOCK
        rows = pl.ds(q0, BLOCK)
        cols = min(q0 + 2 * BLOCK, length)

        def one_head(sub, dq):
            mask = head_mask((BLOCK, PAIR), sub)
            query = jnp.where(mask, q_ref[rows, :], 0).astype(bf16)
            grad = jnp.where(mask, grad_ref[rows, :], 0).astype(bf16)
            lse = jnp.sum(
                jnp.where(lane == first_head + sub, lse_ref[rows, :], 0.0), 1, keepdims=True
            )
            scores = masked_scores(query, k_ref, row_ref, col_ref, q0, cols)
            attention = jnp.exp(scores - lse)
            grad_attention = contract(grad, v_ref[0:cols, :], 1, 1)
            weighted = attention * grad_attention
            centre = jnp.sum(weighted, 1, keepdims=True)
            grad_scores = (weighted - attention * centre).astype(bf16)
            dv_ref[0:cols, :] += contract(attention.astype(bf16), grad, 0, 0)
            dk_ref[0:cols, :] += contract(grad_scores, query, 0, 0)
            return jnp.where(mask, contract(grad_scores, k_ref[0:cols, :], 1, 0), dq)

        dq = lax.fori_loop(0, 2, one_head, jnp.zeros((BLOCK, PAIR), f32)) * HEAD_DIM ** (-0.5)
        out_ref[rows, 0:PAIR] = (dq * cos_ref[rows, :] - swap_halves(dq) * sin_ref[rows, :]).astype(bf16)
    for t in range(length // BLOCK):
        rows = pl.ds(t * BLOCK, BLOCK)
        dk = dk_ref[rows, :]
        out_ref[rows, PAIR : 2 * PAIR] = (
            dk * cos_ref[rows, :] - swap_halves(dk) * sin_ref[rows, :]
        ).astype(bf16)
        out_ref[rows, 2 * PAIR : 3 * PAIR] = dv_ref[rows, :].astype(bf16)
    side = 256

    @pl.loop(0, normed_ref.shape[1] // side)
    def _(k):
        span = pl.ds(pl.multiple_of(k * side, side), side)
        weight_ref[span, :] = contract(normed_ref[:, span], out_ref[...], 0, 0).astype(bf16)


def attend_backward(pair, query, key, value, grad, lse, cosine, sine, row_blocks, col_blocks, normed):
    length, width = normed.shape
    heads = pl.BlockSpec((None, length, PAIR), lambda _: (pair, 0, 0))
    return pl.pallas_call(
        functools.partial(attend_backward_kernel, 2 * pair),
        grid=(1,),
        out_shape=(
            jax.ShapeDtypeStruct((length, 3 * PAIR), bf16), jax.ShapeDtypeStruct((width, 3 * PAIR), bf16),
        ),
        in_specs=[heads] * 3 + [pl.BlockSpec((length, PAIR), lambda _: (0, pair))] + [vmem] * 6,
        out_specs=(vmem, vmem),
        scratch_shapes=[pltpu.VMEM((length, PAIR), f32), pltpu.VMEM((length, PAIR), f32)],
        compiler_params=pltpu.CompilerParams(vmem_limit_bytes=56 * 1024 * 1024),
        cost_estimate=pl.CostEstimate(
            flops=40 * length * length * PAIR + 6 * length * width * PAIR, bytes_accessed=100_000_000,
            transcendentals=2 * length * length,
        ),
        name="attend_backward",
    )(query, key, value, grad, lse, cosine, sine, row_blocks, col_blocks, normed)


def bit_of(index, bit):
    return lax.rem(lax.div(index, bit), 2)


def flip_bit(index, bit):
    return index + bit - 2 * bit * bit_of(index, bit)


def team_mate(me, bits, offset):
    device, place = me, 0
    for k, bit in enumerate(bits):
        moved = (offset >> k) % 2
        place = place + lax.rem(bit_of(me, bit) + moved, 2) * (1 << k)
        device = flip_bit(device, bit) if moved else device
    return device, place


class Links:

    def __init__(self, send_sems, recv_sems):
        self.send_sems, self.recv_sems = send_sems, recv_sems

    def copy(self, slot, src, dst, device):
        return pltpu.make_async_remote_copy(
            src_ref=src, dst_ref=dst, send_sem=self.send_sems.at[slot],
            recv_sem=self.recv_sems.at[slot], device_id=(device,), device_id_type=MESH,
        )


def greet(partners):
    barrier = pltpu.get_barrier_semaphore()
    for partner in partners:
        pl.semaphore_signal(barrier, inc=1, device_id=(partner,), device_id_type=MESH)
    pl.semaphore_wait(barrier, len(partners))


def spread_block(bits, cut, own_ref, out_ref, links, local_sem):
    core, first, second = bits
    me = lax.axis_index(AXIS)
    sibling, next_a, next_b = (flip_bit(me, bit) for bit in bits)
    block = own_ref.shape[0]
    in_a, in_b = bit_of(me, first), bit_of(me, second)
    spans = {None: (0, block), 0: (0, cut), 1: (cut, block - cut)}

    def rows(flip_a, flip_b, part):
        place = bit_of(me, core)
        place = place + 2 * lax.rem(in_a + flip_a, 2) + 4 * lax.rem(in_b + flip_b, 2)
        start, size = spans[part]
        return pl.ds(pl.multiple_of(place * block + start, 16), size)

    def passed(slot, where, device):
        return links.copy(slot, out_ref.at[where], out_ref.at[where], device)

    def first_hand(slot, part, device):
        start, size = spans[part]
        return links.copy(slot, own_ref.at[pl.ds(start, size)], out_ref.at[rows(0, 0, part)], device)

    makers = {
        0: lambda: first_hand(0, 0, next_a),
        1: lambda: first_hand(1, 1, next_b),
        2: lambda: first_hand(2, 1, next_a),
        3: lambda: first_hand(3, 0, next_b),
        4: lambda: links.copy(4, own_ref, out_ref.at[rows(0, 0, None)], sibling),
        5: lambda: passed(5, rows(1, 0, 0), next_b),
        6: lambda: passed(6, rows(1, 0, 0), sibling),
        7: lambda: passed(7, rows(0, 1, 1), next_a),
        8: lambda: passed(8, rows(0, 1, 1), sibling),
        9: lambda: passed(9, rows(1, 0, 1), sibling),
        10: lambda: passed(10, rows(0, 1, 0), sibling),
        11: lambda: passed(11, rows(1, 1, 0), sibling),
        12: lambda: passed(12, rows(1, 1, 1), sibling),
    }
    needs = {0: 0, 1: 1, 2: 1, 3: 0, 4: None, 5: 0, 6: 0, 7: 1, 8: 1, 9: 1, 10: 0, 11: 0, 12: 1}
    copies = {slot: make() for slot, make in makers.items() if spans[needs[slot]][1]}
    keep = pltpu.make_async_copy(own_ref, out_ref.at[rows(0, 0, None)], local_sem)

    def begin():
        for slot in range(5):
            if slot in copies:
                copies[slot].start()
        keep.start()

    def hand_on(arrived, *sent):
        def phase():
            if arrived in copies:
                copies[arrived].wait_recv()
                for slot in sent:
                    copies[slot].start()

        return phase

    def finish():
        for slot in (4, 6, 8, 9, 10, 11, 12):
            if slot in copies:
                copies[slot].wait_recv()
        keep.wait()
        for slot in copies:
            copies[slot].wait_send()

    return [
        begin, hand_on(0, 5, 6), hand_on(1, 7, 8), hand_on(2, 9), hand_on(3, 10),
        hand_on(5, 11), hand_on(7, 12), finish,
    ]


def run(phases):
    for phase in phases:
        phase()


SPREAD_COPIES = 13
SUM_COPIES = 10


def sum_block(bits, cut, swapped, product, total, to_core, from_core, chip_sum, arrived, links):
    core = bits[0]
    (first, weight_a), (second, weight_b) = ((bits[2], 4), (bits[1], 2)) if swapped else ((bits[1], 2), (bits[2], 4))
    me = lax.axis_index(AXIS)
    sibling, next_a, next_b = flip_bit(me, core), flip_bit(me, first), flip_bit(me, second)
    block, width = total.shape
    tile = 512

    def place(step, other_core):
        flip_a, flip_b = 1 - step // 2, 1 - step % 2
        return (
            lax.rem(bit_of(me, core) + other_core, 2)
            + weight_a * lax.rem(bit_of(me, first) + flip_a, 2)
            + weight_b * lax.rem(bit_of(me, second) + flip_b, 2)
        )

    low, high = (0, cut), (cut, block - cut)
    landing = range(6) if cut else {1: 0, 3: 1, 4: 2}

    def link(slot, step, span, device):
        return links.copy(slot, chip_sum.at[step, pl.ds(*span)], arrived.at[landing[slot - 4], pl.ds(0, span[1])], device)

    diag_a, diag_b = (link(4, 0, low, next_a) if cut else None), link(5, 0, high, next_b)
    plain_a, plain_b = (link(6, 1, low, next_a) if cut else None), link(7, 2, high, next_b)
    last_a, last_b = link(8, 1, high, next_a), (link(9, 2, low, next_b) if cut else None)

    def core_copy(step):
        return links.copy(step, to_core.at[step], from_core.at[step], sibling)

    def for_sibling():
        @pl.loop(0, 4)
        def _(step):
            @pl.loop(0, width // tile)
            def _(column):
                columns = pl.ds(pl.multiple_of(column * tile, tile), tile)
                to_core[step, :, columns] = product(place(step, 1), columns).astype(bf16)

            core_copy(step).start()

    def for_chip():
        @pl.loop(0, 4)
        def _(step):
            core_copy(step).wait_recv()

            @pl.loop(0, width // tile)
            def _(column):
                columns = pl.ds(pl.multiple_of(column * tile, tile), tile)
                summed = product(place(step, 0), columns) + from_core[step, :, columns].astype(f32)
                total[:, columns] = summed

                @pl.when(step < 3)
                def _():
                    chip_sum[step, :, columns] = summed.astype(bf16)

            @pl.when(step == 0)
            def _():
                if cut:
                    diag_a.start()
                diag_b.start()

            @pl.when(step == 1)
            def _():
                if cut:
                    plain_a.start()

            @pl.when(step == 2)
            def _():
                plain_b.start()

    def add(step, span, slot):
        rows = pl.ds(*span)
        chip_sum[step, rows, :] = (
            chip_sum[step, rows, :].astype(f32) + arrived[landing[slot], 0 : span[1], :].astype(f32)
        ).astype(bf16)

    def take(span, slot):
        total[pl.ds(*span), :] += arrived[landing[slot], 0 : span[1], :].astype(f32)

    def hand_on():
        if cut:
            diag_a.wait_recv()
            add(2, low, 0)
            last_b.start()
        diag_b.wait_recv()
        add(1, high, 1)
        last_a.start()

    def finish():
        if cut:
            plain_a.wait_recv()
            take(low, 2)
        plain_b.wait_recv()
        take(high, 3)
        if cut:
            last_b.wait_recv()
            take(low, 5)
        last_a.wait_recv()
        take(high, 4)

        @pl.loop(0, 4)
        def _(step):
            core_copy(step).wait_send()

        for copy in (diag_a, diag_b, plain_a, plain_b, last_a, last_b):
            if copy is not None:
                copy.wait_send()

    return for_sibling, for_chip, hand_on, finish


def sum_scratch(block, width, cut):
    return [
        pltpu.VMEM((block, width), f32),
        pltpu.VMEM((4, block, width), bf16),
        pltpu.VMEM((4, block, width), bf16),
        pltpu.VMEM((3, block, width), bf16),
        pltpu.VMEM((6 if cut else 3, block - cut, width), bf16),
        pltpu.SemaphoreType.DMA((SUM_COPIES,)),
        pltpu.SemaphoreType.DMA((SUM_COPIES,)),
    ]


def spread_scratch(block, width):
    return [
        pltpu.VMEM((block, width), bf16),
        pltpu.SemaphoreType.DMA((SPREAD_COPIES,)),
        pltpu.SemaphoreType.DMA((SPREAD_COPIES,)),
        pltpu.SemaphoreType.DMA,
    ]


def link_params(collective_id):
    return pltpu.CompilerParams(
        collective_id=collective_id, has_side_effects=True, vmem_limit_bytes=60 * 1024 * 1024
    )


def cost(flops, size):
    return pl.CostEstimate(flops=int(flops), bytes_accessed=int(size), transcendentals=0)


def row_scale(values):
    return lax.rsqrt(jnp.mean(values * values, -1, keepdims=True) + epsilon)


def front_kernel(
    team, teams, qkv_moves, ffn_moves, carry_bits, tokens_ref, query_ref, key_ref, value_ref, gate_ref, up_ref, small_ref, *refs,
):
    moved = len(carry_bits)
    (carried, refs) = (refs[0], refs[1:]) if moved else (None, refs)
    (normed_out, weights_out, both_out, small_out), refs = refs[:4], refs[4:]
    carried_out, refs = refs[:moved], refs[moved:]
    (tokens_all, mine, both_mine, gain,
    send_sems, recv_sems, local_sem, swap_send, swap_recv, swap_local, line_send, line_recv, small_send, small_recv,
    both_send, both_recv, both_local, out_sems, *carry_sems) = refs
    me = lax.axis_index(AXIS)
    mate, group = lax.rem(me, team), lax.div(me, team)
    devices = team * teams
    mates = [group * team + lax.rem(mate + k, team) for k in range(1, team)]
    above, below = lax.rem(me + team, devices), lax.rem(me + devices - team, devices)
    ffn_mates = [team_mate(me, (1, 2, 8), k) for k in range(team)]
    rows = mine.shape[1]
    swaps, line, small = Links(swap_send, swap_recv), Links(line_send, line_recv), Links(small_send, small_recv)
    both = Links(both_send, both_recv)
    for i, member, source, target, columns in qkv_moves:
        weight = (query_ref, key_ref, value_ref)[i]
        mine[member, :, target : target + columns] = weight[:, source : source + columns]
    greet(
        mates + [lax.rem(me + k * team, devices) for k in range(1, teams)]
        + [device for device, _ in ffn_mates[4:]]
    )

    def share(place):
        return pl.ds(pl.multiple_of(place * rows, rows), rows)

    swap_copies = [
        swaps.copy(k, mine.at[lax.rem(mate + k + 1, team)], weights_out.at[group, share(mate)], mates[k])
        for k in range(team - 1)
    ]
    crossing = [
        Links(*carry_sems).copy(i, carried, carried_out[i], flip_bit(me, bit)) for i, bit in enumerate(carry_bits)
    ]
    for copy in swap_copies:
        copy.start()
    keep = pltpu.make_async_copy(mine.at[mate], weights_out.at[group, share(mate)], swap_local)
    keep.start()
    small_out[me] = small_ref[...]

    others = [lax.rem(me + k * team, devices) for k in range(1, teams)]
    team_rows = pl.ds(pl.multiple_of(group * team, team), team)
    small_near = [
        small.copy(k, small_out.at[me], small_out.at[me], device) for k, device in enumerate(mates)
    ]
    small_far = [
        small.copy(team + k, small_out.at[team_rows], small_out.at[team_rows], device)
        for k, device in enumerate(others)
    ]
    for copy in small_near:
        copy.start()
    spread = spread_block(
        (1, 2, 4), HALF, tokens_ref, tokens_all, Links(send_sems, recv_sems), local_sem
    )
    for i, member, source, target, columns in ffn_moves:
        both_mine[i * team + member, :, target : target + columns] = (gate_ref, up_ref)[i][:, source : source + columns]

    def passed(slot, shard, device):
        return line.copy(slot, weights_out.at[shard], weights_out.at[shard], device)

    steps = teams - 1

    def up(step):
        return passed(step - 1, group - (step - 1), above)

    def down(step):
        return passed(steps + step - 1, group + (step - 1), below)

    def line_start(step):
        pl.when((group < teams - 1) & (group >= step - 1))(lambda: up(step).start())
        pl.when((group > 0) & (group + step - 1 < teams))(lambda: down(step).start())

    def line_wait(step):
        pl.when(group >= step)(lambda: up(step).wait_recv())
        pl.when(group + step < teams)(lambda: down(step).wait_recv())

    def line_sent(step):
        pl.when((group < teams - 1) & (group >= step - 1))(lambda: up(step).wait_send())
        pl.when((group > 0) & (group + step - 1 < teams))(lambda: down(step).wait_send())

    for copy in small_near:
        copy.wait_recv()
    for copy in small_far:
        copy.start()
    own_place = ffn_mates[0][1]
    both_copies = [
        both.copy(
            i * team + k, both_mine.at[i * team + ffn_mates[k][1]], both_out.at[i * team + own_place], ffn_mates[k][0]
        )
        for i in range(2) for k in range(1, team)
    ]
    for copy in both_copies:
        copy.start()
    both_keep = [
        pltpu.make_async_copy(both_mine.at[i * team + own_place], both_out.at[i * team + own_place], both_local.at[i])
        for i in range(2)
    ]
    for copy in both_keep:
        copy.start()
    for copy in swap_copies:
        copy.wait_recv()
    keep.wait()
    line_start(1)
    spread[0]()
    for copy in crossing:
        copy.start()
    for copy in small_far:
        copy.wait_recv()
    spread[1]()
    spread[2]()
    line_wait(1)
    line_start(2)
    spread[3]()
    spread[4]()
    width = tokens_all.shape[1]
    gains = width // devices
    for d in range(devices):
        gain[:, d * gains : (d + 1) * gains] = small_out[d, 0:1, 0:gains]
    for phase in spread[5:]:
        phase()
    block = tokens_ref.shape[0]

    def normed_copy(k):
        span = pl.ds(pl.multiple_of(k * block, block), block)
        return pltpu.make_async_copy(tokens_all.at[span], normed_out.at[span], out_sems.at[k])

    def norm_blocks(first, last):
        @pl.loop(first, last)
        def _(k):
            span = pl.ds(pl.multiple_of(k * block, block), block)
            values = tokens_all[span, :].astype(f32)
            tokens_all[span, :] = (values * row_scale(values) * gain[...]).astype(bf16)
            normed_copy(k).start()

    norm_blocks(0, 2)
    for step in range(2, teams):
        line_wait(step)
        if step < steps:
            line_start(step + 1)
        if step == 2:
            norm_blocks(2, team)
    for k in range(team):
        normed_copy(k).wait()
    for copy in both_copies:
        copy.wait_recv()
    for copy in both_keep:
        copy.wait()
    for copy in swap_copies + both_copies:
        copy.wait_send()
    for step in range(1, teams):
        line_sent(step)
    for copy in small_near + small_far:
        copy.wait_send()
    for copy in crossing:
        copy.wait()


def front(tokens, weights, small, teams, qkv_moves, ffn_moves, carried, carry_bits):
    block, width = tokens.shape
    team = 8
    rows, cols = weights[0].shape[0], 3 * width // team
    both_cols = weights[3].shape[1] // team
    devices = team * teams
    dma = pltpu.SemaphoreType.DMA
    shape = jax.ShapeDtypeStruct
    return pl.pallas_call(
        functools.partial(front_kernel, team, teams, qkv_moves, ffn_moves, carry_bits),
        out_shape=(
            shape((team * block, width), bf16),
            shape((teams, team * rows, cols), bf16),
            shape((2 * team, rows, both_cols), bf16),
            shape((devices,) + small.shape, f32),
        ) + tuple(shape(carried[0].shape, bf16) for _ in carry_bits),
        in_specs=[vmem] * 7 + [anywhere] * len(carried),
        out_specs=(anywhere, anywhere, anywhere, vmem) + (anywhere,) * len(carry_bits),
        scratch_shapes=[
            pltpu.VMEM((team * block, width), bf16), pltpu.VMEM((team, rows, cols), bf16),
            pltpu.VMEM((2 * team, rows, both_cols), bf16), pltpu.VMEM((1, width), f32),
        ]
        + spread_scratch(block, width)[1:]
        + [dma((team - 1,)), dma((team - 1,)), dma, dma((2 * teams,)), dma((2 * teams,)), dma((team + teams,)), dma((team + teams,))]
        + [dma((2 * team,)), dma((2 * team,)), dma((2,)), dma((team,))]
        + [dma((1,))] * (2 * len(carried)),
        compiler_params=link_params(1),
        cost_estimate=cost(0, 200e6),
        name="front",
    )(tokens, *weights, small, *carried)


def branch_kernel(
    carry, swap_bits, spread_bits, left_ref, right_ref, residual_ref, gain_ref, peak_ref, *refs,
):
    if carry:
        (both_own, both_y, both_z, down_own, down_y), refs = refs[:5], refs[5:]
        (h2_ref, out_ref, peak_out, gate_full, up_full, down_full), refs = refs[:6], refs[6:]
        (landed, together, swap_send, swap_recv, own, send_sems, recv_sems, local_sem,
         peak_in, peak_send, peak_recv, carry_send, carry_recv, carry_local) = refs
    else:
        (h2_ref, out_ref, peak_out), refs = refs[:3], refs[3:]
        (landed, together, swap_send, swap_recv, own, send_sems, recv_sems, local_sem,
         peak_in, peak_send, peak_recv) = refs
    me = lax.axis_index(AXIS)
    team, block, _ = landed.shape
    bits = [1 << k for k in range(peak_in.shape[0])]
    mates = [team_mate(me, swap_bits, k) for k in range(team)]
    greet([device for device, _ in mates[1:]] + [flip_bit(me, bit) for bit in bits if bit not in swap_bits])
    own_place = mates[0][1]

    def rows_at(place):
        return pl.ds(pl.multiple_of(place * block, block), block)

    swap_copies = [
        Links(swap_send, swap_recv).copy(k, left_ref.at[rows_at(mates[k][1])], landed.at[own_place], mates[k][0])
        for k in range(1, team)
    ]
    for copy in swap_copies:
        copy.start()
    peaks = Links(peak_send, peak_recv)

    def peak_copy(k):
        return peaks.copy(k, peak_out, peak_in.at[k], flip_bit(me, bits[k]))

    def peak_step(k):
        if k:
            peak_copy(k - 1).wait()
            peak_out[...] = jnp.maximum(peak_out[...], peak_in[k - 1])
        if k < len(bits):
            peak_copy(k).start()

    if carry:
        carried = Links(carry_send, carry_recv)
        high, middle = bit_of(me, 16), bit_of(me, 4)
        by_y, by_z = flip_bit(me, 4), flip_bit(me, 16)

        def rows_of(part, flip_z, flip_y):
            z, y = lax.rem(high + flip_z, 2), lax.rem(middle + flip_y, 2)
            return pl.ds(pl.multiple_of(z * 16 + part * 8 + y * 4, 4), 4)

        early = both_z.shape[0] // 4

        def piece(source, half):
            return source.at[pl.ds(half * 4, 4)]

        def placed(half, flips):
            return (gate_full, up_full)[half // 2].at[rows_of(half % 2, *flips)]

        def unit(flip_z, flip_y):
            return lax.rem(high + flip_z, 2) * 2 + lax.rem(middle + flip_y, 2)

        kept = []
        for source, flips, halves in ((both_own, (0, 0), 4), (both_y, (0, 1), 4), (both_z, (1, 0), early)):
            for half in range(halves):
                kept.append((piece(source, half), placed(half, flips)))
        kept.append((down_own, down_full.at[unit(0, 0)]))
        kept.append((down_y, down_full.at[unit(0, 1)]))
        kept = [pltpu.make_async_copy(a, b, carry_local.at[i]) for i, (a, b) in enumerate(kept)]
        up_z = [
            carried.copy(half, piece(both_own, half), placed(half, (0, 0)), by_z) for half in range(early, 4)
        ]
        early_yz = [
            carried.copy(4 + half, piece(both_z, half), placed(half, (1, 0)), by_y) for half in range(early)
        ]
        up_yz = [
            carried.copy(4 + half, placed(half, (1, 0)), placed(half, (1, 0)), by_y) for half in range(early, 4)
        ]
        down_z = carried.copy(8, down_own, down_full.at[unit(0, 0)], by_z)
        for copy in up_z + kept:
            copy.start()

    peak_out[...] = peak_ref[...]
    peak_step(0)
    landed[own_place] = left_ref[rows_at(own_place), :]
    for copy in swap_copies:
        copy.wait_recv()
    if carry:
        for copy in early_yz:
            copy.start()
    share = landed.shape[2]
    for b in range(team):
        together[:, b * share : (b + 1) * share] = landed[b]
    tile = 512

    @pl.loop(0, own.shape[1] // tile)
    def _(column):
        columns = pl.ds(pl.multiple_of(column * tile, tile), tile)
        h2_ref[:, columns] = residual_ref[:, columns].astype(f32) + contract(
            together[...], right_ref[:, columns], 1, 0
        )

    h2 = h2_ref[...]
    own[...] = (h2 * row_scale(h2) * gain_ref[...]).astype(bf16)
    spread = spread_block(spread_bits, BRANCH_CUT, own, out_ref, Links(send_sems, recv_sems), local_sem)
    spread[0]()
    if carry:
        for over, on in zip(up_z, up_yz):
            over.wait_recv()
            on.start()
        down_z.start()
    for k, phase in enumerate(spread[1:-1]):
        phase()
        if k < len(bits):
            peak_step(k + 1)
    for k in range(len(spread) - 2, len(bits)):
        peak_step(k + 1)
    spread[-1]()
    for copy in swap_copies:
        copy.wait_send()
    if carry:
        for copy in kept:
            copy.wait()
        for copy in early_yz + up_yz + [down_z]:
            copy.wait_recv()
        for copy in up_z + early_yz + up_yz + [down_z]:
            copy.wait_send()


def branch(left, right, residual, gain, peak, carry, swap_bits, spread_bits, bit_count):
    block, width = residual.shape
    dma = pltpu.SemaphoreType.DMA
    shape = jax.ShapeDtypeStruct
    out_shape = [shape((block, width), f32), shape((8 * block, width), bf16), shape((8, 128), f32)]
    scratch = [pltpu.VMEM((8, block, left.shape[1]), bf16), pltpu.VMEM((block, width), bf16), dma((8,)), dma((8,))]
    scratch += spread_scratch(block, width)
    scratch += [pltpu.VMEM((bit_count, 8, 128), f32), dma((bit_count,)), dma((bit_count,))]
    if carry:
        out_shape += [
            shape((32,) + carry[0].shape[1:], bf16), shape((32,) + carry[0].shape[1:], bf16),
            shape((4,) + carry[3].shape, bf16),
        ]
        scratch += [dma((9,)), dma((9,)), dma((14,))]
    return pl.pallas_call(
        functools.partial(branch_kernel, bool(carry), swap_bits, spread_bits),
        out_shape=tuple(out_shape),
        in_specs=[vmem] * (5 + len(carry)),
        out_specs=tuple([vmem, anywhere, vmem] + [anywhere] * (len(out_shape) - 3)),
        scratch_shapes=scratch,
        compiler_params=link_params(2),
        cost_estimate=cost(16 * block * left.shape[1] * width, 300e6),
        name="attention_branch",
    )(left, right, residual, gain, peak, *carry)


def norm_back(values, gain, upstream):
    scaled = upstream * gain
    scale = row_scale(values)
    inner = jnp.mean(scaled * values, -1, keepdims=True)
    return scale * scaled - scale * scale * scale * values * inner


def ffn_back_kernel(
    cross, sum_bits, swap_bits, gate_ref, up_ref, gate_w_ref, up_w_ref, normed_ref, out_w_ref, h2_ref, cot_ref, gain_ref, *refs,
):
    (part_ref, over_ref, refs) = (refs[0], refs[1], refs[2:]) if cross else (None, None, refs)
    (residual_ref, branch_ref, heads_out, d_up_out, d_gate_own), refs = refs[:5], refs[5:]
    (d_gate_in, part_in, over_in), refs = (refs[:3], refs[3:]) if cross else ((None,) * 3, refs)
    (total, to_core, from_core, chip_sum, arrived, sum_send, sum_recv,
     swap_send, swap_recv, local_sem, stage, stage_sems, own_sems, *more) = refs
    if cross:
        cross_send, cross_recv = more
        crossing = Links(cross_send, cross_recv)
    else:
        (stage_gate,) = more
    me = lax.axis_index(AXIS)
    block, width = total.shape
    team = 1 << len(swap_bits)
    mates = [team_mate(me, swap_bits, k) for k in range(team)]
    greet(
        [device for device, _ in mates[1:]] + [flip_bit(me, bit) for bit in sum_bits if bit not in swap_bits]
        + ([flip_bit(me, 16)] if cross else [])
    )

    def product(place, columns):
        rows = pl.ds(pl.multiple_of(place * block, block), block)
        return contract(gate_ref[rows, :], gate_w_ref[columns, :], 1, 1) + contract(
            up_ref[rows, :], up_w_ref[columns, :], 1, 1
        )

    side, columns_ff = stage.shape[1:]
    count = width // side
    y_side, by_y = bit_of(me, 4), flip_bit(me, 4)
    if cross:
        part_copy = crossing.copy(count // 2, part_ref, part_in, by_y)
        over_copy = crossing.copy(count // 2 + 1, over_ref, over_in, flip_bit(me, 16))
        part_copy.start()

    def parked(i, part):
        row = i * side
        rows = pl.ds(pl.multiple_of(lax.rem(row, block), 16), side)
        return from_core.at[lax.div(row, block), rows, pl.ds(part * columns_ff, columns_ff)]

    def cross_copy(i):
        return crossing.copy(i, parked(i, 0), d_gate_in.at[i], by_y)

    def own_copy(i):
        return pltpu.make_async_copy(parked(i, 1), d_gate_own.at[i], own_sems.at[i])

    def tile_of(step):
        if not cross:
            return step
        theirs = step < count // 2
        return jnp.where(theirs, 2 * step + 1 - y_side, 2 * step - count + y_side)

    def up_copy(step):
        span = pl.ds(pl.multiple_of(tile_of(step) * side, side), side)
        slot = lax.rem(step, 2)
        return pltpu.make_async_copy(stage.at[slot], d_up_out.at[span], stage_sems.at[slot])

    def gate_copy(step):
        span = pl.ds(pl.multiple_of(step * side, side), side)
        slot = lax.rem(step, 2)
        return pltpu.make_async_copy(stage_gate.at[slot], d_gate_own.at[span], own_sems.at[slot])

    def gradients(first, last):
        @pl.loop(first, last)
        def _(step):
            @pl.when(step >= 2)
            def _():
                up_copy(step - 2).wait()
                if not cross:
                    gate_copy(step - 2).wait()

            columns = normed_ref[:, pl.ds(pl.multiple_of(tile_of(step) * side, side), side)]
            stage[lax.rem(step, 2)] = contract(columns, up_ref[...], 0, 0).astype(bf16)
            up_copy(step).start()
            tile = contract(columns, gate_ref[...], 0, 0).astype(bf16)
            if not cross:
                stage_gate[lax.rem(step, 2)] = tile
                gate_copy(step).start()
                return

            @pl.when(step < count // 2)
            def _():
                parked(step, 0)[...] = tile
                cross_copy(step).start()

            @pl.when(step >= count // 2)
            def _():
                parked(step - count // 2, 1)[...] = tile
                own_copy(step - count // 2).start()

    for_sibling, for_chip, hand_on, finish = sum_block(
        sum_bits, HALF, False, product, total, to_core, from_core, chip_sum, arrived, Links(sum_send, sum_recv)
    )
    for_sibling()
    for_chip()
    if cross:
        over_copy.start()
    gradients(0, 1)
    hand_on()
    gradients(1, count - 2)
    finish()
    residual = cot_ref[...].astype(f32) + norm_back(h2_ref[...], gain_ref[...], total[...])
    residual_ref[...] = residual
    branch_ref[...] = residual.astype(bf16)
    share = width // team
    for b in range(team):
        part = slice(b * share, (b + 1) * share)
        to_core[0, :, part] = contract(branch_ref[...], out_w_ref[part, :], 1, 1).astype(bf16)
    own_place = mates[0][1]
    own_rows = pl.ds(pl.multiple_of(own_place * block, block), block)
    def heads_of(place):
        return to_core.at[0, :, pl.ds(pl.multiple_of(place * share, share), share)]

    swap_copies = [
        Links(swap_send, swap_recv).copy(k, heads_of(mates[k][1]), heads_out.at[own_rows], mates[k][0])
        for k in range(1, team)
    ]
    keep = pltpu.make_async_copy(heads_of(own_place), heads_out.at[own_rows], local_sem)
    for copy in swap_copies + [keep]:
        copy.start()
    gradients(count - 2, count)
    for copy in swap_copies:
        copy.wait_recv()
    for copy in swap_copies:
        copy.wait_send()
    keep.wait()
    for step in range(count - 2, count):
        up_copy(step).wait()
        if not cross:
            gate_copy(step).wait()
    if cross:
        part_copy.wait()
        over_copy.wait()

        @pl.loop(0, count // 2)
        def _(i):
            own_copy(i).wait()
            cross_copy(i).wait()


def ffn_back(gate, up, gate_w, up_w, normed, out_w, h2, cot, gain, part, side, sum_bits, swap_bits):
    block, width = h2.shape
    shape = jax.ShapeDtypeStruct
    dma = pltpu.SemaphoreType.DMA
    ff_cols, cross = gate.shape[1], side % 128 == 0
    side = side if cross else 256
    tiles = width // side // 2
    if cross:
        d_gate = (shape((tiles, side, ff_cols), bf16),) * 2 + (shape(part[0].shape, bf16),) * 2
        more = [dma((tiles + 2,)), dma((tiles + 2,))]
    else:
        d_gate, more = (shape((width, ff_cols), bf16),), [pltpu.VMEM((2, side, ff_cols), bf16)]
    return pl.pallas_call(
        functools.partial(ffn_back_kernel, cross, sum_bits, swap_bits),
        out_shape=(
            shape((block, width), f32), shape((block, width), bf16), shape((8 * block, width // 8), bf16),
            shape((width, ff_cols), bf16),
        ) + d_gate,
        in_specs=[vmem] * 9 + [anywhere] * len(part),
        out_specs=(vmem, vmem) + (anywhere,) * (2 + len(d_gate)),
        scratch_shapes=sum_scratch(block, width, HALF)
        + [dma((8,)), dma((8,)), dma]
        + [pltpu.VMEM((2, side, ff_cols), bf16), dma((2,)), dma((tiles,))]
        + more,
        compiler_params=link_params(3),
        cost_estimate=cost(96 * block * ff_cols * width, 200e6),
        name="ffn_back",
    )(gate, up, gate_w, up_w, normed, out_w, h2, cot, gain, *part)


def last_sums_kernel(
    carry_bits, sum_bits, ffn_bits, left_ref, other_ref, right_ref, tokens_ref, gain_ref, residual_ref, hidden_ref,
    down_ref, h2_ref, gate_ref, *refs,
):
    moved = len(carry_bits)
    carried, (out_ref, mixed_ref, gate_out), refs = refs[:moved], refs[moved : moved + 3], refs[moved + 3 :]
    carried_out, scratch = refs[:moved], refs[moved:]
    if moved:
        carry_sems, scratch = scratch[-2:], scratch[:-2]
    (swap_send, swap_recv, swap_local), scratch = scratch[-3:], scratch[:-3]
    count = len(scratch) // 2
    me = lax.axis_index(AXIS)
    total, ffn_total = scratch[0], scratch[count]
    block = total.shape[0]
    mates = [team_mate(me, ffn_bits, k) for k in range(8)]
    partners = [flip_bit(me, bit) for bit in sum_bits if bit not in ffn_bits]
    greet(partners + [device for device, _ in mates[1:]] + [flip_bit(me, bit) for bit in carry_bits])
    crossing = [
        Links(*carry_sems).copy(i, carried[i], carried_out[i], flip_bit(me, bit)) for i, bit in enumerate(carry_bits)
    ]
    for copy in crossing:
        copy.start()
    swaps, own_place = Links(swap_send, swap_recv), mates[0][1]
    swap_copies = [
        swaps.copy(k, gate_ref.at[mates[k][1]], gate_out.at[own_place], mates[k][0]) for k in range(1, 8)
    ]
    keep = pltpu.make_async_copy(gate_ref.at[own_place], gate_out.at[own_place], swap_local)

    def rows_of(place):
        return pl.ds(pl.multiple_of(place * block, block), block)

    def product(place, columns):
        rows = rows_of(place)
        middle = left_ref.shape[1]
        return contract(left_ref[rows, :], right_ref[columns, 0:middle], 1, 1) + contract(
            other_ref[rows, :], right_ref[columns, middle : 2 * middle], 1, 1
        )

    def ffn_product(place, columns):
        return contract(hidden_ref[rows_of(place), :], down_ref[:, columns], 1, 0)

    first = sum_block(sum_bits, LAST_CUT, False, product, *scratch[: count - 2], Links(*scratch[count - 2 : count]))
    second = sum_block(ffn_bits, HALF, True, ffn_product, *scratch[count:-2], Links(*scratch[-2:]))
    run(first[:2])
    run(second[:2])
    for copy in swap_copies + [keep]:
        copy.start()
    for one, other in zip(first[2:], second[2:]):
        one()
        other()
    out_ref[...] = residual_ref[...] + norm_back(
        tokens_ref[...].astype(f32), gain_ref[...], total[...]
    )
    mixed_ref[...] = (h2_ref[...] + ffn_total[...]).astype(bf16)
    for copy in swap_copies:
        copy.wait_recv()
    for copy in swap_copies:
        copy.wait_send()
    keep.wait()
    for copy in crossing:
        copy.wait()


def last_sums(left, other, right, tokens, gain, residual, hidden, down, h2, d_gate, carry, carry_bits, sum_bits, ffn_bits):
    block, width = tokens.shape
    return pl.pallas_call(
        functools.partial(last_sums_kernel, carry_bits, sum_bits, ffn_bits),
        out_shape=(
            jax.ShapeDtypeStruct((block, width), f32), jax.ShapeDtypeStruct((block, width), bf16),
            jax.ShapeDtypeStruct(d_gate.shape, bf16),
        ) + tuple(jax.ShapeDtypeStruct(x.shape, x.dtype) for x in carry),
        in_specs=[vmem] * 9 + [anywhere] * (1 + len(carry)),
        out_specs=(vmem, vmem, anywhere) + (anywhere,) * len(carry),
        scratch_shapes=sum_scratch(block, width, LAST_CUT) + sum_scratch(block, width, HALF)
        + [pltpu.SemaphoreType.DMA((8,)), pltpu.SemaphoreType.DMA((8,)), pltpu.SemaphoreType.DMA]
        + [pltpu.SemaphoreType.DMA((1,))] * (2 * len(carry)),
        compiler_params=link_params(4),
        cost_estimate=cost(16 * block * right.size // 8, 300e6),
        name="last_sums",
    )(left, other, right, tokens, gain, residual, hidden, down, h2, d_gate, *carry)


def exchange_kernel(teams, sources, *refs):
    mine, landed, (send_sems, recv_sems, local_sems) = refs[:sources], refs[sources : 2 * sources], refs[2 * sources :]
    me = lax.axis_index(AXIS)
    members = mine[0].shape[0]
    links = Links(send_sems, recv_sems)
    greeted = {}
    for bits in teams:
        for k in range(1, members):
            device, _ = team_mate(me, bits, k)
            greeted[tuple(sorted(bit for j, bit in enumerate(bits) if (k >> j) % 2))] = device
    greet(list(greeted.values()))
    copies, kept = [], []
    for i, (source, target, bits) in enumerate(zip(mine, landed, teams)):
        own = team_mate(me, bits, 0)[1]
        kept.append(pltpu.make_async_copy(source.at[own], target.at[own], local_sems.at[i]))
        for k in range(1, members):
            device, place = team_mate(me, bits, k)
            copies.append(links.copy(i * members + k, source.at[place], target.at[own], device))
    for copy in copies + kept:
        copy.start()
    for copy in copies:
        copy.wait()
    for copy in kept:
        copy.wait()


def exchange(parts, teams):
    dma = pltpu.SemaphoreType.DMA
    slots = len(parts) * parts[0].shape[0]
    return pl.pallas_call(
        functools.partial(exchange_kernel, teams, len(parts)),
        out_shape=tuple(jax.ShapeDtypeStruct(part.shape, part.dtype) for part in parts),
        in_specs=[vmem] * len(parts),
        out_specs=tuple([vmem] * len(parts)),
        scratch_shapes=[dma((slots,)), dma((slots,)), dma((len(parts),))],
        compiler_params=link_params(5),
        cost_estimate=cost(1e6, 40e6),
        name="exchange",
    )(*parts)


def home_kernel(places, gain_of, sources, *refs):
    count = len(places)
    kinds = max(gain_of) + 1
    parts, weights, gains = refs[:sources], refs[sources : sources + count], refs[sources + count : sources + count + kinds]
    outs, gain_outs = refs[-count - kinds : -kinds], refs[-kinds:]
    totals = [jnp.zeros(gain.shape, f32) for gain in gains]
    for i, (out, weight) in enumerate(zip(outs, weights)):
        for source, member, first, target, columns in places[i]:
            out[:, target : target + columns] = parts[source][member, :, first : first + columns].astype(f32)
        for first in range(0, out.shape[1], 1024):
            product = out[:, first : first + 1024] * weight[:, first : first + 1024].astype(f32)
            totals[gain_of[i]] += jnp.sum(product, 1, keepdims=True)
    for gain, total, out in zip(gains, totals, gain_outs):
        out[...] = jnp.broadcast_to(total / gain[...], (out.shape[1], 128)).T[0:1, :]


def home(parts, weights, gains, gain_of, places):
    shape = jax.ShapeDtypeStruct
    count = len(weights)
    gains = [gain.astype(f32).reshape(-1, 1) for gain in gains]
    return pl.pallas_call(
        functools.partial(home_kernel, places, gain_of, len(parts)),
        out_shape=tuple(shape(w.shape, f32) for w in weights) + tuple(shape((1, g.shape[0]), f32) for g in gains),
        in_specs=[vmem] * (len(parts) + count + len(gains)),
        out_specs=tuple([vmem] * (count + len(gains))),
        compiler_params=pltpu.CompilerParams(vmem_limit_bytes=40 * 1024 * 1024),
        cost_estimate=cost(1e6, 30e6),
        name="home",
    )(*parts, *weights, *gains)


def body(
    tokens, block_of, clip_limit, norm_attn, w_query, w_key, w_value, w_out,
    norm_ffn, w_gate, w_up, w_down, cotangent,
):
    tok_rows, width = tokens.shape
    devices = lax.axis_size(AXIS)
    team = SEQ // tok_rows
    teams = devices // team
    head_total = width // HEAD_DIM
    heads = head_total // team
    head_cols = heads * HEAD_DIM
    ff_rows = w_down.shape[0]
    weight_rows = w_gate.shape[0]
    ff_cols = w_gate.shape[1] // team
    device = lax.axis_index(AXIS)
    mate = device % team
    bit_count = devices.bit_length() - 1
    attn_bits, ffn_bits = (1, 2, 4), (1, 2, 8)
    data_bits = [4] + [1 << k for k in range(4, bit_count)]
    in_team = [[g * team + b for b in range(team)] for g in range(teams)]
    across = [[g * team + b for g in range(teams)] for b in range(team)]
    ffn_team = [
        [g * 16 + z * 8 + y * 4 + c for z in range(2) for c in range(4)]
        for g in range(devices // 16)
        for y in range(2)
    ]

    def flip(x, bit):
        return lax.ppermute(x, AXIS, [(i, i ^ bit) for i in range(devices)])

    def gather_across(x):
        return lax.all_gather(x, AXIS, axis=0, tiled=True, axis_index_groups=across)

    def scatter_across(x):
        return lax.psum_scatter(
            x.astype(bf16), AXIS, scatter_dimension=0, tiled=True, axis_index_groups=across
        )

    def dim_of(bit):
        return bit_count - bit.bit_length()

    def data_pieces(x):
        pieces = {0: x}
        for bit in reversed(data_bits):
            for key in list(pieces):
                pieces[key | bit] = flip(pieces[key], bit)
        return pieces

    def place_pieces(pieces, dims, shape):
        total = jnp.zeros(shape, bf16)
        for key, piece in pieces.items():
            start = [0] * len(shape)
            size = list(shape)
            for bit in data_bits:
                start[dims[bit]] = ((device // bit) + (1 if key & bit else 0)) % 2
                size[dims[bit]] = 1
            total = lax.dynamic_update_slice(total, piece.reshape(size), start)
        return total

    def after_bit(dims, bit):
        return {b: d - (d > dims[bit]) for b, d in dims.items() if b != bit}

    def data_sum(x, dims, bits):
        for bit in bits:
            mine = (device // bit) % 2
            keep = lax.dynamic_index_in_dim(x, mine, dims[bit], False)
            sent = flip(lax.dynamic_index_in_dim(x, 1 - mine, dims[bit], False), bit)
            x = (keep.astype(f32) + sent.astype(f32)).astype(bf16)
            dims = after_bit(dims, bit)
        return x

    row_dims = {bit: dim_of(bit) for bit in data_bits}
    row_shape = (2,) * bit_count
    unit_dims = {bit: i for i, bit in enumerate(reversed(data_bits))}
    unit_shape = (2,) * len(data_bits)

    def tie(*values):
        return lax.optimization_barrier(values)

    qkv_moves = tuple(
        (i, b, (g * team + b) * HEAD_DIM, (3 * (g // 2) + i) * PAIR + (g % 2) * HEAD_DIM, HEAD_DIM)
        for i in range(3) for g in range(heads) for b in range(team)
    )
    ffn_units = tuple(
        (z * 4 + c, (2 * h + y) * ff_rows, (h * 16 + z * 8 + y * 4 + c) * ff_rows)
        for h in range(devices // 16) for z in range(2) for y in range(2) for c in range(4)
    )
    ffn_moves = tuple(
        (i, member, source, target, ff_rows)
        for i in range(2) for member, target, source in ffn_units
    )
    gain_row = jnp.concatenate([norm_attn, norm_ffn]).astype(f32)
    gain_row = jnp.pad(gain_row, (0, 128 - 2 * weight_rows)).reshape(1, 128)
    block_rows = block_of.astype(f32).reshape(tok_rows // 128, 128)
    small = jnp.concatenate([gain_row, block_rows, jnp.zeros((7 - tok_rows // 128, 128), f32)])
    ahead = data_bits == [4, 16]
    normed_attn, qkv_w, both_mine, gathered, *down_moved = front(
        tokens, (w_query, w_key, w_value, w_gate, w_up), small, teams, qkv_moves, ffn_moves,
        [w_down] if ahead else [], (4,) if ahead else (),
    )
    qkv_w = qkv_w.reshape(width, 3 * head_cols)
    gain_attn = gathered[:, 0, :weight_rows].reshape(1, width)
    gain_ffn = gathered[:, 0, weight_rows : 2 * weight_rows].reshape(1, width)
    blocks = lax.dynamic_slice_in_dim(gathered, device - mate, team, 0)
    blocks = blocks[:, 1 : 1 + tok_rows // 128].astype(jnp.int32).reshape(SEQ)
    row_blocks, col_blocks = blocks.reshape(1, SEQ), blocks.reshape(SEQ, 1)
    if weight_rows == HEAD_DIM:
        both_mine, qkv_w, out_mine = tie(both_mine, qkv_w, gather_across(w_out))
        out_w = lax.all_gather(out_mine, AXIS, axis=0, tiled=True, axis_index_groups=in_team)
    else:
        out_w = lax.all_gather(w_out, AXIS, axis=0, tiled=True)
        out_w = out_w.reshape(heads, team, HEAD_DIM, width).transpose(1, 0, 2, 3).reshape(width, width)

    def whole_rows(mine):
        shape = row_shape + (weight_rows, ff_cols)
        return place_pieces(data_pieces(mine), row_dims, shape).reshape(width, ff_cols)

    cosine, sine = rope_tables(SEQ, PAIR)
    if data_bits == [4, 16]:
        carry = [both_mine, flip(both_mine, 4), flip(both_mine[: 4 * EARLY_HALVES], 16), w_down, *down_moved]
    else:
        carry = []
    query, key, value, attended, lse, peak = attend_forward(
        normed_attn, qkv_w, cosine, sine, row_blocks, col_blocks
    )
    cot_mine = cotangent
    peaks = jnp.where(
        (jnp.arange(head_total) % team) == mate, jnp.repeat(peak[0, :heads], team), -jnp.inf
    )
    peaks = jnp.broadcast_to(jnp.pad(peaks, (0, 128 - head_total))[None], (8, 128))
    if carry:
        carry[1], carry[2], attended, cot_mine = tie(carry[1], carry[2], attended, cotangent)
    after_attn, normed_ffn, peaks, *full = branch(
        attended, out_w, tokens, gain_ffn, peaks, carry, attn_bits, ffn_bits, bit_count
    )
    head_peak = peaks[0, :head_total]
    if carry:
        gate_w, up_w = (w.reshape(width, ff_cols) for w in full[:2])
        z_side, y_side = (device // 16) % 2, (device // 4) % 2
        passed = lax.dynamic_index_in_dim(full[2], (1 - z_side) * 2 + y_side, 0, True)
        down_w = lax.dynamic_update_slice(
            full[2], flip(passed, 4), ((1 - z_side) * 2 + 1 - y_side, 0, 0)
        ).reshape(ff_cols, width)
    else:
        gate_w, up_w = whole_rows(both_mine[:team]), whole_rows(both_mine[team:])
        down_w = place_pieces(
            data_pieces(w_down), unit_dims, unit_shape + (ff_rows, width)
        ).reshape(ff_cols, width)
    gate_pre = contract(normed_ffn, gate_w, 1, 0)
    up_pre = contract(normed_ffn, up_w, 1, 0)
    sigmoid_gate = jax.nn.sigmoid(gate_pre)
    silu_gate = gate_pre * sigmoid_gate
    hidden = (silu_gate * up_pre).astype(bf16)

    team_cot = lax.all_gather(cot_mine, AXIS, axis=0, tiled=True, axis_index_groups=ffn_team)
    d_down = contract(hidden, team_cot, 0, 0).astype(bf16).reshape(unit_shape + (ff_rows, width))
    team_cot, d_down = tie(team_cot, d_down)
    d_hidden = contract(team_cot, down_w, 1, 1)
    grad_gate = (d_hidden * up_pre * sigmoid_gate * (1.0 + gate_pre * (1.0 - sigmoid_gate))).astype(bf16)
    grad_up = (d_hidden * silu_gate).astype(bf16)

    unit_rest, row_rest = after_bit(unit_dims, data_bits[0]), after_bit(row_dims, data_bits[0])
    row_values = (weight_rows, ff_cols)
    crosses = data_bits == [4, 16]
    if crosses:
        y_side, z_side = (device // 4) % 2, (device // 16) % 2
        kept = lax.dynamic_index_in_dim(d_down, y_side, unit_dims[4], False)
        sent = lax.dynamic_index_in_dim(d_down, 1 - y_side, unit_dims[4], False)
        mine, theirs = (lax.dynamic_index_in_dim(kept, z, 0, False) for z in (z_side, 1 - z_side))
        to_mine, to_theirs = (lax.dynamic_index_in_dim(sent, z, 0, False) for z in (z_side, 1 - z_side))
        theirs = (theirs.astype(f32) + flip(to_theirs, 4).astype(f32)).astype(bf16)
        grad_gate, theirs = tie(grad_gate, theirs)
        beside = [to_mine, theirs]
    else:
        beside = []
    d_residual, branch_mine, grad_attended, d_up, *d_gate = ffn_back(
        grad_gate, grad_up, gate_w, up_w, normed_ffn, out_w, after_attn, cotangent, gain_ffn, beside, 4 * weight_rows,
        ffn_bits, attn_bits,
    )
    if crosses:
        d_down = mine.astype(f32) + d_gate[2].astype(f32) + d_gate[3].astype(f32)
        d_gate = (d_gate[0].astype(f32) + d_gate[1].astype(f32)).astype(bf16)
        d_gate = d_gate.reshape((2,) * (bit_count - 1) + row_values)
    else:
        d_down = data_sum(d_down, unit_dims, data_bits[:1])
        d_gate = data_sum(d_gate[0].reshape(row_shape + row_values), row_dims, data_bits[:1])
    if not crosses:
        d_down = data_sum(d_down, unit_rest, data_bits[1:]).astype(f32)
    grad_attended, d_gate = tie(grad_attended, d_gate)
    d_gate = data_sum(d_gate, row_rest, data_bits[1:])
    branch_grad = lax.all_gather(branch_mine, AXIS, axis=0, tiled=True, axis_index_groups=in_team)

    def heads_back(pair):
        return attend_backward(
            pair, query, key, value, grad_attended, lse, cosine, sine, row_blocks, col_blocks, normed_attn
        )

    grad_pairs, shares = [None] * (heads // 2), [None] * (heads // 2)
    grad_pairs[0], share = heads_back(0)
    grad_attended, d_gate, d_up, share, branch_grad = tie(grad_attended, d_gate, d_up, share, branch_grad)
    shares[0] = scatter_across(share)
    d_up = data_sum(d_up.reshape(row_shape + row_values), row_dims, data_bits[:1])
    for p in range(1, heads // 2):
        grad_pairs[p], share = heads_back(p)
        grad_pairs[p], share, d_up = tie(grad_pairs[p], share, d_up)
        shares[p] = scatter_across(share)
    sent, sent_bits = [], ()
    if crosses:
        kept_up = lax.dynamic_index_in_dim(d_up, z_side, row_rest[16], False)
        sent, sent_bits = [lax.dynamic_index_in_dim(d_up, 1 - z_side, row_rest[16], False)], (16,)
        kept_up, sent[0] = (d.reshape(team, weight_rows, ff_cols) for d in (kept_up, sent[0]))
    else:
        d_up = data_sum(d_up, row_rest, data_bits[1:])
    grad_pairs[0], shares[0] = tie(grad_pairs[0], shares[0])
    d_gate = d_gate.reshape(team, weight_rows, ff_cols)
    d_tokens, mixed, d_gate, *landed = last_sums(
        *grad_pairs, qkv_w, tokens, gain_attn, d_residual, hidden, down_w, after_attn, d_gate, sent, sent_bits,
        attn_bits, ffn_bits,
    )
    if crosses:
        d_up = (kept_up.astype(f32) + landed[0].astype(f32)).astype(bf16)
    d_tokens, attended = tie(d_tokens, attended)
    out_part = contract(attended, branch_grad, 0, 0)
    if weight_rows == HEAD_DIM:
        d_out = scatter_across(out_part).astype(f32)
    else:
        spread = jnp.where(
            (jnp.arange(team) == mate)[None, :, None, None],
            out_part.reshape(heads, 1, HEAD_DIM, width), 0.0,
        ).reshape(width, width)
        d_out = lax.psum_scatter(spread, AXIS, scatter_dimension=0, tiled=True)
    places = [[], [], []]
    for i, b, source, target, columns in qkv_moves:
        places[i].append((target // (3 * PAIR), b, target % (3 * PAIR), source, columns))
    places += [
        [(heads // 2 + i, member, target, source, ff_rows) for member, target, source in ffn_units] for i in range(2)
    ]
    shares = [share.reshape(team, weight_rows, 3 * PAIR) for share in shares]
    *shares, d_up = exchange(
        shares + [d_up.reshape(team, weight_rows, ff_cols)], (attn_bits,) * (heads // 2) + (ffn_bits,)
    )
    d_query, d_key, d_value, d_gate, d_up, d_norm_attn, d_norm_ffn = home(
        shares + [d_gate, d_up], (w_query, w_key, w_value, w_gate, w_up), (norm_attn, norm_ffn), (0, 0, 0, 1, 1),
        tuple(tuple(p) for p in places),
    )
    d_norm_attn, d_norm_ffn = d_norm_attn[0], d_norm_ffn[0]
    clip_value = clip_limit.astype(f32)
    factor = jnp.sqrt(clip_value / jnp.maximum(head_peak, clip_value))
    factors = jnp.repeat(factor, HEAD_DIM)[None, :]
    clipped_query = (w_query.astype(f32) * factors).astype(bf16)
    clipped_key = (w_key.astype(f32) * factors).astype(bf16)
    return (
        mixed, d_tokens, d_norm_attn, d_query, d_key, d_value, d_out, d_norm_ffn,
        d_gate, d_up, d_down, head_peak, clipped_query, clipped_key,
    )


def solution(mesh):
    rows, whole = P(AXIS, None), P(AXIS)
    return jax.shard_map(
        body,
        mesh=mesh,
        in_specs=(rows, whole, P(), whole, rows, rows, rows, rows, whole, rows, rows, rows, rows),
        out_specs=(
            rows, rows, whole, rows, rows, rows, rows, whole, rows, rows, rows, P(), rows, rows,
        ),
        check_vma=False,
    )
```

```python
import functools

import jax
import jax.numpy as jnp
import numpy as np
from jax import lax
from jax.experimental import pallas as pl
from jax.experimental.pallas import tpu as pltpu
from jax.sharding import PartitionSpec as P

HEAD_DIM = 64
SEQ = 2048
BLOCK = 256
HALF = 128
LAST_CUT = 0
EARLY_HALVES = 3
BRANCH_CUT = 64
AXIS = "fsdp"
MESH = pl.DeviceIdType.MESH

epsilon = 1e-05
rope_base = 130000.0
bf16 = jnp.bfloat16
f32 = jnp.float32
vmem = pl.BlockSpec(memory_space=pltpu.VMEM)
anywhere = pl.BlockSpec(memory_space=pl.ANY)


def contract(left, right, left_dim, right_dim):
    return lax.dot_general(
        left, right, (((left_dim,), (right_dim,)), ((), ())), preferred_element_type=f32
    )


def rope_tables(length, width):
    half_dim = HEAD_DIM // 2
    inverse = rope_base ** (-np.arange(half_dim) * 2.0 / HEAD_DIM)
    angles = (np.arange(length, dtype=np.float32)[:, None] * inverse.astype(np.float32)).astype(np.float64)
    cosine, sine = np.cos(angles).astype(np.float32), np.sin(angles).astype(np.float32)
    repeats = width // HEAD_DIM
    return (
        jnp.asarray(np.tile(np.concatenate([cosine, cosine], 1), (1, repeats))),
        jnp.asarray(np.tile(np.concatenate([-sine, sine], 1), (1, repeats))),
    )


def swap_halves(rows):
    width = rows.shape[1]
    half = HEAD_DIM // 2
    lane = lax.broadcasted_iota(jnp.int32, rows.shape, 1)
    return jnp.where(
        lane % HEAD_DIM < half, pltpu.roll(rows, width - half, 1), pltpu.roll(rows, half, 1)
    )


PAIR = 2 * HEAD_DIM


def head_mask(shape, head):
    lane = lax.broadcasted_iota(jnp.int32, shape, 1)
    return (lane >= head * HEAD_DIM) & (lane < (head + 1) * HEAD_DIM)


def masked_scores(query, key_ref, row_ref, col_ref, q0, cols):
    tail = min(2 * BLOCK, cols)
    scores = contract(query, key_ref[0:cols, :], 1, 1)
    shown = row_ref[:, pl.ds(cols - tail, tail)] <= col_ref[pl.ds(q0, BLOCK), :]
    hidden = jnp.where(shown, scores[:, cols - tail :], -jnp.inf)
    return jnp.concatenate([scores[:, : cols - tail], hidden], 1) if tail < cols else hidden


def attend_forward_kernel(
    normed_ref, qkv_w_ref, cos_ref, sin_ref, row_ref, col_ref, q_ref, k_ref, v_ref, out_ref, lse_ref, peak_ref
):
    pairs, length, _ = q_ref.shape

    @pl.loop(0, length // BLOCK)
    def _(t):
        rows = pl.ds(pl.multiple_of(t * BLOCK, BLOCK), BLOCK)
        cosine, sine = cos_ref[rows, :], sin_ref[rows, :]
        for pair in range(pairs):
            first = 3 * pair * PAIR
            qkv = contract(normed_ref[rows, :], qkv_w_ref[:, first : first + 3 * PAIR], 1, 0)
            query = qkv[:, 0:PAIR]
            query = (query * cosine + swap_halves(query) * sine).astype(bf16)
            q_ref[pair, rows, :] = (query.astype(f32) * HEAD_DIM ** (-0.5)).astype(bf16)
            key = qkv[:, PAIR : 2 * PAIR]
            k_ref[pair, rows, :] = (key * cosine + swap_halves(key) * sine).astype(bf16)
            v_ref[pair, rows, :] = qkv[:, 2 * PAIR : 3 * PAIR].astype(bf16)

    peak_ref[...] = jnp.full(peak_ref.shape, -jnp.inf, f32)
    lane = lax.broadcasted_iota(jnp.int32, (BLOCK, 128), 1)
    for t in range(length // BLOCK):
        q0 = t * BLOCK
        rows = pl.ds(q0, BLOCK)
        cols = min(q0 + 2 * BLOCK, length)

        @pl.loop(0, pairs)
        def _(pair):
            total = jnp.zeros((BLOCK, PAIR), f32)
            for sub in range(2):
                head = 2 * pair + sub
                mask = head_mask((BLOCK, PAIR), sub)
                query = jnp.where(mask, q_ref[pair, rows, :], 0).astype(bf16)
                scores = masked_scores(query, k_ref.at[pair], row_ref, col_ref, q0, cols)
                row_max = jnp.max(scores, 1, keepdims=True)
                numerators = jnp.exp(scores - row_max)
                totals = jnp.sum(numerators, 1, keepdims=True)
                mixed = contract(numerators.astype(bf16), v_ref[pair, 0:cols, :], 1, 0) / totals
                total = jnp.where(mask, mixed, total)
                lse_ref[rows, :] = jnp.where(lane == head, row_max + jnp.log(totals), lse_ref[rows, :])
                peak_ref[...] = jnp.where(
                    lax.broadcasted_iota(jnp.int32, peak_ref.shape, 1) == head,
                    jnp.maximum(peak_ref[...], jnp.max(row_max)),
                    peak_ref[...],
                )
            out_ref[rows, pl.ds(pl.multiple_of(pair * PAIR, PAIR), PAIR)] = total.astype(bf16)


def attend_forward(normed, qkv_w, cosine, sine, row_blocks, col_blocks):
    length = normed.shape[0]
    pairs = qkv_w.shape[1] // (3 * PAIR)
    shape = jax.ShapeDtypeStruct
    return pl.pallas_call(
        attend_forward_kernel,
        out_shape=(
            shape((pairs, length, PAIR), bf16),
            shape((pairs, length, PAIR), bf16),
            shape((pairs, length, PAIR), bf16),
            shape((length, pairs * PAIR), bf16),
            shape((length, 128), f32),
            shape((8, 128), f32),
        ),
        in_specs=[vmem] * 6,
        out_specs=tuple([vmem] * 6),
        compiler_params=pltpu.CompilerParams(vmem_limit_bytes=56 * 1024 * 1024),
        cost_estimate=pl.CostEstimate(
            flops=16 * pairs * length * length * PAIR + 2 * normed.size * qkv_w.shape[1], bytes_accessed=100_000_000,
            transcendentals=2 * pairs * length * length,
        ),
        name="attend_forward",
    )(normed, qkv_w, cosine, sine, row_blocks, col_blocks)


def attend_backward_kernel(
    first_head, q_ref, k_ref, v_ref, grad_ref, lse_ref, cos_ref, sin_ref, row_ref, col_ref, normed_ref,
    out_ref, weight_ref, dk_ref, dv_ref,
):
    length = q_ref.shape[0]
    dk_ref[...] = jnp.zeros_like(dk_ref)
    dv_ref[...] = jnp.zeros_like(dv_ref)
    lane = lax.broadcasted_iota(jnp.int32, (BLOCK, 128), 1)
    for t in range(length // BLOCK):
        q0 = t * BLOCK
        rows = pl.ds(q0, BLOCK)
        cols = min(q0 + 2 * BLOCK, length)

        def one_head(sub, dq):
            mask = head_mask((BLOCK, PAIR), sub)
            query = jnp.where(mask, q_ref[rows, :], 0).astype(bf16)
            grad = jnp.where(mask, grad_ref[rows, :], 0).astype(bf16)
            lse = jnp.sum(
                jnp.where(lane == first_head + sub, lse_ref[rows, :], 0.0), 1, keepdims=True
            )
            scores = masked_scores(query, k_ref, row_ref, col_ref, q0, cols)
            attention = jnp.exp(scores - lse)
            grad_attention = contract(grad, v_ref[0:cols, :], 1, 1)
            weighted = attention * grad_attention
            centre = jnp.sum(weighted, 1, keepdims=True)
            grad_scores = (weighted - attention * centre).astype(bf16)
            dv_ref[0:cols, :] += contract(attention.astype(bf16), grad, 0, 0)
            dk_ref[0:cols, :] += contract(grad_scores, query, 0, 0)
            return jnp.where(mask, contract(grad_scores, k_ref[0:cols, :], 1, 0), dq)

        dq = lax.fori_loop(0, 2, one_head, jnp.zeros((BLOCK, PAIR), f32)) * HEAD_DIM ** (-0.5)
        out_ref[rows, 0:PAIR] = (dq * cos_ref[rows, :] - swap_halves(dq) * sin_ref[rows, :]).astype(bf16)
    for t in range(length // BLOCK):
        rows = pl.ds(t * BLOCK, BLOCK)
        dk = dk_ref[rows, :]
        out_ref[rows, PAIR : 2 * PAIR] = (
            dk * cos_ref[rows, :] - swap_halves(dk) * sin_ref[rows, :]
        ).astype(bf16)
        out_ref[rows, 2 * PAIR : 3 * PAIR] = dv_ref[rows, :].astype(bf16)
    side = 256

    @pl.loop(0, normed_ref.shape[1] // side)
    def _(k):
        span = pl.ds(pl.multiple_of(k * side, side), side)
        weight_ref[span, :] = contract(normed_ref[:, span], out_ref[...], 0, 0).astype(bf16)


def attend_backward(pair, query, key, value, grad, lse, cosine, sine, row_blocks, col_blocks, normed):
    length, width = normed.shape
    heads = pl.BlockSpec((None, length, PAIR), lambda _: (pair, 0, 0))
    return pl.pallas_call(
        functools.partial(attend_backward_kernel, 2 * pair),
        grid=(1,),
        out_shape=(
            jax.ShapeDtypeStruct((length, 3 * PAIR), bf16), jax.ShapeDtypeStruct((width, 3 * PAIR), bf16),
        ),
        in_specs=[heads] * 3 + [pl.BlockSpec((length, PAIR), lambda _: (0, pair))] + [vmem] * 6,
        out_specs=(vmem, vmem),
        scratch_shapes=[pltpu.VMEM((length, PAIR), f32), pltpu.VMEM((length, PAIR), f32)],
        compiler_params=pltpu.CompilerParams(vmem_limit_bytes=56 * 1024 * 1024),
        cost_estimate=pl.CostEstimate(
            flops=40 * length * length * PAIR + 6 * length * width * PAIR, bytes_accessed=100_000_000,
            transcendentals=2 * length * length,
        ),
        name="attend_backward",
    )(query, key, value, grad, lse, cosine, sine, row_blocks, col_blocks, normed)


def bit_of(index, bit):
    return lax.rem(lax.div(index, bit), 2)


def flip_bit(index, bit):
    return index + bit - 2 * bit * bit_of(index, bit)


def team_mate(me, bits, offset):
    device, place = me, 0
    for k, bit in enumerate(bits):
        moved = (offset >> k) % 2
        place = place + lax.rem(bit_of(me, bit) + moved, 2) * (1 << k)
        device = flip_bit(device, bit) if moved else device
    return device, place


class Links:

    def __init__(self, send_sems, recv_sems):
        self.send_sems, self.recv_sems = send_sems, recv_sems

    def copy(self, slot, src, dst, device):
        return pltpu.make_async_remote_copy(
            src_ref=src, dst_ref=dst, send_sem=self.send_sems.at[slot],
            recv_sem=self.recv_sems.at[slot], device_id=(device,), device_id_type=MESH,
        )


def greet(partners):
    barrier = pltpu.get_barrier_semaphore()
    for partner in partners:
        pl.semaphore_signal(barrier, inc=1, device_id=(partner,), device_id_type=MESH)
    pl.semaphore_wait(barrier, len(partners))


def spread_block(bits, cut, own_ref, out_ref, links, local_sem):
    core, first, second = bits
    me = lax.axis_index(AXIS)
    sibling, next_a, next_b = (flip_bit(me, bit) for bit in bits)
    block = own_ref.shape[0]
    in_a, in_b = bit_of(me, first), bit_of(me, second)
    spans = {None: (0, block), 0: (0, cut), 1: (cut, block - cut)}

    def rows(flip_a, flip_b, part):
        place = bit_of(me, core)
        place = place + 2 * lax.rem(in_a + flip_a, 2) + 4 * lax.rem(in_b + flip_b, 2)
        start, size = spans[part]
        return pl.ds(pl.multiple_of(place * block + start, 16), size)

    def passed(slot, where, device):
        return links.copy(slot, out_ref.at[where], out_ref.at[where], device)

    def first_hand(slot, part, device):
        start, size = spans[part]
        return links.copy(slot, own_ref.at[pl.ds(start, size)], out_ref.at[rows(0, 0, part)], device)

    makers = {
        0: lambda: first_hand(0, 0, next_a),
        1: lambda: first_hand(1, 1, next_b),
        2: lambda: first_hand(2, 1, next_a),
        3: lambda: first_hand(3, 0, next_b),
        4: lambda: links.copy(4, own_ref, out_ref.at[rows(0, 0, None)], sibling),
        5: lambda: passed(5, rows(1, 0, 0), next_b),
        6: lambda: passed(6, rows(1, 0, 0), sibling),
        7: lambda: passed(7, rows(0, 1, 1), next_a),
        8: lambda: passed(8, rows(0, 1, 1), sibling),
        9: lambda: passed(9, rows(1, 0, 1), sibling),
        10: lambda: passed(10, rows(0, 1, 0), sibling),
        11: lambda: passed(11, rows(1, 1, 0), sibling),
        12: lambda: passed(12, rows(1, 1, 1), sibling),
    }
    needs = {0: 0, 1: 1, 2: 1, 3: 0, 4: None, 5: 0, 6: 0, 7: 1, 8: 1, 9: 1, 10: 0, 11: 0, 12: 1}
    copies = {slot: make() for slot, make in makers.items() if spans[needs[slot]][1]}
    keep = pltpu.make_async_copy(own_ref, out_ref.at[rows(0, 0, None)], local_sem)

    def begin():
        for slot in range(5):
            if slot in copies:
                copies[slot].start()
        keep.start()

    def hand_on(arrived, *sent):
        def phase():
            if arrived in copies:
                copies[arrived].wait_recv()
                for slot in sent:
                    copies[slot].start()

        return phase

    def finish():
        for slot in (4, 6, 8, 9, 10, 11, 12):
            if slot in copies:
                copies[slot].wait_recv()
        keep.wait()
        for slot in copies:
            copies[slot].wait_send()

    return [
        begin, hand_on(0, 5, 6), hand_on(1, 7, 8), hand_on(2, 9), hand_on(3, 10),
        hand_on(5, 11), hand_on(7, 12), finish,
    ]


def run(phases):
    for phase in phases:
        phase()


SPREAD_COPIES = 13
SUM_COPIES = 10


def sum_block(bits, cut, swapped, product, total, to_core, from_core, chip_sum, arrived, links):
    core = bits[0]
    (first, weight_a), (second, weight_b) = ((bits[2], 4), (bits[1], 2)) if swapped else ((bits[1], 2), (bits[2], 4))
    me = lax.axis_index(AXIS)
    sibling, next_a, next_b = flip_bit(me, core), flip_bit(me, first), flip_bit(me, second)
    block, width = total.shape
    tile = 512

    def place(step, other_core):
        flip_a, flip_b = 1 - step // 2, 1 - step % 2
        return (
            lax.rem(bit_of(me, core) + other_core, 2)
            + weight_a * lax.rem(bit_of(me, first) + flip_a, 2)
            + weight_b * lax.rem(bit_of(me, second) + flip_b, 2)
        )

    low, high = (0, cut), (cut, block - cut)
    landing = range(6) if cut else {1: 0, 3: 1, 4: 2}

    def link(slot, step, span, device):
        return links.copy(slot, chip_sum.at[step, pl.ds(*span)], arrived.at[landing[slot - 4], pl.ds(0, span[1])], device)

    diag_a, diag_b = (link(4, 0, low, next_a) if cut else None), link(5, 0, high, next_b)
    plain_a, plain_b = (link(6, 1, low, next_a) if cut else None), link(7, 2, high, next_b)
    last_a, last_b = link(8, 1, high, next_a), (link(9, 2, low, next_b) if cut else None)

    def core_copy(step):
        return links.copy(step, to_core.at[step], from_core.at[step], sibling)

    def for_sibling():
        @pl.loop(0, 4)
        def _(step):
            @pl.loop(0, width // tile)
            def _(column):
                columns = pl.ds(pl.multiple_of(column * tile, tile), tile)
                to_core[step, :, columns] = product(place(step, 1), columns).astype(bf16)

            core_copy(step).start()

    def for_chip():
        @pl.loop(0, 4)
        def _(step):
            core_copy(step).wait_recv()

            @pl.loop(0, width // tile)
            def _(column):
                columns = pl.ds(pl.multiple_of(column * tile, tile), tile)
                summed = product(place(step, 0), columns) + from_core[step, :, columns].astype(f32)
                total[:, columns] = summed

                @pl.when(step < 3)
                def _():
                    chip_sum[step, :, columns] = summed.astype(bf16)

            @pl.when(step == 0)
            def _():
                if cut:
                    diag_a.start()
                diag_b.start()

            @pl.when(step == 1)
            def _():
                if cut:
                    plain_a.start()

            @pl.when(step == 2)
            def _():
                plain_b.start()

    def add(step, span, slot):
        rows = pl.ds(*span)
        chip_sum[step, rows, :] = (
            chip_sum[step, rows, :].astype(f32) + arrived[landing[slot], 0 : span[1], :].astype(f32)
        ).astype(bf16)

    def take(span, slot):
        total[pl.ds(*span), :] += arrived[landing[slot], 0 : span[1], :].astype(f32)

    def hand_on():
        if cut:
            diag_a.wait_recv()
            add(2, low, 0)
            last_b.start()
        diag_b.wait_recv()
        add(1, high, 1)
        last_a.start()

    def finish():
        if cut:
            plain_a.wait_recv()
            take(low, 2)
        plain_b.wait_recv()
        take(high, 3)
        if cut:
            last_b.wait_recv()
            take(low, 5)
        last_a.wait_recv()
        take(high, 4)

        @pl.loop(0, 4)
        def _(step):
            core_copy(step).wait_send()

        for copy in (diag_a, diag_b, plain_a, plain_b, last_a, last_b):
            if copy is not None:
                copy.wait_send()

    return for_sibling, for_chip, hand_on, finish


def sum_scratch(block, width, cut):
    return [
        pltpu.VMEM((block, width), f32),
        pltpu.VMEM((4, block, width), bf16),
        pltpu.VMEM((4, block, width), bf16),
        pltpu.VMEM((3, block, width), bf16),
        pltpu.VMEM((6 if cut else 3, block - cut, width), bf16),
        pltpu.SemaphoreType.DMA((SUM_COPIES,)),
        pltpu.SemaphoreType.DMA((SUM_COPIES,)),
    ]


def spread_scratch(block, width):
    return [
        pltpu.VMEM((block, width), bf16),
        pltpu.SemaphoreType.DMA((SPREAD_COPIES,)),
        pltpu.SemaphoreType.DMA((SPREAD_COPIES,)),
        pltpu.SemaphoreType.DMA,
    ]


def link_params(collective_id):
    return pltpu.CompilerParams(
        collective_id=collective_id, has_side_effects=True, vmem_limit_bytes=60 * 1024 * 1024
    )


def cost(flops, size):
    return pl.CostEstimate(flops=int(flops), bytes_accessed=int(size), transcendentals=0)


def row_scale(values):
    return lax.rsqrt(jnp.mean(values * values, -1, keepdims=True) + epsilon)


def front_kernel(
    team, teams, qkv_moves, ffn_moves, carry_bits, tokens_ref, query_ref, key_ref, value_ref, gate_ref, up_ref, small_ref, *refs,
):
    moved = len(carry_bits)
    (carried, refs) = (refs[0], refs[1:]) if moved else (None, refs)
    (normed_out, weights_out, both_out, small_out), refs = refs[:4], refs[4:]
    carried_out, refs = refs[:moved], refs[moved:]
    (tokens_all, mine, both_mine, gain,
    send_sems, recv_sems, local_sem, swap_send, swap_recv, swap_local, line_send, line_recv, small_send, small_recv,
    both_send, both_recv, both_local, out_sems, *carry_sems) = refs
    me = lax.axis_index(AXIS)
    mate, group = lax.rem(me, team), lax.div(me, team)
    devices = team * teams
    mates = [group * team + lax.rem(mate + k, team) for k in range(1, team)]
    above, below = lax.rem(me + team, devices), lax.rem(me + devices - team, devices)
    ffn_mates = [team_mate(me, (1, 2, 8), k) for k in range(team)]
    rows = mine.shape[1]
    swaps, line, small = Links(swap_send, swap_recv), Links(line_send, line_recv), Links(small_send, small_recv)
    both = Links(both_send, both_recv)
    for i, member, source, target, columns in qkv_moves:
        weight = (query_ref, key_ref, value_ref)[i]
        mine[member, :, target : target + columns] = weight[:, source : source + columns]
    greet(
        mates + [lax.rem(me + k * team, devices) for k in range(1, teams)]
        + [device for device, _ in ffn_mates[4:]]
    )

    def share(place):
        return pl.ds(pl.multiple_of(place * rows, rows), rows)

    swap_copies = [
        swaps.copy(k, mine.at[lax.rem(mate + k + 1, team)], weights_out.at[group, share(mate)], mates[k])
        for k in range(team - 1)
    ]
    crossing = [
        Links(*carry_sems).copy(i, carried, carried_out[i], flip_bit(me, bit)) for i, bit in enumerate(carry_bits)
    ]
    for copy in swap_copies:
        copy.start()
    keep = pltpu.make_async_copy(mine.at[mate], weights_out.at[group, share(mate)], swap_local)
    keep.start()
    small_out[me] = small_ref[...]

    others = [lax.rem(me + k * team, devices) for k in range(1, teams)]
    team_rows = pl.ds(pl.multiple_of(group * team, team), team)
    small_near = [
        small.copy(k, small_out.at[me], small_out.at[me], device) for k, device in enumerate(mates)
    ]
    small_far = [
        small.copy(team + k, small_out.at[team_rows], small_out.at[team_rows], device)
        for k, device in enumerate(others)
    ]
    for copy in small_near:
        copy.start()
    spread = spread_block(
        (1, 2, 4), HALF, tokens_ref, tokens_all, Links(send_sems, recv_sems), local_sem
    )
    for i, member, source, target, columns in ffn_moves:
        both_mine[i * team + member, :, target : target + columns] = (gate_ref, up_ref)[i][:, source : source + columns]

    def passed(slot, shard, device):
        return line.copy(slot, weights_out.at[shard], weights_out.at[shard], device)

    steps = teams - 1

    def up(step):
        return passed(step - 1, group - (step - 1), above)

    def down(step):
        return passed(steps + step - 1, group + (step - 1), below)

    def line_start(step):
        pl.when((group < teams - 1) & (group >= step - 1))(lambda: up(step).start())
        pl.when((group > 0) & (group + step - 1 < teams))(lambda: down(step).start())

    def line_wait(step):
        pl.when(group >= step)(lambda: up(step).wait_recv())
        pl.when(group + step < teams)(lambda: down(step).wait_recv())

    def line_sent(step):
        pl.when((group < teams - 1) & (group >= step - 1))(lambda: up(step).wait_send())
        pl.when((group > 0) & (group + step - 1 < teams))(lambda: down(step).wait_send())

    for copy in small_near:
        copy.wait_recv()
    for copy in small_far:
        copy.start()
    own_place = ffn_mates[0][1]
    both_copies = [
        both.copy(
            i * team + k, both_mine.at[i * team + ffn_mates[k][1]], both_out.at[i * team + own_place], ffn_mates[k][0]
        )
        for i in range(2) for k in range(1, team)
    ]
    for copy in both_copies:
        copy.start()
    both_keep = [
        pltpu.make_async_copy(both_mine.at[i * team + own_place], both_out.at[i * team + own_place], both_local.at[i])
        for i in range(2)
    ]
    for copy in both_keep:
        copy.start()
    for copy in swap_copies:
        copy.wait_recv()
    keep.wait()
    line_start(1)
    spread[0]()
    for copy in crossing:
        copy.start()
    for copy in small_far:
        copy.wait_recv()
    spread[1]()
    spread[2]()
    line_wait(1)
    line_start(2)
    spread[3]()
    spread[4]()
    width = tokens_all.shape[1]
    gains = width // devices
    for d in range(devices):
        gain[:, d * gains : (d + 1) * gains] = small_out[d, 0:1, 0:gains]
    for phase in spread[5:]:
        phase()
    block = tokens_ref.shape[0]

    def normed_copy(k):
        span = pl.ds(pl.multiple_of(k * block, block), block)
        return pltpu.make_async_copy(tokens_all.at[span], normed_out.at[span], out_sems.at[k])

    def norm_blocks(first, last):
        @pl.loop(first, last)
        def _(k):
            span = pl.ds(pl.multiple_of(k * block, block), block)
            values = tokens_all[span, :].astype(f32)
            tokens_all[span, :] = (values * row_scale(values) * gain[...]).astype(bf16)
            normed_copy(k).start()

    norm_blocks(0, 2)
    for step in range(2, teams):
        line_wait(step)
        if step < steps:
            line_start(step + 1)
        if step == 2:
            norm_blocks(2, team)
    for k in range(team):
        normed_copy(k).wait()
    for copy in both_copies:
        copy.wait_recv()
    for copy in both_keep:
        copy.wait()
    for copy in swap_copies + both_copies:
        copy.wait_send()
    for step in range(1, teams):
        line_sent(step)
    for copy in small_near + small_far:
        copy.wait_send()
    for copy in crossing:
        copy.wait()


def front(tokens, weights, small, teams, qkv_moves, ffn_moves, carried, carry_bits):
    block, width = tokens.shape
    team = 8
    rows, cols = weights[0].shape[0], 3 * width // team
    both_cols = weights[3].shape[1] // team
    devices = team * teams
    dma = pltpu.SemaphoreType.DMA
    shape = jax.ShapeDtypeStruct
    return pl.pallas_call(
        functools.partial(front_kernel, team, teams, qkv_moves, ffn_moves, carry_bits),
        out_shape=(
            shape((team * block, width), bf16),
            shape((teams, team * rows, cols), bf16),
            shape((2 * team, rows, both_cols), bf16),
            shape((devices,) + small.shape, f32),
        ) + tuple(shape(carried[0].shape, bf16) for _ in carry_bits),
        in_specs=[vmem] * 7 + [anywhere] * len(carried),
        out_specs=(anywhere, anywhere, anywhere, vmem) + (anywhere,) * len(carry_bits),
        scratch_shapes=[
            pltpu.VMEM((team * block, width), bf16), pltpu.VMEM((team, rows, cols), bf16),
            pltpu.VMEM((2 * team, rows, both_cols), bf16), pltpu.VMEM((1, width), f32),
        ]
        + spread_scratch(block, width)[1:]
        + [dma((team - 1,)), dma((team - 1,)), dma, dma((2 * teams,)), dma((2 * teams,)), dma((team + teams,)), dma((team + teams,))]
        + [dma((2 * team,)), dma((2 * team,)), dma((2,)), dma((team,))]
        + [dma((1,))] * (2 * len(carried)),
        compiler_params=link_params(1),
        cost_estimate=cost(0, 200e6),
        name="front",
    )(tokens, *weights, small, *carried)


def branch_kernel(
    carry, swap_bits, spread_bits, left_ref, right_ref, residual_ref, gain_ref, peak_ref, *refs,
):
    if carry:
        (both_own, both_y, both_z, down_own, down_y), refs = refs[:5], refs[5:]
        (h2_ref, out_ref, peak_out, gate_full, up_full, down_full), refs = refs[:6], refs[6:]
        (landed, together, swap_send, swap_recv, own, send_sems, recv_sems, local_sem,
         peak_in, peak_send, peak_recv, carry_send, carry_recv, carry_local) = refs
    else:
        (h2_ref, out_ref, peak_out), refs = refs[:3], refs[3:]
        (landed, together, swap_send, swap_recv, own, send_sems, recv_sems, local_sem,
         peak_in, peak_send, peak_recv) = refs
    me = lax.axis_index(AXIS)
    team, block, _ = landed.shape
    bits = [1 << k for k in range(peak_in.shape[0])]
    mates = [team_mate(me, swap_bits, k) for k in range(team)]
    greet([device for device, _ in mates[1:]] + [flip_bit(me, bit) for bit in bits if bit not in swap_bits])
    own_place = mates[0][1]

    def rows_at(place):
        return pl.ds(pl.multiple_of(place * block, block), block)

    swap_copies = [
        Links(swap_send, swap_recv).copy(k, left_ref.at[rows_at(mates[k][1])], landed.at[own_place], mates[k][0])
        for k in range(1, team)
    ]
    for copy in swap_copies:
        copy.start()
    peaks = Links(peak_send, peak_recv)

    def peak_copy(k):
        return peaks.copy(k, peak_out, peak_in.at[k], flip_bit(me, bits[k]))

    def peak_step(k):
        if k:
            peak_copy(k - 1).wait()
            peak_out[...] = jnp.maximum(peak_out[...], peak_in[k - 1])
        if k < len(bits):
            peak_copy(k).start()

    if carry:
        carried = Links(carry_send, carry_recv)
        high, middle = bit_of(me, 16), bit_of(me, 4)
        by_y, by_z = flip_bit(me, 4), flip_bit(me, 16)

        def rows_of(part, flip_z, flip_y):
            z, y = lax.rem(high + flip_z, 2), lax.rem(middle + flip_y, 2)
            return pl.ds(pl.multiple_of(z * 16 + part * 8 + y * 4, 4), 4)

        early = both_z.shape[0] // 4

        def piece(source, half):
            return source.at[pl.ds(half * 4, 4)]

        def placed(half, flips):
            return (gate_full, up_full)[half // 2].at[rows_of(half % 2, *flips)]

        def unit(flip_z, flip_y):
            return lax.rem(high + flip_z, 2) * 2 + lax.rem(middle + flip_y, 2)

        kept = []
        for source, flips, halves in ((both_own, (0, 0), 4), (both_y, (0, 1), 4), (both_z, (1, 0), early)):
            for half in range(halves):
                kept.append((piece(source, half), placed(half, flips)))
        kept.append((down_own, down_full.at[unit(0, 0)]))
        kept.append((down_y, down_full.at[unit(0, 1)]))
        kept = [pltpu.make_async_copy(a, b, carry_local.at[i]) for i, (a, b) in enumerate(kept)]
        up_z = [
            carried.copy(half, piece(both_own, half), placed(half, (0, 0)), by_z) for half in range(early, 4)
        ]
        early_yz = [
            carried.copy(4 + half, piece(both_z, half), placed(half, (1, 0)), by_y) for half in range(early)
        ]
        up_yz = [
            carried.copy(4 + half, placed(half, (1, 0)), placed(half, (1, 0)), by_y) for half in range(early, 4)
        ]
        down_z = carried.copy(8, down_own, down_full.at[unit(0, 0)], by_z)
        for copy in up_z + kept:
            copy.start()

    peak_out[...] = peak_ref[...]
    peak_step(0)
    landed[own_place] = left_ref[rows_at(own_place), :]
    for copy in swap_copies:
        copy.wait_recv()
    if carry:
        for copy in early_yz:
            copy.start()
    share = landed.shape[2]
    for b in range(team):
        together[:, b * share : (b + 1) * share] = landed[b]
    tile = 512

    @pl.loop(0, own.shape[1] // tile)
    def _(column):
        columns = pl.ds(pl.multiple_of(column * tile, tile), tile)
        h2_ref[:, columns] = residual_ref[:, columns].astype(f32) + contract(
            together[...], right_ref[:, columns], 1, 0
        )

    h2 = h2_ref[...]
    own[...] = (h2 * row_scale(h2) * gain_ref[...]).astype(bf16)
    spread = spread_block(spread_bits, BRANCH_CUT, own, out_ref, Links(send_sems, recv_sems), local_sem)
    spread[0]()
    if carry:
        for over, on in zip(up_z, up_yz):
            over.wait_recv()
            on.start()
        down_z.start()
    for k, phase in enumerate(spread[1:-1]):
        phase()
        if k < len(bits):
            peak_step(k + 1)
    for k in range(len(spread) - 2, len(bits)):
        peak_step(k + 1)
    spread[-1]()
    for copy in swap_copies:
        copy.wait_send()
    if carry:
        for copy in kept:
            copy.wait()
        for copy in early_yz + up_yz + [down_z]:
            copy.wait_recv()
        for copy in up_z + early_yz + up_yz + [down_z]:
            copy.wait_send()


def branch(left, right, residual, gain, peak, carry, swap_bits, spread_bits, bit_count):
    block, width = residual.shape
    dma = pltpu.SemaphoreType.DMA
    shape = jax.ShapeDtypeStruct
    out_shape = [shape((block, width), f32), shape((8 * block, width), bf16), shape((8, 128), f32)]
    scratch = [pltpu.VMEM((8, block, left.shape[1]), bf16), pltpu.VMEM((block, width), bf16), dma((8,)), dma((8,))]
    scratch += spread_scratch(block, width)
    scratch += [pltpu.VMEM((bit_count, 8, 128), f32), dma((bit_count,)), dma((bit_count,))]
    if carry:
        out_shape += [
            shape((32,) + carry[0].shape[1:], bf16), shape((32,) + carry[0].shape[1:], bf16),
            shape((4,) + carry[3].shape, bf16),
        ]
        scratch += [dma((9,)), dma((9,)), dma((14,))]
    return pl.pallas_call(
        functools.partial(branch_kernel, bool(carry), swap_bits, spread_bits),
        out_shape=tuple(out_shape),
        in_specs=[vmem] * (5 + len(carry)),
        out_specs=tuple([vmem, anywhere, vmem] + [anywhere] * (len(out_shape) - 3)),
        scratch_shapes=scratch,
        compiler_params=link_params(2),
        cost_estimate=cost(16 * block * left.shape[1] * width, 300e6),
        name="attention_branch",
    )(left, right, residual, gain, peak, *carry)


def norm_back(values, gain, upstream):
    scaled = upstream * gain
    scale = row_scale(values)
    inner = jnp.mean(scaled * values, -1, keepdims=True)
    return scale * scaled - scale * scale * scale * values * inner


def ffn_back_kernel(
    cross, sum_bits, swap_bits, gate_ref, up_ref, gate_w_ref, up_w_ref, normed_ref, out_w_ref, h2_ref, cot_ref, gain_ref, *refs,
):
    (part_ref, over_ref, refs) = (refs[0], refs[1], refs[2:]) if cross else (None, None, refs)
    (residual_ref, branch_ref, heads_out, d_up_out, d_gate_own), refs = refs[:5], refs[5:]
    (d_gate_in, part_in, over_in), refs = (refs[:3], refs[3:]) if cross else ((None,) * 3, refs)
    (total, to_core, from_core, chip_sum, arrived, sum_send, sum_recv,
     swap_send, swap_recv, local_sem, stage, stage_sems, own_sems, *more) = refs
    if cross:
        cross_send, cross_recv = more
        crossing = Links(cross_send, cross_recv)
    else:
        (stage_gate,) = more
    me = lax.axis_index(AXIS)
    block, width = total.shape
    team = 1 << len(swap_bits)
    mates = [team_mate(me, swap_bits, k) for k in range(team)]
    greet(
        [device for device, _ in mates[1:]] + [flip_bit(me, bit) for bit in sum_bits if bit not in swap_bits]
        + ([flip_bit(me, 16)] if cross else [])
    )

    def product(place, columns):
        rows = pl.ds(pl.multiple_of(place * block, block), block)
        return contract(gate_ref[rows, :], gate_w_ref[columns, :], 1, 1) + contract(
            up_ref[rows, :], up_w_ref[columns, :], 1, 1
        )

    side, columns_ff = stage.shape[1:]
    count = width // side
    y_side, by_y = bit_of(me, 4), flip_bit(me, 4)
    if cross:
        part_copy = crossing.copy(count // 2, part_ref, part_in, by_y)
        over_copy = crossing.copy(count // 2 + 1, over_ref, over_in, flip_bit(me, 16))
        part_copy.start()

    def parked(i, part):
        row = i * side
        rows = pl.ds(pl.multiple_of(lax.rem(row, block), 16), side)
        return from_core.at[lax.div(row, block), rows, pl.ds(part * columns_ff, columns_ff)]

    def cross_copy(i):
        return crossing.copy(i, parked(i, 0), d_gate_in.at[i], by_y)

    def own_copy(i):
        return pltpu.make_async_copy(parked(i, 1), d_gate_own.at[i], own_sems.at[i])

    def tile_of(step):
        if not cross:
            return step
        theirs = step < count // 2
        return jnp.where(theirs, 2 * step + 1 - y_side, 2 * step - count + y_side)

    def up_copy(step):
        span = pl.ds(pl.multiple_of(tile_of(step) * side, side), side)
        slot = lax.rem(step, 2)
        return pltpu.make_async_copy(stage.at[slot], d_up_out.at[span], stage_sems.at[slot])

    def gate_copy(step):
        span = pl.ds(pl.multiple_of(step * side, side), side)
        slot = lax.rem(step, 2)
        return pltpu.make_async_copy(stage_gate.at[slot], d_gate_own.at[span], own_sems.at[slot])

    def gradients(first, last):
        @pl.loop(first, last)
        def _(step):
            @pl.when(step >= 2)
            def _():
                up_copy(step - 2).wait()
                if not cross:
                    gate_copy(step - 2).wait()

            columns = normed_ref[:, pl.ds(pl.multiple_of(tile_of(step) * side, side), side)]
            stage[lax.rem(step, 2)] = contract(columns, up_ref[...], 0, 0).astype(bf16)
            up_copy(step).start()
            tile = contract(columns, gate_ref[...], 0, 0).astype(bf16)
            if not cross:
                stage_gate[lax.rem(step, 2)] = tile
                gate_copy(step).start()
                return

            @pl.when(step < count // 2)
            def _():
                parked(step, 0)[...] = tile
                cross_copy(step).start()

            @pl.when(step >= count // 2)
            def _():
                parked(step - count // 2, 1)[...] = tile
                own_copy(step - count // 2).start()

    for_sibling, for_chip, hand_on, finish = sum_block(
        sum_bits, HALF, False, product, total, to_core, from_core, chip_sum, arrived, Links(sum_send, sum_recv)
    )
    for_sibling()
    for_chip()
    if cross:
        over_copy.start()
    gradients(0, 1)
    hand_on()
    gradients(1, count - 2)
    finish()
    residual = cot_ref[...].astype(f32) + norm_back(h2_ref[...], gain_ref[...], total[...])
    residual_ref[...] = residual
    branch_ref[...] = residual.astype(bf16)
    share = width // team
    for b in range(team):
        part = slice(b * share, (b + 1) * share)
        to_core[0, :, part] = contract(branch_ref[...], out_w_ref[part, :], 1, 1).astype(bf16)
    own_place = mates[0][1]
    own_rows = pl.ds(pl.multiple_of(own_place * block, block), block)
    def heads_of(place):
        return to_core.at[0, :, pl.ds(pl.multiple_of(place * share, share), share)]

    swap_copies = [
        Links(swap_send, swap_recv).copy(k, heads_of(mates[k][1]), heads_out.at[own_rows], mates[k][0])
        for k in range(1, team)
    ]
    keep = pltpu.make_async_copy(heads_of(own_place), heads_out.at[own_rows], local_sem)
    for copy in swap_copies + [keep]:
        copy.start()
    gradients(count - 2, count)
    for copy in swap_copies:
        copy.wait_recv()
    for copy in swap_copies:
        copy.wait_send()
    keep.wait()
    for step in range(count - 2, count):
        up_copy(step).wait()
        if not cross:
            gate_copy(step).wait()
    if cross:
        part_copy.wait()
        over_copy.wait()

        @pl.loop(0, count // 2)
        def _(i):
            own_copy(i).wait()
            cross_copy(i).wait()


def ffn_back(gate, up, gate_w, up_w, normed, out_w, h2, cot, gain, part, side, sum_bits, swap_bits):
    block, width = h2.shape
    shape = jax.ShapeDtypeStruct
    dma = pltpu.SemaphoreType.DMA
    ff_cols, cross = gate.shape[1], side % 128 == 0
    side = side if cross else 256
    tiles = width // side // 2
    if cross:
        d_gate = (shape((tiles, side, ff_cols), bf16),) * 2 + (shape(part[0].shape, bf16),) * 2
        more = [dma((tiles + 2,)), dma((tiles + 2,))]
    else:
        d_gate, more = (shape((width, ff_cols), bf16),), [pltpu.VMEM((2, side, ff_cols), bf16)]
    return pl.pallas_call(
        functools.partial(ffn_back_kernel, cross, sum_bits, swap_bits),
        out_shape=(
            shape((block, width), f32), shape((block, width), bf16), shape((8 * block, width // 8), bf16),
            shape((width, ff_cols), bf16),
        ) + d_gate,
        in_specs=[vmem] * 9 + [anywhere] * len(part),
        out_specs=(vmem, vmem) + (anywhere,) * (2 + len(d_gate)),
        scratch_shapes=sum_scratch(block, width, HALF)
        + [dma((8,)), dma((8,)), dma]
        + [pltpu.VMEM((2, side, ff_cols), bf16), dma((2,)), dma((tiles,))]
        + more,
        compiler_params=link_params(3),
        cost_estimate=cost(96 * block * ff_cols * width, 200e6),
        name="ffn_back",
    )(gate, up, gate_w, up_w, normed, out_w, h2, cot, gain, *part)


def last_sums_kernel(
    carry_bits, sum_bits, ffn_bits, left_ref, other_ref, right_ref, tokens_ref, gain_ref, residual_ref, hidden_ref,
    down_ref, h2_ref, gate_ref, *refs,
):
    moved = len(carry_bits)
    carried, (out_ref, mixed_ref, gate_out), refs = refs[:moved], refs[moved : moved + 3], refs[moved + 3 :]
    carried_out, scratch = refs[:moved], refs[moved:]
    if moved:
        carry_sems, scratch = scratch[-2:], scratch[:-2]
    (swap_send, swap_recv, swap_local), scratch = scratch[-3:], scratch[:-3]
    count = len(scratch) // 2
    me = lax.axis_index(AXIS)
    total, ffn_total = scratch[0], scratch[count]
    block = total.shape[0]
    mates = [team_mate(me, ffn_bits, k) for k in range(8)]
    partners = [flip_bit(me, bit) for bit in sum_bits if bit not in ffn_bits]
    greet(partners + [device for device, _ in mates[1:]] + [flip_bit(me, bit) for bit in carry_bits])
    crossing = [
        Links(*carry_sems).copy(i, carried[i], carried_out[i], flip_bit(me, bit)) for i, bit in enumerate(carry_bits)
    ]
    for copy in crossing:
        copy.start()
    swaps, own_place = Links(swap_send, swap_recv), mates[0][1]
    swap_copies = [
        swaps.copy(k, gate_ref.at[mates[k][1]], gate_out.at[own_place], mates[k][0]) for k in range(1, 8)
    ]
    keep = pltpu.make_async_copy(gate_ref.at[own_place], gate_out.at[own_place], swap_local)

    def rows_of(place):
        return pl.ds(pl.multiple_of(place * block, block), block)

    def product(place, columns):
        rows = rows_of(place)
        middle = left_ref.shape[1]
        return contract(left_ref[rows, :], right_ref[columns, 0:middle], 1, 1) + contract(
            other_ref[rows, :], right_ref[columns, middle : 2 * middle], 1, 1
        )

    def ffn_product(place, columns):
        return contract(hidden_ref[rows_of(place), :], down_ref[:, columns], 1, 0)

    first = sum_block(sum_bits, LAST_CUT, False, product, *scratch[: count - 2], Links(*scratch[count - 2 : count]))
    second = sum_block(ffn_bits, HALF, True, ffn_product, *scratch[count:-2], Links(*scratch[-2:]))
    run(first[:2])
    run(second[:2])
    for copy in swap_copies + [keep]:
        copy.start()
    for one, other in zip(first[2:], second[2:]):
        one()
        other()
    out_ref[...] = residual_ref[...] + norm_back(
        tokens_ref[...].astype(f32), gain_ref[...], total[...]
    )
    mixed_ref[...] = (h2_ref[...] + ffn_total[...]).astype(bf16)
    for copy in swap_copies:
        copy.wait_recv()
    for copy in swap_copies:
        copy.wait_send()
    keep.wait()
    for copy in crossing:
        copy.wait()


def last_sums(left, other, right, tokens, gain, residual, hidden, down, h2, d_gate, carry, carry_bits, sum_bits, ffn_bits):
    block, width = tokens.shape
    return pl.pallas_call(
        functools.partial(last_sums_kernel, carry_bits, sum_bits, ffn_bits),
        out_shape=(
            jax.ShapeDtypeStruct((block, width), f32), jax.ShapeDtypeStruct((block, width), bf16),
            jax.ShapeDtypeStruct(d_gate.shape, bf16),
        ) + tuple(jax.ShapeDtypeStruct(x.shape, x.dtype) for x in carry),
        in_specs=[vmem] * 9 + [anywhere] * (1 + len(carry)),
        out_specs=(vmem, vmem, anywhere) + (anywhere,) * len(carry),
        scratch_shapes=sum_scratch(block, width, LAST_CUT) + sum_scratch(block, width, HALF)
        + [pltpu.SemaphoreType.DMA((8,)), pltpu.SemaphoreType.DMA((8,)), pltpu.SemaphoreType.DMA]
        + [pltpu.SemaphoreType.DMA((1,))] * (2 * len(carry)),
        compiler_params=link_params(4),
        cost_estimate=cost(16 * block * right.size // 8, 300e6),
        name="last_sums",
    )(left, other, right, tokens, gain, residual, hidden, down, h2, d_gate, *carry)


def exchange_kernel(teams, sources, *refs):
    mine, landed, (send_sems, recv_sems, local_sems) = refs[:sources], refs[sources : 2 * sources], refs[2 * sources :]
    me = lax.axis_index(AXIS)
    members = mine[0].shape[0]
    links = Links(send_sems, recv_sems)
    greeted = {}
    for bits in teams:
        for k in range(1, members):
            device, _ = team_mate(me, bits, k)
            greeted[tuple(sorted(bit for j, bit in enumerate(bits) if (k >> j) % 2))] = device
    greet(list(greeted.values()))
    copies, kept = [], []
    for i, (source, target, bits) in enumerate(zip(mine, landed, teams)):
        own = team_mate(me, bits, 0)[1]
        kept.append(pltpu.make_async_copy(source.at[own], target.at[own], local_sems.at[i]))
        for k in range(1, members):
            device, place = team_mate(me, bits, k)
            copies.append(links.copy(i * members + k, source.at[place], target.at[own], device))
    for copy in copies + kept:
        copy.start()
    for copy in copies:
        copy.wait()
    for copy in kept:
        copy.wait()


def exchange(parts, teams):
    dma = pltpu.SemaphoreType.DMA
    slots = len(parts) * parts[0].shape[0]
    return pl.pallas_call(
        functools.partial(exchange_kernel, teams, len(parts)),
        out_shape=tuple(jax.ShapeDtypeStruct(part.shape, part.dtype) for part in parts),
        in_specs=[vmem] * len(parts),
        out_specs=tuple([vmem] * len(parts)),
        scratch_shapes=[dma((slots,)), dma((slots,)), dma((len(parts),))],
        compiler_params=link_params(5),
        cost_estimate=cost(1e6, 40e6),
        name="exchange",
    )(*parts)


def home_kernel(places, gain_of, sources, *refs):
    count = len(places)
    kinds = max(gain_of) + 1
    parts, weights, gains = refs[:sources], refs[sources : sources + count], refs[sources + count : sources + count + kinds]
    outs, gain_outs = refs[-count - kinds : -kinds], refs[-kinds:]
    totals = [jnp.zeros(gain.shape, f32) for gain in gains]
    for i, (out, weight) in enumerate(zip(outs, weights)):
        for source, member, first, target, columns in places[i]:
            out[:, target : target + columns] = parts[source][member, :, first : first + columns].astype(f32)
        for first in range(0, out.shape[1], 1024):
            product = out[:, first : first + 1024] * weight[:, first : first + 1024].astype(f32)
            totals[gain_of[i]] += jnp.sum(product, 1, keepdims=True)
    for gain, total, out in zip(gains, totals, gain_outs):
        out[...] = jnp.broadcast_to(total / gain[...], (out.shape[1], 128)).T[0:1, :]


def home(parts, weights, gains, gain_of, places):
    shape = jax.ShapeDtypeStruct
    count = len(weights)
    gains = [gain.astype(f32).reshape(-1, 1) for gain in gains]
    return pl.pallas_call(
        functools.partial(home_kernel, places, gain_of, len(parts)),
        out_shape=tuple(shape(w.shape, f32) for w in weights) + tuple(shape((1, g.shape[0]), f32) for g in gains),
        in_specs=[vmem] * (len(parts) + count + len(gains)),
        out_specs=tuple([vmem] * (count + len(gains))),
        compiler_params=pltpu.CompilerParams(vmem_limit_bytes=40 * 1024 * 1024),
        cost_estimate=cost(1e6, 30e6),
        name="home",
    )(*parts, *weights, *gains)


def body(
    tokens, block_of, clip_limit, norm_attn, w_query, w_key, w_value, w_out,
    norm_ffn, w_gate, w_up, w_down, cotangent,
):
    tok_rows, width = tokens.shape
    devices = lax.axis_size(AXIS)
    team = SEQ // tok_rows
    teams = devices // team
    head_total = width // HEAD_DIM
    heads = head_total // team
    head_cols = heads * HEAD_DIM
    ff_rows = w_down.shape[0]
    weight_rows = w_gate.shape[0]
    ff_cols = w_gate.shape[1] // team
    device = lax.axis_index(AXIS)
    mate = device % team
    bit_count = devices.bit_length() - 1
    attn_bits, ffn_bits = (1, 2, 4), (1, 2, 8)
    data_bits = [4] + [1 << k for k in range(4, bit_count)]
    in_team = [[g * team + b for b in range(team)] for g in range(teams)]
    across = [[g * team + b for g in range(teams)] for b in range(team)]
    ffn_team = [
        [g * 16 + z * 8 + y * 4 + c for z in range(2) for c in range(4)]
        for g in range(devices // 16)
        for y in range(2)
    ]

    def flip(x, bit):
        return lax.ppermute(x, AXIS, [(i, i ^ bit) for i in range(devices)])

    def gather_across(x):
        return lax.all_gather(x, AXIS, axis=0, tiled=True, axis_index_groups=across)

    def scatter_across(x):
        return lax.psum_scatter(
            x.astype(bf16), AXIS, scatter_dimension=0, tiled=True, axis_index_groups=across
        )

    def dim_of(bit):
        return bit_count - bit.bit_length()

    def data_pieces(x):
        pieces = {0: x}
        for bit in reversed(data_bits):
            for key in list(pieces):
                pieces[key | bit] = flip(pieces[key], bit)
        return pieces

    def place_pieces(pieces, dims, shape):
        total = jnp.zeros(shape, bf16)
        for key, piece in pieces.items():
            start = [0] * len(shape)
            size = list(shape)
            for bit in data_bits:
                start[dims[bit]] = ((device // bit) + (1 if key & bit else 0)) % 2
                size[dims[bit]] = 1
            total = lax.dynamic_update_slice(total, piece.reshape(size), start)
        return total

    def after_bit(dims, bit):
        return {b: d - (d > dims[bit]) for b, d in dims.items() if b != bit}

    def data_sum(x, dims, bits):
        for bit in bits:
            mine = (device // bit) % 2
            keep = lax.dynamic_index_in_dim(x, mine, dims[bit], False)
            sent = flip(lax.dynamic_index_in_dim(x, 1 - mine, dims[bit], False), bit)
            x = (keep.astype(f32) + sent.astype(f32)).astype(bf16)
            dims = after_bit(dims, bit)
        return x

    row_dims = {bit: dim_of(bit) for bit in data_bits}
    row_shape = (2,) * bit_count
    unit_dims = {bit: i for i, bit in enumerate(reversed(data_bits))}
    unit_shape = (2,) * len(data_bits)

    def tie(*values):
        return lax.optimization_barrier(values)

    qkv_moves = tuple(
        (i, b, (g * team + b) * HEAD_DIM, (3 * (g // 2) + i) * PAIR + (g % 2) * HEAD_DIM, HEAD_DIM)
        for i in range(3) for g in range(heads) for b in range(team)
    )
    ffn_units = tuple(
        (z * 4 + c, (2 * h + y) * ff_rows, (h * 16 + z * 8 + y * 4 + c) * ff_rows)
        for h in range(devices // 16) for z in range(2) for y in range(2) for c in range(4)
    )
    ffn_moves = tuple(
        (i, member, source, target, ff_rows)
        for i in range(2) for member, target, source in ffn_units
    )
    gain_row = jnp.concatenate([norm_attn, norm_ffn]).astype(f32)
    gain_row = jnp.pad(gain_row, (0, 128 - 2 * weight_rows)).reshape(1, 128)
    block_rows = block_of.astype(f32).reshape(tok_rows // 128, 128)
    small = jnp.concatenate([gain_row, block_rows, jnp.zeros((7 - tok_rows // 128, 128), f32)])
    ahead = data_bits == [4, 16]
    normed_attn, qkv_w, both_mine, gathered, *down_moved = front(
        tokens, (w_query, w_key, w_value, w_gate, w_up), small, teams, qkv_moves, ffn_moves,
        [w_down] if ahead else [], (4,) if ahead else (),
    )
    qkv_w = qkv_w.reshape(width, 3 * head_cols)
    gain_attn = gathered[:, 0, :weight_rows].reshape(1, width)
    gain_ffn = gathered[:, 0, weight_rows : 2 * weight_rows].reshape(1, width)
    blocks = lax.dynamic_slice_in_dim(gathered, device - mate, team, 0)
    blocks = blocks[:, 1 : 1 + tok_rows // 128].astype(jnp.int32).reshape(SEQ)
    row_blocks, col_blocks = blocks.reshape(1, SEQ), blocks.reshape(SEQ, 1)
    if weight_rows == HEAD_DIM:
        both_mine, qkv_w, out_mine = tie(both_mine, qkv_w, gather_across(w_out))
        out_w = lax.all_gather(out_mine, AXIS, axis=0, tiled=True, axis_index_groups=in_team)
    else:
        out_w = lax.all_gather(w_out, AXIS, axis=0, tiled=True)
        out_w = out_w.reshape(heads, team, HEAD_DIM, width).transpose(1, 0, 2, 3).reshape(width, width)

    def whole_rows(mine):
        shape = row_shape + (weight_rows, ff_cols)
        return place_pieces(data_pieces(mine), row_dims, shape).reshape(width, ff_cols)

    cosine, sine = rope_tables(SEQ, PAIR)
    if data_bits == [4, 16]:
        carry = [both_mine, flip(both_mine, 4), flip(both_mine[: 4 * EARLY_HALVES], 16), w_down, *down_moved]
    else:
        carry = []
    query, key, value, attended, lse, peak = attend_forward(
        normed_attn, qkv_w, cosine, sine, row_blocks, col_blocks
    )
    cot_mine = cotangent
    peaks = jnp.where(
        (jnp.arange(head_total) % team) == mate, jnp.repeat(peak[0, :heads], team), -jnp.inf
    )
    peaks = jnp.broadcast_to(jnp.pad(peaks, (0, 128 - head_total))[None], (8, 128))
    if carry:
        carry[1], carry[2], attended, cot_mine = tie(carry[1], carry[2], attended, cotangent)
    after_attn, normed_ffn, peaks, *full = branch(
        attended, out_w, tokens, gain_ffn, peaks, carry, attn_bits, ffn_bits, bit_count
    )
    head_peak = peaks[0, :head_total]
    if carry:
        gate_w, up_w = (w.reshape(width, ff_cols) for w in full[:2])
        z_side, y_side = (device // 16) % 2, (device // 4) % 2
        passed = lax.dynamic_index_in_dim(full[2], (1 - z_side) * 2 + y_side, 0, True)
        down_w = lax.dynamic_update_slice(
            full[2], flip(passed, 4), ((1 - z_side) * 2 + 1 - y_side, 0, 0)
        ).reshape(ff_cols, width)
    else:
        gate_w, up_w = whole_rows(both_mine[:team]), whole_rows(both_mine[team:])
        down_w = place_pieces(
            data_pieces(w_down), unit_dims, unit_shape + (ff_rows, width)
        ).reshape(ff_cols, width)
    gate_pre = contract(normed_ffn, gate_w, 1, 0)
    up_pre = contract(normed_ffn, up_w, 1, 0)
    sigmoid_gate = jax.nn.sigmoid(gate_pre)
    silu_gate = gate_pre * sigmoid_gate
    hidden = (silu_gate * up_pre).astype(bf16)

    team_cot = lax.all_gather(cot_mine, AXIS, axis=0, tiled=True, axis_index_groups=ffn_team)
    d_down = contract(hidden, team_cot, 0, 0).astype(bf16).reshape(unit_shape + (ff_rows, width))
    team_cot, d_down = tie(team_cot, d_down)
    d_hidden = contract(team_cot, down_w, 1, 1)
    grad_gate = (d_hidden * up_pre * sigmoid_gate * (1.0 + gate_pre * (1.0 - sigmoid_gate))).astype(bf16)
    grad_up = (d_hidden * silu_gate).astype(bf16)

    unit_rest, row_rest = after_bit(unit_dims, data_bits[0]), after_bit(row_dims, data_bits[0])
    row_values = (weight_rows, ff_cols)
    crosses = data_bits == [4, 16]
    if crosses:
        y_side, z_side = (device // 4) % 2, (device // 16) % 2
        kept = lax.dynamic_index_in_dim(d_down, y_side, unit_dims[4], False)
        sent = lax.dynamic_index_in_dim(d_down, 1 - y_side, unit_dims[4], False)
        mine, theirs = (lax.dynamic_index_in_dim(kept, z, 0, False) for z in (z_side, 1 - z_side))
        to_mine, to_theirs = (lax.dynamic_index_in_dim(sent, z, 0, False) for z in (z_side, 1 - z_side))
        theirs = (theirs.astype(f32) + flip(to_theirs, 4).astype(f32)).astype(bf16)
        grad_gate, theirs = tie(grad_gate, theirs)
        beside = [to_mine, theirs]
    else:
        beside = []
    d_residual, branch_mine, grad_attended, d_up, *d_gate = ffn_back(
        grad_gate, grad_up, gate_w, up_w, normed_ffn, out_w, after_attn, cotangent, gain_ffn, beside, 4 * weight_rows,
        ffn_bits, attn_bits,
    )
    if crosses:
        d_down = mine.astype(f32) + d_gate[2].astype(f32) + d_gate[3].astype(f32)
        d_gate = (d_gate[0].astype(f32) + d_gate[1].astype(f32)).astype(bf16)
        d_gate = d_gate.reshape((2,) * (bit_count - 1) + row_values)
    else:
        d_down = data_sum(d_down, unit_dims, data_bits[:1])
        d_gate = data_sum(d_gate[0].reshape(row_shape + row_values), row_dims, data_bits[:1])
    if not crosses:
        d_down = data_sum(d_down, unit_rest, data_bits[1:]).astype(f32)
    grad_attended, d_gate = tie(grad_attended, d_gate)
    d_gate = data_sum(d_gate, row_rest, data_bits[1:])
    branch_grad = lax.all_gather(branch_mine, AXIS, axis=0, tiled=True, axis_index_groups=in_team)

    def heads_back(pair):
        return attend_backward(
            pair, query, key, value, grad_attended, lse, cosine, sine, row_blocks, col_blocks, normed_attn
        )

    grad_pairs, shares = [None] * (heads // 2), [None] * (heads // 2)
    grad_pairs[0], share = heads_back(0)
    grad_attended, d_gate, d_up, share, branch_grad = tie(grad_attended, d_gate, d_up, share, branch_grad)
    shares[0] = scatter_across(share)
    d_up = data_sum(d_up.reshape(row_shape + row_values), row_dims, data_bits[:1])
    for p in range(1, heads // 2):
        grad_pairs[p], share = heads_back(p)
        grad_pairs[p], share, d_up = tie(grad_pairs[p], share, d_up)
        shares[p] = scatter_across(share)
    sent, sent_bits = [], ()
    if crosses:
        kept_up = lax.dynamic_index_in_dim(d_up, z_side, row_rest[16], False)
        sent, sent_bits = [lax.dynamic_index_in_dim(d_up, 1 - z_side, row_rest[16], False)], (16,)
        kept_up, sent[0] = (d.reshape(team, weight_rows, ff_cols) for d in (kept_up, sent[0]))
    else:
        d_up = data_sum(d_up, row_rest, data_bits[1:])
    grad_pairs[0], shares[0] = tie(grad_pairs[0], shares[0])
    d_gate = d_gate.reshape(team, weight_rows, ff_cols)
    d_tokens, mixed, d_gate, *landed = last_sums(
        *grad_pairs, qkv_w, tokens, gain_attn, d_residual, hidden, down_w, after_attn, d_gate, sent, sent_bits,
        attn_bits, ffn_bits,
    )
    if crosses:
        d_up = (kept_up.astype(f32) + landed[0].astype(f32)).astype(bf16)
    d_tokens, attended = tie(d_tokens, attended)
    out_part = contract(attended, branch_grad, 0, 0)
    if weight_rows == HEAD_DIM:
        d_out = scatter_across(out_part).astype(f32)
    else:
        spread = jnp.where(
            (jnp.arange(team) == mate)[None, :, None, None],
            out_part.reshape(heads, 1, HEAD_DIM, width), 0.0,
        ).reshape(width, width)
        d_out = lax.psum_scatter(spread, AXIS, scatter_dimension=0, tiled=True)
    places = [[], [], []]
    for i, b, source, target, columns in qkv_moves:
        places[i].append((target // (3 * PAIR), b, target % (3 * PAIR), source, columns))
    places += [
        [(heads // 2 + i, member, target, source, ff_rows) for member, target, source in ffn_units] for i in range(2)
    ]
    shares = [share.reshape(team, weight_rows, 3 * PAIR) for share in shares]
    *shares, d_up = exchange(
        shares + [d_up.reshape(team, weight_rows, ff_cols)], (attn_bits,) * (heads // 2) + (ffn_bits,)
    )
    d_query, d_key, d_value, d_gate, d_up, d_norm_attn, d_norm_ffn = home(
        shares + [d_gate, d_up], (w_query, w_key, w_value, w_gate, w_up), (norm_attn, norm_ffn), (0, 0, 0, 1, 1),
        tuple(tuple(p) for p in places),
    )
    d_norm_attn, d_norm_ffn = d_norm_attn[0], d_norm_ffn[0]
    clip_value = clip_limit.astype(f32)
    factor = jnp.sqrt(clip_value / jnp.maximum(head_peak, clip_value))
    factors = jnp.repeat(factor, HEAD_DIM)[None, :]
    clipped_query = (w_query.astype(f32) * factors).astype(bf16)
    clipped_key = (w_key.astype(f32) * factors).astype(bf16)
    return (
        mixed, d_tokens, d_norm_attn, d_query, d_key, d_value, d_out, d_norm_ffn,
        d_gate, d_up, d_down, head_peak, clipped_query, clipped_key,
    )


def solution(mesh):
    rows, whole = P(AXIS, None), P(AXIS)
    return jax.shard_map(
        body,
        mesh=mesh,
        in_specs=(rows, whole, P(), whole, rows, rows, rows, rows, whole, rows, rows, rows, rows),
        out_specs=(
            rows, rows, whole, rows, rows, rows, rows, whole, rows, rows, rows, P(), rows, rows,
        ),
        check_vma=False,
    )
```
